32 devices in a mesh: node: 8 (over z, y), feat: 4 (over x, core).
Axes of the slice: x: 2, y: 2, z: 4, core: 2. Of those that a mesh axis runs over, the one named last changes fastest.
Arguments:
- features: bfloat16 [4096, 128], P('node', 'feat'), may hold values from -10 to 10
- send_rows: int32 [8, 8, 64], P('node'), may hold values from 0 to 511
- send_count: int32 [8, 8], P('node'), may hold values from 1 to 64, 256 in all within a row
- tile_src: int32 [32, 16], P('node'), may hold values from 0 to 7
- tile_val: bfloat16 [32, 16, 128, 128], P('node'), may hold values from 0 to 0.0009765625
- labels: int32 [4096], P('node'), may hold values from 0 to 171
- w_self1: bfloat16 [128, 1024], P('feat'), may hold values from -0.5 to 0.5
- w_neigh1: bfloat16 [128, 1024], P('feat'), may hold values from -0.5 to 0.5
- w_self2: bfloat16 [1024, 172], P('feat'), may hold values from -0.5 to 0.5
- w_neigh2: bfloat16 [1024, 172], P('feat'), may hold values from -0.1875 to 0.1875
Outputs:
- mean_loss: float32 [], replicated
- grad_self1: float32 [128, 1024], P('feat')
- grad_neigh1: float32 [128, 1024], P('feat')
- grad_self2: float32 [1024, 172], P('feat')
- grad_neigh2: float32 [1024, 172], P('feat')
The draws below stay inside these ranges and needn't reach their ends.
Inputs may be any that keep to these rules, and one draw needn't show every extreme that they name: `send_rows`: row indices within the sending partition's 512 rows. Each row of send_count sums to 256 and holds 64 at least once. `tile_src`: block numbers of the destination partition's source rows: numbers below 4 name its own rows, the others its halo slots.
All inputs are finite; a program needn't handle non-finite values.
Results may differ from the reference program's by a relative error of at most 0.00095.
The reference program's roundings to bfloat16 on the way count: a program that leaves them out, or rounds other values in their place, can miss the bound.
Values may be sent and summed in bfloat16 or wider, within the bound.
No kernel may reach another device: no remote copies, remote signals or barrier semaphores. Data moves between devices by JAX's collectives and lax.ppermute only.
A program may use at most 64 MiB of HBM per device.

```python
import math
import jax
import jax.numpy as jnp
import numpy as np
from jax import lax

F_IN = 128
HID = 1024
CLASSES = 172
NODE_DEV = 512
CAP = 64
K = 16
NODES = 4096
N_NODE = 8


def draw_features(key, part):
    base = jnp.clip(jax.random.normal(key, (NODES, F_IN), jnp.float32), -4.0, 4.0)
    return base.astype(jnp.bfloat16)


def draw_w_self2(key, part):
    noise = jnp.clip(jax.random.normal(key, (HID, CLASSES), jnp.float32), -4.0, 4.0)
    return (noise * HID ** (-0.5)).astype(jnp.bfloat16)


def place_ends(entries, own_key, low, largest):
    longest = entries.shape.index(max(entries.shape))
    spots = []
    for shift in (0, 1):
        where = [jax.random.randint(jax.random.fold_in(own_key, axis), (), 0, length) for axis, length in enumerate(entries.shape)]
        where[longest] = (where[longest] + shift) % entries.shape[longest]
        spots.append(tuple(where))
    return entries.at[spots[0]].set(low).at[spots[1]].set(largest)


def shard_levels(own_key, dims, shards, low, top_value):
    factor_of, own = 1.0, jax.random.fold_in(own_key, 6)
    for dim, blocks in shards:
        draws = jnp.exp(jax.random.uniform(jax.random.fold_in(own, dim), (blocks,), jnp.float32, low / len(shards), top_value / len(shards)))
        factor_of = factor_of * jnp.repeat(draws, dims[dim] // blocks).reshape([-1 if axis == dim else 1 for axis in range(len(dims))])
    return factor_of


def split_up(amount, total, limit, lean):
    portions = [(1 << 20) // math.isqrt(grade ** lean) + 1 for grade in range(2, amount + 1)]
    surplus, holding = total - limit - (amount - 1), [1] * (amount - 1)
    while surplus > 0:
        free = [i for i in range(amount - 1) if holding[i] < limit]
        whole, remaining = sum([portions[i] for i in free]), surplus
        for i in free:
            more = min(limit - holding[i], max(1, remaining * portions[i] // whole), surplus)
            holding[i] = holding[i] + more
            surplus = surplus - more
    return np.array([limit] + holding)


def uneven(own_key, number_of, total, limit, skew):
    if number_of == 2:
        one = jax.random.randint(own_key, (), max(1, total - limit), min(limit, total - 1) + 1)
        return jnp.stack([one, total - one])
    tallies = jnp.asarray(split_up(number_of, total, limit, skew), jnp.int32)
    pairs = (number_of - 1) // 2
    source_of, taker = tallies[1:1 + 2 * pairs:2], tallies[2:2 + 2 * pairs:2]
    slack = jnp.minimum(source_of - 1, limit - taker)
    moved = jax.random.randint(jax.random.fold_in(own_key, 1), (pairs,), 0, 1 << 20) % (slack + 1)
    tallies = tallies.at[1:1 + 2 * pairs:2].set(source_of - moved).at[2:2 + 2 * pairs:2].set(taker + moved)
    return tallies[jax.random.permutation(jax.random.fold_in(own_key, 2), number_of)]


def centred(stream_key, dims, width, most, shards=(), held_as=jnp.bfloat16):
    factor_of = shard_levels(stream_key, dims, shards, -0.22, 0.18) if shards else 1.0
    entries = jax.random.normal(stream_key, dims, jnp.float32) * width * factor_of
    return jnp.minimum(jnp.maximum(entries, -most), most).astype(held_as)


def setup_inputs(seed: int = 0) -> dict:
    seeds = jax.random.split(jax.random.key(seed), 11)
    return {
        "features": draw_features(jax.random.fold_in(seeds[10], 71), 0),
        "send_rows": place_ends(jax.random.randint(seeds[1], (N_NODE, N_NODE, CAP), 0, NODE_DEV), jax.random.fold_in(seeds[1], 1), 0, NODE_DEV - 1).astype(jnp.int32),
        "send_count": jax.vmap(lambda own: uneven(own, N_NODE, N_NODE * CAP // 2, CAP, 2))(jax.random.split(seeds[2], N_NODE)).reshape((N_NODE, N_NODE)).astype(jnp.int32),
        "tile_src": place_ends(jax.random.randint(seeds[3], (NODES // 128, K), 0, (NODE_DEV + N_NODE * CAP) // 128), jax.random.fold_in(seeds[3], 1), 0, ((NODE_DEV + N_NODE * CAP) // 128) - 1).astype(jnp.int32),
        "tile_val": jnp.clip(0.0009765625 * jax.random.uniform(seeds[4], (NODES // 128, K, 128, 128), jnp.float32) ** shard_levels(seeds[4], (NODES // 128, K, 128, 128), ((0, 8),), -0.2, 0.2), 0.0, 0.0009765625).astype(jnp.bfloat16),
        "labels": place_ends(jax.random.randint(seeds[5], (NODES,), 0, CLASSES), jax.random.fold_in(seeds[5], 1), 0, CLASSES - 1).astype(jnp.int32),
        "w_self1": centred(seeds[6], (F_IN, HID), F_IN ** -0.5, 0.5, ((0, 4),)),
        "w_neigh1": centred(seeds[7], (F_IN, HID), F_IN ** -0.5, 0.5, ((0, 4),)),
        "w_self2": draw_w_self2(jax.random.fold_in(seeds[10], 71), 0),
        "w_neigh2": centred(seeds[9], (HID, CLASSES), HID ** -0.5, 0.1875, ((0, 4),)),
    }


def halo_rows(values, send_rows, send_count, dest_part):
    slot_total = send_rows.shape[2]
    offsets = (jnp.arange(N_NODE, dtype=jnp.int32) * NODE_DEV)[:, None]
    row_index = (send_rows[:, dest_part, :] + offsets).reshape(-1).astype(jnp.int32)
    picked = jnp.take(values, row_index, axis=0)
    in_use = (jnp.arange(slot_total, dtype=jnp.int32)[None, :] < send_count[:, dest_part][:, None]).reshape(-1)
    return (jnp.where(in_use[:, None], picked, jnp.zeros_like(picked)), row_index, in_use)

def aggregate_all(values, send_rows, send_count, tile_src, tile_val):
    col_count = values.shape[1]
    part_src = tile_src.reshape(N_NODE, NODE_DEV // 128, K)
    part_val = tile_val.reshape(N_NODE, NODE_DEV // 128, K, 128, 128)

    def one_part(packed):
        dest_part, src_ids, tile_block = packed
        own_rows = lax.dynamic_slice_in_dim(values, dest_part * NODE_DEV, NODE_DEV, 0)
        arrived = halo_rows(values, send_rows, send_count, dest_part)[0]
        blocks = jnp.concatenate([own_rows, arrived], 0).reshape(-1, 128, col_count)
        chosen = jnp.take(blocks, src_ids, axis=0)
        summed = jnp.einsum('bkij,bkjh->bih', tile_block.astype(jnp.float32), chosen.astype(jnp.float32), precision=lax.Precision.HIGHEST)
        return summed.reshape(NODE_DEV, col_count).astype(jnp.bfloat16)
    result = lax.map(one_part, (jnp.arange(N_NODE, dtype=jnp.int32), part_src, part_val))
    return result.reshape(N_NODE * NODE_DEV, col_count)

def spread_all(grads, send_rows, send_count, tile_src, tile_val):
    col_count = grads.shape[1]
    src_total = NODE_DEV + N_NODE * CAP
    block_total = src_total // 128
    part_src = tile_src.reshape(N_NODE, NODE_DEV // 128, K)
    part_val = tile_val.reshape(N_NODE, NODE_DEV // 128, K, 128, 128)

    def one_part(carried, packed):
        dest_part, src_ids, tile_block = packed
        own_grads = lax.dynamic_slice_in_dim(grads, dest_part * NODE_DEV, NODE_DEV, 0)
        per_tile = jnp.einsum('bkij,bih->bkjh', tile_block.astype(jnp.float32), own_grads.reshape(-1, 128, col_count).astype(jnp.float32), precision=lax.Precision.HIGHEST)
        one_hot = (src_ids.reshape(-1)[None, :] == jnp.arange(block_total, dtype=jnp.int32)[:, None]).astype(jnp.float32)
        landed = jnp.dot(one_hot, per_tile.reshape(one_hot.shape[1], -1), precision=lax.Precision.HIGHEST, preferred_element_type=jnp.float32).reshape(src_total, col_count)
        own_index = (dest_part * NODE_DEV + jnp.arange(NODE_DEV, dtype=jnp.int32)).astype(jnp.int32)
        carried = carried.at[own_index].add(landed[:NODE_DEV])
        unused, row_index, in_use = halo_rows(grads, send_rows, send_count, dest_part)
        halo_part = jnp.where(in_use[:, None], landed[NODE_DEV:], jnp.zeros_like(landed[NODE_DEV:]))
        carried = carried.at[row_index].add(halo_part)
        return (carried, None)
    start_value = jnp.zeros((N_NODE * NODE_DEV, col_count), jnp.float32)
    result, unused = lax.scan(one_part, start_value, (jnp.arange(N_NODE, dtype=jnp.int32), part_src, part_val))
    return result

def cross_entropy(logits, labels, grad_scale):
    row_max = lax.optimization_barrier(jnp.max(logits, axis=1, keepdims=True))
    shifted = logits - row_max
    total_exp = lax.optimization_barrier(jnp.sum(jnp.exp(shifted), axis=1, keepdims=True))
    classes = jnp.arange(logits.shape[1], dtype=jnp.int32)
    target = (labels[:, None] == classes[None, :]).astype(jnp.float32)
    row_loss = jnp.log(total_exp)[:, 0] - lax.optimization_barrier(jnp.sum(shifted * target, axis=1))
    grads = ((jnp.exp(shifted) / total_exp - target) * grad_scale).astype(jnp.bfloat16)
    return (row_loss, grads)

def reference(features, send_rows, send_count, tile_src, tile_val, labels, w_self1, w_neigh1, w_self2, w_neigh2):
    node_total = N_NODE * NODE_DEV
    agg_one = aggregate_all(features, send_rows, send_count, tile_src, tile_val)
    pre_act = jnp.dot(features, w_self1, preferred_element_type=jnp.float32)
    pre_act = pre_act + jnp.dot(agg_one, w_neigh1, preferred_element_type=jnp.float32)
    activated, pullback = jax.vjp(lambda inner: jax.nn.gelu(inner, approximate=True), pre_act)
    hidden = activated.astype(jnp.bfloat16)
    agg_two = aggregate_all(hidden, send_rows, send_count, tile_src, tile_val)
    logits = jnp.dot(hidden, w_self2, preferred_element_type=jnp.float32)
    logits = logits + jnp.dot(agg_two, w_neigh2, preferred_element_type=jnp.float32)
    grad_scale = float(node_total) ** (-0.5)
    row_loss, dlogits = cross_entropy(logits, labels, grad_scale)
    mean_loss = jnp.sum(row_loss) / node_total
    grad_self2 = jnp.dot(hidden.T, dlogits, preferred_element_type=jnp.float32)
    grad_neigh2 = jnp.dot(agg_two.T, dlogits, preferred_element_type=jnp.float32)
    back_grad = jnp.dot(dlogits, w_neigh2.T, preferred_element_type=jnp.float32).astype(jnp.bfloat16)
    direct = jnp.dot(dlogits, w_self2.T, preferred_element_type=jnp.float32)
    back_hidden = direct + spread_all(back_grad, send_rows, send_count, tile_src, tile_val)
    back_pre = pullback(back_hidden)[0].astype(jnp.bfloat16)
    grad_self1 = jnp.dot(features.T, back_pre, preferred_element_type=jnp.float32)
    grad_neigh1 = jnp.dot(agg_one.T, back_pre, preferred_element_type=jnp.float32)
    return (mean_loss, grad_self1, grad_neigh1, grad_self2, grad_neigh2)
```

```python
import functools
import math

import jax
import jax.numpy as jnp
from jax import lax
from jax.experimental import pallas as pl
from jax.experimental.pallas import tpu as pltpu
from jax.sharding import PartitionSpec as P

BLOCK = 128
FEW = 8
F32 = jnp.float32
BF16 = jnp.bfloat16
VMEM = pl.BlockSpec(memory_space=pltpu.VMEM)
SMEM = pl.BlockSpec(memory_space=pltpu.SMEM)


def mm(a, b):
    return lax.dot_general(a, b, (((1,), (0,)), ((), ())), preferred_element_type=F32)


def mm_nt(a, b):
    return lax.dot_general(a, b, (((1,), (1,)), ((), ())), preferred_element_type=F32)


def mm_tn(a, b):
    return lax.dot_general(a, b, (((0,), (0,)), ((), ())), preferred_element_type=F32)


def halves(value):
    high = value.astype(BF16)
    return high, (value - high.astype(F32)).astype(BF16)


def gelu_parts(v):
    inner = math.sqrt(2.0 / math.pi) * (v + 0.044715 * (v * v * v))
    t = jnp.tanh(inner)
    return 0.5 * (1.0 + t), t


def gelu(v):
    return v * gelu_parts(v)[0]


def gelu_slope(v):
    cdf, t = gelu_parts(v)
    inner_slope = math.sqrt(2.0 / math.pi) * (1.0 + 3 * 0.044715 * (v * v))
    return cdf + 0.5 * v * (1.0 - t * t) * inner_slope


def call(body, outs, args, specs, scratch=(), flops=0, moved=0):
    return pl.pallas_call(
        body,
        out_shape=[jax.ShapeDtypeStruct(shape, dtype) for shape, dtype in outs],
        in_specs=specs,
        out_specs=[VMEM] * len(outs),
        scratch_shapes=list(scratch),
        compiler_params=pltpu.CompilerParams(vmem_limit_bytes=56 * 2**20),
        cost_estimate=pl.CostEstimate(flops=flops, bytes_accessed=moved, transcendentals=0),
    )(*args)


def prepare_kernel(tile_src, count, tile_val, send_rows, a_ref, pick_ref, dense):
    blocks, per_block = tile_val.shape[0], tile_val.shape[1]
    own = blocks * BLOCK
    dense[...] = jnp.zeros_like(dense)
    for b in range(blocks):

        def add(k, _, b=b):
            at = pl.ds(pl.multiple_of(tile_src[b, k] * BLOCK, BLOCK), BLOCK)
            rows = pl.ds(b * BLOCK, BLOCK)
            dense[rows, at] = dense[rows, at] + tile_val[b, k].astype(F32)
            return 0

        lax.fori_loop(0, per_block, add, 0)
    for b in range(blocks):
        rows = pl.ds(b * BLOCK, BLOCK)
        high, low = halves(dense[rows, :])
        a_ref[rows, :] = high
        a_ref[pl.ds(own + b * BLOCK, BLOCK), :] = low
    dests, slots = send_rows.shape
    columns = send_rows[...].astype(F32).T
    row_id = lax.broadcasted_iota(jnp.int32, (slots, own), 1).astype(F32)
    slot_id = lax.broadcasted_iota(jnp.int32, (slots, own), 0)
    for d in range(dests):
        hit = (columns[:, d : d + 1] == row_id) & (slot_id < count[0, d])
        pick_ref[pl.ds(d * slots, slots), :] = jnp.where(hit, 1.0, 0.0).astype(BF16)


def spread_out(ids, packed, outs, node_count):
    slots = packed.shape[0] // node_count
    if len(outs) == 1:
        outs[0][...] = packed[...]
        return
    for k, out in enumerate(outs):
        dest = lax.rem(ids[0] + k, node_count)
        out[...] = packed[pl.ds(pl.multiple_of(dest * slots, slots), slots), :]


def bring_in(ids, pieces, landed, node_count):
    slots = landed.shape[0] // node_count
    if len(pieces) == 1:
        landed[...] = pieces[0][...]
        return
    for k, piece in enumerate(pieces):
        source = lax.rem(ids[0] + node_count - k, node_count)
        landed[pl.ds(pl.multiple_of(source * slots, slots), slots), :] = piece[...]


def pack_kernel(node_count, groups, sent, ids, pick, *refs):
    pieces, (full, *outs), (turned, packed) = refs[:groups], refs[groups : groups + 1 + sent], refs[groups + 1 + sent :]
    step = pieces[0].shape[0]
    for k, piece in enumerate(pieces):
        turned[pl.ds(k * step, step), :] = piece[...]
    rows = turned[...].T
    full[...] = rows
    packed[...] = mm(pick[...], rows).astype(BF16)
    spread_out(ids, packed, outs, node_count)


def first_kernel(node_count, sent, ids, pick, a_ref, full, *refs):
    pieces, (agg, source, *outs), (packed,) = refs[:sent], refs[sent : 2 * sent + 2], refs[2 * sent + 2 :]
    own = full.shape[0]
    bring_in(ids, pieces, source, node_count)
    both = mm(a_ref[:, :own], full[...]) + mm(a_ref[:, own:], source[...])
    rounded = (both[:own] + both[own:]).astype(BF16)
    agg[...] = rounded
    packed[...] = mm(pick[...], rounded).astype(BF16)
    spread_out(ids, packed, outs, node_count)


def own_kernel(groups, ids, full, agg, a_ref, turned, *refs):
    selfs, neighs, w_selfs, w_neighs = (refs[i * groups : (i + 1) * groups] for i in range(4))
    w_one, w_two, slope, part, logits, mine, left = refs[4 * groups : 4 * groups + 7]
    (hidden,) = refs[4 * groups + 7 :]
    own, cols = full.shape
    step = selfs[0].shape[0]
    classes, units = w_selfs[0].shape
    w_two[...] = jnp.zeros_like(w_two)
    pad = w_two.shape[0] // 2
    for k in range(groups):
        w_one[pl.ds(k * step, step), :] = selfs[k][...]
        w_one[pl.ds(cols + k * step, step), :] = neighs[k][...]
        group = lax.rem(ids[1] + groups - k, groups)
        at = pl.ds(pl.multiple_of(group * units, units), units)
        w_two[pl.ds(0, classes), at] = w_selfs[k][...]
        w_two[pl.ds(pad, classes), at] = w_neighs[k][...]
    left[pl.ds(0, step), :] = turned[...]
    left[pl.ds(step, step), :] = agg[...].T[:step]
    both = jnp.concatenate([full[...], agg[...]], axis=1)
    total = None
    for j in range(groups):
        at = pl.ds(j * units, units)
        pre = mm(both, w_one[:, at])
        slope[:, at] = gelu_slope(pre)
        out = gelu(pre).astype(BF16)
        hidden[:, at] = out
        spread = mm(a_ref[:, :own], out)
        part[:, at] = spread[:own] + spread[own:]
        term = mm_nt(w_two[:pad, at], out)
        total = term if total is None else total + term
    logits[...] = total
    mine[...] = hidden[:, pl.ds(pl.multiple_of(ids[1] * units, units), units)]


def second_kernel(node_count, groups, sent, class_count, grad_scale, ids, a_ref, source, w_one, w_two, part, logits, labels, *refs):
    pieces = refs[:sent]
    turned, mine, loss, kept, *outs = refs[sent : 2 * sent + 4]
    landed, agg, packed = refs[2 * sent + 4 :]
    own = part.shape[0]
    units = mine.shape[1]
    pad = logits.shape[0]
    bring_in(ids, pieces, landed, node_count)
    chunk = min(own, landed.shape[0])
    total = logits[...]
    for j in range(groups):
        at = pl.ds(j * units, units)

        def one(r, held, at=at):
            rows = pl.ds(pl.multiple_of(r * chunk, chunk), chunk)
            srcs = pl.ds(pl.multiple_of(own + r * chunk, BLOCK), chunk)
            both = jnp.concatenate([source[rows, :], landed[rows, :]], axis=1)
            out = gelu(mm(both, w_one[:, at])).astype(BF16)
            spread = mm(a_ref[:, srcs], out)
            return held + spread[:own] + spread[own:]

        held = part[:, at]
        for r in range(landed.shape[0] // chunk) if landed.shape[0] == chunk else ():
            held = one(r, held)
        if landed.shape[0] != chunk:
            held = lax.fori_loop(0, landed.shape[0] // chunk, one, held)
        rounded = held.astype(BF16)
        agg[:, at] = rounded
        total = total + mm_nt(w_two[pad:, at], rounded)
    class_id = lax.broadcasted_iota(jnp.int32, total.shape, 0)
    real = class_id < class_count
    top = jnp.max(jnp.where(real, total, -jnp.inf), axis=0, keepdims=True)
    shifted = total - top
    powers = jnp.where(real, jnp.exp(shifted), 0.0)
    sums = jnp.sum(powers, axis=0, keepdims=True)
    target = (class_id == labels[...]).astype(F32)
    row_loss = jnp.log(sums) - jnp.sum(shifted * target, axis=0, keepdims=True)
    loss[...] = jnp.broadcast_to(jnp.sum(row_loss, axis=1, keepdims=True), loss.shape)
    grads = ((powers / sums - target) * grad_scale).astype(BF16)
    turned[...] = grads
    back = mm(grads, a_ref[:own, :])
    kept[...] = back[:, :own]
    packed[...] = back[:, own:].T.astype(BF16)
    spread_out(ids, packed, outs, node_count)
    mine[...] = agg[:, pl.ds(pl.multiple_of(ids[1] * units, units), units)]


def weights_kernel(class_count, turned, self_rows, agg_rows, loss, self_out, agg_out):
    own_grads = mm(turned[...], self_rows[...])
    row = lax.broadcasted_iota(jnp.int32, own_grads.shape, 0)
    self_out[...] = jnp.where(row == class_count, loss[0:1, 0:1], own_grads)
    agg_out[...] = mm(turned[...], agg_rows[...])[:class_count]


def direct_kernel(turned, kept, w_two, out):
    pad = turned.shape[0]
    high, low = halves(kept[...].T)
    rows = turned[...].T
    for j in range(out.shape[1] // 256):
        at = pl.ds(j * 256, 256)
        out[:, at] = mm(rows, w_two[:pad, at]) + mm(high, w_two[pad:, at]) + mm(low, w_two[pad:, at])


def back_kernel(node_count, sent, split, ids, pick, direct, slope, w_two, left, *refs):
    pieces = refs[:sent]
    outs, (landed, grads) = refs[sent:-2], refs[-2:]
    pad = w_two.shape[0] // 2
    bring_in(ids, pieces, landed, node_count)
    high, low = halves(mm_tn(pick[...], landed[...]))
    for j in range(direct.shape[1] // 256):
        at = pl.ds(j * 256, 256)
        total = direct[:, at] + mm(high, w_two[pad:, at]) + mm(low, w_two[pad:, at])
        grads[:, at] = mm(left[...], (total * slope[:, at]).astype(BF16))
    if not split:
        step = left.shape[0] // 2
        outs[0][...] = grads[:step]
        outs[1][...] = grads[step:]
        return
    width = grads.shape[1] // node_count
    for k, out in enumerate(outs):
        dest = lax.rem(ids[0] + k, node_count)
        out[...] = grads[:, pl.ds(pl.multiple_of(dest * width, width), width)]


def sum_kernel(*refs):
    *pieces, out = refs
    total = pieces[0][...]
    for piece in pieces[1:]:
        total = total + piece[...]
    out[...] = total


def place_kernel(node_count, ids, *refs):
    pieces, (top, bottom) = refs[:node_count], refs[node_count:]
    step, width = top.shape[0], pieces[0].shape[1]
    for k, piece in enumerate(pieces):
        source = lax.rem(ids[0] + node_count - k, node_count)
        at = pl.ds(pl.multiple_of(source * width, width), width)
        top[:, at] = piece[pl.ds(0, step), :]
        bottom[:, at] = piece[pl.ds(step, step), :]


def shifted(value, axis, count, k):
    return lax.ppermute(value, axis, [(i, (i + k) % count) for i in range(count)])


def exchange(pieces, count):
    if len(pieces) == 1:
        whole = pieces[0]
        return [lax.all_to_all(whole.reshape(count, -1, whole.shape[1]), "node", 0, 0, tiled=True).reshape(whole.shape)]
    return [pieces[0]] + [shifted(pieces[k], "node", count, k) for k in range(1, count)]


def gather_shifted(value, count):
    return [value] + [shifted(value, "feat", count, k) for k in range(1, count)]


def shards(features, send_rows, send_count, tile_src, tile_val, labels, w_self1, w_neigh1, w_self2, w_neigh2):
    nodes, groups = lax.axis_size("node"), lax.axis_size("feat")
    own, step = features.shape
    slots = send_rows.shape[2]
    halo = nodes * slots
    total_src = own + halo
    cols = step * groups
    width = w_self1.shape[1]
    units, classes = w_self2.shape
    pad = -(-(classes + 1) // 16) * 16
    split = nodes <= FEW
    sent = nodes if split else 1
    piece_rows = halo // sent
    grad_scale = 1.0 / math.sqrt(own * nodes)
    ids = jnp.stack([lax.axis_index("node"), lax.axis_index("feat")]).astype(jnp.int32)

    turned = features.T
    turned_all = gather_shifted(turned, groups)
    selfs = gather_shifted(w_self1, groups)
    neighs = gather_shifted(w_neigh1, groups)
    w_selfs = gather_shifted(w_self2.T, groups)
    w_neighs = gather_shifted(w_neigh2.T, groups)

    a_mat, pick = call(
        prepare_kernel,
        [((2 * own, total_src), BF16), ((halo, own), BF16)],
        (tile_src, send_count, tile_val, send_rows[0]),
        [SMEM, SMEM, VMEM, VMEM],
        [pltpu.VMEM((own, total_src), F32)],
        moved=tile_val.size * 4,
    )
    full, *outs = call(
        functools.partial(pack_kernel, nodes, groups, sent),
        [((own, cols), BF16)] + [((piece_rows, cols), BF16)] * sent,
        (ids, pick, *turned_all),
        [SMEM] + [VMEM] * (1 + groups),
        [pltpu.VMEM((cols, own), BF16), pltpu.VMEM((halo, cols), BF16)],
        flops=2 * halo * own * cols,
        moved=halo * own * 2,
    )
    arrived = exchange(outs, nodes)
    agg, source, *outs = call(
        functools.partial(first_kernel, nodes, sent),
        [((own, cols), BF16), ((halo, cols), BF16)] + [((piece_rows, cols), BF16)] * sent,
        (ids, pick, a_mat, full, *arrived),
        [SMEM] + [VMEM] * (3 + sent),
        [pltpu.VMEM((halo, cols), BF16)],
        flops=4 * own * total_src * cols,
        moved=4 * own * total_src,
    )
    arrived = exchange(outs, nodes)
    w_one, w_two, slope, part, logits, mine, left = call(
        functools.partial(own_kernel, groups),
        [
            ((2 * cols, width), BF16),
            ((2 * pad, width), BF16),
            ((own, width), F32),
            ((own, width), F32),
            ((pad, own), F32),
            ((own, units), BF16),
            ((2 * step, own), BF16),
        ],
        (ids, full, agg, a_mat, turned, *selfs, *neighs, *w_selfs, *w_neighs),
        [SMEM] + [VMEM] * (4 + 4 * groups),
        [pltpu.VMEM((own, width), BF16)],
        flops=4 * own * own * width,
        moved=12 * own * width,
    )
    turned_grads, agg_mine, loss, kept, *outs = call(
        functools.partial(second_kernel, nodes, groups, sent, classes, grad_scale),
        [((pad, own), BF16), ((own, units), BF16), ((8, 128), F32), ((pad, own), F32)]
        + [((piece_rows, pad), BF16)] * sent,
        (ids, a_mat, source, w_one, w_two, part, logits, labels.reshape(1, own), *arrived),
        [SMEM] + [VMEM] * (7 + sent),
        [pltpu.VMEM((halo, cols), BF16), pltpu.VMEM((own, width), BF16), pltpu.VMEM((halo, pad), BF16)],
        flops=4 * own * halo * width,
        moved=12 * own * width,
    )
    arrived = exchange(outs, nodes)
    grad_self2, grad_neigh2 = call(
        functools.partial(weights_kernel, classes),
        [((pad, units), F32), ((classes, units), F32)],
        (turned_grads, mine, agg_mine, loss),
        [VMEM] * 4,
        flops=4 * pad * own * units,
        moved=4 * own * units,
    )
    grad_self2, grad_neigh2 = lax.psum((grad_self2, grad_neigh2), "node")
    loss, grad_self2 = grad_self2[classes, 0], grad_self2[:classes]
    (direct,) = call(
        direct_kernel,
        [((own, width), F32)],
        (turned_grads, kept, w_two),
        [VMEM] * 3,
        flops=6 * own * pad * width,
        moved=8 * own * width,
    )
    outs = call(
        functools.partial(back_kernel, nodes, sent, split),
        [((2 * step, width // nodes), F32)] * nodes if split else [((step, width), F32)] * 2,
        (ids, pick, direct, slope, w_two, left, *arrived),
        [SMEM] + [VMEM] * (5 + sent),
        [pltpu.VMEM((halo, pad), BF16), pltpu.VMEM((2 * step, width), F32)],
        flops=6 * own * pad * width,
        moved=12 * own * width,
    )
    if split:
        summed = call(sum_kernel, [((2 * step, width // nodes), F32)], exchange(outs, nodes), [VMEM] * nodes)[0]
        gathered = [summed] + [shifted(summed, "node", nodes, k) for k in range(1, nodes)]
        grad_self1, grad_neigh1 = call(
            functools.partial(place_kernel, nodes),
            [((step, width), F32)] * 2,
            (ids, *gathered),
            [SMEM] + [VMEM] * nodes,
        )
    else:
        grad_self1, grad_neigh1 = lax.psum(tuple(outs), "node")
    return (loss / (own * nodes), grad_self1, grad_neigh1, grad_self2.T, grad_neigh2.T)


def solution(mesh):
    in_specs = (
        P("node", "feat"),
        P("node", None, None),
        P("node", None),
        P("node", None),
        P("node", None, None, None),
        P("node"),
        P("feat", None),
        P("feat", None),
        P("feat", None),
        P("feat", None),
    )
    out_specs = (P(), P("feat", None), P("feat", None), P("feat", None), P("feat", None))
    return jax.shard_map(shards, mesh=mesh, in_specs=in_specs, out_specs=out_specs, check_vma=False)
```

```python
import functools
import math

import jax
import jax.numpy as jnp
from jax import lax
from jax.experimental import pallas as pl
from jax.experimental.pallas import tpu as pltpu
from jax.sharding import PartitionSpec as P

BLOCK = 128
F32 = jnp.float32
BF16 = jnp.bfloat16
VMEM = pl.BlockSpec(memory_space=pltpu.VMEM)
SMEM = pl.BlockSpec(memory_space=pltpu.SMEM)


def mm(a, b):
    return lax.dot_general(a, b, (((1,), (0,)), ((), ())), preferred_element_type=F32)


def mm_nt(a, b):
    return lax.dot_general(a, b, (((1,), (1,)), ((), ())), preferred_element_type=F32)


def mm_tn(a, b):
    return lax.dot_general(a, b, (((0,), (0,)), ((), ())), preferred_element_type=F32)


def halves(value):
    high = value.astype(BF16)
    return high, (value - high.astype(F32)).astype(BF16)


def gelu_parts(v):
    inner = math.sqrt(2.0 / math.pi) * (v + 0.044715 * (v * v * v))
    t = jnp.tanh(inner)
    return 0.5 * (1.0 + t), t


def gelu(v):
    return v * gelu_parts(v)[0]


def gelu_slope(v):
    cdf, t = gelu_parts(v)
    inner_slope = math.sqrt(2.0 / math.pi) * (1.0 + 3 * 0.044715 * (v * v))
    return cdf + 0.5 * v * (1.0 - t * t) * inner_slope


def size_of(shape, dtype):
    rows = -(-shape[-2] // 16) * 16 if len(shape) > 1 else 1
    return math.prod(shape[:-2]) * rows * (-(-shape[-1] // 128) * 128) * jnp.dtype(dtype).itemsize


def call(body, outs, args, specs, scratch=(), flops=0, moved=0):
    room = sum(size_of(shape, dtype) for shape, dtype in outs) + sum(size_of(shape, dtype) for shape, dtype in scratch)
    room += sum(size_of(arg.shape, arg.dtype) for arg, spec in zip(args, specs) if spec is VMEM)
    return pl.pallas_call(
        body,
        out_shape=[jax.ShapeDtypeStruct(shape, dtype) for shape, dtype in outs],
        in_specs=specs,
        out_specs=[VMEM] * len(outs),
        scratch_shapes=[pltpu.VMEM(shape, dtype) for shape, dtype in scratch],
        compiler_params=pltpu.CompilerParams(vmem_limit_bytes=min(room + 8 * 2**20, 56 * 2**20)),
        cost_estimate=pl.CostEstimate(flops=flops, bytes_accessed=moved, transcendentals=0),
    )(*args)


def weights_pack_kernel(w_self1, w_neigh1, w_self2, w_neigh2, out):
    step, units = w_self1.shape[0], out.shape[1]
    classes = w_self2.shape[0]
    groups = w_self1.shape[1] // units
    base = 2 * step * groups
    pad = (out.shape[0] - base) // 2
    for j in range(groups):
        at = pl.ds(j * units, units)
        out[pl.ds(2 * step * j, step), :] = w_self1[:, at]
        out[pl.ds(2 * step * j + step, step), :] = w_neigh1[:, at]
    out[pl.ds(base, 2 * pad), :] = jnp.zeros((2 * pad, units), BF16)
    out[pl.ds(base, classes), :] = w_self2[...]
    out[pl.ds(base + pad, classes), :] = w_neigh2[...]


def pack_kernel(groups, ids, count, send_rows, *refs):
    pieces, (pick, full, packed), (turned,) = refs[:groups], refs[groups : groups + 3], refs[groups + 3 :]
    step, own = pieces[0].shape
    dests, slots = send_rows.shape
    columns = send_rows[...].astype(F32).T
    row_id = lax.broadcasted_iota(jnp.int32, (slots, own), 1).astype(F32)
    slot_id = lax.broadcasted_iota(jnp.int32, (slots, own), 0)
    for d in range(dests):
        hit = (columns[:, d : d + 1] == row_id) & (slot_id < count[0, d])
        pick[pl.ds(d * slots, slots), :] = jnp.where(hit, 1.0, 0.0).astype(BF16)
    for k, piece in enumerate(pieces):
        group = lax.rem(ids[0] + groups - k, groups)
        turned[pl.ds(pl.multiple_of(group * step, step), step), :] = piece[...]
    rows = turned[...].T
    full[...] = rows
    packed[...] = mm(pick[...], rows).astype(BF16)


def prepare_kernel(tile_src, tile_val, a_ref, dense):
    blocks, per_block = tile_val.shape[0], tile_val.shape[1]
    own = blocks * BLOCK
    dense[...] = jnp.zeros_like(dense)
    for b in range(blocks):

        def add(k, _, b=b):
            at = pl.ds(pl.multiple_of(tile_src[b, k] * BLOCK, BLOCK), BLOCK)
            rows = pl.ds(b * BLOCK, BLOCK)
            dense[rows, at] = dense[rows, at] + tile_val[b, k].astype(F32)
            return 0

        lax.fori_loop(0, per_block, add, 0)
    for b in range(blocks):
        rows = pl.ds(b * BLOCK, BLOCK)
        high, low = halves(dense[rows, :])
        a_ref[rows, :] = high
        a_ref[pl.ds(own + b * BLOCK, BLOCK), :] = low


def first_kernel(pick, a_ref, full, source, agg, packed):
    own = full.shape[0]
    both = mm(a_ref[:, :own], full[...]) + mm(a_ref[:, own:], source[...])
    rounded = (both[:own] + both[own:]).astype(BF16)
    agg[...] = rounded
    packed[...] = mm(pick[...], rounded).astype(BF16)


def own_kernel(ids, full, agg, a_ref, turned, weights, w_one, w_two, slope, part, logits, mine, left, hidden, agg_turned):
    groups, _, units = weights.shape
    own, cols = full.shape
    step = turned.shape[0]
    pad = logits.shape[0]
    base = 2 * step * groups
    for g in range(groups):
        for j in range(groups):
            at = pl.ds(j * units, units)
            w_one[pl.ds(g * step, step), at] = weights[g, pl.ds(2 * step * j, step), :]
            w_one[pl.ds(cols + g * step, step), at] = weights[g, pl.ds(2 * step * j + step, step), :]
        w_two[:, pl.ds(g * units, units)] = weights[g, pl.ds(base, 2 * pad), :]
    left[pl.ds(0, step), :] = turned[...]
    agg_turned[...] = agg[...].T
    left[pl.ds(step, step), :] = agg_turned[pl.ds(pl.multiple_of(ids[0] * step, step), step), :]
    both = jnp.concatenate([full[...], agg[...]], axis=1)
    total = None
    for j in range(groups):
        at = pl.ds(j * units, units)
        pre = mm(both, w_one[:, at])
        slope[:, at] = gelu_slope(pre)
        out = gelu(pre).astype(BF16)
        hidden[:, at] = out
        spread = mm(a_ref[:, :own], out)
        part[:, at] = spread[:own] + spread[own:]
        term = mm_nt(w_two[:pad, at], out)
        total = term if total is None else total + term
    logits[...] = total
    mine[...] = hidden[:, pl.ds(pl.multiple_of(ids[0] * units, units), units)]


def second_kernel(
    groups, class_count, grad_scale, ids, a_ref, source, landed, w_one, w_two, part, logits, labels,
    turned, mine, loss, kept, packed, agg,
):
    own = part.shape[0]
    units = mine.shape[1]
    pad = logits.shape[0]
    chunk = min(own, landed.shape[0])
    total = logits[...]
    for j in range(groups):
        at = pl.ds(j * units, units)

        def one(r, held, at=at):
            rows = pl.ds(pl.multiple_of(r * chunk, chunk), chunk)
            srcs = pl.ds(pl.multiple_of(own + r * chunk, BLOCK), chunk)
            both = jnp.concatenate([source[rows, :], landed[rows, :]], axis=1)
            out = gelu(mm(both, w_one[:, at])).astype(BF16)
            spread = mm(a_ref[:, srcs], out)
            return held + spread[:own] + spread[own:]

        if landed.shape[0] == chunk:
            held = one(0, part[:, at])
        else:
            held = lax.fori_loop(0, landed.shape[0] // chunk, one, part[:, at])
        rounded = held.astype(BF16)
        agg[:, at] = rounded
        total = total + mm_nt(w_two[pad:, at], rounded)
    class_id = lax.broadcasted_iota(jnp.int32, total.shape, 0)
    real = class_id < class_count
    top = jnp.max(jnp.where(real, total, -jnp.inf), axis=0, keepdims=True)
    shifted = total - top
    powers = jnp.where(real, jnp.exp(shifted), 0.0)
    sums = jnp.sum(powers, axis=0, keepdims=True)
    target = (class_id == labels[...]).astype(F32)
    row_loss = jnp.log(sums) - jnp.sum(shifted * target, axis=0, keepdims=True)
    loss[...] = jnp.broadcast_to(jnp.sum(row_loss, axis=1, keepdims=True), loss.shape)
    grads = ((powers / sums - target) * grad_scale).astype(BF16)
    turned[...] = grads
    back = mm(grads, a_ref[:own, :])
    kept[...] = back[:, :own]
    packed[...] = back[:, own:].T.astype(BF16)
    mine[...] = agg[:, pl.ds(pl.multiple_of(ids[0] * units, units), units)]


def cut(rows, lanes, parts):
    across = lanes // BLOCK
    down = parts // across
    height = rows // down
    return [(slice(p % down * height, (p % down + 1) * height), slice(p // down * BLOCK, (p // down + 1) * BLOCK)) for p in range(parts)]


def weight_grads_kernel(class_count, parts, turned, self_rows, agg_rows, loss, out, *scratch):
    own_grads = mm(turned[...], self_rows[...])
    row = lax.broadcasted_iota(jnp.int32, own_grads.shape, 0)
    own_grads = jnp.where(row == class_count, loss[0:1, 0:1], own_grads)
    agg_grads = mm(turned[...], agg_rows[...])
    units = own_grads.shape[1]
    if not parts:
        out[:, :units] = own_grads
        out[:, units:] = agg_grads
        return
    (both,) = scratch
    both[:, :units] = own_grads
    both[:, units:] = agg_grads
    for p, (rows, lanes) in enumerate(cut(*both.shape, parts)):
        out[p] = both[rows, lanes]


def direct_kernel(turned, kept, w_two, out):
    pad = turned.shape[0]
    high, low = halves(kept[...].T)
    rows = turned[...].T
    for j in range(out.shape[1] // 256):
        at = pl.ds(j * 256, 256)
        out[:, at] = mm(rows, w_two[:pad, at]) + mm(high, w_two[pad:, at]) + mm(low, w_two[pad:, at])


def back_kernel(parts, pick, direct, slope, w_two, left, landed, out):
    pad = w_two.shape[0] // 2
    high, low = halves(mm_tn(pick[...], landed[...]))
    for j in range(direct.shape[1] // 256):
        at = pl.ds(j * 256, 256)
        total = direct[:, at] + mm(high, w_two[pad:, at]) + mm(low, w_two[pad:, at])
        grads = mm(left[...], (total * slope[:, at]).astype(BF16))
        if parts:
            width = out.shape[2]
            for i in range(256 // width):
                out[j * 256 // width + i] = grads[:, i * width : (i + 1) * width]
        else:
            out[:, at] = grads


def sum_kernel(pieces, out):
    total = pieces[0]
    for k in range(1, pieces.shape[0]):
        total = total + pieces[k]
    for k in range(out.shape[0]):
        out[k] = total


def place_kernel(class_count, node_total, first, second, self1, neigh1, self2, neigh2, loss, both):
    step = self1.shape[0]
    width = first.shape[2]
    for p in range(first.shape[0]):
        self1[:, pl.ds(p * width, width)] = first[p, pl.ds(0, step), :]
        neigh1[:, pl.ds(p * width, width)] = first[p, pl.ds(step, step), :]
    for p, (rows, lanes) in enumerate(cut(*both.shape, second.shape[0])):
        both[rows, lanes] = second[p]
    units = self2.shape[1]
    self2[...] = both[:class_count, :units]
    neigh2[...] = both[:class_count, units:]
    loss[...] = both[class_count : class_count + 1, 0:1] / node_total


def swap(value, count):
    blocks = value.reshape(count, -1, value.shape[-1])
    return lax.all_to_all(blocks, "node", 0, 0, tiled=True)


def gather_shifted(value, count):
    return [value] + [lax.ppermute(value, "feat", [(i, (i + k) % count) for i in range(count)]) for k in range(1, count)]


def shards(features, send_rows, send_count, tile_src, tile_val, labels, w_self1, w_neigh1, w_self2, w_neigh2):
    nodes, groups = lax.axis_size("node"), lax.axis_size("feat")
    own, step = features.shape
    slots = send_rows.shape[2]
    halo = nodes * slots
    total_src = own + halo
    cols = step * groups
    width = w_self1.shape[1]
    units, classes = w_self2.shape
    pad = -(-(classes + 1) // 16) * 16
    across = 2 * units // BLOCK
    parts = nodes if nodes % across == 0 and pad % (8 * (nodes // across)) == 0 and width % (nodes * BLOCK) == 0 else 0
    node_total = own * nodes
    grad_scale = 1.0 / math.sqrt(node_total)
    ids = lax.axis_index("feat").astype(jnp.int32).reshape(1)

    turned = features.T
    turned_all = gather_shifted(turned, groups)
    (packed_weights,) = call(
        weights_pack_kernel,
        [((2 * step * groups + 2 * pad, units), BF16)],
        (w_self1, w_neigh1, w_self2.T, w_neigh2.T),
        [VMEM] * 4,
        moved=4 * 2**20,
    )
    weights = lax.all_gather(packed_weights, "feat")
    pick, full, packed = call(
        functools.partial(pack_kernel, groups),
        [((halo, own), BF16), ((own, cols), BF16), ((halo, cols), BF16)],
        (ids, send_count, send_rows[0], *turned_all),
        [SMEM] * 2 + [VMEM] * (1 + groups),
        [((cols, own), BF16)],
        flops=2 * halo * own * cols,
        moved=halo * own * 2,
    )
    source = swap(packed, nodes).reshape(halo, cols)
    (a_mat,) = call(
        prepare_kernel,
        [((2 * own, total_src), BF16)],
        (tile_src, tile_val),
        [SMEM, VMEM],
        [((own, total_src), F32)],
        moved=tile_val.size * 8,
    )
    agg, packed = call(
        first_kernel,
        [((own, cols), BF16), ((halo, cols), BF16)],
        (pick, a_mat, full, source),
        [VMEM] * 4,
        flops=4 * own * total_src * cols,
        moved=4 * own * total_src,
    )
    landed = swap(packed, nodes).reshape(halo, cols)
    w_one, w_two, slope, part, logits, mine, left = call(
        own_kernel,
        [
            ((2 * cols, width), BF16),
            ((2 * pad, width), BF16),
            ((own, width), F32),
            ((own, width), F32),
            ((pad, own), F32),
            ((own, units), BF16),
            ((2 * step, own), BF16),
        ],
        (ids, full, agg, a_mat, turned, weights),
        [SMEM] + [VMEM] * 5,
        [((own, width), BF16), ((cols, own), BF16)],
        flops=8 * own * own * width,
        moved=16 * own * width,
    )
    turned_grads, agg_mine, loss, kept, packed = call(
        functools.partial(second_kernel, groups, classes, grad_scale),
        [((pad, own), BF16), ((own, units), BF16), ((8, 128), F32), ((pad, own), F32), ((halo, pad), BF16)],
        (ids, a_mat, source, landed, w_one, w_two, part, logits, labels.reshape(1, own)),
        [SMEM] + [VMEM] * 8,
        [((own, width), BF16)],
        flops=4 * own * halo * width,
        moved=12 * own * width,
    )
    landed = swap(packed, nodes).reshape(halo, pad)
    shape = (parts, pad * 2 * units // (BLOCK * parts), BLOCK) if parts else (pad, 2 * units)
    (grads2,) = call(
        functools.partial(weight_grads_kernel, classes, parts),
        [(shape, F32)],
        (turned_grads, mine, agg_mine, loss),
        [VMEM] * 4,
        [((pad, 2 * units), F32)] if parts else [],
        flops=4 * pad * own * units,
        moved=4 * own * units,
    )
    if parts:
        grads2 = swap(grads2, nodes)
    (direct,) = call(
        direct_kernel,
        [((own, width), F32)],
        (turned_grads, kept, w_two),
        [VMEM] * 3,
        flops=6 * own * pad * width,
        moved=8 * own * width,
    )
    (grads1,) = call(
        functools.partial(back_kernel, parts),
        [((parts, 2 * step, width // parts) if parts else (2 * step, width), F32)],
        (pick, direct, slope, w_two, left, landed),
        [VMEM] * 6,
        flops=6 * own * pad * width,
        moved=12 * own * width,
    )
    if not parts:
        grads1, grads2 = lax.psum((grads1, grads2), "node")
        loss = grads2[classes, 0] / node_total
        return (loss, grads1[:step], grads1[step:], grads2[:classes, :units].T, grads2[:classes, units:].T)
    first = swap(grads1, nodes)
    (second,) = call(sum_kernel, [(grads2.shape, F32)], (grads2,), [VMEM], moved=2**20)
    second = swap(second, nodes)
    (first,) = call(sum_kernel, [(first.shape, F32)], (first,), [VMEM], moved=2**20)
    first = swap(first, nodes)
    grad_self1, grad_neigh1, grad_self2, grad_neigh2, loss = call(
        functools.partial(place_kernel, classes, node_total),
        [((step, width), F32)] * 2 + [((classes, units), F32)] * 2 + [((1, 1), F32)],
        (first, second),
        [VMEM] * 2,
        [((pad, 2 * units), F32)],
    )
    return (loss.reshape(()), grad_self1, grad_neigh1, grad_self2.T, grad_neigh2.T)


def solution(mesh):
    in_specs = (
        P("node", "feat"),
        P("node", None, None),
        P("node", None),
        P("node", None),
        P("node", None, None, None),
        P("node"),
        P("feat", None),
        P("feat", None),
        P("feat", None),
        P("feat", None),
    )
    out_specs = (P(), P("feat", None), P("feat", None), P("feat", None), P("feat", None))
    return jax.shard_map(shards, mesh=mesh, in_specs=in_specs, out_specs=out_specs, check_vma=False)
```

```python
import functools
import math

import jax
import jax.numpy as jnp
from jax import lax
from jax.experimental import pallas as pl
from jax.experimental.pallas import tpu as pltpu
from jax.sharding import PartitionSpec as P

BLOCK = 128
F32 = jnp.float32
BF16 = jnp.bfloat16
VMEM = pl.BlockSpec(memory_space=pltpu.VMEM)
HBM = pl.BlockSpec(memory_space=pltpu.HBM)
SMEM = pl.BlockSpec(memory_space=pltpu.SMEM)


def mm(a, b):
    return lax.dot_general(a, b, (((1,), (0,)), ((), ())), preferred_element_type=F32)


def mm_nt(a, b):
    return lax.dot_general(a, b, (((1,), (1,)), ((), ())), preferred_element_type=F32)


def mm_tn(a, b):
    return lax.dot_general(a, b, (((0,), (0,)), ((), ())), preferred_element_type=F32)


def halves(value):
    high = value.astype(BF16)
    return high, (value - high.astype(F32)).astype(BF16)


def gelu_parts(v):
    inner = math.sqrt(2.0 / math.pi) * (v + 0.044715 * (v * v * v))
    t = jnp.tanh(inner)
    return 0.5 * (1.0 + t), t


def gelu(v):
    return v * gelu_parts(v)[0]


def gelu_slope(v):
    cdf, t = gelu_parts(v)
    inner_slope = math.sqrt(2.0 / math.pi) * (1.0 + 3 * 0.044715 * (v * v))
    return cdf + 0.5 * v * (1.0 - t * t) * inner_slope


def call(body, outs, args, scratch, copies, flops=0, moved=0, out_specs=None):
    return pl.pallas_call(
        body,
        out_shape=[jax.ShapeDtypeStruct(shape, dtype) for shape, dtype in outs],
        in_specs=[SMEM if arg.dtype == jnp.int32 and arg.size < 512 else HBM for arg in args],
        out_specs=out_specs or [HBM] * len(outs),
        scratch_shapes=[pltpu.VMEM(shape, dtype) for shape, dtype in scratch] + [pltpu.SemaphoreType.DMA((copies,))],
        compiler_params=pltpu.CompilerParams(vmem_limit_bytes=58 * 2**20),
        cost_estimate=pl.CostEstimate(flops=flops, bytes_accessed=moved, transcendentals=0),
    )(*args)


class Copies:
    def __init__(self, sems):
        self.sems, self.used, self.open = sems, 0, []

    def __call__(self, src, dst):
        copy = pltpu.make_async_copy(src, dst, self.sems.at[self.used])
        copy.start()
        self.used += 1
        return copy

    def later(self, src, dst):
        self.open.append(self(src, dst))

    def finish(self):
        for copy in self.open:
            copy.wait()


def prepare_kernel(tile_src, count, tile_val, send_rows, a_out, pick_out, tiles, rows_in, dense, a_ref, pick, sems):
    copies = Copies(sems)
    blocks, per_block = tile_val.shape[0], tile_val.shape[1]
    own = blocks * BLOCK
    rows_copy = copies(send_rows, rows_in)
    tile_copies = [copies(tile_val.at[b], tiles.at[b]) for b in range(blocks)]
    dense[...] = jnp.zeros_like(dense)
    rows_copy.wait()
    dests, slots = rows_in.shape
    columns = rows_in[...].astype(F32).T
    row_id = lax.broadcasted_iota(jnp.int32, (slots, own), 1).astype(F32)
    slot_id = lax.broadcasted_iota(jnp.int32, (slots, own), 0)
    for d in range(dests):
        hit = (columns[:, d : d + 1] == row_id) & (slot_id < count[0, d])
        pick[pl.ds(d * slots, slots), :] = jnp.where(hit, 1.0, 0.0).astype(BF16)
    copies.later(pick, pick_out)
    for b in range(blocks):
        rows = pl.ds(b * BLOCK, BLOCK)
        low_rows = pl.ds(own + b * BLOCK, BLOCK)
        tile_copies[b].wait()

        def add(k, _, b=b, rows=rows):
            at = pl.ds(pl.multiple_of(tile_src[b, k] * BLOCK, BLOCK), BLOCK)
            dense[rows, at] = dense[rows, at] + tiles[b, k].astype(F32)
            return 0

        lax.fori_loop(0, per_block, add, 0)
        high, low = halves(dense[rows, :])
        a_ref[rows, :] = high
        a_ref[low_rows, :] = low
        copies.later(a_ref.at[rows], a_out.at[rows])
        copies.later(a_ref.at[low_rows], a_out.at[low_rows])
    copies.finish()


def pack_kernel(
    groups, ids, pick_in, w_self1, w_neigh1, w_self2, w_neigh2, *refs
):
    pieces = refs[:groups]
    full_out, packed_out, weights_out, pick, turned, full, packed, firsts, seconds, weights, sems = refs[groups:]
    copies = Copies(sems)
    step = pieces[0].shape[0]
    classes, units = w_self2.shape
    base = 2 * step * groups
    pad = (weights.shape[0] - base) // 2
    loads = [copies(pick_in, pick)]
    for k, piece in enumerate(pieces):
        group = lax.rem(ids[0] + groups - k, groups)
        loads.append(copies(piece, turned.at[pl.ds(pl.multiple_of(group * step, step), step)]))
    w_loads = [copies(w_self1, firsts.at[0]), copies(w_neigh1, firsts.at[1]), copies(w_self2, seconds.at[0]), copies(w_neigh2, seconds.at[1])]
    weights[pl.ds(base, 2 * pad), :] = jnp.zeros((2 * pad, units), BF16)
    for load in loads:
        load.wait()
    rows = turned[...].T
    full[...] = rows
    copies.later(full, full_out)
    packed[...] = mm(pick[...], rows).astype(BF16)
    copies.later(packed, packed_out)
    for load in w_loads:
        load.wait()
    for j in range(groups):
        at = pl.ds(j * units, units)
        weights[pl.ds(2 * step * j, step), :] = firsts[0, :, at]
        weights[pl.ds(2 * step * j + step, step), :] = firsts[1, :, at]
    weights[pl.ds(base, classes), :] = seconds[0]
    weights[pl.ds(base + pad, classes), :] = seconds[1]
    copies.later(weights, weights_out)
    copies.finish()


def first_kernel(pick_in, a_in, full_in, source_in, agg_out, packed_out, pick, a_ref, full, source, agg, packed, sems):
    copies = Copies(sems)
    own, total = full.shape[0], a_ref.shape[1]
    front, rest = pl.ds(0, own), pl.ds(own, total - own)
    loads = [
        copies(full_in, full),
        copies(a_in.at[:, front], a_ref.at[:, front]),
        copies(source_in, source),
        copies(a_in.at[:, rest], a_ref.at[:, rest]),
        copies(pick_in, pick),
    ]
    loads[0].wait()
    loads[1].wait()
    both = mm(a_ref[:, :own], full[...])
    loads[2].wait()
    loads[3].wait()
    both = both + mm(a_ref[:, own:], source[...])
    agg[...] = (both[:own] + both[own:]).astype(BF16)
    copies.later(agg, agg_out)
    loads[4].wait()
    packed[...] = mm(pick[...], agg[...]).astype(BF16)
    copies.later(packed, packed_out)
    copies.finish()


def own_kernel(
    ids, full_in, agg_in, a_in, turned_in, weights_in,
    w_one_out, w_two_out, slope_out, part_out, logits_out, mine_out, left_out,
    full, agg, a_ref, left, weights, w_one, w_two, slope, part, logits, hidden, agg_turned, sems,
):
    copies = Copies(sems)
    groups, _, units = weights.shape
    own, cols = full.shape
    step = turned_in.shape[0]
    pad = logits.shape[0]
    base = 2 * step * groups
    loads = [
        copies(weights_in, weights),
        copies(full_in, full),
        copies(agg_in, agg),
        copies(a_in.at[:, pl.ds(0, own)], a_ref),
        copies(turned_in, left.at[pl.ds(0, step)]),
    ]
    loads[0].wait()
    for g in range(groups):
        for j in range(groups):
            w_one[j, pl.ds(g * step, step), :] = weights[g, pl.ds(2 * step * j, step), :]
            w_one[j, pl.ds(cols + g * step, step), :] = weights[g, pl.ds(2 * step * j + step, step), :]
        w_two[g] = weights[g, pl.ds(base, 2 * pad), :]
    copies.later(w_one, w_one_out)
    copies.later(w_two, w_two_out)
    loads[1].wait()
    loads[2].wait()
    agg_turned[...] = agg[...].T
    loads[4].wait()
    left[pl.ds(step, step), :] = agg_turned[pl.ds(pl.multiple_of(ids[0] * step, step), step), :]
    copies.later(left, left_out)
    both = jnp.concatenate([full[...], agg[...]], axis=1)
    total = None
    for j in range(groups):
        pre = mm(both, w_one[j])
        slope[j] = gelu_slope(pre)
        copies.later(slope.at[j], slope_out.at[j])
        out = gelu(pre).astype(BF16)
        hidden[j] = out
        if j == 0:
            loads[3].wait()
        spread = mm(a_ref[...], out)
        part[j] = spread[:own] + spread[own:]
        copies.later(part.at[j], part_out.at[j])
        term = mm_nt(w_two[j, :pad], out)
        total = term if total is None else total + term
    logits[...] = total
    copies.later(logits, logits_out)
    copies.later(hidden.at[ids[0]], mine_out)
    copies.finish()


def second_kernel(
    class_count, grad_scale, ids, a_in, source_in, landed_in, w_one_in, w_two_in, part_in, logits_in, labels_in,
    turned_out, mine_out, loss_out, kept_out, packed_out,
    a_ref, source, landed, w_one, w_two, part, logits, labels, turned, loss, kept, packed, agg, sems,
):
    copies = Copies(sems)
    groups, own, units = part.shape
    pad = logits.shape[0]
    halo = landed.shape[0]
    slots = halo // packed.shape[0]
    chunk = min(own, halo)
    loads = [
        copies(source_in, source),
        copies(landed_in, landed),
        copies(w_one_in, w_one),
        copies(a_in.at[:, pl.ds(own, halo)], a_ref.at[:, pl.ds(own, halo)]),
        copies(logits_in, logits),
        copies(w_two_in, w_two),
        copies(labels_in, labels),
        copies(a_in.at[pl.ds(0, own), pl.ds(0, own)], a_ref.at[pl.ds(0, own), pl.ds(0, own)]),
    ]
    part_loads = [copies(part_in.at[j], part.at[j]) for j in range(groups)]
    for load in loads[:3]:
        load.wait()
    total = None
    for j in range(groups):

        def one(r, held, j=j):
            rows = pl.ds(pl.multiple_of(r * chunk, chunk), chunk)
            srcs = pl.ds(pl.multiple_of(own + r * chunk, BLOCK), chunk)
            both = jnp.concatenate([source[rows, :], landed[rows, :]], axis=1)
            out = gelu(mm(both, w_one[j])).astype(BF16)
            if j == 0 and halo == chunk:
                loads[3].wait()
            spread = mm(a_ref[:, srcs], out)
            spread = spread[:own] + spread[own:]
            if halo == chunk:
                part_loads[j].wait()
                return part[j] + spread
            return held + spread

        if halo == chunk:
            held = one(0, None)
        else:
            if j == 0:
                loads[3].wait()
            part_loads[j].wait()
            held = lax.fori_loop(0, halo // chunk, one, part[j])
        agg[j] = held.astype(BF16)
        if j == 0:
            loads[4].wait()
            loads[5].wait()
            total = logits[...]
        total = total + mm_nt(w_two[j, pad:], agg[j])
    copies.later(agg.at[ids[0]], mine_out)
    class_id = lax.broadcasted_iota(jnp.int32, total.shape, 0)
    real = class_id < class_count
    top = jnp.max(jnp.where(real, total, -jnp.inf), axis=0, keepdims=True)
    shifted = total - top
    powers = jnp.where(real, jnp.exp(shifted), 0.0)
    sums = jnp.sum(powers, axis=0, keepdims=True)
    loads[6].wait()
    target = (class_id == labels[...]).astype(F32)
    turned[...] = ((powers / sums - target) * grad_scale).astype(BF16)
    copies.later(turned, turned_out)
    loads[7].wait()
    back = mm(turned[...], a_ref[:own, own:]).T.astype(BF16)
    for d in range(packed.shape[0]):
        put_message(packed, d, back[d * slots : (d + 1) * slots])
    copies.later(packed, packed_out)
    kept[...] = mm(turned[...], a_ref[:own, :own])
    copies.later(kept, kept_out)
    row_loss = jnp.log(sums) - jnp.sum(shifted * target, axis=0, keepdims=True)
    loss[...] = jnp.broadcast_to(jnp.sum(row_loss, axis=1, keepdims=True), loss.shape)
    copies.later(loss, loss_out)
    copies.finish()


def message_shape(slots, pad):
    compact = BLOCK < pad <= BLOCK + BLOCK // 2 and slots % 32 == 0
    return (slots + slots // 2, BLOCK) if compact else (slots, pad)


def put_message(packed, d, rows):
    slots, pad = rows.shape
    if packed.shape[1:] == (slots, pad):
        packed[d] = rows
        return
    half, tail = slots // 2, pad - BLOCK
    packed[d, :slots, :] = rows[:, :BLOCK]
    filler = jnp.zeros((half, BLOCK // 2 - tail), BF16)
    packed[d, slots:, :] = jnp.concatenate([rows[:half, BLOCK:], filler, rows[half:, BLOCK:], filler], axis=1)


def take_message(packed, d, landed):
    slots, pad = landed.shape[0] // packed.shape[0], landed.shape[1]
    if packed.shape[1:] == (slots, pad):
        landed[pl.ds(d * slots, slots), :] = packed[d]
        return
    half, tail = slots // 2, pad - BLOCK
    landed[pl.ds(d * slots, slots), :BLOCK] = packed[d, :slots, :]
    landed[pl.ds(d * slots, half), BLOCK:] = packed[d, slots:, :tail]
    landed[pl.ds(d * slots + half, half), BLOCK:] = packed[d, slots:, BLOCK // 2 : BLOCK // 2 + tail]


def cut(rows, lanes, parts):
    across = lanes // BLOCK
    down = parts // across
    height = rows // down
    return [(slice(p % down * height, (p % down + 1) * height), slice(p // down * BLOCK, (p // down + 1) * BLOCK)) for p in range(parts)]


def middle_kernel(
    class_count, parts, turned_in, self_in, agg_in, loss_in, kept_in, w_two_in,
    second_out, direct_out,
    turned, self_rows, agg_rows, loss, kept, w_two, both, direct, sems,
):
    copies = Copies(sems)
    loads = [
        copies(turned_in, turned),
        copies(kept_in, kept),
        copies(w_two_in, w_two),
        copies(self_in, self_rows),
        copies(agg_in, agg_rows),
        copies(loss_in, loss),
    ]
    pad = turned.shape[0]
    units = self_rows.shape[1]
    loads[0].wait()
    loads[1].wait()
    high, low = halves(kept[...].T)
    rows = turned[...].T
    loads[2].wait()
    for j in range(direct.shape[0]):
        direct[j] = mm(rows, w_two[j, :pad]) + mm(high, w_two[j, pad:]) + mm(low, w_two[j, pad:])
        copies.later(direct.at[j], direct_out.at[j])
    for load in loads[3:]:
        load.wait()
    own_grads = mm(turned[...], self_rows[...])
    row = lax.broadcasted_iota(jnp.int32, own_grads.shape, 0)
    both[:, :units] = jnp.where(row == class_count, loss[0:1, 0:1], own_grads)
    both[:, units:] = mm(turned[...], agg_rows[...])
    if parts:
        for p, (rows, lanes) in enumerate(cut(*both.shape, parts)):
            copies.later(both.at[rows, lanes], second_out.at[p])
    else:
        copies.later(both, second_out)
    copies.finish()


def back_kernel(
    parts, pick_in, direct_in, slope_in, w_two_in, left_in, landed_in, second_in, out,
    pick, direct, slope, w_two, left, landed, rows, grads, sems,
):
    copies = Copies(sems)
    step = left.shape[0]
    groups, _, units = direct.shape
    pad = landed.shape[1] if w_two.ndim == 2 else w_two.shape[1] // 2
    loads = [copies(landed_in, landed), copies(pick_in, pick), copies(w_two_in, w_two)]
    both_loads = [(copies(direct_in.at[j], direct.at[j]), copies(slope_in.at[j], slope.at[j])) for j in range(groups)]
    left_load = copies(left_in, left)
    if parts:
        copies.later(second_in, out.at[:, pl.ds(step, second_in.shape[1])])
    loads[0].wait()
    for d in range(landed.shape[0]):
        take_message(landed, d, rows)
    loads[1].wait()
    high, low = halves(mm_tn(pick[...], rows[...]))
    loads[2].wait()
    for j in range(groups):
        for load in both_loads[j]:
            load.wait()
        total = direct[j] + mm(high, w_two[j, pad:]) + mm(low, w_two[j, pad:])
        if j == 0:
            left_load.wait()
        grads[j] = mm(left[...], (total * slope[j]).astype(BF16))
        if parts:
            width = BLOCK
            for i in range(units // width):
                copies.later(grads.at[j, :, pl.ds(i * width, width)], out.at[j * units // width + i, pl.ds(0, step)])
        else:
            copies.later(grads.at[j], out.at[:, pl.ds(j * units, units)])
    copies.finish()


def sum_kernel(pieces_in, out, pieces, total, sems):
    copies = Copies(sems)
    count = pieces.shape[0]
    loads = [copies(pieces_in.at[k], pieces.at[k]) for k in range(count)]
    for load in loads:
        load.wait()
    held = pieces[0]
    for k in range(1, count):
        held = held + pieces[k]
    total[...] = held
    for k in range(count):
        copies.later(total, out.at[k])
    copies.finish()


def place_kernel(class_count, node_total, pieces, self1, neigh1, self2, neigh2, loss, both, sems):
    copies = Copies(sems)
    step = self1.shape[0]
    loads = []
    for p, (rows, lanes) in enumerate(cut(*both.shape, pieces.shape[0])):
        loads.append(copies(pieces.at[p, pl.ds(2 * step, pieces.shape[1] - 2 * step)], both.at[rows, lanes]))
    for p in range(pieces.shape[0]):
        at = pl.ds(p * BLOCK, BLOCK)
        copies.later(pieces.at[p, pl.ds(0, step)], self1.at[:, at])
        copies.later(pieces.at[p, pl.ds(step, step)], neigh1.at[:, at])
    for load in loads:
        load.wait()
    units = self2.shape[1]
    self2[...] = both[:class_count, :units]
    neigh2[...] = both[:class_count, units:]
    loss[...] = both[class_count : class_count + 1, 0:1] / node_total
    copies.finish()


def swap(value, count):
    blocks = value.reshape(count, -1, value.shape[-1])
    return lax.all_to_all(blocks, "node", 0, 0, tiled=True)


def gather_shifted(value, count):
    return [value] + [lax.ppermute(value, "feat", [(i, (i + k) % count) for i in range(count)]) for k in range(1, count)]


def shards(features, send_rows, send_count, tile_src, tile_val, labels, w_self1, w_neigh1, w_self2, w_neigh2):
    nodes, groups = lax.axis_size("node"), lax.axis_size("feat")
    own, step = features.shape
    slots = send_rows.shape[2]
    halo = nodes * slots
    total_src = own + halo
    cols = step * groups
    width = w_self1.shape[1]
    units, classes = w_self2.shape
    pad = -(-(classes + 1) // 16) * 16
    across = 2 * units // BLOCK
    parts = nodes if nodes % across == 0 and pad % (8 * (nodes // across)) == 0 and width == nodes * BLOCK else 0
    node_total = own * nodes
    grad_scale = 1.0 / math.sqrt(node_total)
    ids = lax.axis_index("feat").astype(jnp.int32).reshape(1)
    blocks = own // BLOCK
    packed_rows = 2 * step * groups + 2 * pad

    turned = features.T
    turned_all = gather_shifted(turned, groups)
    a_mat, pick = call(
        prepare_kernel,
        [((2 * own, total_src), BF16), ((halo, own), BF16)],
        (tile_src, send_count, tile_val, send_rows[0]),
        [(tile_val.shape, BF16), ((nodes, slots), jnp.int32), ((own, total_src), F32), ((2 * own, total_src), BF16), ((halo, own), BF16)],
        2 + 3 * blocks,
        moved=tile_val.size * 4,
    )
    full, packed, packed_weights = call(
        functools.partial(pack_kernel, groups),
        [((own, cols), BF16), ((halo, cols), BF16), ((packed_rows, units), BF16)],
        (ids, pick, w_self1, w_neigh1, w_self2.T, w_neigh2.T, *turned_all),
        [
            ((halo, own), BF16),
            ((cols, own), BF16),
            ((own, cols), BF16),
            ((halo, cols), BF16),
            ((2, step, width), BF16),
            ((2, classes, units), BF16),
            ((packed_rows, units), BF16),
        ],
        8 + groups,
        flops=2 * halo * own * cols,
        moved=halo * own * 2,
    )
    weights = lax.all_gather(packed_weights, "feat")
    source = swap(packed, nodes).reshape(halo, cols)
    agg, packed = call(
        first_kernel,
        [((own, cols), BF16), ((halo, cols), BF16)],
        (pick, a_mat, full, source),
        [((halo, own), BF16), ((2 * own, total_src), BF16), ((own, cols), BF16), ((halo, cols), BF16), ((own, cols), BF16), ((halo, cols), BF16)],
        7,
        flops=4 * own * total_src * cols,
        moved=4 * own * total_src,
    )
    landed = swap(packed, nodes).reshape(halo, cols)
    chunked = (groups, own, units)
    w_one, w_two, slope, part, logits, mine, left = call(
        own_kernel,
        [
            ((groups, 2 * cols, units), BF16),
            ((groups, 2 * pad, units), BF16),
            (chunked, F32),
            (chunked, F32),
            ((pad, own), F32),
            ((own, units), BF16),
            ((2 * step, own), BF16),
        ],
        (ids, full, agg, a_mat, turned, weights),
        [
            ((own, cols), BF16),
            ((own, cols), BF16),
            ((2 * own, own), BF16),
            ((2 * step, own), BF16),
            ((groups, packed_rows, units), BF16),
            ((groups, 2 * cols, units), BF16),
            ((groups, 2 * pad, units), BF16),
            (chunked, F32),
            (chunked, F32),
            ((pad, own), F32),
            (chunked, BF16),
            ((cols, own), BF16),
        ],
        10 + 2 * groups,
        flops=8 * own * own * width,
        moved=16 * own * width,
    )
    message = (nodes, *message_shape(slots, pad))
    turned_grads, agg_mine, loss, kept, packed = call(
        functools.partial(second_kernel, classes, grad_scale),
        [((pad, own), BF16), ((own, units), BF16), ((8, 128), F32), ((pad, own), F32), (message, BF16)],
        (ids, a_mat, source, landed, w_one, w_two, part, logits, labels.reshape(1, own)),
        [
            ((2 * own, total_src), BF16),
            ((halo, cols), BF16),
            ((halo, cols), BF16),
            ((groups, 2 * cols, units), BF16),
            ((groups, 2 * pad, units), BF16),
            (chunked, F32),
            ((pad, own), F32),
            ((1, own), jnp.int32),
            ((pad, own), BF16),
            ((8, 128), F32),
            ((pad, own), F32),
            (message, BF16),
            (chunked, BF16),
        ],
        13 + groups,
        flops=4 * own * halo * width,
        moved=12 * own * width,
    )
    landed = swap(packed, nodes)
    second_shape = (parts, pad * 2 * units // (BLOCK * parts), BLOCK) if parts else (pad, 2 * units)
    second, direct = call(
        functools.partial(middle_kernel, classes, parts),
        [(second_shape, F32), (chunked, F32)],
        (turned_grads, mine, agg_mine, loss, kept, w_two),
        [
            ((pad, own), BF16),
            ((own, units), BF16),
            ((own, units), BF16),
            ((8, 128), F32),
            ((pad, own), F32),
            ((groups, 2 * pad, units), BF16),
            ((pad, 2 * units), F32),
            (chunked, F32),
        ],
        6 + groups + max(parts, 1),
        flops=10 * own * pad * width,
        moved=8 * own * width,
    )
    out_shape = (parts, 2 * step + second_shape[1], BLOCK) if parts else (2 * step, width)
    (grads,) = call(
        functools.partial(back_kernel, parts),
        [(out_shape, F32)],
        (pick, direct, slope, w_two, left, landed, second),
        [
            ((halo, own), BF16),
            (chunked, F32),
            (chunked, F32),
            ((groups, 2 * pad, units), BF16),
            ((2 * step, own), BF16),
            (message, BF16),
            ((halo, pad), BF16),
            ((groups, 2 * step, units), F32),
        ],
        5 + 2 * groups + max(parts, groups),
        flops=6 * own * pad * width,
        moved=12 * own * width,
    )
    if not parts:
        grads, second = lax.psum((grads, second), "node")
        loss = second[classes, 0] / node_total
        return (loss, grads[:step], grads[step:], second[:classes, :units].T, second[:classes, units:].T)
    grads = swap(grads, nodes)
    (grads,) = call(sum_kernel, [(out_shape, F32)], (grads,), [(out_shape, F32), (out_shape[1:], F32)], 2 * nodes, moved=2**20)
    grads = swap(grads, nodes)
    grad_self1, grad_neigh1, grad_self2, grad_neigh2, loss = call(
        functools.partial(place_kernel, classes, node_total),
        [((step, width), F32)] * 2 + [((classes, units), F32)] * 2 + [((1, 1), F32)],
        (grads,),
        [((pad, 2 * units), F32)],
        3 * nodes,
        out_specs=[HBM, HBM, VMEM, VMEM, VMEM],
    )
    return (loss.reshape(()), grad_self1, grad_neigh1, grad_self2.T, grad_neigh2.T)


def solution(mesh):
    in_specs = (
        P("node", "feat"),
        P("node", None, None),
        P("node", None),
        P("node", None),
        P("node", None, None, None),
        P("node"),
        P("feat", None),
        P("feat", None),
        P("feat", None),
        P("feat", None),
    )
    out_specs = (P(), P("feat", None), P("feat", None), P("feat", None), P("feat", None))
    return jax.shard_map(shards, mesh=mesh, in_specs=in_specs, out_specs=out_specs, check_vma=False)
```

```python
import functools
import math

import jax
import jax.numpy as jnp
from jax import lax
from jax.experimental import pallas as pl
from jax.experimental.pallas import tpu as pltpu
from jax.sharding import PartitionSpec as P

BLOCK = 128
F32 = jnp.float32
BF16 = jnp.bfloat16
VMEM = pl.BlockSpec(memory_space=pltpu.VMEM)
HBM = pl.BlockSpec(memory_space=pltpu.HBM)
SMEM = pl.BlockSpec(memory_space=pltpu.SMEM)


def mm(a, b):
    return lax.dot_general(a, b, (((1,), (0,)), ((), ())), preferred_element_type=F32)


def mm_nt(a, b):
    return lax.dot_general(a, b, (((1,), (1,)), ((), ())), preferred_element_type=F32)


def mm_tn(a, b):
    return lax.dot_general(a, b, (((0,), (0,)), ((), ())), preferred_element_type=F32)


def halves(value):
    high = value.astype(BF16)
    return high, (value - high.astype(F32)).astype(BF16)


def gelu_parts(v):
    inner = math.sqrt(2.0 / math.pi) * (v + 0.044715 * (v * v * v))
    t = jnp.tanh(inner)
    return 0.5 * (1.0 + t), t


def gelu(v):
    return v * gelu_parts(v)[0]


def gelu_slope(v):
    cdf, t = gelu_parts(v)
    inner_slope = math.sqrt(2.0 / math.pi) * (1.0 + 3 * 0.044715 * (v * v))
    return cdf + 0.5 * v * (1.0 - t * t) * inner_slope


def call(body, outs, args, scratch, copies, flops=0, moved=0, out_specs=None, near=0, room=58):
    return pl.pallas_call(
        body,
        out_shape=[jax.ShapeDtypeStruct(shape, dtype) for shape, dtype in outs],
        in_specs=[SMEM if arg.dtype == jnp.int32 and arg.size < 512 else HBM for arg in args[: len(args) - near]] + [VMEM] * near,
        out_specs=out_specs or [HBM] * len(outs),
        scratch_shapes=[pltpu.VMEM(shape, dtype) for shape, dtype in scratch] + [pltpu.SemaphoreType.DMA((copies,))],
        compiler_params=pltpu.CompilerParams(vmem_limit_bytes=room * 2**20),
        cost_estimate=pl.CostEstimate(flops=flops, bytes_accessed=moved, transcendentals=0),
    )(*args)


class Copies:
    def __init__(self, sems):
        self.sems, self.used, self.open = sems, 0, []

    def __call__(self, src, dst):
        copy = pltpu.make_async_copy(src, dst, self.sems.at[self.used])
        copy.start()
        self.used += 1
        return copy

    def later(self, src, dst):
        self.open.append(self(src, dst))

    def finish(self):
        for copy in self.open:
            copy.wait()


def prepare_kernel(tile_src, count, tile_val, send_rows, a_out, pick_out, tiles, rows_in, dense, a_ref, pick, sems):
    copies = Copies(sems)
    blocks, per_block = tile_val.shape[0], tile_val.shape[1]
    own = blocks * BLOCK
    rows_copy = copies(send_rows, rows_in)
    tile_copies = [copies(tile_val.at[b], tiles.at[b]) for b in range(blocks)]
    dense[...] = jnp.zeros_like(dense)
    rows_copy.wait()
    dests, slots = rows_in.shape
    columns = rows_in[...].astype(F32).T
    row_id = lax.broadcasted_iota(jnp.int32, (slots, own), 1).astype(F32)
    slot_id = lax.broadcasted_iota(jnp.int32, (slots, own), 0)
    for d in range(dests):
        hit = (columns[:, d : d + 1] == row_id) & (slot_id < count[0, d])
        pick[pl.ds(d * slots, slots), :] = jnp.where(hit, 1.0, 0.0).astype(BF16)
    copies.later(pick, pick_out)
    for b in range(blocks):
        rows = pl.ds(b * BLOCK, BLOCK)
        low_rows = pl.ds(own + b * BLOCK, BLOCK)
        tile_copies[b].wait()

        def add(k, _, b=b, rows=rows):
            at = pl.ds(pl.multiple_of(tile_src[b, k] * BLOCK, BLOCK), BLOCK)
            dense[rows, at] = dense[rows, at] + tiles[b, k].astype(F32)
            return 0

        lax.fori_loop(0, per_block, add, 0)
        high, low = halves(dense[rows, :])
        a_ref[rows, :] = high
        a_ref[low_rows, :] = low
        copies.later(a_ref.at[rows], a_out.at[rows])
        copies.later(a_ref.at[low_rows], a_out.at[low_rows])
    copies.finish()


def pack_kernel(
    groups, ids, pick_in, w_self1, w_neigh1, w_self2, w_neigh2, *refs
):
    pieces = refs[:groups]
    full_out, packed_out, weights_out, pick, turned, full, packed, firsts, seconds, weights, sems = refs[groups:]
    copies = Copies(sems)
    step = pieces[0].shape[0]
    classes, units = w_self2.shape
    base = 2 * step * groups
    pad = (weights.shape[0] - base) // 2
    loads = [copies(pick_in, pick)]
    loads.append(copies(pieces[0], turned.at[pl.ds(pl.multiple_of(ids[0] * step, step), step)]))
    for k, piece in enumerate(pieces[1:], 1):
        group = lax.rem(ids[0] + groups - k, groups)
        turned[pl.ds(pl.multiple_of(group * step, step), step), :] = piece[...]
    w_loads = [copies(w_self1, firsts.at[0]), copies(w_neigh1, firsts.at[1]), copies(w_self2, seconds.at[0]), copies(w_neigh2, seconds.at[1])]
    weights[pl.ds(base, 2 * pad), :] = jnp.zeros((2 * pad, units), BF16)
    for load in loads:
        load.wait()
    rows = turned[...].T
    full[...] = rows
    copies.later(full, full_out)
    packed[...] = mm(pick[...], rows).astype(BF16)
    copies.later(packed, packed_out)
    for load in w_loads:
        load.wait()
    for j in range(groups):
        at = pl.ds(j * units, units)
        weights[pl.ds(2 * step * j, step), :] = firsts[0, :, at]
        weights[pl.ds(2 * step * j + step, step), :] = firsts[1, :, at]
    weights[pl.ds(base, classes), :] = seconds[0]
    weights[pl.ds(base + pad, classes), :] = seconds[1]
    copies.later(weights, weights_out)
    copies.finish()


def near_kernel(a_in, full_in, out, a_ref, full, near, sems):
    copies = Copies(sems)
    own = full.shape[0]
    loads = [copies(full_in, full), copies(a_in.at[:, pl.ds(0, own)], a_ref)]
    for load in loads:
        load.wait()
    both = mm(a_ref[...], full[...])
    near[...] = both[:own] + both[own:]
    copies(near, out).wait()


def first_kernel(pick_in, a_in, near_in, source_in, agg_out, packed_out, pick, a_ref, near, source, agg, packed, sems):
    copies = Copies(sems)
    own = near.shape[0]
    loads = [
        copies(source_in, source),
        copies(a_in.at[:, pl.ds(own, source.shape[0])], a_ref),
        copies(near_in, near),
        copies(pick_in, pick),
    ]
    for load in loads[:3]:
        load.wait()
    both = mm(a_ref[...], source[...])
    agg[...] = (near[...] + both[:own] + both[own:]).astype(BF16)
    copies.later(agg, agg_out)
    loads[3].wait()
    packed[...] = mm(pick[...], agg[...]).astype(BF16)
    copies.later(packed, packed_out)
    copies.finish()


def own_kernel(
    ids, full_in, agg_in, a_in, turned_in, weights_in,
    w_one_out, w_two_out, slope_out, part_out, logits_out, mine_out, left_out,
    full, agg, a_ref, left, weights, w_one, w_two, slope, part, logits, hidden, agg_turned, sems,
):
    copies = Copies(sems)
    groups, _, units = weights.shape
    own, cols = full.shape
    step = turned_in.shape[0]
    pad = logits.shape[0]
    base = 2 * step * groups
    loads = [
        copies(weights_in, weights),
        copies(full_in, full),
        copies(agg_in, agg),
        copies(a_in.at[:, pl.ds(0, own)], a_ref),
        copies(turned_in, left.at[pl.ds(0, step)]),
    ]
    loads[0].wait()
    for g in range(groups):
        for j in range(groups):
            w_one[j, pl.ds(g * step, step), :] = weights[g, pl.ds(2 * step * j, step), :]
            w_one[j, pl.ds(cols + g * step, step), :] = weights[g, pl.ds(2 * step * j + step, step), :]
        w_two[g] = weights[g, pl.ds(base, 2 * pad), :]
    copies.later(w_one, w_one_out)
    copies.later(w_two, w_two_out)
    loads[1].wait()
    loads[2].wait()
    agg_turned[...] = agg[...].T
    loads[4].wait()
    left[pl.ds(step, step), :] = agg_turned[pl.ds(pl.multiple_of(ids[0] * step, step), step), :]
    copies.later(left, left_out)
    both = jnp.concatenate([full[...], agg[...]], axis=1)
    total = None
    for j in range(groups):
        pre = mm(both, w_one[j])
        slope[j] = gelu_slope(pre)
        copies.later(slope.at[j], slope_out.at[j])
        out = gelu(pre).astype(BF16)
        hidden[j] = out
        if j == 0:
            loads[3].wait()
        spread = mm(a_ref[...], out)
        part[j] = spread[:own] + spread[own:]
        copies.later(part.at[j], part_out.at[j])
        term = mm_nt(w_two[j, :pad], out)
        total = term if total is None else total + term
    logits[...] = total
    copies.later(logits, logits_out)
    copies.later(hidden.at[ids[0]], mine_out)
    copies.finish()


def second_kernel(
    class_count, grad_scale, ids, a_in, source_in, landed_in, w_one_in, w_two_in, part_in, logits_in, labels_in,
    turned_out, mine_out, loss_out, packed_out,
    a_ref, source, landed, w_one, w_two, part, logits, labels, turned, loss, packed, agg, sems,
):
    copies = Copies(sems)
    groups, own, units = part.shape
    pad = logits.shape[0]
    halo = landed.shape[0]
    slots = halo // packed.shape[0]
    chunk = min(own, halo)
    loads = [
        copies(source_in, source),
        copies(landed_in, landed),
        copies(w_one_in, w_one),
        copies(a_in.at[:, pl.ds(own, halo)], a_ref),
        copies(logits_in, logits),
        copies(w_two_in, w_two),
        copies(labels_in, labels),
    ]
    part_loads = [copies(part_in.at[j], part.at[j]) for j in range(groups)]
    for load in loads[:3]:
        load.wait()
    total = None
    for j in range(groups):

        def one(r, held, j=j):
            rows = pl.ds(pl.multiple_of(r * chunk, chunk), chunk)
            srcs = pl.ds(pl.multiple_of(r * chunk, chunk), chunk)
            both = jnp.concatenate([source[rows, :], landed[rows, :]], axis=1)
            out = gelu(mm(both, w_one[j])).astype(BF16)
            if j == 0 and halo == chunk:
                loads[3].wait()
            spread = mm(a_ref[:, srcs], out)
            spread = spread[:own] + spread[own:]
            if halo == chunk:
                part_loads[j].wait()
                return part[j] + spread
            return held + spread

        if halo == chunk:
            held = one(0, None)
        else:
            if j == 0:
                loads[3].wait()
            part_loads[j].wait()
            held = lax.fori_loop(0, halo // chunk, one, part[j])
        agg[j] = held.astype(BF16)
        if j == 0:
            loads[4].wait()
            loads[5].wait()
            total = logits[...]
        total = total + mm_nt(w_two[j, pad:], agg[j])
    copies.later(agg.at[ids[0]], mine_out)
    class_id = lax.broadcasted_iota(jnp.int32, total.shape, 0)
    real = class_id < class_count
    top = jnp.max(jnp.where(real, total, -jnp.inf), axis=0, keepdims=True)
    shifted = total - top
    powers = jnp.where(real, jnp.exp(shifted), 0.0)
    sums = jnp.sum(powers, axis=0, keepdims=True)
    loads[6].wait()
    target = (class_id == labels[...]).astype(F32)
    turned[...] = ((powers / sums - target) * grad_scale).astype(BF16)
    copies.later(turned, turned_out)
    row_loss = jnp.log(sums) - jnp.sum(shifted * target, axis=0, keepdims=True)
    loss[...] = jnp.broadcast_to(jnp.sum(row_loss, axis=1, keepdims=True), loss.shape)
    copies.later(loss, loss_out)
    back = mm(turned[...], a_ref[:own, :]).T.astype(BF16)
    for d in range(packed.shape[0]):
        put_message(packed, d, back[d * slots : (d + 1) * slots])
    copies.later(packed, packed_out)
    copies.finish()


def message_shape(slots, pad):
    compact = BLOCK < pad <= BLOCK + BLOCK // 2 and slots % 32 == 0
    return (slots + slots // 2, BLOCK) if compact else (slots, pad)


def put_message(packed, d, rows):
    slots, pad = rows.shape
    if packed.shape[1:] == (slots, pad):
        packed[d] = rows
        return
    half, tail = slots // 2, pad - BLOCK
    packed[d, :slots, :] = rows[:, :BLOCK]
    filler = jnp.zeros((half, BLOCK // 2 - tail), BF16)
    packed[d, slots:, :] = jnp.concatenate([rows[:half, BLOCK:], filler, rows[half:, BLOCK:], filler], axis=1)


def take_message(packed, d, landed):
    slots, pad = landed.shape[0] // packed.shape[0], landed.shape[1]
    if packed.shape[1:] == (slots, pad):
        landed[pl.ds(d * slots, slots), :] = packed[d]
        return
    half, tail = slots // 2, pad - BLOCK
    landed[pl.ds(d * slots, slots), :BLOCK] = packed[d, :slots, :]
    landed[pl.ds(d * slots, half), BLOCK:] = packed[d, slots:, :tail]
    landed[pl.ds(d * slots + half, half), BLOCK:] = packed[d, slots:, BLOCK // 2 : BLOCK // 2 + tail]


def cut(rows, lanes, parts):
    across = lanes // BLOCK
    down = parts // across
    height = rows // down
    return [(slice(p % down * height, (p % down + 1) * height), slice(p // down * BLOCK, (p // down + 1) * BLOCK)) for p in range(parts)]


def middle_kernel(
    class_count, parts, turned_in, self_in, agg_in, loss_in, a_in, w_two_in,
    second_out, direct_out,
    turned, self_rows, agg_rows, loss, a_ref, w_two, both, direct, sems,
):
    copies = Copies(sems)
    loads = [
        copies(turned_in, turned),
        copies(a_in.at[pl.ds(0, a_ref.shape[0]), pl.ds(0, a_ref.shape[1])], a_ref),
        copies(w_two_in, w_two),
        copies(self_in, self_rows),
        copies(agg_in, agg_rows),
        copies(loss_in, loss),
    ]
    pad = turned.shape[0]
    units = self_rows.shape[1]
    loads[0].wait()
    loads[1].wait()
    high, low = halves(mm(turned[...], a_ref[...]).T)
    rows = turned[...].T
    loads[2].wait()
    for j in range(direct.shape[0]):
        direct[j] = mm(rows, w_two[j, :pad]) + mm(high, w_two[j, pad:]) + mm(low, w_two[j, pad:])
        copies.later(direct.at[j], direct_out.at[j])
    for load in loads[3:]:
        load.wait()
    own_grads = mm(turned[...], self_rows[...])
    row = lax.broadcasted_iota(jnp.int32, own_grads.shape, 0)
    both[:, :units] = jnp.where(row == class_count, loss[0:1, 0:1], own_grads)
    both[:, units:] = mm(turned[...], agg_rows[...])
    if parts:
        for p, (rows, lanes) in enumerate(cut(*both.shape, parts)):
            copies.later(both.at[rows, lanes], second_out.at[p])
    else:
        copies.later(both, second_out)
    copies.finish()


def back_kernel(
    parts, pick_in, direct_in, slope_in, w_two_in, left_in, landed_in, second_in, out,
    pick, direct, slope, w_two, left, landed, rows, grads, sems,
):
    copies = Copies(sems)
    step = left.shape[0]
    groups, _, units = direct.shape
    pad = landed.shape[1] if w_two.ndim == 2 else w_two.shape[1] // 2
    loads = [copies(landed_in, landed), copies(pick_in, pick), copies(w_two_in, w_two)]
    both_loads = [(copies(direct_in.at[j], direct.at[j]), copies(slope_in.at[j], slope.at[j])) for j in range(groups)]
    left_load = copies(left_in, left)
    if parts:
        second_load = copies(second_in, grads.at[:, pl.ds(step, second_in.shape[1])])
    loads[0].wait()
    for d in range(landed.shape[0]):
        take_message(landed, d, rows)
    loads[1].wait()
    high, low = halves(mm_tn(pick[...], rows[...]))
    loads[2].wait()
    for j in range(groups):
        for load in both_loads[j]:
            load.wait()
        total = direct[j] + mm(high, w_two[j, pad:]) + mm(low, w_two[j, pad:])
        if j == 0:
            left_load.wait()
        result = mm(left[...], (total * slope[j]).astype(BF16))
        if parts:
            if j == 0:
                second_load.wait()
            for i in range(units // BLOCK):
                p = j * units // BLOCK + i
                grads[p, :step, :] = result[:, i * BLOCK : (i + 1) * BLOCK]
                copies.later(grads.at[p], out.at[p])
        else:
            grads[j] = result
            copies.later(grads.at[j], out.at[:, pl.ds(j * units, units)])
    copies.finish()


def sum_kernel(pieces_in, out, pieces, total, sems):
    copies = Copies(sems)
    count = pieces.shape[0]
    loads = [copies(pieces_in.at[k], pieces.at[k]) for k in range(count)]
    for load in loads:
        load.wait()
    held = pieces[0]
    for k in range(1, count):
        held = held + pieces[k]
    total[...] = held
    for k in range(count):
        copies.later(total, out.at[k])
    copies.finish()


def place_kernel(class_count, node_total, pieces, self1, neigh1, self2, neigh2, loss, both, sems):
    copies = Copies(sems)
    step = self1.shape[0]
    loads = []
    for p, (rows, lanes) in enumerate(cut(*both.shape, pieces.shape[0])):
        loads.append(copies(pieces.at[p, pl.ds(2 * step, pieces.shape[1] - 2 * step)], both.at[rows, lanes]))
    for p in range(pieces.shape[0]):
        at = pl.ds(p * BLOCK, BLOCK)
        copies.later(pieces.at[p, pl.ds(0, step)], self1.at[:, at])
        copies.later(pieces.at[p, pl.ds(step, step)], neigh1.at[:, at])
    for load in loads:
        load.wait()
    units = self2.shape[1]
    self2[...] = both[:class_count, :units]
    neigh2[...] = both[:class_count, units:]
    loss[...] = both[class_count : class_count + 1, 0:1] / node_total
    copies.finish()


def swap(value, count):
    blocks = value.reshape(count, -1, value.shape[-1])
    return lax.all_to_all(blocks, "node", 0, 0, tiled=True)


def gather_shifted(value, count):
    return [value] + [lax.ppermute(value, "feat", [(i, (i + k) % count) for i in range(count)]) for k in range(1, count)]


def shards(features, send_rows, send_count, tile_src, tile_val, labels, w_self1, w_neigh1, w_self2, w_neigh2):
    nodes, groups = lax.axis_size("node"), lax.axis_size("feat")
    own, step = features.shape
    slots = send_rows.shape[2]
    halo = nodes * slots
    total_src = own + halo
    cols = step * groups
    width = w_self1.shape[1]
    units, classes = w_self2.shape
    pad = -(-(classes + 1) // 16) * 16
    across = 2 * units // BLOCK
    parts = nodes if nodes % across == 0 and pad % (8 * (nodes // across)) == 0 and width == nodes * BLOCK else 0
    node_total = own * nodes
    grad_scale = 1.0 / math.sqrt(node_total)
    ids = lax.axis_index("feat").astype(jnp.int32).reshape(1)
    blocks = own // BLOCK
    packed_rows = 2 * step * groups + 2 * pad

    turned = features.T
    turned_all = gather_shifted(turned, groups)
    a_mat, pick = call(
        prepare_kernel,
        [((2 * own, total_src), BF16), ((halo, own), BF16)],
        (tile_src, send_count, tile_val, send_rows[0]),
        [(tile_val.shape, BF16), ((nodes, slots), jnp.int32), ((own, total_src), F32), ((2 * own, total_src), BF16), ((halo, own), BF16)],
        2 + 3 * blocks,
        moved=tile_val.size * 4,
    )
    full, packed, packed_weights = call(
        functools.partial(pack_kernel, groups),
        [((own, cols), BF16), ((halo, cols), BF16), ((packed_rows, units), BF16)],
        (ids, pick, w_self1, w_neigh1, w_self2.T, w_neigh2.T, *turned_all),
        [
            ((halo, own), BF16),
            ((cols, own), BF16),
            ((own, cols), BF16),
            ((halo, cols), BF16),
            ((2, step, width), BF16),
            ((2, classes, units), BF16),
            ((packed_rows, units), BF16),
        ],
        9,
        flops=2 * halo * own * cols,
        moved=halo * own * 2,
        near=groups - 1,
        room=12 + halo * own // 2**18,
    )
    weights = lax.all_gather(packed_weights, "feat")
    source = swap(packed, nodes).reshape(halo, cols)
    (near,) = call(
        near_kernel,
        [((own, cols), F32)],
        (a_mat, full),
        [((2 * own, own), BF16), ((own, cols), BF16), ((own, cols), F32)],
        3,
        flops=4 * own * own * cols,
        moved=4 * own * own,
    )
    agg, packed = call(
        first_kernel,
        [((own, cols), BF16), ((halo, cols), BF16)],
        (pick, a_mat, near, source),
        [((halo, own), BF16), ((2 * own, halo), BF16), ((own, cols), F32), ((halo, cols), BF16), ((own, cols), BF16), ((halo, cols), BF16)],
        6,
        flops=4 * own * total_src * cols,
        moved=4 * own * total_src,
    )
    landed = swap(packed, nodes).reshape(halo, cols)
    chunked = (groups, own, units)
    w_one, w_two, slope, part, logits, mine, left = call(
        own_kernel,
        [
            ((groups, 2 * cols, units), BF16),
            ((groups, 2 * pad, units), BF16),
            (chunked, F32),
            (chunked, F32),
            ((pad, own), F32),
            ((own, units), BF16),
            ((2 * step, own), BF16),
        ],
        (ids, full, agg, a_mat, turned, weights),
        [
            ((own, cols), BF16),
            ((own, cols), BF16),
            ((2 * own, own), BF16),
            ((2 * step, own), BF16),
            ((groups, packed_rows, units), BF16),
            ((groups, 2 * cols, units), BF16),
            ((groups, 2 * pad, units), BF16),
            (chunked, F32),
            (chunked, F32),
            ((pad, own), F32),
            (chunked, BF16),
            ((cols, own), BF16),
        ],
        10 + 2 * groups,
        flops=8 * own * own * width,
        moved=16 * own * width,
    )
    message = (nodes, *message_shape(slots, pad))
    turned_grads, agg_mine, loss, packed = call(
        functools.partial(second_kernel, classes, grad_scale),
        [((pad, own), BF16), ((own, units), BF16), ((8, 128), F32), (message, BF16)],
        (ids, a_mat, source, landed, w_one, w_two, part, logits, labels.reshape(1, own)),
        [
            ((2 * own, halo), BF16),
            ((halo, cols), BF16),
            ((halo, cols), BF16),
            ((groups, 2 * cols, units), BF16),
            ((groups, 2 * pad, units), BF16),
            (chunked, F32),
            ((pad, own), F32),
            ((1, own), jnp.int32),
            ((pad, own), BF16),
            ((8, 128), F32),
            (message, BF16),
            (chunked, BF16),
        ],
        11 + groups,
        flops=4 * own * halo * width,
        moved=12 * own * width,
    )
    landed = swap(packed, nodes)
    second_shape = (parts, pad * 2 * units // (BLOCK * parts), BLOCK) if parts else (pad, 2 * units)
    second, direct = call(
        functools.partial(middle_kernel, classes, parts),
        [(second_shape, F32), (chunked, F32)],
        (turned_grads, mine, agg_mine, loss, a_mat, w_two),
        [
            ((pad, own), BF16),
            ((own, units), BF16),
            ((own, units), BF16),
            ((8, 128), F32),
            ((own, own), BF16),
            ((groups, 2 * pad, units), BF16),
            ((pad, 2 * units), F32),
            (chunked, F32),
        ],
        6 + groups + max(parts, 1),
        flops=10 * own * pad * width,
        moved=8 * own * width,
    )
    out_shape = (parts, 2 * step + second_shape[1], BLOCK) if parts else (2 * step, width)
    (grads,) = call(
        functools.partial(back_kernel, parts),
        [(out_shape, F32)],
        (pick, direct, slope, w_two, left, landed, second),
        [
            ((halo, own), BF16),
            (chunked, F32),
            (chunked, F32),
            ((groups, 2 * pad, units), BF16),
            ((2 * step, own), BF16),
            (message, BF16),
            ((halo, pad), BF16),
            (out_shape, F32) if parts else ((groups, 2 * step, units), F32),
        ],
        5 + 2 * groups + max(parts, groups),
        flops=6 * own * pad * width,
        moved=12 * own * width,
    )
    if not parts:
        grads, second = lax.psum((grads, second), "node")
        loss = second[classes, 0] / node_total
        return (loss, grads[:step], grads[step:], second[:classes, :units].T, second[:classes, units:].T)
    grads = swap(grads, nodes)
    (grads,) = call(sum_kernel, [(out_shape, F32)], (grads,), [(out_shape, F32), (out_shape[1:], F32)], 2 * nodes, moved=2**20)
    grads = swap(grads, nodes)
    grad_self1, grad_neigh1, grad_self2, grad_neigh2, loss = call(
        functools.partial(place_kernel, classes, node_total),
        [((step, width), F32)] * 2 + [((classes, units), F32)] * 2 + [((1, 1), F32)],
        (grads,),
        [((pad, 2 * units), F32)],
        3 * nodes,
        out_specs=[VMEM] * 5,
    )
    return (loss.reshape(()), grad_self1, grad_neigh1, grad_self2.T, grad_neigh2.T)


def solution(mesh):
    in_specs = (
        P("node", "feat"),
        P("node", None, None),
        P("node", None),
        P("node", None),
        P("node", None, None, None),
        P("node"),
        P("feat", None),
        P("feat", None),
        P("feat", None),
        P("feat", None),
    )
    out_specs = (P(), P("feat", None), P("feat", None), P("feat", None), P("feat", None))
    return jax.shard_map(shards, mesh=mesh, in_specs=in_specs, out_specs=out_specs, check_vma=False)
```

```python
import functools
import math

import jax
import jax.numpy as jnp
from jax import lax
from jax.experimental import pallas as pl
from jax.experimental.pallas import tpu as pltpu
from jax.sharding import PartitionSpec as P

BLOCK = 128
F32 = jnp.float32
BF16 = jnp.bfloat16
VMEM = pl.BlockSpec(memory_space=pltpu.VMEM)
HBM = pl.BlockSpec(memory_space=pltpu.HBM)
SMEM = pl.BlockSpec(memory_space=pltpu.SMEM)


def mm(a, b):
    return lax.dot_general(a, b, (((1,), (0,)), ((), ())), preferred_element_type=F32)


def mm_nt(a, b):
    return lax.dot_general(a, b, (((1,), (1,)), ((), ())), preferred_element_type=F32)


def mm_tn(a, b):
    return lax.dot_general(a, b, (((0,), (0,)), ((), ())), preferred_element_type=F32)


def halves(value):
    high = value.astype(BF16)
    return high, (value - high.astype(F32)).astype(BF16)


def gelu_parts(v):
    inner = math.sqrt(2.0 / math.pi) * (v + 0.044715 * (v * v * v))
    t = jnp.tanh(inner)
    return 0.5 * (1.0 + t), t


def gelu(v):
    return v * gelu_parts(v)[0]


def gelu_slope(v):
    cdf, t = gelu_parts(v)
    inner_slope = math.sqrt(2.0 / math.pi) * (1.0 + 3 * 0.044715 * (v * v))
    return cdf + 0.5 * v * (1.0 - t * t) * inner_slope


def call(body, outs, args, scratch, copies, flops=0, moved=0, out_specs=None, near=0):
    return pl.pallas_call(
        body,
        out_shape=[jax.ShapeDtypeStruct(shape, dtype) for shape, dtype in outs],
        in_specs=[SMEM if arg.dtype == jnp.int32 and arg.size < 512 else HBM for arg in args[: len(args) - near]] + [VMEM] * near,
        out_specs=out_specs or [HBM] * len(outs),
        scratch_shapes=[pltpu.VMEM(shape, dtype) for shape, dtype in scratch] + [pltpu.SemaphoreType.DMA((copies,))],
        compiler_params=pltpu.CompilerParams(vmem_limit_bytes=58 * 2**20),
        cost_estimate=pl.CostEstimate(flops=flops, bytes_accessed=moved, transcendentals=0),
    )(*args)


class Copies:
    def __init__(self, sems):
        self.sems, self.used, self.open = sems, 0, []

    def __call__(self, src, dst):
        copy = pltpu.make_async_copy(src, dst, self.sems.at[self.used])
        copy.start()
        self.used += 1
        return copy

    def later(self, src, dst):
        self.open.append(self(src, dst))

    def finish(self):
        for copy in self.open:
            copy.wait()


def prepare_kernel(tile_src, count, tile_val, send_rows, a_out, pick_out, tiles, rows_in, dense, a_ref, pick, sems):
    copies = Copies(sems)
    blocks, per_block = tile_val.shape[0], tile_val.shape[1]
    own = blocks * BLOCK
    rows_copy = copies(send_rows, rows_in)
    tile_copies = [copies(tile_val.at[b], tiles.at[b]) for b in range(blocks)]
    dense[...] = jnp.zeros_like(dense)
    rows_copy.wait()
    dests, slots = rows_in.shape
    columns = rows_in[...].astype(F32).T
    row_id = lax.broadcasted_iota(jnp.int32, (slots, own), 1).astype(F32)
    slot_id = lax.broadcasted_iota(jnp.int32, (slots, own), 0)
    for d in range(dests):
        hit = (columns[:, d : d + 1] == row_id) & (slot_id < count[0, d])
        pick[pl.ds(d * slots, slots), :] = jnp.where(hit, 1.0, 0.0).astype(BF16)
    copies.later(pick, pick_out)
    for b in range(blocks):
        rows = pl.ds(b * BLOCK, BLOCK)
        low_rows = pl.ds(own + b * BLOCK, BLOCK)
        tile_copies[b].wait()

        def add(k, _, b=b, rows=rows):
            at = pl.ds(pl.multiple_of(tile_src[b, k] * BLOCK, BLOCK), BLOCK)
            dense[rows, at] = dense[rows, at] + tiles[b, k].astype(F32)
            return 0

        lax.fori_loop(0, per_block, add, 0)
        high, low = halves(dense[rows, :])
        a_ref[rows, :] = high
        a_ref[low_rows, :] = low
        copies.later(a_ref.at[rows], a_out.at[rows])
        copies.later(a_ref.at[low_rows], a_out.at[low_rows])
    copies.finish()


def pack_kernel(
    groups, ids, pick_in, w_self1, w_neigh1, w_self2, w_neigh2, *refs
):
    pieces = refs[:groups]
    full_out, packed_out, weights_out, pick, turned, full, packed, firsts, seconds, weights, sems = refs[groups:]
    copies = Copies(sems)
    step = pieces[0].shape[0]
    classes, units = w_self2.shape
    base = 2 * step * groups
    pad = (weights.shape[0] - base) // 2
    loads = [copies(pick_in, pick)]
    loads.append(copies(pieces[0], turned.at[pl.ds(pl.multiple_of(ids[0] * step, step), step)]))
    for k, piece in enumerate(pieces[1:], 1):
        group = lax.rem(ids[0] + groups - k, groups)
        turned[pl.ds(pl.multiple_of(group * step, step), step), :] = piece[...]
    w_loads = [copies(w_self1, firsts.at[0]), copies(w_neigh1, firsts.at[1]), copies(w_self2, seconds.at[0]), copies(w_neigh2, seconds.at[1])]
    weights[pl.ds(base, 2 * pad), :] = jnp.zeros((2 * pad, units), BF16)
    for load in loads:
        load.wait()
    rows = turned[...].T
    full[...] = rows
    copies.later(full, full_out)
    packed[...] = mm(pick[...], rows).astype(BF16)
    copies.later(packed, packed_out)
    for load in w_loads:
        load.wait()
    for j in range(groups):
        at = pl.ds(j * units, units)
        weights[pl.ds(2 * step * j, step), :] = firsts[0, :, at]
        weights[pl.ds(2 * step * j + step, step), :] = firsts[1, :, at]
    weights[pl.ds(base, classes), :] = seconds[0]
    weights[pl.ds(base + pad, classes), :] = seconds[1]
    copies.later(weights, weights_out)
    copies.finish()


def near_kernel(a_in, full_in, out, a_ref, full, near, sems):
    copies = Copies(sems)
    own = full.shape[0]
    loads = [copies(full_in, full), copies(a_in.at[:, pl.ds(0, own)], a_ref)]
    for load in loads:
        load.wait()
    both = mm(a_ref[...], full[...])
    near[...] = both[:own] + both[own:]
    copies(near, out).wait()


def first_kernel(pick_in, a_in, near_in, source_in, agg_out, packed_out, pick, a_ref, near, source, agg, packed, sems):
    copies = Copies(sems)
    own = near.shape[0]
    loads = [
        copies(source_in, source),
        copies(a_in.at[:, pl.ds(own, source.shape[0])], a_ref),
        copies(near_in, near),
        copies(pick_in, pick),
    ]
    for load in loads[:3]:
        load.wait()
    both = mm(a_ref[...], source[...])
    agg[...] = (near[...] + both[:own] + both[own:]).astype(BF16)
    copies.later(agg, agg_out)
    loads[3].wait()
    packed[...] = mm(pick[...], agg[...]).astype(BF16)
    copies.later(packed, packed_out)
    copies.finish()


def own_kernel(
    ids, full_in, agg_in, a_in, turned_in, weights_in,
    w_one_out, w_two_out, slope_out, part_out, logits_out, mine_out, left_out,
    full, agg, a_ref, left, weights, w_one, w_two, slope, part, logits, hidden, agg_turned, sems,
):
    copies = Copies(sems)
    groups, _, units = weights.shape
    own, cols = full.shape
    step = turned_in.shape[0]
    pad = logits.shape[0]
    base = 2 * step * groups
    loads = [
        copies(weights_in, weights),
        copies(full_in, full),
        copies(agg_in, agg),
        copies(a_in.at[:, pl.ds(0, own)], a_ref),
        copies(turned_in, left.at[pl.ds(0, step)]),
    ]
    loads[0].wait()
    for g in range(groups):
        for j in range(groups):
            w_one[j, pl.ds(g * step, step), :] = weights[g, pl.ds(2 * step * j, step), :]
            w_one[j, pl.ds(cols + g * step, step), :] = weights[g, pl.ds(2 * step * j + step, step), :]
        w_two[g] = weights[g, pl.ds(base, 2 * pad), :]
    copies.later(w_one, w_one_out)
    copies.later(w_two, w_two_out)
    loads[1].wait()
    loads[2].wait()
    agg_turned[...] = agg[...].T
    loads[4].wait()
    left[pl.ds(step, step), :] = agg_turned[pl.ds(pl.multiple_of(ids[0] * step, step), step), :]
    copies.later(left, left_out)
    both = jnp.concatenate([full[...], agg[...]], axis=1)
    total = None
    for j in range(groups):
        pre = mm(both, w_one[j])
        slope[j] = gelu_slope(pre)
        copies.later(slope.at[j], slope_out.at[j])
        out = gelu(pre).astype(BF16)
        hidden[j] = out
        if j == 0:
            loads[3].wait()
        spread = mm(a_ref[...], out)
        part[j] = spread[:own] + spread[own:]
        copies.later(part.at[j], part_out.at[j])
        term = mm_nt(w_two[j, :pad], out)
        total = term if total is None else total + term
    logits[...] = total
    copies.later(logits, logits_out)
    copies.later(hidden.at[ids[0]], mine_out)
    copies.finish()


def second_kernel(
    class_count, grad_scale, ids, a_in, source_in, landed_in, w_one_in, w_two_in, part_in, logits_in, labels_in,
    turned_out, mine_out, loss_out, packed_out,
    a_ref, source, landed, w_one, w_two, part, logits, labels, turned, loss, packed, agg, sems,
):
    copies = Copies(sems)
    groups, own, units = part.shape
    pad = logits.shape[0]
    halo = landed.shape[0]
    slots = halo // packed.shape[0]
    chunk = min(own, halo)
    loads = [
        copies(source_in, source),
        copies(landed_in, landed),
        copies(w_one_in, w_one),
        copies(a_in.at[:, pl.ds(own, halo)], a_ref),
        copies(logits_in, logits),
        copies(w_two_in, w_two),
        copies(labels_in, labels),
    ]
    part_loads = [copies(part_in.at[j], part.at[j]) for j in range(groups)]
    for load in loads[:3]:
        load.wait()
    total = None
    for j in range(groups):

        def one(r, held, j=j):
            rows = pl.ds(pl.multiple_of(r * chunk, chunk), chunk)
            srcs = pl.ds(pl.multiple_of(r * chunk, chunk), chunk)
            both = jnp.concatenate([source[rows, :], landed[rows, :]], axis=1)
            out = gelu(mm(both, w_one[j])).astype(BF16)
            if j == 0 and halo == chunk:
                loads[3].wait()
            spread = mm(a_ref[:, srcs], out)
            spread = spread[:own] + spread[own:]
            if halo == chunk:
                part_loads[j].wait()
                return part[j] + spread
            return held + spread

        if halo == chunk:
            held = one(0, None)
        else:
            if j == 0:
                loads[3].wait()
            part_loads[j].wait()
            held = lax.fori_loop(0, halo // chunk, one, part[j])
        agg[j] = held.astype(BF16)
        if j == 0:
            loads[4].wait()
            loads[5].wait()
            total = logits[...]
        total = total + mm_nt(w_two[j, pad:], agg[j])
    copies.later(agg.at[ids[0]], mine_out)
    class_id = lax.broadcasted_iota(jnp.int32, total.shape, 0)
    real = class_id < class_count
    top = jnp.max(jnp.where(real, total, -jnp.inf), axis=0, keepdims=True)
    shifted = total - top
    powers = jnp.where(real, jnp.exp(shifted), 0.0)
    sums = jnp.sum(powers, axis=0, keepdims=True)
    loads[6].wait()
    target = (class_id == labels[...]).astype(F32)
    turned[...] = ((powers / sums - target) * grad_scale).astype(BF16)
    copies.later(turned, turned_out)
    row_loss = jnp.log(sums) - jnp.sum(shifted * target, axis=0, keepdims=True)
    loss[...] = jnp.broadcast_to(jnp.sum(row_loss, axis=1, keepdims=True), loss.shape)
    copies.later(loss, loss_out)
    back = mm(turned[...], a_ref[:own, :]).T.astype(BF16)
    for d in range(packed.shape[0]):
        put_message(packed, d, back[d * slots : (d + 1) * slots])
    copies.later(packed, packed_out)
    copies.finish()


def message_shape(slots, pad):
    compact = BLOCK < pad <= BLOCK + BLOCK // 2 and slots % 32 == 0
    return (slots + slots // 2, BLOCK) if compact else (slots, pad)


def put_message(packed, d, rows):
    slots, pad = rows.shape
    if packed.shape[1:] == (slots, pad):
        packed[d] = rows
        return
    half, tail = slots // 2, pad - BLOCK
    packed[d, :slots, :] = rows[:, :BLOCK]
    filler = jnp.zeros((half, BLOCK // 2 - tail), BF16)
    packed[d, slots:, :] = jnp.concatenate([rows[:half, BLOCK:], filler, rows[half:, BLOCK:], filler], axis=1)


def take_message(packed, d, landed):
    slots, pad = landed.shape[0] // packed.shape[0], landed.shape[1]
    if packed.shape[1:] == (slots, pad):
        landed[pl.ds(d * slots, slots), :] = packed[d]
        return
    half, tail = slots // 2, pad - BLOCK
    landed[pl.ds(d * slots, slots), :BLOCK] = packed[d, :slots, :]
    landed[pl.ds(d * slots, half), BLOCK:] = packed[d, slots:, :tail]
    landed[pl.ds(d * slots + half, half), BLOCK:] = packed[d, slots:, BLOCK // 2 : BLOCK // 2 + tail]


def second_grads_kernel(class_count, turned_in, self_in, agg_in, loss_in, out, turned, self_rows, agg_rows, loss, both, sems):
    copies = Copies(sems)
    loads = [copies(turned_in, turned), copies(self_in, self_rows), copies(loss_in, loss), copies(agg_in, agg_rows)]
    units = self_rows.shape[1]
    for load in loads[:3]:
        load.wait()
    own_grads = mm(turned[...], self_rows[...])
    row = lax.broadcasted_iota(jnp.int32, own_grads.shape, 0)
    both[:, :units] = jnp.where(row == class_count, loss[0:1, 0:1], own_grads)
    copies.later(both.at[:, pl.ds(0, units)], out.at[:, pl.ds(0, units)])
    loads[3].wait()
    both[:, units:] = mm(turned[...], agg_rows[...])
    copies.later(both.at[:, pl.ds(units, units)], out.at[:, pl.ds(units, units)])
    copies.finish()


def direct_kernel(turned_in, a_in, w_two_in, after, out, turned, a_ref, w_two, direct, sems):
    copies = Copies(sems)
    own = a_ref.shape[0]
    pad = turned.shape[0]
    loads = [copies(turned_in, turned), copies(a_in.at[pl.ds(0, own), pl.ds(0, own)], a_ref), copies(w_two_in, w_two)]
    loads[0].wait()
    loads[1].wait()
    high, low = halves(mm(turned[...], a_ref[...]).T)
    rows = turned[...].T
    loads[2].wait()
    for j in range(direct.shape[0]):
        direct[j] = mm(rows, w_two[j, :pad]) + mm(high, w_two[j, pad:]) + mm(low, w_two[j, pad:])
        copies.later(direct.at[j], out.at[j])
    copies.finish()


def back_kernel(
    parts, pick_in, direct_in, slope_in, w_two_in, left_in, landed_in, out,
    pick, direct, slope, w_two, left, landed, rows, grads, sems,
):
    copies = Copies(sems)
    groups, _, units = direct.shape
    pad = w_two.shape[1] // 2
    loads = [copies(landed_in, landed), copies(pick_in, pick), copies(w_two_in, w_two)]
    both_loads = [(copies(direct_in.at[j], direct.at[j]), copies(slope_in.at[j], slope.at[j])) for j in range(groups)]
    left_load = copies(left_in, left)
    loads[0].wait()
    for d in range(landed.shape[0]):
        take_message(landed, d, rows)
    loads[1].wait()
    high, low = halves(mm_tn(pick[...], rows[...]))
    loads[2].wait()
    for j in range(groups):
        for load in both_loads[j]:
            load.wait()
        total = direct[j] + mm(high, w_two[j, pad:]) + mm(low, w_two[j, pad:])
        if j == 0:
            left_load.wait()
        result = mm(left[...], (total * slope[j]).astype(BF16))
        if parts:
            for i in range(units // BLOCK):
                p = j * units // BLOCK + i
                grads[p] = result[:, i * BLOCK : (i + 1) * BLOCK]
                copies.later(grads.at[p], out.at[p])
        else:
            grads[j] = result
            copies.later(grads.at[j], out.at[:, pl.ds(j * units, units)])
    copies.finish()


def sum_kernel(pieces_in, out, pieces, total, sems):
    copies = Copies(sems)
    count = pieces.shape[0]
    loads = [copies(pieces_in.at[k], pieces.at[k]) for k in range(count)]
    for load in loads:
        load.wait()
    held = pieces[0]
    for k in range(1, count):
        held = held + pieces[k]
    total[...] = held
    for k in range(count):
        copies.later(total, out.at[k])
    copies.finish()


def place_kernel(class_count, node_total, pieces, second, other, self1, neigh1, self2, neigh2, loss, one, two, sems):
    copies = Copies(sems)
    step = self1.shape[0]
    units = self2.shape[1]
    loads = [copies(second, one), copies(other, two)]
    for p in range(pieces.shape[0]):
        at = pl.ds(p * BLOCK, BLOCK)
        copies.later(pieces.at[p, pl.ds(0, step)], self1.at[:, at])
        copies.later(pieces.at[p, pl.ds(step, step)], neigh1.at[:, at])
    for load in loads:
        load.wait()
    self2[...] = one[:class_count, :units] + two[:class_count, :units]
    neigh2[...] = one[:class_count, units:] + two[:class_count, units:]
    row = slice(class_count, class_count + 1)
    loss[...] = (one[row, 0:1] + two[row, 0:1]) / node_total
    copies.finish()


def swap(value, count):
    blocks = value.reshape(count, -1, value.shape[-1])
    return lax.all_to_all(blocks, "node", 0, 0, tiled=True)


def gather_shifted(value, count):
    return [value] + [lax.ppermute(value, "feat", [(i, (i + k) % count) for i in range(count)]) for k in range(1, count)]


def shards(features, send_rows, send_count, tile_src, tile_val, labels, w_self1, w_neigh1, w_self2, w_neigh2):
    nodes, groups = lax.axis_size("node"), lax.axis_size("feat")
    own, step = features.shape
    slots = send_rows.shape[2]
    halo = nodes * slots
    total_src = own + halo
    cols = step * groups
    width = w_self1.shape[1]
    units, classes = w_self2.shape
    pad = -(-(classes + 1) // 16) * 16
    parts = nodes if nodes % 2 == 0 and width == nodes * BLOCK else 0
    node_total = own * nodes
    grad_scale = 1.0 / math.sqrt(node_total)
    ids = lax.axis_index("feat").astype(jnp.int32).reshape(1)
    blocks = own // BLOCK
    packed_rows = 2 * step * groups + 2 * pad

    turned = features.T
    turned_all = gather_shifted(turned, groups)
    a_mat, pick = call(
        prepare_kernel,
        [((2 * own, total_src), BF16), ((halo, own), BF16)],
        (tile_src, send_count, tile_val, send_rows[0]),
        [(tile_val.shape, BF16), ((nodes, slots), jnp.int32), ((own, total_src), F32), ((2 * own, total_src), BF16), ((halo, own), BF16)],
        2 + 3 * blocks,
        moved=tile_val.size * 4,
    )
    full, packed, packed_weights = call(
        functools.partial(pack_kernel, groups),
        [((own, cols), BF16), ((halo, cols), BF16), ((packed_rows, units), BF16)],
        (ids, pick, w_self1, w_neigh1, w_self2.T, w_neigh2.T, *turned_all),
        [
            ((halo, own), BF16),
            ((cols, own), BF16),
            ((own, cols), BF16),
            ((halo, cols), BF16),
            ((2, step, width), BF16),
            ((2, classes, units), BF16),
            ((packed_rows, units), BF16),
        ],
        9,
        flops=2 * halo * own * cols,
        moved=halo * own * 2,
        near=groups - 1,
    )
    weights = lax.all_gather(packed_weights, "feat")
    source = swap(packed, nodes).reshape(halo, cols)
    (near,) = call(
        near_kernel,
        [((own, cols), F32)],
        (a_mat, full),
        [((2 * own, own), BF16), ((own, cols), BF16), ((own, cols), F32)],
        3,
        flops=4 * own * own * cols,
        moved=4 * own * own,
    )
    agg, packed = call(
        first_kernel,
        [((own, cols), BF16), ((halo, cols), BF16)],
        (pick, a_mat, near, source),
        [((halo, own), BF16), ((2 * own, halo), BF16), ((own, cols), F32), ((halo, cols), BF16), ((own, cols), BF16), ((halo, cols), BF16)],
        6,
        flops=4 * own * total_src * cols,
        moved=4 * own * total_src,
    )
    landed = swap(packed, nodes).reshape(halo, cols)
    chunked = (groups, own, units)
    w_one, w_two, slope, part, logits, mine, left = call(
        own_kernel,
        [
            ((groups, 2 * cols, units), BF16),
            ((groups, 2 * pad, units), BF16),
            (chunked, F32),
            (chunked, F32),
            ((pad, own), F32),
            ((own, units), BF16),
            ((2 * step, own), BF16),
        ],
        (ids, full, agg, a_mat, turned, weights),
        [
            ((own, cols), BF16),
            ((own, cols), BF16),
            ((2 * own, own), BF16),
            ((2 * step, own), BF16),
            ((groups, packed_rows, units), BF16),
            ((groups, 2 * cols, units), BF16),
            ((groups, 2 * pad, units), BF16),
            (chunked, F32),
            (chunked, F32),
            ((pad, own), F32),
            (chunked, BF16),
            ((cols, own), BF16),
        ],
        10 + 2 * groups,
        flops=8 * own * own * width,
        moved=16 * own * width,
    )
    message = (nodes, *message_shape(slots, pad))
    turned_grads, agg_mine, loss, packed = call(
        functools.partial(second_kernel, classes, grad_scale),
        [((pad, own), BF16), ((own, units), BF16), ((8, 128), F32), (message, BF16)],
        (ids, a_mat, source, landed, w_one, w_two, part, logits, labels.reshape(1, own)),
        [
            ((2 * own, halo), BF16),
            ((halo, cols), BF16),
            ((halo, cols), BF16),
            ((groups, 2 * cols, units), BF16),
            ((groups, 2 * pad, units), BF16),
            (chunked, F32),
            ((pad, own), F32),
            ((1, own), jnp.int32),
            ((pad, own), BF16),
            ((8, 128), F32),
            (message, BF16),
            (chunked, BF16),
        ],
        11 + groups,
        flops=4 * own * halo * width,
        moved=12 * own * width,
    )
    landed = swap(packed, nodes)
    (local_second,) = call(
        functools.partial(second_grads_kernel, classes),
        [((pad, 2 * units), F32)],
        (turned_grads, mine, agg_mine, loss),
        [((pad, own), BF16), ((own, units), BF16), ((own, units), BF16), ((8, 128), F32), ((pad, 2 * units), F32)],
        6,
        flops=4 * own * pad * units,
        moved=4 * own * units,
    )
    second = local_second
    if parts:
        second = lax.psum(second, "node", axis_index_groups=[list(range(y, nodes, 2)) for y in range(2)])
    (direct,) = call(
        direct_kernel,
        [(chunked, F32)],
        (turned_grads, a_mat, w_two, local_second),
        [((pad, own), BF16), ((own, own), BF16), ((groups, 2 * pad, units), BF16), (chunked, F32)],
        3 + groups,
        flops=6 * own * pad * width,
        moved=8 * own * width,
    )
    out_shape = (parts, 2 * step, BLOCK) if parts else (2 * step, width)
    (grads,) = call(
        functools.partial(back_kernel, parts),
        [(out_shape, F32)],
        (pick, direct, slope, w_two, left, landed),
        [
            ((halo, own), BF16),
            (chunked, F32),
            (chunked, F32),
            ((groups, 2 * pad, units), BF16),
            ((2 * step, own), BF16),
            (message, BF16),
            ((halo, pad), BF16),
            (out_shape, F32) if parts else ((groups, 2 * step, units), F32),
        ],
        4 + 2 * groups + max(parts, groups),
        flops=6 * own * pad * width,
        moved=12 * own * width,
    )
    if not parts:
        grads, second = lax.psum((grads, second), "node")
        loss = second[classes, 0] / node_total
        return (loss, grads[:step], grads[step:], second[:classes, :units].T, second[:classes, units:].T)
    grads = swap(grads, nodes)
    (grads,) = call(sum_kernel, [(out_shape, F32)], (grads,), [(out_shape, F32), (out_shape[1:], F32)], 2 * nodes, moved=2**20)
    grads = swap(grads, nodes)
    other = lax.ppermute(second, "node", [(i, i ^ 1) for i in range(nodes)])
    grad_self1, grad_neigh1, grad_self2, grad_neigh2, loss = call(
        functools.partial(place_kernel, classes, node_total),
        [((step, width), F32)] * 2 + [((classes, units), F32)] * 2 + [((1, 1), F32)],
        (grads, second, other),
        [((pad, 2 * units), F32)] * 2,
        2 + 2 * nodes,
        out_specs=[VMEM] * 5,
    )
    return (loss.reshape(()), grad_self1, grad_neigh1, grad_self2.T, grad_neigh2.T)


def solution(mesh):
    in_specs = (
        P("node", "feat"),
        P("node", None, None),
        P("node", None),
        P("node", None),
        P("node", None, None, None),
        P("node"),
        P("feat", None),
        P("feat", None),
        P("feat", None),
        P("feat", None),
    )
    out_specs = (P(), P("feat", None), P("feat", None), P("feat", None), P("feat", None))
    return jax.shard_map(shards, mesh=mesh, in_specs=in_specs, out_specs=out_specs, check_vma=False)
```

```python
import functools
import math

import jax
import jax.numpy as jnp
from jax import lax
from jax.experimental import pallas as pl
from jax.experimental.pallas import tpu as pltpu
from jax.sharding import PartitionSpec as P

BLOCK = 128
F32 = jnp.float32
BF16 = jnp.bfloat16
VMEM = pl.BlockSpec(memory_space=pltpu.VMEM)
HBM = pl.BlockSpec(memory_space=pltpu.HBM)
SMEM = pl.BlockSpec(memory_space=pltpu.SMEM)


def mm(a, b):
    return lax.dot_general(a, b, (((1,), (0,)), ((), ())), preferred_element_type=F32)


def mm_nt(a, b):
    return lax.dot_general(a, b, (((1,), (1,)), ((), ())), preferred_element_type=F32)


def mm_tn(a, b):
    return lax.dot_general(a, b, (((0,), (0,)), ((), ())), preferred_element_type=F32)


def halves(value):
    high = value.astype(BF16)
    return high, (value - high.astype(F32)).astype(BF16)


def spread(a, rows):
    own = a.shape[0]
    parts = []
    for c in range(rows.shape[0] // own):
        part = rows[c * own : (c + 1) * own]
        parts += [part, part]
    return mm(a, jnp.concatenate(parts, axis=0))


def gelu_parts(v):
    inner = math.sqrt(2.0 / math.pi) * (v + 0.044715 * (v * v * v))
    t = jnp.tanh(inner)
    return 0.5 * (1.0 + t), t


def gelu(v):
    return v * gelu_parts(v)[0]


def gelu_slope(v):
    cdf, t = gelu_parts(v)
    inner_slope = math.sqrt(2.0 / math.pi) * (1.0 + 3 * 0.044715 * (v * v))
    return cdf + 0.5 * v * (1.0 - t * t) * inner_slope


def call(body, outs, args, scratch, copies, flops=0, moved=0, out_specs=None, near=0):
    beside = sum(arg.size * arg.dtype.itemsize for arg in args[len(args) - near :]) if near else -4 * 2**20
    return pl.pallas_call(
        body,
        out_shape=[jax.ShapeDtypeStruct(shape, dtype) for shape, dtype in outs],
        in_specs=[SMEM if arg.dtype == jnp.int32 and arg.size < 512 else HBM for arg in args[: len(args) - near]] + [VMEM] * near,
        out_specs=out_specs or [HBM] * len(outs),
        scratch_shapes=[pltpu.VMEM(shape, dtype) for shape, dtype in scratch] + [pltpu.SemaphoreType.DMA((copies,))],
        compiler_params=pltpu.CompilerParams(vmem_limit_bytes=54 * 2**20 - beside - 2048),
        cost_estimate=pl.CostEstimate(flops=flops, bytes_accessed=moved, transcendentals=0),
    )(*args)


class Copies:
    def __init__(self, sems):
        self.sems, self.used, self.open = sems, 0, []

    def __call__(self, src, dst):
        copy = pltpu.make_async_copy(src, dst, self.sems.at[self.used])
        copy.start()
        self.used += 1
        return copy

    def later(self, src, dst):
        self.open.append(self(src, dst))

    def finish(self):
        for copy in self.open:
            copy.wait()


def prepare_kernel(tile_src, count, tile_val, send_rows, a_out, pick_out, tiles, rows_in, dense, a_ref, pick, sems):
    copies = Copies(sems)
    blocks, per_block = tile_val.shape[0], tile_val.shape[1]
    own = blocks * BLOCK
    rows_copy = copies(send_rows, rows_in)
    tile_copies = [copies(tile_val.at[b], tiles.at[b]) for b in range(blocks)]
    dense[...] = jnp.zeros_like(dense)
    rows_copy.wait()
    dests, slots = rows_in.shape
    columns = rows_in[...].astype(F32).T
    row_id = lax.broadcasted_iota(jnp.int32, (slots, own), 1).astype(F32)
    slot_id = lax.broadcasted_iota(jnp.int32, (slots, own), 0)
    for d in range(dests):
        hit = (columns[:, d : d + 1] == row_id) & (slot_id < count[0, d])
        pick[pl.ds(d * slots, slots), :] = jnp.where(hit, 1.0, 0.0).astype(BF16)
    copies.later(pick, pick_out)
    for b in range(blocks):
        rows = pl.ds(b * BLOCK, BLOCK)
        tile_copies[b].wait()

        def add(k, _, b=b, rows=rows):
            at = pl.ds(pl.multiple_of(tile_src[b, k] * BLOCK, BLOCK), BLOCK)
            dense[rows, at] = dense[rows, at] + tiles[b, k].astype(F32)
            return 0

        lax.fori_loop(0, per_block, add, 0)
        for c in range(dense.shape[1] // own):
            high, low = halves(dense[rows, pl.ds(c * own, own)])
            a_ref[rows, pl.ds(2 * c * own, own)] = high
            a_ref[rows, pl.ds((2 * c + 1) * own, own)] = low
        copies.later(a_ref.at[rows], a_out.at[rows])
    copies.finish()


def pack_kernel(
    groups, ids, pick_in, w_self1, w_neigh1, w_self2, w_neigh2, *refs
):
    pieces = refs[:groups]
    full_out, packed_out, weights_out, pick, turned, full, packed, firsts, seconds, weights, sems = refs[groups:]
    copies = Copies(sems)
    step = pieces[0].shape[0]
    classes, units = w_self2.shape
    base = 2 * step * groups
    pad = (weights.shape[0] - base) // 2
    loads = [copies(pick_in, pick)]
    loads.append(copies(pieces[0], turned.at[pl.ds(pl.multiple_of(ids[0] * step, step), step)]))
    for k, piece in enumerate(pieces[1:], 1):
        group = lax.rem(ids[0] + groups - k, groups)
        turned[pl.ds(pl.multiple_of(group * step, step), step), :] = piece[...]
    w_loads = [copies(w_self1, firsts.at[0]), copies(w_neigh1, firsts.at[1]), copies(w_self2, seconds.at[0]), copies(w_neigh2, seconds.at[1])]
    weights[pl.ds(base, 2 * pad), :] = jnp.zeros((2 * pad, units), BF16)
    for load in loads:
        load.wait()
    rows = turned[...].T
    full[...] = rows
    copies.later(full, full_out)
    packed[...] = mm(pick[...], rows).astype(BF16)
    copies.later(packed, packed_out)
    for load in w_loads:
        load.wait()
    for j in range(groups):
        at = pl.ds(j * units, units)
        weights[pl.ds(2 * step * j, step), :] = firsts[0, :, at]
        weights[pl.ds(2 * step * j + step, step), :] = firsts[1, :, at]
    weights[pl.ds(base, classes), :] = seconds[0]
    weights[pl.ds(base + pad, classes), :] = seconds[1]
    copies.later(weights, weights_out)
    copies.finish()


def near_kernel(a_in, full_in, out, a_ref, full, near, sems):
    copies = Copies(sems)
    own = full.shape[0]
    loads = [copies(full_in, full), copies(a_in.at[:, pl.ds(0, 2 * own)], a_ref)]
    for load in loads:
        load.wait()
    near[...] = spread(a_ref[...], full[...])
    copies(near, out).wait()


def first_kernel(pick_in, a_in, near_in, source, agg_out, packed_out, source_out, pick, a_ref, near, agg, packed, sems):
    copies = Copies(sems)
    own = near.shape[0]
    copies.later(source, source_out)
    loads = [
        copies(a_in.at[:, pl.ds(2 * own, 2 * source.shape[0])], a_ref),
        copies(near_in, near),
        copies(pick_in, pick),
    ]
    for load in loads[:2]:
        load.wait()
    agg[...] = (near[...] + spread(a_ref[...], source[...])).astype(BF16)
    copies.later(agg, agg_out)
    loads[2].wait()
    packed[...] = mm(pick[...], agg[...]).astype(BF16)
    copies.later(packed, packed_out)
    copies.finish()


def own_kernel(
    ids, full_in, agg_in, a_in, turned_in, weights_in,
    w_one_out, w_two_out, slope_out, part_out, logits_out, mine_out, left_out,
    full, agg, a_ref, left, weights, w_one, w_two, slope, part, logits, hidden, agg_turned, sems,
):
    copies = Copies(sems)
    groups, _, units = weights.shape
    own, cols = full.shape
    step = turned_in.shape[0]
    pad = logits.shape[0]
    base = 2 * step * groups
    loads = [
        copies(weights_in, weights),
        copies(full_in, full),
        copies(agg_in, agg),
        copies(a_in.at[:, pl.ds(0, 2 * own)], a_ref),
        copies(turned_in, left.at[pl.ds(0, step)]),
    ]
    loads[0].wait()
    for g in range(groups):
        for j in range(groups):
            w_one[j, pl.ds(g * step, step), :] = weights[g, pl.ds(2 * step * j, step), :]
            w_one[j, pl.ds(cols + g * step, step), :] = weights[g, pl.ds(2 * step * j + step, step), :]
        w_two[g] = weights[g, pl.ds(base, 2 * pad), :]
    copies.later(w_one, w_one_out)
    copies.later(w_two, w_two_out)
    loads[1].wait()
    loads[2].wait()
    agg_turned[...] = agg[...].T
    loads[4].wait()
    left[pl.ds(step, step), :] = agg_turned[pl.ds(pl.multiple_of(ids[0] * step, step), step), :]
    copies.later(left, left_out)
    both = jnp.concatenate([full[...], agg[...]], axis=1)
    total = None
    for j in range(groups):
        pre = mm(both, w_one[j])
        slope[j] = gelu_slope(pre)
        copies.later(slope.at[j], slope_out.at[j])
        out = gelu(pre).astype(BF16)
        hidden[j] = out
        if j == 0:
            loads[3].wait()
        part[j] = spread(a_ref[...], out)
        copies.later(part.at[j], part_out.at[j])
        term = mm_nt(w_two[j, :pad], out)
        total = term if total is None else total + term
    logits[...] = total
    copies.later(logits, logits_out)
    copies.later(hidden.at[ids[0]], mine_out)
    copies.finish()


def second_kernel(
    class_count, grad_scale, ids, a_in, source_in, w_one_in, w_two_in, part_in, logits_in, labels_in, landed,
    turned_out, mine_out, loss_out, packed_out,
    a_ref, source, w_one, w_two, part, logits, labels, turned, loss, packed, agg, sems,
):
    copies = Copies(sems)
    groups, own, units = part.shape
    pad = logits.shape[0]
    halo = landed.shape[0]
    slots = halo // packed.shape[0]
    chunk = own
    loads = [
        copies(source_in, source),
        copies(w_one_in, w_one),
        copies(a_in.at[:, pl.ds(2 * own, 2 * halo)], a_ref),
        copies(logits_in, logits),
        copies(w_two_in, w_two),
        copies(labels_in, labels),
    ]
    part_loads = [copies(part_in.at[j], part.at[j]) for j in range(groups)]
    for load in loads[:2]:
        load.wait()
    total = None
    for j in range(groups):

        def one(r, held, j=j):
            rows = pl.ds(pl.multiple_of(r * chunk, chunk), chunk)
            srcs = pl.ds(pl.multiple_of(2 * r * chunk, chunk), 2 * chunk)
            both = jnp.concatenate([source[rows, :], landed[rows, :]], axis=1)
            out = gelu(mm(both, w_one[j])).astype(BF16)
            if j == 0 and halo == chunk:
                loads[2].wait()
            more = spread(a_ref[:, srcs], out)
            if halo == chunk:
                part_loads[j].wait()
                return part[j] + more
            return held + more

        if halo == chunk:
            held = one(0, None)
        else:
            if j == 0:
                loads[2].wait()
            part_loads[j].wait()
            held = lax.fori_loop(0, halo // chunk, one, part[j])
        agg[j] = held.astype(BF16)
        if j == 0:
            loads[3].wait()
            loads[4].wait()
            total = logits[...]
        total = total + mm_nt(w_two[j, pad:], agg[j])
    copies.later(agg.at[ids[0]], mine_out)
    class_id = lax.broadcasted_iota(jnp.int32, total.shape, 0)
    real = class_id < class_count
    top = jnp.max(jnp.where(real, total, -jnp.inf), axis=0, keepdims=True)
    shifted = total - top
    powers = jnp.where(real, jnp.exp(shifted), 0.0)
    sums = jnp.sum(powers, axis=0, keepdims=True)
    loads[5].wait()
    target = (class_id == labels[...]).astype(F32)
    turned[...] = ((powers / sums - target) * grad_scale).astype(BF16)
    copies.later(turned, turned_out)
    row_loss = jnp.log(sums) - jnp.sum(shifted * target, axis=0, keepdims=True)
    loss[...] = jnp.broadcast_to(jnp.sum(row_loss, axis=1, keepdims=True), loss.shape)
    copies.later(loss, loss_out)
    per_chunk = own // slots
    for c in range(halo // own):
        back = mm(turned[...], a_ref[:, pl.ds(2 * c * own, own)]).T.astype(BF16)
        for d in range(per_chunk):
            put_message(packed, c * per_chunk + d, back[d * slots : (d + 1) * slots])
    copies.later(packed, packed_out)
    copies.finish()


def message_shape(slots, pad):
    compact = BLOCK < pad <= BLOCK + BLOCK // 2 and slots % 32 == 0
    return (slots + slots // 2, BLOCK) if compact else (slots, pad)


def put_message(packed, d, rows):
    slots, pad = rows.shape
    if packed.shape[1:] == (slots, pad):
        packed[d] = rows
        return
    half, tail = slots // 2, pad - BLOCK
    packed[d, :slots, :] = rows[:, :BLOCK]
    filler = jnp.zeros((half, BLOCK // 2 - tail), BF16)
    packed[d, slots:, :] = jnp.concatenate([rows[:half, BLOCK:], filler, rows[half:, BLOCK:], filler], axis=1)


def take_message(packed, d, landed):
    slots, pad = landed.shape[0] // packed.shape[0], landed.shape[1]
    if packed.shape[1:] == (slots, pad):
        landed[pl.ds(d * slots, slots), :] = packed[d]
        return
    half, tail = slots // 2, pad - BLOCK
    landed[pl.ds(d * slots, slots), :BLOCK] = packed[d, :slots, :]
    landed[pl.ds(d * slots, half), BLOCK:] = packed[d, slots:, :tail]
    landed[pl.ds(d * slots + half, half), BLOCK:] = packed[d, slots:, BLOCK // 2 : BLOCK // 2 + tail]


def cut(rows, lanes, parts):
    across = lanes // BLOCK
    down = parts // across
    height = rows // down
    return [(slice(p % down * height, (p % down + 1) * height), slice(p // down * BLOCK, (p // down + 1) * BLOCK)) for p in range(parts)]


def middle_kernel(
    class_count, parts, turned_in, self_in, agg_in, loss_in, a_in, w_two_in,
    second_out, direct_out,
    turned, self_rows, agg_rows, loss, a_ref, w_two, both, direct, sems,
):
    copies = Copies(sems)
    loads = [
        copies(turned_in, turned),
        copies(a_in.at[pl.ds(0, a_ref.shape[0]), pl.ds(0, a_ref.shape[1])], a_ref),
        copies(w_two_in, w_two),
        copies(self_in, self_rows),
        copies(agg_in, agg_rows),
        copies(loss_in, loss),
    ]
    pad = turned.shape[0]
    units = self_rows.shape[1]
    loads[0].wait()
    loads[1].wait()
    high, low = halves(mm(turned[...], a_ref[...]))
    rows = jnp.concatenate([turned[...], high, low], axis=0).T
    loads[2].wait()
    for j in range(direct.shape[0]):
        direct[j] = mm(rows, jnp.concatenate([w_two[j], w_two[j, pad:]], axis=0))
        copies.later(direct.at[j], direct_out.at[j])
    for load in loads[3:]:
        load.wait()
    own_grads = mm(turned[...], self_rows[...])
    row = lax.broadcasted_iota(jnp.int32, own_grads.shape, 0)
    both[:, :units] = jnp.where(row == class_count, loss[0:1, 0:1], own_grads)
    both[:, units:] = mm(turned[...], agg_rows[...])
    if parts:
        for p, (rows, lanes) in enumerate(cut(*both.shape, parts)):
            copies.later(both.at[rows, lanes], second_out.at[p])
    else:
        copies.later(both, second_out)
    copies.finish()


def back_kernel(
    parts, pick_in, direct_in, slope_in, w_two_in, left_in, second_in, landed, out,
    pick, direct, slope, w_two, left, rows, grads, sems,
):
    copies = Copies(sems)
    step = left.shape[0]
    groups, _, units = direct.shape
    pad = landed.shape[1] if w_two.ndim == 2 else w_two.shape[1] // 2
    loads = [copies(pick_in, pick), copies(w_two_in, w_two)]
    both_loads = [(copies(direct_in.at[j], direct.at[j]), copies(slope_in.at[j], slope.at[j])) for j in range(groups)]
    left_load = copies(left_in, left)
    if parts:
        second_load = copies(second_in, grads.at[:, pl.ds(step, second_in.shape[1])])
    for d in range(landed.shape[0]):
        take_message(landed, d, rows)
    loads[0].wait()
    high, low = halves(mm_tn(rows[...], pick[...]))
    both = jnp.concatenate([high, low], axis=0).T
    loads[1].wait()
    for j in range(groups):
        more = mm(both, jnp.concatenate([w_two[j, pad:], w_two[j, pad:]], axis=0))
        for load in both_loads[j]:
            load.wait()
        total = direct[j] + more
        if j == 0:
            left_load.wait()
        result = mm(left[...], (total * slope[j]).astype(BF16))
        if parts:
            if j == 0:
                second_load.wait()
            for i in range(units // BLOCK):
                p = j * units // BLOCK + i
                grads[p, :step, :] = result[:, i * BLOCK : (i + 1) * BLOCK]
                copies.later(grads.at[p], out.at[p])
        else:
            grads[j] = result
            copies.later(grads.at[j], out.at[:, pl.ds(j * units, units)])
    copies.finish()


def sum_kernel(pieces_in, out, pieces, total, sems):
    copies = Copies(sems)
    count = pieces.shape[0]
    loads = [copies(pieces_in.at[k], pieces.at[k]) for k in range(count)]
    for load in loads:
        load.wait()
    held = pieces[0]
    for k in range(1, count):
        held = held + pieces[k]
    total[...] = held
    for k in range(count):
        copies.later(total, out.at[k])
    copies.finish()


def place_kernel(class_count, node_total, pieces, self1, neigh1, self2, neigh2, loss, both, sems):
    copies = Copies(sems)
    step = self1.shape[0]
    loads = []
    for p, (rows, lanes) in enumerate(cut(*both.shape, pieces.shape[0])):
        loads.append(copies(pieces.at[p, pl.ds(2 * step, pieces.shape[1] - 2 * step)], both.at[rows, lanes]))
    for p in range(pieces.shape[0]):
        at = pl.ds(p * BLOCK, BLOCK)
        copies.later(pieces.at[p, pl.ds(0, step)], self1.at[:, at])
        copies.later(pieces.at[p, pl.ds(step, step)], neigh1.at[:, at])
    for load in loads:
        load.wait()
    units = self2.shape[1]
    self2[...] = both[:class_count, :units]
    neigh2[...] = both[:class_count, units:]
    loss[...] = both[class_count : class_count + 1, 0:1] / node_total
    copies.finish()


def swap(value, count):
    blocks = value.reshape(count, -1, value.shape[-1])
    return lax.all_to_all(blocks, "node", 0, 0, tiled=True)


def gather_shifted(value, count):
    return [value] + [lax.ppermute(value, "feat", [(i, (i + k) % count) for i in range(count)]) for k in range(1, count)]


def shards(features, send_rows, send_count, tile_src, tile_val, labels, w_self1, w_neigh1, w_self2, w_neigh2):
    nodes, groups = lax.axis_size("node"), lax.axis_size("feat")
    own, step = features.shape
    slots = send_rows.shape[2]
    halo = nodes * slots
    total_src = own + halo
    cols = step * groups
    width = w_self1.shape[1]
    units, classes = w_self2.shape
    pad = -(-(classes + 1) // 16) * 16
    across = 2 * units // BLOCK
    parts = nodes if nodes % across == 0 and pad % (8 * (nodes // across)) == 0 and width == nodes * BLOCK else 0
    node_total = own * nodes
    grad_scale = 1.0 / math.sqrt(node_total)
    ids = lax.axis_index("feat").astype(jnp.int32).reshape(1)
    blocks = own // BLOCK
    packed_rows = 2 * step * groups + 2 * pad

    turned = features.T
    turned_all = gather_shifted(turned, groups)
    a_mat, pick = call(
        prepare_kernel,
        [((own, 2 * total_src), BF16), ((halo, own), BF16)],
        (tile_src, send_count, tile_val, send_rows[0]),
        [(tile_val.shape, BF16), ((nodes, slots), jnp.int32), ((own, total_src), F32), ((own, 2 * total_src), BF16), ((halo, own), BF16)],
        2 + 2 * blocks,
        moved=tile_val.size * 4,
    )
    full, packed, packed_weights = call(
        functools.partial(pack_kernel, groups),
        [((own, cols), BF16), ((halo, cols), BF16), ((packed_rows, units), BF16)],
        (ids, pick, w_self1, w_neigh1, w_self2.T, w_neigh2.T, *turned_all),
        [
            ((halo, own), BF16),
            ((cols, own), BF16),
            ((own, cols), BF16),
            ((halo, cols), BF16),
            ((2, step, width), BF16),
            ((2, classes, units), BF16),
            ((packed_rows, units), BF16),
        ],
        9,
        flops=2 * halo * own * cols,
        moved=halo * own * 2,
        near=groups - 1,
    )
    weights = lax.all_gather(packed_weights, "feat")
    source = swap(packed, nodes).reshape(halo, cols)
    (near,) = call(
        near_kernel,
        [((own, cols), F32)],
        (a_mat, full),
        [((own, 2 * own), BF16), ((own, cols), BF16), ((own, cols), F32)],
        3,
        flops=4 * own * own * cols,
        moved=4 * own * own,
    )
    agg, packed, source = call(
        first_kernel,
        [((own, cols), BF16), ((halo, cols), BF16), ((halo, cols), BF16)],
        (pick, a_mat, near, source),
        [((halo, own), BF16), ((own, 2 * halo), BF16), ((own, cols), F32), ((own, cols), BF16), ((halo, cols), BF16)],
        6,
        flops=4 * own * total_src * cols,
        moved=4 * own * total_src,
        near=1,
    )
    landed = swap(packed, nodes).reshape(halo, cols)
    chunked = (groups, own, units)
    w_one, w_two, slope, part, logits, mine, left = call(
        own_kernel,
        [
            ((groups, 2 * cols, units), BF16),
            ((groups, 2 * pad, units), BF16),
            (chunked, F32),
            (chunked, F32),
            ((pad, own), F32),
            ((own, units), BF16),
            ((2 * step, own), BF16),
        ],
        (ids, full, agg, a_mat, turned, weights),
        [
            ((own, cols), BF16),
            ((own, cols), BF16),
            ((own, 2 * own), BF16),
            ((2 * step, own), BF16),
            ((groups, packed_rows, units), BF16),
            ((groups, 2 * cols, units), BF16),
            ((groups, 2 * pad, units), BF16),
            (chunked, F32),
            (chunked, F32),
            ((pad, own), F32),
            (chunked, BF16),
            ((cols, own), BF16),
        ],
        10 + 2 * groups,
        flops=8 * own * own * width,
        moved=16 * own * width,
    )
    message = (nodes, *message_shape(slots, pad))
    turned_grads, agg_mine, loss, packed = call(
        functools.partial(second_kernel, classes, grad_scale),
        [((pad, own), BF16), ((own, units), BF16), ((8, 128), F32), (message, BF16)],
        (ids, a_mat, source, w_one, w_two, part, logits, labels.reshape(1, own), landed),
        [
            ((own, 2 * halo), BF16),
            ((halo, cols), BF16),
            ((groups, 2 * cols, units), BF16),
            ((groups, 2 * pad, units), BF16),
            (chunked, F32),
            ((pad, own), F32),
            ((1, own), jnp.int32),
            ((pad, own), BF16),
            ((8, 128), F32),
            (message, BF16),
            (chunked, BF16),
        ],
        10 + groups,
        flops=4 * own * halo * width,
        moved=12 * own * width,
        near=1,
    )
    landed = swap(packed, nodes)
    second_shape = (parts, pad * 2 * units // (BLOCK * parts), BLOCK) if parts else (pad, 2 * units)
    second, direct = call(
        functools.partial(middle_kernel, classes, parts),
        [(second_shape, F32), (chunked, F32)],
        (turned_grads, mine, agg_mine, loss, a_mat, w_two),
        [
            ((pad, own), BF16),
            ((own, units), BF16),
            ((own, units), BF16),
            ((8, 128), F32),
            ((own, own), BF16),
            ((groups, 2 * pad, units), BF16),
            ((pad, 2 * units), F32),
            (chunked, F32),
        ],
        6 + groups + max(parts, 1),
        flops=10 * own * pad * width,
        moved=8 * own * width,
    )
    out_shape = (parts, 2 * step + second_shape[1], BLOCK) if parts else (2 * step, width)
    (grads,) = call(
        functools.partial(back_kernel, parts),
        [(out_shape, F32)],
        (pick, direct, slope, w_two, left, second, landed),
        [
            ((halo, own), BF16),
            (chunked, F32),
            (chunked, F32),
            ((groups, 2 * pad, units), BF16),
            ((2 * step, own), BF16),
            ((halo, pad), BF16),
            (out_shape, F32) if parts else ((groups, 2 * step, units), F32),
        ],
        4 + 2 * groups + max(parts, groups),
        flops=6 * own * pad * width,
        moved=12 * own * width,
        near=1,
    )
    if not parts:
        grads, second = lax.psum((grads, second), "node")
        loss = second[classes, 0] / node_total
        return (loss, grads[:step], grads[step:], second[:classes, :units].T, second[:classes, units:].T)
    grads = swap(grads, nodes)
    (grads,) = call(sum_kernel, [(out_shape, F32)], (grads,), [(out_shape, F32), (out_shape[1:], F32)], 2 * nodes, moved=2**20)
    grads = swap(grads, nodes)
    grad_self1, grad_neigh1, grad_self2, grad_neigh2, loss = call(
        functools.partial(place_kernel, classes, node_total),
        [((step, width), F32)] * 2 + [((classes, units), F32)] * 2 + [((1, 1), F32)],
        (grads,),
        [((pad, 2 * units), F32)],
        3 * nodes,
        out_specs=[VMEM] * 5,
    )
    return (loss.reshape(()), grad_self1, grad_neigh1, grad_self2.T, grad_neigh2.T)


def solution(mesh):
    in_specs = (
        P("node", "feat"),
        P("node", None, None),
        P("node", None),
        P("node", None),
        P("node", None, None, None),
        P("node"),
        P("feat", None),
        P("feat", None),
        P("feat", None),
        P("feat", None),
    )
    out_specs = (P(), P("feat", None), P("feat", None), P("feat", None), P("feat", None))
    return jax.shard_map(shards, mesh=mesh, in_specs=in_specs, out_specs=out_specs, check_vma=False)
```

```python
import functools
import math

import jax
import jax.numpy as jnp
from jax import lax
from jax.experimental import pallas as pl
from jax.experimental.pallas import tpu as pltpu
from jax.sharding import PartitionSpec as P

BLOCK = 128
F32 = jnp.float32
BF16 = jnp.bfloat16
VMEM = pl.BlockSpec(memory_space=pltpu.VMEM)
HBM = pl.BlockSpec(memory_space=pltpu.HBM)
SMEM = pl.BlockSpec(memory_space=pltpu.SMEM)


def mm(a, b):
    return lax.dot_general(a, b, (((1,), (0,)), ((), ())), preferred_element_type=F32)


def mm_nt(a, b):
    return lax.dot_general(a, b, (((1,), (1,)), ((), ())), preferred_element_type=F32)


def mm_tn(a, b):
    return lax.dot_general(a, b, (((0,), (0,)), ((), ())), preferred_element_type=F32)


def halves(value):
    high = value.astype(BF16)
    return high, (value - high.astype(F32)).astype(BF16)


def spread(a, rows):
    own = a.shape[0]
    parts = []
    for c in range(rows.shape[0] // own):
        part = rows[c * own : (c + 1) * own]
        parts += [part, part]
    return mm(a, jnp.concatenate(parts, axis=0))


def gelu_parts(v):
    inner = math.sqrt(2.0 / math.pi) * (v + 0.044715 * (v * v * v))
    t = jnp.tanh(inner)
    return 0.5 * (1.0 + t), t


def gelu(v):
    return v * gelu_parts(v)[0]


def gelu_slope(v):
    cdf, t = gelu_parts(v)
    inner_slope = math.sqrt(2.0 / math.pi) * (1.0 + 3 * 0.044715 * (v * v))
    return cdf + 0.5 * v * (1.0 - t * t) * inner_slope


def size_of(shape, dtype):
    rows = -(-shape[-2] // 16) * 16 if len(shape) > 1 else 1
    return math.prod(shape[:-2]) * rows * (-(-shape[-1] // 128) * 128) * jnp.dtype(dtype).itemsize


def call(body, outs, args, scratch=(), copies=0, flops=0, moved=0, grant=0):
    specs = [SMEM if arg.dtype == jnp.int32 and arg.size < 512 else VMEM for arg in args]
    if copies:
        specs = [spec if spec is SMEM else HBM for spec in specs]
    room = sum(size_of(shape, dtype) for shape, dtype in [*outs, *scratch])
    room += sum(size_of(arg.shape, arg.dtype) for arg, spec in zip(args, specs) if spec is VMEM)
    return pl.pallas_call(
        body,
        out_shape=[jax.ShapeDtypeStruct(shape, dtype) for shape, dtype in outs],
        in_specs=specs,
        out_specs=[HBM if copies else VMEM] * len(outs),
        scratch_shapes=[pltpu.VMEM(shape, dtype) for shape, dtype in scratch]
        + ([pltpu.SemaphoreType.DMA((copies,))] if copies else []),
        compiler_params=pltpu.CompilerParams(vmem_limit_bytes=grant or min(room + 8 * 2**20, 56 * 2**20)),
        cost_estimate=pl.CostEstimate(flops=flops, bytes_accessed=moved, transcendentals=0),
    )(*args)


def prepare_kernel(
    tile_src, tile_val, w_self1, w_neigh1, w_self2, w_neigh2,
    a_out, weights_out, a_ref, weights, tiles, firsts, seconds, dense, sems,
):
    started = []

    def copy(src, dst):
        started.append(pltpu.make_async_copy(src, dst, sems.at[len(started)]))
        started[-1].start()
        return started[-1]

    blocks, per_block = tile_val.shape[0], tile_val.shape[1]
    own = blocks * BLOCK
    pairs = [(w_self1, firsts.at[0]), (w_neigh1, firsts.at[1]), (w_self2, seconds.at[0]), (w_neigh2, seconds.at[1])]
    w_copies = [copy(src, dst) for src, dst in pairs]
    tile_copies = [copy(tile_val.at[b], tiles.at[b]) for b in range(blocks)]
    dense[...] = jnp.zeros_like(dense)
    step = firsts.shape[1]
    classes, units = seconds.shape[1:]
    groups = firsts.shape[2] // units
    base = 2 * step * groups
    pad = (weights.shape[0] - base) // 2
    weights[pl.ds(base, 2 * pad), :] = jnp.zeros((2 * pad, units), BF16)
    for load in w_copies:
        load.wait()
    for j in range(groups):
        at = pl.ds(j * units, units)
        weights[pl.ds(2 * step * j, step), :] = firsts[0, :, at]
        weights[pl.ds(2 * step * j + step, step), :] = firsts[1, :, at]
    weights[pl.ds(base, classes), :] = seconds[0]
    weights[pl.ds(base + pad, classes), :] = seconds[1]
    stores = [copy(weights, weights_out)]
    for b in range(blocks):
        rows = pl.ds(b * BLOCK, BLOCK)
        tile_copies[b].wait()

        def add(k, _, b=b, rows=rows):
            at = pl.ds(pl.multiple_of(tile_src[b, k] * BLOCK, BLOCK), BLOCK)
            dense[rows, at] = dense[rows, at] + tiles[b, k].astype(F32)
            return 0

        lax.fori_loop(0, per_block, add, 0)
        for c in range(dense.shape[1] // own):
            high, low = halves(dense[rows, pl.ds(c * own, own)])
            a_ref[rows, pl.ds(2 * c * own, own)] = high
            a_ref[rows, pl.ds((2 * c + 1) * own, own)] = low
        stores.append(copy(a_ref.at[rows], a_out.at[rows]))
    for store in stores:
        store.wait()


def pack_kernel(groups, count, send_rows, *refs):
    pieces, (pick, full, packed), (turned,) = refs[:groups], refs[groups : groups + 3], refs[groups + 3 :]
    step, own = pieces[0].shape
    dests, slots = send_rows.shape
    columns = send_rows[...].astype(F32).T
    row_id = lax.broadcasted_iota(jnp.int32, (slots, own), 1).astype(F32)
    slot_id = lax.broadcasted_iota(jnp.int32, (slots, own), 0)
    for d in range(dests):
        hit = (columns[:, d : d + 1] == row_id) & (slot_id < count[0, d])
        pick[pl.ds(d * slots, slots), :] = jnp.where(hit, 1.0, 0.0).astype(BF16)
    for k, piece in enumerate(pieces):
        turned[pl.ds(k * step, step), :] = piece[...]
    full[...] = turned[...].T
    packed[...] = mm(pick[...], full[...]).astype(BF16)


def first_kernel(pick, a_ref, full, source, turned, agg, left, packed):
    own = full.shape[0]
    step = turned.shape[0]
    total = spread(a_ref[:, : 2 * own], full[...]) + spread(a_ref[:, 2 * own :], source[...])
    agg[...] = total.astype(BF16)
    packed[...] = mm(pick[...], agg[...]).astype(BF16)
    left[:step] = turned[...]
    left[step:] = agg[...].T[:step]


def forward_kernel(
    class_count, grad_scale, groups, ids, a_ref, full, agg, source, landed, labels, *refs
):
    weights = refs[:groups]
    turned, mine, agg_mine, loss, slope, packed = refs[groups:]
    own, cols = full.shape
    units = weights[0].shape[1]
    halo = landed.shape[0]
    step = cols // groups
    base = 2 * step * groups
    pad = turned.shape[0]
    slots = halo // packed.shape[0]
    near = jnp.concatenate([full[...], agg[...]], axis=1)
    total = jnp.zeros((pad, own), F32)
    for k in range(groups):
        group = lax.rem(ids[0] + groups - k, groups)
        begin = [pl.multiple_of(2 * step * group + part * step, step) for part in (0, 1)]
        w_one = jnp.concatenate([w[pl.ds(at, step), :] for at in begin for w in weights], axis=0)
        pre = mm(near, w_one)
        slope[k] = gelu_slope(pre)
        out = gelu(pre).astype(BF16)
        if halo == own:
            both = jnp.concatenate([source[...], landed[...]], axis=1)
            far = gelu(mm(both, w_one)).astype(BF16)
            held = spread(a_ref[...], jnp.concatenate([out, far], axis=0))
        else:

            def one(r, held, w_one=w_one):
                rows = pl.ds(pl.multiple_of(r * own, own), own)
                srcs = pl.ds(pl.multiple_of(2 * (r + 1) * own, own), 2 * own)
                both = jnp.concatenate([source[rows, :], landed[rows, :]], axis=1)
                return held + spread(a_ref[:, srcs], gelu(mm(both, w_one)).astype(BF16))

            held = lax.fori_loop(0, halo // own, one, spread(a_ref[:, : 2 * own], out))
        rounded = held.astype(BF16)
        if k == 0:
            mine[...] = out
            agg_mine[...] = rounded
        total = total + mm_nt(weights[k][pl.ds(base, pad), :], out) + mm_nt(weights[k][pl.ds(base + pad, pad), :], rounded)
    class_id = lax.broadcasted_iota(jnp.int32, total.shape, 0)
    real = class_id < class_count
    top = jnp.max(jnp.where(real, total, -jnp.inf), axis=0, keepdims=True)
    shifted = total - top
    powers = jnp.where(real, jnp.exp(shifted), 0.0)
    sums = jnp.sum(powers, axis=0, keepdims=True)
    target = (class_id == labels[...]).astype(F32)
    turned[...] = ((powers / sums - target) * grad_scale).astype(BF16)
    row_loss = jnp.log(sums) - jnp.sum(shifted * target, axis=0, keepdims=True)
    loss[...] = jnp.broadcast_to(jnp.sum(row_loss, axis=1, keepdims=True), loss.shape)
    per_chunk = own // slots
    for c in range(halo // own):
        back = mm(turned[...], a_ref[:, pl.ds(2 * (c + 1) * own, own)]).T.astype(BF16)
        for d in range(per_chunk):
            put_message(packed, c * per_chunk + d, back[d * slots : (d + 1) * slots])


def message_shape(slots, pad):
    compact = BLOCK < pad <= BLOCK + BLOCK // 2 and slots % 32 == 0
    return (slots + slots // 2, BLOCK) if compact else (slots, pad)


def put_message(packed, d, rows):
    slots, pad = rows.shape
    if packed.shape[1:] == (slots, pad):
        packed[d] = rows
        return
    half, tail = slots // 2, pad - BLOCK
    packed[d, :slots, :] = rows[:, :BLOCK]
    filler = jnp.zeros((half, BLOCK // 2 - tail), BF16)
    packed[d, slots:, :] = jnp.concatenate([rows[:half, BLOCK:], filler, rows[half:, BLOCK:], filler], axis=1)


def take_message(packed, d, landed):
    slots, pad = landed.shape[0] // packed.shape[0], landed.shape[1]
    if packed.shape[1:] == (slots, pad):
        landed[pl.ds(d * slots, slots), :] = packed[d]
        return
    half, tail = slots // 2, pad - BLOCK
    landed[pl.ds(d * slots, slots), :BLOCK] = packed[d, :slots, :]
    landed[pl.ds(d * slots, half), BLOCK:] = packed[d, slots:, :tail]
    landed[pl.ds(d * slots + half, half), BLOCK:] = packed[d, slots:, BLOCK // 2 : BLOCK // 2 + tail]


def cut(rows, lanes, parts):
    across = lanes // BLOCK
    down = parts // across
    height = rows // down
    return [(slice(p % down * height, (p % down + 1) * height), slice(p // down * BLOCK, (p // down + 1) * BLOCK)) for p in range(parts)]


def backward_kernel(
    class_count, parts, groups, ids, turned, pick, a_ref, slope, left, mine, agg_mine, loss, landed, *refs
):
    weights = refs[:groups]
    if parts:
        out, rows, both = refs[groups:]
    else:
        out, both, rows = refs[groups:]
    own, units = mine.shape
    pad = turned.shape[0]
    step = left.shape[0] // 2
    base = 2 * step * groups
    own_grads = mm(turned[...], mine[...])
    row = lax.broadcasted_iota(jnp.int32, own_grads.shape, 0)
    both[:, :units] = jnp.where(row == class_count, loss[0:1, 0:1], own_grads)
    both[:, units:] = mm(turned[...], agg_mine[...])
    for d in range(landed.shape[0]):
        take_message(landed, d, rows)
    high, low = halves(mm(turned[...], a_ref[:, :own]) + mm_tn(rows[...], pick[...]))
    wide = jnp.concatenate([turned[...], high, low], axis=0).T
    for k in range(groups):
        group = lax.rem(ids[0] + groups - k, groups)
        w_neigh = weights[k][pl.ds(base + pad, pad), :]
        total = mm(wide, jnp.concatenate([weights[k][pl.ds(base, pad), :], w_neigh, w_neigh], axis=0))
        result = mm(left[...], (total * slope[k]).astype(BF16))
        if parts:
            for i in range(units // BLOCK):
                out[group * (units // BLOCK) + i, pl.ds(0, 2 * step), :] = result[:, i * BLOCK : (i + 1) * BLOCK]
        else:
            out[:, pl.ds(pl.multiple_of(group * units, units), units)] = result
    if parts:
        for p, (height, lanes) in enumerate(cut(*both.shape, parts)):
            out[p, pl.ds(2 * step, out.shape[1] - 2 * step), :] = both[height, lanes]


def sum_kernel(pieces, out):
    held = pieces[0]
    for k in range(1, pieces.shape[0]):
        held = held + pieces[k]
    for k in range(pieces.shape[0]):
        out[k] = held


def place_kernel(class_count, node_total, pieces, self1, neigh1, self2, neigh2, loss, both):
    step = self1.shape[0]
    for p, (rows, lanes) in enumerate(cut(*both.shape, pieces.shape[0])):
        both[rows, lanes] = pieces[p, pl.ds(2 * step, pieces.shape[1] - 2 * step), :]
    for p in range(pieces.shape[0]):
        at = pl.ds(p * BLOCK, BLOCK)
        self1[:, at] = pieces[p, pl.ds(0, step), :]
        neigh1[:, at] = pieces[p, pl.ds(step, step), :]
    units = self2.shape[1]
    self2[...] = both[:class_count, :units]
    neigh2[...] = both[:class_count, units:]
    loss[...] = both[class_count : class_count + 1, 0:1] / node_total


def swap(value, count):
    blocks = value.reshape(count, -1, value.shape[-1])
    return lax.all_to_all(blocks, "node", 0, 0, tiled=True)


def gather_shifted(value, count):
    return [value] + [lax.ppermute(value, "feat", [(i, (i + k) % count) for i in range(count)]) for k in range(1, count)]


def shards(features, send_rows, send_count, tile_src, tile_val, labels, w_self1, w_neigh1, w_self2, w_neigh2):
    nodes, groups = lax.axis_size("node"), lax.axis_size("feat")
    own, step = features.shape
    slots = send_rows.shape[2]
    halo = nodes * slots
    total_src = own + halo
    cols = step * groups
    width = w_self1.shape[1]
    units, classes = w_self2.shape
    pad = -(-(classes + 1) // 16) * 16
    across = 2 * units // BLOCK
    parts = nodes if nodes % across == 0 and pad % (8 * (nodes // across)) == 0 and width == nodes * BLOCK else 0
    node_total = own * nodes
    grad_scale = 1.0 / math.sqrt(node_total)
    ids = lax.axis_index("feat").astype(jnp.int32).reshape(1)
    blocks = own // BLOCK
    packed_rows = 2 * step * groups + 2 * pad

    turned = features.T
    turned_all = gather_shifted(turned, groups)
    a_mat, packed_weights = call(
        prepare_kernel,
        [((own, 2 * total_src), BF16), ((packed_rows, units), BF16)],
        (tile_src, tile_val, w_self1, w_neigh1, w_self2.T, w_neigh2.T),
        [
            ((own, 2 * total_src), BF16),
            ((packed_rows, units), BF16),
            (tile_val.shape, BF16),
            ((2, step, width), BF16),
            ((2, classes, units), BF16),
            ((own, total_src), F32),
        ],
        copies=5 + 2 * blocks,
        moved=tile_val.size * 4,
        grant=58 * 2**20,
    )
    weights = gather_shifted(packed_weights, groups)
    pick, full, packed = call(
        functools.partial(pack_kernel, groups),
        [((halo, own), BF16), ((own, cols), BF16), ((halo, cols), BF16)],
        (send_count, send_rows[0], *turned_all),
        [((cols, own), BF16)],
        flops=2 * halo * own * cols,
        moved=halo * own * 2,
    )
    source = swap(packed, nodes).reshape(halo, cols)
    agg, left, packed = call(
        first_kernel,
        [((own, cols), BF16), ((2 * step, own), BF16), ((halo, cols), BF16)],
        (pick, a_mat, full, source, turned),
        flops=4 * own * total_src * cols,
        moved=4 * own * total_src,
    )
    landed = swap(packed, nodes).reshape(halo, cols)
    message = (nodes, *message_shape(slots, pad))
    turned_grads, mine, agg_mine, loss, slope, packed = call(
        functools.partial(forward_kernel, classes, grad_scale, groups),
        [
            ((pad, own), BF16),
            ((own, units), BF16),
            ((own, units), BF16),
            ((8, 128), F32),
            ((groups, own, units), F32),
            (message, BF16),
        ],
        (ids, a_mat, full, agg, source, landed, labels.reshape(1, own), *weights),
        flops=8 * own * total_src * width,
        moved=16 * own * width,
    )
    landed = swap(packed, nodes)
    second_shape = (pad, 2 * units)
    grads_shape = (parts, 2 * step + pad * 2 * units // (BLOCK * parts), BLOCK) if parts else (2 * step, width)
    grads, *second = call(
        functools.partial(backward_kernel, classes, parts, groups),
        [(grads_shape, F32)] + ([] if parts else [(second_shape, F32)]),
        (ids, turned_grads, pick, a_mat, slope, left, mine, agg_mine, loss, landed, *weights),
        [((halo, pad), BF16)] + ([(second_shape, F32)] if parts else []),
        flops=8 * own * pad * width,
        moved=12 * own * width,
    )
    if not parts:
        grads, second = lax.psum((grads, second[0]), "node")
        loss = second[classes, 0] / node_total
        return (loss, grads[:step], grads[step:], second[:classes, :units].T, second[:classes, units:].T)
    grads = swap(grads, nodes)
    (grads,) = call(sum_kernel, [(grads_shape, F32)], (grads,), moved=2**20)
    grads = swap(grads, nodes)
    grad_self1, grad_neigh1, grad_self2, grad_neigh2, loss = call(
        functools.partial(place_kernel, classes, node_total),
        [((step, width), F32)] * 2 + [((classes, units), F32)] * 2 + [((1, 1), F32)],
        (grads,),
        [(second_shape, F32)],
    )
    return (loss.reshape(()), grad_self1, grad_neigh1, grad_self2.T, grad_neigh2.T)


def solution(mesh):
    in_specs = (
        P("node", "feat"),
        P("node", None, None),
        P("node", None),
        P("node", None),
        P("node", None, None, None),
        P("node"),
        P("feat", None),
        P("feat", None),
        P("feat", None),
        P("feat", None),
    )
    out_specs = (P(), P("feat", None), P("feat", None), P("feat", None), P("feat", None))
    return jax.shard_map(shards, mesh=mesh, in_specs=in_specs, out_specs=out_specs, check_vma=False)
```

```python
import functools
import math

import jax
import jax.numpy as jnp
from jax import lax
from jax.experimental import pallas as pl
from jax.experimental.pallas import tpu as pltpu
from jax.sharding import PartitionSpec as P

BLOCK = 128
F32 = jnp.float32
BF16 = jnp.bfloat16
VMEM = pl.BlockSpec(memory_space=pltpu.VMEM)
HBM = pl.BlockSpec(memory_space=pltpu.HBM)
SMEM = pl.BlockSpec(memory_space=pltpu.SMEM)


def mm(a, b):
    return lax.dot_general(a, b, (((1,), (0,)), ((), ())), preferred_element_type=F32)


def mm_nt(a, b):
    return lax.dot_general(a, b, (((1,), (1,)), ((), ())), preferred_element_type=F32)


def mm_tn(a, b):
    return lax.dot_general(a, b, (((0,), (0,)), ((), ())), preferred_element_type=F32)


def halves(value):
    high = value.astype(BF16)
    return high, (value - high.astype(F32)).astype(BF16)


def spread(a, rows):
    own = a.shape[0]
    parts = []
    for c in range(rows.shape[0] // own):
        part = rows[c * own : (c + 1) * own]
        parts += [part, part]
    return mm(a, jnp.concatenate(parts, axis=0))


def activate(v, with_slope):
    scale = math.sqrt(2.0 / math.pi)
    square = v * v
    t = jnp.tanh(v * (scale + (scale * 0.044715) * square))
    half = 0.5 * v
    out = (half + half * t).astype(BF16)
    if not with_slope:
        return out
    return out, (0.5 + 0.5 * t) + half * (1.0 - t * t) * (scale + (scale * 3 * 0.044715) * square)


def size_of(shape, dtype):
    rows = -(-shape[-2] // 16) * 16 if len(shape) > 1 else 1
    return math.prod(shape[:-2]) * rows * (-(-shape[-1] // 128) * 128) * jnp.dtype(dtype).itemsize


def call(body, outs, args, scratch=(), copies=0, flops=0, moved=0, grant=0):
    specs = [SMEM if arg.dtype == jnp.int32 and arg.size < 512 else VMEM for arg in args]
    if copies:
        specs = [spec if spec is SMEM else HBM for spec in specs]
    room = sum(size_of(shape, dtype) for shape, dtype in [*outs, *scratch])
    room += sum(size_of(arg.shape, arg.dtype) for arg, spec in zip(args, specs) if spec is VMEM)
    return pl.pallas_call(
        body,
        out_shape=[jax.ShapeDtypeStruct(shape, dtype) for shape, dtype in outs],
        in_specs=specs,
        out_specs=[HBM if copies else VMEM] * len(outs),
        scratch_shapes=[pltpu.VMEM(shape, dtype) for shape, dtype in scratch]
        + ([pltpu.SemaphoreType.DMA((copies,))] if copies else []),
        compiler_params=pltpu.CompilerParams(vmem_limit_bytes=grant or min(room + 8 * 2**20, 56 * 2**20)),
        cost_estimate=pl.CostEstimate(flops=flops, bytes_accessed=moved, transcendentals=0),
    )(*args)


def prepare_kernel(
    tile_src, tile_val, w_self1, w_neigh1, w_self2, w_neigh2,
    a_out, weights_out, a_ref, weights, tiles, firsts, seconds, dense, sems,
):
    started = []

    def copy(src, dst):
        started.append(pltpu.make_async_copy(src, dst, sems.at[len(started)]))
        started[-1].start()
        return started[-1]

    blocks, per_block = tile_val.shape[0], tile_val.shape[1]
    own = blocks * BLOCK
    pairs = [(w_self1, firsts.at[0]), (w_neigh1, firsts.at[1]), (w_self2, seconds.at[0]), (w_neigh2, seconds.at[1])]
    w_copies = [copy(src, dst) for src, dst in pairs]
    tile_copies = [copy(tile_val.at[b], tiles.at[b]) for b in range(blocks)]
    dense[...] = jnp.zeros_like(dense)
    step = firsts.shape[1]
    classes, units = seconds.shape[1:]
    groups = firsts.shape[2] // units
    base = 2 * step * groups
    pad = (weights.shape[0] - base) // 2
    weights[pl.ds(base, 2 * pad), :] = jnp.zeros((2 * pad, units), BF16)
    for load in w_copies:
        load.wait()
    for j in range(groups):
        at = pl.ds(j * units, units)
        weights[pl.ds(2 * step * j, step), :] = firsts[0, :, at]
        weights[pl.ds(2 * step * j + step, step), :] = firsts[1, :, at]
    weights[pl.ds(base, classes), :] = seconds[0]
    weights[pl.ds(base + pad, classes), :] = seconds[1]
    stores = [copy(weights, weights_out)]
    for b in range(blocks):
        rows = pl.ds(b * BLOCK, BLOCK)
        tile_copies[b].wait()

        def add(k, _, b=b, rows=rows):
            at = pl.ds(pl.multiple_of(tile_src[b, k] * BLOCK, BLOCK), BLOCK)
            dense[rows, at] = dense[rows, at] + tiles[b, k].astype(F32)
            return 0

        lax.fori_loop(0, per_block, add, 0)
        for c in range(dense.shape[1] // own):
            high, low = halves(dense[rows, pl.ds(c * own, own)])
            a_ref[rows, pl.ds(2 * c * own, own)] = high
            a_ref[rows, pl.ds((2 * c + 1) * own, own)] = low
        stores.append(copy(a_ref.at[rows], a_out.at[rows]))
    for store in stores:
        store.wait()


def pack_kernel(groups, count, send_rows, *refs):
    pieces, (pick, full, packed), (turned,) = refs[:groups], refs[groups : groups + 3], refs[groups + 3 :]
    step, own = pieces[0].shape
    dests, slots = send_rows.shape
    columns = send_rows[...].astype(F32).T
    row_id = lax.broadcasted_iota(jnp.int32, (slots, own), 1).astype(F32)
    slot_id = lax.broadcasted_iota(jnp.int32, (slots, own), 0)
    for d in range(dests):
        hit = (columns[:, d : d + 1] == row_id) & (slot_id < count[0, d])
        pick[pl.ds(d * slots, slots), :] = jnp.where(hit, 1.0, 0.0).astype(BF16)
    for k, piece in enumerate(pieces):
        turned[pl.ds(k * step, step), :] = piece[...]
    full[...] = turned[...].T
    packed[...] = mm(pick[...], full[...]).astype(BF16)


def first_kernel(pick, a_ref, full, source, state, packed):
    own, cols = full.shape
    total = spread(a_ref[:, : 2 * own], full[...]) + spread(a_ref[:, 2 * own :], source[...])
    agg = total.astype(BF16)
    packed[...] = mm(pick[...], agg).astype(BF16)
    state[:own, :cols] = full[...]
    state[:own, cols:] = agg
    state[own:, :cols] = source[...]
    state[own:, cols:] = jnp.zeros_like(source)


def forward_kernel(
    class_count, grad_scale, groups, ids, a_ref, state, landed, labels, *refs
):
    weights = refs[:groups]
    turned, mine, agg_mine, loss, slope, packed = refs[groups:]
    halo, cols = landed.shape
    own = state.shape[0] - halo
    units = weights[0].shape[1]
    step = cols // groups
    base = 2 * step * groups
    pad = turned.shape[0]
    slots = halo // packed.shape[0]
    near = state[:own, :]
    total = jnp.zeros((pad, own), F32)
    for k in range(groups):
        group = lax.rem(ids[0] + groups - k, groups)
        begin = [pl.multiple_of(2 * step * group + part * step, step) for part in (0, 1)]
        w_one = jnp.concatenate([w[pl.ds(at, step), :] for at in begin for w in weights], axis=0)
        out, slope[k] = activate(mm(near, w_one), True)
        if halo == own:
            both = jnp.concatenate([state[own:, :cols], landed[...]], axis=1)
            far = activate(mm(both, w_one), False)
            held = spread(a_ref[...], jnp.concatenate([out, far], axis=0))
        else:

            def one(r, held, w_one=w_one):
                rows = pl.ds(pl.multiple_of(r * own, own), own)
                srcs = pl.ds(pl.multiple_of(2 * (r + 1) * own, own), 2 * own)
                lower = pl.ds(pl.multiple_of((r + 1) * own, own), own)
                both = jnp.concatenate([state[lower, :cols], landed[rows, :]], axis=1)
                return held + spread(a_ref[:, srcs], activate(mm(both, w_one), False))

            held = lax.fori_loop(0, halo // own, one, spread(a_ref[:, : 2 * own], out))
        rounded = held.astype(BF16)
        if k == 0:
            mine[...] = out
            agg_mine[...] = rounded
        total = total + mm_nt(weights[k][pl.ds(base, pad), :], out) + mm_nt(weights[k][pl.ds(base + pad, pad), :], rounded)
    class_id = lax.broadcasted_iota(jnp.int32, total.shape, 0)
    real = class_id < class_count
    top = jnp.max(jnp.where(real, total, -jnp.inf), axis=0, keepdims=True)
    shifted = total - top
    powers = jnp.where(real, jnp.exp(shifted), 0.0)
    sums = jnp.sum(powers, axis=0, keepdims=True)
    target = (class_id == labels[...]).astype(F32)
    turned[...] = ((powers / sums - target) * grad_scale).astype(BF16)
    row_loss = jnp.log(sums) - jnp.sum(shifted * target, axis=0, keepdims=True)
    loss[...] = jnp.broadcast_to(jnp.sum(row_loss, axis=1, keepdims=True), loss.shape)
    per_chunk = own // slots
    for c in range(halo // own):
        back = mm(turned[...], a_ref[:, pl.ds(2 * (c + 1) * own, own)]).T.astype(BF16)
        for d in range(per_chunk):
            put_message(packed, c * per_chunk + d, back[d * slots : (d + 1) * slots])


def message_shape(slots, pad):
    compact = BLOCK < pad <= BLOCK + BLOCK // 2 and slots % 32 == 0
    return (slots + slots // 2, BLOCK) if compact else (slots, pad)


def put_message(packed, d, rows):
    slots, pad = rows.shape
    if packed.shape[1:] == (slots, pad):
        packed[d] = rows
        return
    half, tail = slots // 2, pad - BLOCK
    packed[d, :slots, :] = rows[:, :BLOCK]
    filler = jnp.zeros((half, BLOCK // 2 - tail), BF16)
    packed[d, slots:, :] = jnp.concatenate([rows[:half, BLOCK:], filler, rows[half:, BLOCK:], filler], axis=1)


def take_message(packed, d, landed):
    slots, pad = landed.shape[0] // packed.shape[0], landed.shape[1]
    if packed.shape[1:] == (slots, pad):
        landed[pl.ds(d * slots, slots), :] = packed[d]
        return
    half, tail = slots // 2, pad - BLOCK
    landed[pl.ds(d * slots, slots), :BLOCK] = packed[d, :slots, :]
    landed[pl.ds(d * slots, half), BLOCK:] = packed[d, slots:, :tail]
    landed[pl.ds(d * slots + half, half), BLOCK:] = packed[d, slots:, BLOCK // 2 : BLOCK // 2 + tail]


def cut(rows, lanes, parts):
    across = lanes // BLOCK
    down = parts // across
    height = rows // down
    return [(slice(p % down * height, (p % down + 1) * height), slice(p // down * BLOCK, (p // down + 1) * BLOCK)) for p in range(parts)]


def backward_kernel(
    class_count, parts, groups, ids, turned, pick, a_ref, slope, features, state, mine, agg_mine, loss, landed, *refs
):
    weights = refs[:groups]
    if parts:
        out, rows, both = refs[groups:]
    else:
        out, both, rows = refs[groups:]
    own, units = mine.shape
    pad = turned.shape[0]
    step = features.shape[0]
    base = 2 * step * groups
    own_grads = mm(turned[...], mine[...])
    row = lax.broadcasted_iota(jnp.int32, own_grads.shape, 0)
    both[:, :units] = jnp.where(row == class_count, loss[0:1, 0:1], own_grads)
    both[:, units:] = mm(turned[...], agg_mine[...])
    for d in range(landed.shape[0]):
        take_message(landed, d, rows)
    high, low = halves(mm(turned[...], a_ref[:, :own]) + mm_tn(rows[...], pick[...]))
    wide = jnp.concatenate([turned[...], high, low], axis=0).T
    cols = state.shape[1] // 2
    left = jnp.concatenate([features[...], state[:own, cols:].T[:step]], axis=0)
    for k in range(groups):
        group = lax.rem(ids[0] + groups - k, groups)
        w_neigh = weights[k][pl.ds(base + pad, pad), :]
        total = mm(wide, jnp.concatenate([weights[k][pl.ds(base, pad), :], w_neigh, w_neigh], axis=0))
        result = mm(left, (total * slope[k]).astype(BF16))
        if parts:
            for i in range(units // BLOCK):
                out[group * (units // BLOCK) + i, pl.ds(0, 2 * step), :] = result[:, i * BLOCK : (i + 1) * BLOCK]
        else:
            out[:, pl.ds(pl.multiple_of(group * units, units), units)] = result
    if parts:
        for p, (height, lanes) in enumerate(cut(*both.shape, parts)):
            out[p, pl.ds(2 * step, out.shape[1] - 2 * step), :] = both[height, lanes]


def sum_kernel(pieces, out):
    held = pieces[0]
    for k in range(1, pieces.shape[0]):
        held = held + pieces[k]
    for k in range(pieces.shape[0]):
        out[k] = held


def place_kernel(class_count, node_total, pieces, self1, neigh1, self2, neigh2, loss, both):
    step = self1.shape[0]
    for p, (rows, lanes) in enumerate(cut(*both.shape, pieces.shape[0])):
        both[rows, lanes] = pieces[p, pl.ds(2 * step, pieces.shape[1] - 2 * step), :]
    for p in range(pieces.shape[0]):
        at = pl.ds(p * BLOCK, BLOCK)
        self1[:, at] = pieces[p, pl.ds(0, step), :]
        neigh1[:, at] = pieces[p, pl.ds(step, step), :]
    units = self2.shape[1]
    self2[...] = both[:class_count, :units]
    neigh2[...] = both[:class_count, units:]
    loss[...] = both[class_count : class_count + 1, 0:1] / node_total


def swap(value, count):
    blocks = value.reshape(count, -1, value.shape[-1])
    return lax.all_to_all(blocks, "node", 0, 0, tiled=True)


def gather_shifted(value, count):
    return [value] + [lax.ppermute(value, "feat", [(i, (i + k) % count) for i in range(count)]) for k in range(1, count)]


def shards(features, send_rows, send_count, tile_src, tile_val, labels, w_self1, w_neigh1, w_self2, w_neigh2):
    nodes, groups = lax.axis_size("node"), lax.axis_size("feat")
    own, step = features.shape
    slots = send_rows.shape[2]
    halo = nodes * slots
    total_src = own + halo
    cols = step * groups
    width = w_self1.shape[1]
    units, classes = w_self2.shape
    pad = -(-(classes + 1) // 16) * 16
    across = 2 * units // BLOCK
    parts = nodes if nodes % across == 0 and pad % (8 * (nodes // across)) == 0 and width == nodes * BLOCK else 0
    node_total = own * nodes
    grad_scale = 1.0 / math.sqrt(node_total)
    ids = lax.axis_index("feat").astype(jnp.int32).reshape(1)
    blocks = own // BLOCK
    packed_rows = 2 * step * groups + 2 * pad

    turned = features.T
    turned_all = gather_shifted(turned, groups)
    a_mat, packed_weights = call(
        prepare_kernel,
        [((own, 2 * total_src), BF16), ((packed_rows, units), BF16)],
        (tile_src, tile_val, w_self1, w_neigh1, w_self2.T, w_neigh2.T),
        [
            ((own, 2 * total_src), BF16),
            ((packed_rows, units), BF16),
            (tile_val.shape, BF16),
            ((2, step, width), BF16),
            ((2, classes, units), BF16),
            ((own, total_src), F32),
        ],
        copies=5 + 2 * blocks,
        moved=tile_val.size * 4,
        grant=58 * 2**20,
    )
    packed_weights, *turned_all = lax.optimization_barrier((packed_weights, *turned_all))
    weights = gather_shifted(packed_weights, groups)
    pick, full, packed = call(
        functools.partial(pack_kernel, groups),
        [((halo, own), BF16), ((own, cols), BF16), ((halo, cols), BF16)],
        (send_count, send_rows[0], *turned_all),
        [((cols, own), BF16)],
        flops=2 * halo * own * cols,
        moved=halo * own * 2,
    )
    source = swap(packed, nodes).reshape(halo, cols)
    state, packed = call(
        first_kernel,
        [((total_src, 2 * cols), BF16), ((halo, cols), BF16)],
        (pick, a_mat, full, source),
        flops=4 * own * total_src * cols,
        moved=4 * own * total_src,
    )
    packed, *weights = lax.optimization_barrier((packed, *weights))
    landed = swap(packed, nodes).reshape(halo, cols)
    message = (nodes, *message_shape(slots, pad))
    turned_grads, mine, agg_mine, loss, slope, packed = call(
        functools.partial(forward_kernel, classes, grad_scale, groups),
        [
            ((pad, own), BF16),
            ((own, units), BF16),
            ((own, units), BF16),
            ((8, 128), F32),
            ((groups, own, units), F32),
            (message, BF16),
        ],
        (ids, a_mat, state, landed, labels.reshape(1, own), *weights),
        flops=8 * own * total_src * width,
        moved=16 * own * width,
    )
    landed = swap(packed, nodes)
    second_shape = (pad, 2 * units)
    grads_shape = (parts, 2 * step + pad * 2 * units // (BLOCK * parts), BLOCK) if parts else (2 * step, width)
    grads, *second = call(
        functools.partial(backward_kernel, classes, parts, groups),
        [(grads_shape, F32)] + ([] if parts else [(second_shape, F32)]),
        (ids, turned_grads, pick, a_mat, slope, turned, state, mine, agg_mine, loss, landed, *weights),
        [((halo, pad), BF16)] + ([(second_shape, F32)] if parts else []),
        flops=8 * own * pad * width,
        moved=12 * own * width,
    )
    if not parts:
        grads, second = lax.psum((grads, second[0]), "node")
        loss = second[classes, 0] / node_total
        return (loss, grads[:step], grads[step:], second[:classes, :units].T, second[:classes, units:].T)
    grads = swap(grads, nodes)
    (grads,) = call(sum_kernel, [(grads_shape, F32)], (grads,), moved=2**20)
    grads = swap(grads, nodes)
    grad_self1, grad_neigh1, grad_self2, grad_neigh2, loss = call(
        functools.partial(place_kernel, classes, node_total),
        [((step, width), F32)] * 2 + [((classes, units), F32)] * 2 + [((1, 1), F32)],
        (grads,),
        [(second_shape, F32)],
    )
    return (loss.reshape(()), grad_self1, grad_neigh1, grad_self2.T, grad_neigh2.T)


def solution(mesh):
    in_specs = (
        P("node", "feat"),
        P("node", None, None),
        P("node", None),
        P("node", None),
        P("node", None, None, None),
        P("node"),
        P("feat", None),
        P("feat", None),
        P("feat", None),
        P("feat", None),
    )
    out_specs = (P(), P("feat", None), P("feat", None), P("feat", None), P("feat", None))
    return jax.shard_map(shards, mesh=mesh, in_specs=in_specs, out_specs=out_specs, check_vma=False)
```

```python
import functools
import math

import jax
import jax.numpy as jnp
from jax import lax
from jax.experimental import pallas as pl
from jax.experimental.pallas import tpu as pltpu
from jax.sharding import PartitionSpec as P

BLOCK = 128
F32 = jnp.float32
BF16 = jnp.bfloat16
VMEM = pl.BlockSpec(memory_space=pltpu.VMEM)
HBM = pl.BlockSpec(memory_space=pltpu.HBM)
SMEM = pl.BlockSpec(memory_space=pltpu.SMEM)


def mm(a, b):
    return lax.dot_general(a, b, (((1,), (0,)), ((), ())), preferred_element_type=F32)


def mm_nt(a, b):
    return lax.dot_general(a, b, (((1,), (1,)), ((), ())), preferred_element_type=F32)


def mm_tn(a, b):
    return lax.dot_general(a, b, (((0,), (0,)), ((), ())), preferred_element_type=F32)


def halves(value):
    high = value.astype(BF16)
    return high, (value - high.astype(F32)).astype(BF16)


def spread(a, rows):
    own = a.shape[0]
    parts = []
    for c in range(rows.shape[0] // own):
        part = rows[c * own : (c + 1) * own]
        parts += [part, part]
    return mm(a, jnp.concatenate(parts, axis=0))


def activate(v, with_slope):
    scale = math.sqrt(2.0 / math.pi)
    square = v * v
    t = jnp.tanh(v * (scale + (scale * 0.044715) * square))
    half = 0.5 * v
    out = (half + half * t).astype(BF16)
    if not with_slope:
        return out
    return out, (0.5 + 0.5 * t) + half * (1.0 - t * t) * (scale + (scale * 3 * 0.044715) * square)


def size_of(shape, dtype):
    rows = -(-shape[-2] // 16) * 16 if len(shape) > 1 else 1
    return math.prod(shape[:-2]) * rows * (-(-shape[-1] // 128) * 128) * jnp.dtype(dtype).itemsize


def call(body, outs, args, scratch=(), copies=0, flops=0, moved=0, grant=0):
    specs = [SMEM if arg.dtype == jnp.int32 and arg.size < 512 else VMEM for arg in args]
    if copies:
        specs = [spec if spec is SMEM else HBM for spec in specs]
    room = sum(size_of(shape, dtype) for shape, dtype in [*outs, *scratch])
    room += sum(size_of(arg.shape, arg.dtype) for arg, spec in zip(args, specs) if spec is VMEM)
    return pl.pallas_call(
        body,
        out_shape=[jax.ShapeDtypeStruct(shape, dtype) for shape, dtype in outs],
        in_specs=specs,
        out_specs=[VMEM] * len(outs),
        scratch_shapes=[pltpu.VMEM(shape, dtype) for shape, dtype in scratch]
        + ([pltpu.SemaphoreType.DMA((copies,))] if copies else []),
        compiler_params=pltpu.CompilerParams(vmem_limit_bytes=grant or min(room + 8 * 2**20, 56 * 2**20)),
        cost_estimate=pl.CostEstimate(flops=flops, bytes_accessed=moved, transcendentals=0),
    )(*args)


def prepare_kernel(tile_src, tile_val, a_ref, tiles, dense, sems):
    blocks, per_block = tile_val.shape[0], tile_val.shape[1]
    own = blocks * BLOCK
    copies = [pltpu.make_async_copy(tile_val.at[b], tiles.at[b], sems.at[b]) for b in range(blocks)]
    for copy in copies:
        copy.start()
    dense[...] = jnp.zeros_like(dense)
    for b in range(blocks):
        rows = pl.ds(b * BLOCK, BLOCK)
        copies[b].wait()

        def add(k, _, b=b, rows=rows):
            at = pl.ds(pl.multiple_of(tile_src[b, k] * BLOCK, BLOCK), BLOCK)
            dense[rows, at] = dense[rows, at] + tiles[b, k].astype(F32)
            return 0

        lax.fori_loop(0, per_block, add, 0)
        for c in range(dense.shape[1] // own):
            high, low = halves(dense[rows, pl.ds(c * own, own)])
            a_ref[rows, pl.ds(2 * c * own, own)] = high
            a_ref[rows, pl.ds((2 * c + 1) * own, own)] = low


def pack_kernel(groups, count, send_rows, w_self1, w_neigh1, w_self2, w_neigh2, *refs):
    pieces, (pick, full, packed, weights), (turned,) = refs[:groups], refs[groups : groups + 4], refs[groups + 4 :]
    step, own = pieces[0].shape
    classes, units = w_self2.shape
    base = 2 * step * groups
    pad = (weights.shape[0] - base) // 2
    for j in range(groups):
        at = pl.ds(j * units, units)
        weights[pl.ds(2 * step * j, step), :] = w_self1[:, at]
        weights[pl.ds(2 * step * j + step, step), :] = w_neigh1[:, at]
    weights[pl.ds(base, 2 * pad), :] = jnp.zeros((2 * pad, units), BF16)
    weights[pl.ds(base, classes), :] = w_self2[...]
    weights[pl.ds(base + pad, classes), :] = w_neigh2[...]
    dests, slots = send_rows.shape
    columns = send_rows[...].astype(F32).T
    row_id = lax.broadcasted_iota(jnp.int32, (slots, own), 1).astype(F32)
    slot_id = lax.broadcasted_iota(jnp.int32, (slots, own), 0)
    for d in range(dests):
        hit = (columns[:, d : d + 1] == row_id) & (slot_id < count[0, d])
        pick[pl.ds(d * slots, slots), :] = jnp.where(hit, 1.0, 0.0).astype(BF16)
    for k, piece in enumerate(pieces):
        turned[pl.ds(k * step, step), :] = piece[...]
    full[...] = turned[...].T
    packed[...] = mm(pick[...], full[...]).astype(BF16)


def first_kernel(pick, a_ref, full, source, state, packed):
    own, cols = full.shape
    total = spread(a_ref[:, : 2 * own], full[...]) + spread(a_ref[:, 2 * own :], source[...])
    agg = total.astype(BF16)
    packed[...] = mm(pick[...], agg).astype(BF16)
    state[:own, :cols] = full[...]
    state[:own, cols:] = agg
    state[own:, :cols] = source[...]
    state[own:, cols:] = jnp.zeros_like(source)


def forward_kernel(
    class_count, grad_scale, groups, ids, a_ref, state, landed, labels, *refs
):
    weights = refs[:groups]
    turned, mine, agg_mine, loss, slope, packed = refs[groups:]
    halo, cols = landed.shape
    own = state.shape[0] - halo
    units = weights[0].shape[1]
    step = cols // groups
    base = 2 * step * groups
    pad = turned.shape[0]
    slots = halo // packed.shape[0]
    near = state[:own, :]
    total = jnp.zeros((pad, own), F32)
    for k in range(groups):
        group = lax.rem(ids[0] + groups - k, groups)
        begin = [pl.multiple_of(2 * step * group + part * step, step) for part in (0, 1)]
        w_one = jnp.concatenate([w[pl.ds(at, step), :] for at in begin for w in weights], axis=0)
        out, slope[k] = activate(mm(near, w_one), True)
        if halo == own:
            both = jnp.concatenate([state[own:, :cols], landed[...]], axis=1)
            far = activate(mm(both, w_one), False)
            held = spread(a_ref[...], jnp.concatenate([out, far], axis=0))
        else:

            def one(r, held, w_one=w_one):
                rows = pl.ds(pl.multiple_of(r * own, own), own)
                srcs = pl.ds(pl.multiple_of(2 * (r + 1) * own, own), 2 * own)
                lower = pl.ds(pl.multiple_of((r + 1) * own, own), own)
                both = jnp.concatenate([state[lower, :cols], landed[rows, :]], axis=1)
                return held + spread(a_ref[:, srcs], activate(mm(both, w_one), False))

            held = lax.fori_loop(0, halo // own, one, spread(a_ref[:, : 2 * own], out))
        rounded = held.astype(BF16)
        if k == 0:
            mine[...] = out
            agg_mine[...] = rounded
        total = total + mm_nt(weights[k][pl.ds(base, pad), :], out) + mm_nt(weights[k][pl.ds(base + pad, pad), :], rounded)
    class_id = lax.broadcasted_iota(jnp.int32, total.shape, 0)
    real = class_id < class_count
    top = jnp.max(jnp.where(real, total, -jnp.inf), axis=0, keepdims=True)
    shifted = total - top
    powers = jnp.where(real, jnp.exp(shifted), 0.0)
    sums = jnp.sum(powers, axis=0, keepdims=True)
    target = (class_id == labels[...]).astype(F32)
    turned[...] = ((powers / sums - target) * grad_scale).astype(BF16)
    row_loss = jnp.log(sums) - jnp.sum(shifted * target, axis=0, keepdims=True)
    loss[...] = jnp.broadcast_to(jnp.sum(row_loss, axis=1, keepdims=True), loss.shape)
    per_chunk = own // slots
    for c in range(halo // own):
        back = mm(turned[...], a_ref[:, pl.ds(2 * (c + 1) * own, own)]).T.astype(BF16)
        for d in range(per_chunk):
            put_message(packed, c * per_chunk + d, back[d * slots : (d + 1) * slots])


def message_shape(slots, pad):
    compact = BLOCK < pad <= BLOCK + BLOCK // 2 and slots % 32 == 0
    return (slots + slots // 2, BLOCK) if compact else (slots, pad)


def put_message(packed, d, rows):
    slots, pad = rows.shape
    if packed.shape[1:] == (slots, pad):
        packed[d] = rows
        return
    half, tail = slots // 2, pad - BLOCK
    packed[d, :slots, :] = rows[:, :BLOCK]
    filler = jnp.zeros((half, BLOCK // 2 - tail), BF16)
    packed[d, slots:, :] = jnp.concatenate([rows[:half, BLOCK:], filler, rows[half:, BLOCK:], filler], axis=1)


def take_message(packed, d, landed):
    slots, pad = landed.shape[0] // packed.shape[0], landed.shape[1]
    if packed.shape[1:] == (slots, pad):
        landed[pl.ds(d * slots, slots), :] = packed[d]
        return
    half, tail = slots // 2, pad - BLOCK
    landed[pl.ds(d * slots, slots), :BLOCK] = packed[d, :slots, :]
    landed[pl.ds(d * slots, half), BLOCK:] = packed[d, slots:, :tail]
    landed[pl.ds(d * slots + half, half), BLOCK:] = packed[d, slots:, BLOCK // 2 : BLOCK // 2 + tail]


def cut(rows, lanes, parts):
    across = lanes // BLOCK
    down = parts // across
    height = rows // down
    return [(slice(p % down * height, (p % down + 1) * height), slice(p // down * BLOCK, (p // down + 1) * BLOCK)) for p in range(parts)]


def backward_kernel(
    class_count, parts, groups, ids, turned, pick, a_ref, slope, features, state, mine, agg_mine, loss, landed, *refs
):
    weights = refs[:groups]
    if parts:
        out, rows, both = refs[groups:]
    else:
        out, both, rows = refs[groups:]
    own, units = mine.shape
    pad = turned.shape[0]
    step = features.shape[0]
    base = 2 * step * groups
    own_grads = mm(turned[...], mine[...])
    row = lax.broadcasted_iota(jnp.int32, own_grads.shape, 0)
    both[:, :units] = jnp.where(row == class_count, loss[0:1, 0:1], own_grads)
    both[:, units:] = mm(turned[...], agg_mine[...])
    for d in range(landed.shape[0]):
        take_message(landed, d, rows)
    high, low = halves(mm(turned[...], a_ref[:, :own]) + mm_tn(rows[...], pick[...]))
    wide = jnp.concatenate([turned[...], high, low], axis=0).T
    cols = state.shape[1] // 2
    left = jnp.concatenate([features[...], state[:own, cols:].T[:step]], axis=0)
    for k in range(groups):
        group = lax.rem(ids[0] + groups - k, groups)
        w_neigh = weights[k][pl.ds(base + pad, pad), :]
        total = mm(wide, jnp.concatenate([weights[k][pl.ds(base, pad), :], w_neigh, w_neigh], axis=0))
        result = mm(left, (total * slope[k]).astype(BF16))
        if parts:
            for i in range(units // BLOCK):
                out[group * (units // BLOCK) + i, pl.ds(0, 2 * step), :] = result[:, i * BLOCK : (i + 1) * BLOCK]
        else:
            out[:, pl.ds(pl.multiple_of(group * units, units), units)] = result
    if parts:
        for p, (height, lanes) in enumerate(cut(*both.shape, parts)):
            out[p, pl.ds(2 * step, out.shape[1] - 2 * step), :] = both[height, lanes]


def sum_kernel(pieces, out):
    held = pieces[0]
    for k in range(1, pieces.shape[0]):
        held = held + pieces[k]
    for k in range(pieces.shape[0]):
        out[k] = held


def place_kernel(class_count, node_total, pieces, self1, neigh1, self2, neigh2, loss, both):
    step = self1.shape[0]
    for p, (rows, lanes) in enumerate(cut(*both.shape, pieces.shape[0])):
        both[rows, lanes] = pieces[p, pl.ds(2 * step, pieces.shape[1] - 2 * step), :]
    for p in range(pieces.shape[0]):
        at = pl.ds(p * BLOCK, BLOCK)
        self1[:, at] = pieces[p, pl.ds(0, step), :]
        neigh1[:, at] = pieces[p, pl.ds(step, step), :]
    units = self2.shape[1]
    self2[...] = both[:class_count, :units]
    neigh2[...] = both[:class_count, units:]
    loss[...] = both[class_count : class_count + 1, 0:1] / node_total


def swap(value, count):
    blocks = value.reshape(count, -1, value.shape[-1])
    return lax.all_to_all(blocks, "node", 0, 0, tiled=True)


def gather_shifted(value, count):
    return [value] + [lax.ppermute(value, "feat", [(i, (i + k) % count) for i in range(count)]) for k in range(1, count)]


def shards(features, send_rows, send_count, tile_src, tile_val, labels, w_self1, w_neigh1, w_self2, w_neigh2):
    nodes, groups = lax.axis_size("node"), lax.axis_size("feat")
    own, step = features.shape
    slots = send_rows.shape[2]
    halo = nodes * slots
    total_src = own + halo
    cols = step * groups
    width = w_self1.shape[1]
    units, classes = w_self2.shape
    pad = -(-(classes + 1) // 16) * 16
    across = 2 * units // BLOCK
    parts = nodes if nodes % across == 0 and pad % (8 * (nodes // across)) == 0 and width == nodes * BLOCK else 0
    node_total = own * nodes
    grad_scale = 1.0 / math.sqrt(node_total)
    ids = lax.axis_index("feat").astype(jnp.int32).reshape(1)
    blocks = own // BLOCK
    packed_rows = 2 * step * groups + 2 * pad

    turned = features.T
    turned_all = gather_shifted(turned, groups)
    (a_mat,) = call(
        prepare_kernel,
        [((own, 2 * total_src), BF16)],
        (tile_src, tile_val),
        [(tile_val.shape, BF16), ((own, total_src), F32)],
        copies=blocks,
        moved=tile_val.size * 4,
        grant=54 * 2**20 - 4 * own * total_src - 3 * 10**5,
    )
    a_mat, ids, *turned_all = lax.optimization_barrier((a_mat, ids, *turned_all))
    pick, full, packed, packed_weights = call(
        functools.partial(pack_kernel, groups),
        [((halo, own), BF16), ((own, cols), BF16), ((halo, cols), BF16), ((packed_rows, units), BF16)],
        (send_count, send_rows[0], w_self1, w_neigh1, w_self2.T, w_neigh2.T, *turned_all),
        [((cols, own), BF16)],
        flops=2 * halo * own * cols,
        moved=halo * own * 2,
    )
    weights = gather_shifted(packed_weights, groups)
    source = swap(packed, nodes).reshape(halo, cols)
    state, packed = call(
        first_kernel,
        [((total_src, 2 * cols), BF16), ((halo, cols), BF16)],
        (pick, a_mat, full, source),
        flops=4 * own * total_src * cols,
        moved=4 * own * total_src,
    )
    packed, ids, *weights = lax.optimization_barrier((packed, ids, *weights))
    landed = swap(packed, nodes).reshape(halo, cols)
    message = (nodes, *message_shape(slots, pad))
    turned_grads, mine, agg_mine, loss, slope, packed = call(
        functools.partial(forward_kernel, classes, grad_scale, groups),
        [
            ((pad, own), BF16),
            ((own, units), BF16),
            ((own, units), BF16),
            ((8, 128), F32),
            ((groups, own, units), F32),
            (message, BF16),
        ],
        (ids, a_mat, state, landed, labels.reshape(1, own), *weights),
        flops=8 * own * total_src * width,
        moved=16 * own * width,
    )
    landed = swap(packed, nodes)
    second_shape = (pad, 2 * units)
    grads_shape = (parts, 2 * step + pad * 2 * units // (BLOCK * parts), BLOCK) if parts else (2 * step, width)
    grads, *second = call(
        functools.partial(backward_kernel, classes, parts, groups),
        [(grads_shape, F32)] + ([] if parts else [(second_shape, F32)]),
        (ids, turned_grads, pick, a_mat, slope, turned, state, mine, agg_mine, loss, landed, *weights),
        [((halo, pad), BF16)] + ([(second_shape, F32)] if parts else []),
        flops=8 * own * pad * width,
        moved=12 * own * width,
    )
    if not parts:
        grads, second = lax.psum((grads, second[0]), "node")
        loss = second[classes, 0] / node_total
        return (loss, grads[:step], grads[step:], second[:classes, :units].T, second[:classes, units:].T)
    grads = swap(grads, nodes)
    (grads,) = call(sum_kernel, [(grads_shape, F32)], (grads,), moved=2**20)
    grads = swap(grads, nodes)
    grad_self1, grad_neigh1, grad_self2, grad_neigh2, loss = call(
        functools.partial(place_kernel, classes, node_total),
        [((step, width), F32)] * 2 + [((classes, units), F32)] * 2 + [((1, 1), F32)],
        (grads,),
        [(second_shape, F32)],
    )
    return (loss.reshape(()), grad_self1, grad_neigh1, grad_self2.T, grad_neigh2.T)


def solution(mesh):
    in_specs = (
        P("node", "feat"),
        P("node", None, None),
        P("node", None),
        P("node", None),
        P("node", None, None, None),
        P("node"),
        P("feat", None),
        P("feat", None),
        P("feat", None),
        P("feat", None),
    )
    out_specs = (P(), P("feat", None), P("feat", None), P("feat", None), P("feat", None))
    return jax.shard_map(shards, mesh=mesh, in_specs=in_specs, out_specs=out_specs, check_vma=False)
```

```python
import functools
import math

import jax
import jax.numpy as jnp
from jax import lax
from jax.experimental import pallas as pl
from jax.experimental.pallas import tpu as pltpu
from jax.sharding import PartitionSpec as P

BLOCK = 128
F32 = jnp.float32
BF16 = jnp.bfloat16
VMEM = pl.BlockSpec(memory_space=pltpu.VMEM)
HBM = pl.BlockSpec(memory_space=pltpu.HBM)
SMEM = pl.BlockSpec(memory_space=pltpu.SMEM)


def mm(a, b):
    return lax.dot_general(a, b, (((1,), (0,)), ((), ())), preferred_element_type=F32)


def mm_nt(a, b):
    return lax.dot_general(a, b, (((1,), (1,)), ((), ())), preferred_element_type=F32)


def mm_tn(a, b):
    return lax.dot_general(a, b, (((0,), (0,)), ((), ())), preferred_element_type=F32)


def halves(value):
    high = value.astype(BF16)
    return high, (value - high.astype(F32)).astype(BF16)


def spread(a, rows):
    own = a.shape[0]
    parts = []
    for c in range(rows.shape[0] // own):
        part = rows[c * own : (c + 1) * own]
        parts += [part, part]
    return mm(a, jnp.concatenate(parts, axis=0))


def activate(v, with_slope):
    scale = math.sqrt(2.0 / math.pi)
    square = v * v
    t = jnp.tanh(v * (scale + (scale * 0.044715) * square))
    half = 0.5 * v
    out = (half + half * t).astype(BF16)
    if not with_slope:
        return out
    return out, (0.5 + 0.5 * t) + half * (1.0 - t * t) * (scale + (scale * 3 * 0.044715) * square)


def size_of(shape, dtype):
    rows = -(-shape[-2] // 16) * 16 if len(shape) > 1 else 1
    return math.prod(shape[:-2]) * rows * (-(-shape[-1] // 128) * 128) * jnp.dtype(dtype).itemsize


def call(body, outs, args, scratch=(), copies=0, flops=0, moved=0, grant=0):
    specs = [SMEM if arg.dtype == jnp.int32 and arg.size < 512 else VMEM for arg in args]
    if copies:
        specs = [spec if spec is SMEM else HBM for spec in specs]
    room = sum(size_of(shape, dtype) for shape, dtype in [*outs, *scratch])
    room += sum(size_of(arg.shape, arg.dtype) for arg, spec in zip(args, specs) if spec is VMEM)
    return pl.pallas_call(
        body,
        out_shape=[jax.ShapeDtypeStruct(shape, dtype) for shape, dtype in outs],
        in_specs=specs,
        out_specs=[VMEM] * len(outs),
        scratch_shapes=[pltpu.VMEM(shape, dtype) for shape, dtype in scratch]
        + ([pltpu.SemaphoreType.DMA((copies,))] if copies else []),
        compiler_params=pltpu.CompilerParams(vmem_limit_bytes=grant or min(room + 8 * 2**20, 56 * 2**20)),
        cost_estimate=pl.CostEstimate(flops=flops, bytes_accessed=moved, transcendentals=0),
    )(*args)


def prepare_kernel(tile_src, tile_val, a_ref, tiles, dense, sems):
    blocks, per_block = tile_val.shape[0], tile_val.shape[1]
    own = blocks * BLOCK
    copies = [pltpu.make_async_copy(tile_val.at[b], tiles.at[b], sems.at[b]) for b in range(blocks)]
    for copy in copies:
        copy.start()
    dense[...] = jnp.zeros_like(dense)
    for b in range(blocks):
        rows = pl.ds(b * BLOCK, BLOCK)
        copies[b].wait()

        def add(k, _, b=b, rows=rows):
            at = pl.ds(pl.multiple_of(tile_src[b, k] * BLOCK, BLOCK), BLOCK)
            dense[rows, at] = dense[rows, at] + tiles[b, k].astype(F32)
            return 0

        lax.fori_loop(0, per_block, add, 0)
        for c in range(dense.shape[1] // own):
            high, low = halves(dense[rows, pl.ds(c * own, own)])
            a_ref[rows, pl.ds(2 * c * own, own)] = high
            a_ref[rows, pl.ds((2 * c + 1) * own, own)] = low


def pack_kernel(groups, count, send_rows, w_self1, w_neigh1, w_self2, w_neigh2, *refs):
    pieces, (pick, full, packed, weights), (turned,) = refs[:groups], refs[groups : groups + 4], refs[groups + 4 :]
    step, own = pieces[0].shape
    classes, units = w_self2.shape
    base = 2 * step * groups
    pad = (weights.shape[0] - base) // 2
    for j in range(groups):
        at = pl.ds(j * units, units)
        weights[pl.ds(2 * step * j, step), :] = w_self1[:, at]
        weights[pl.ds(2 * step * j + step, step), :] = w_neigh1[:, at]
    weights[pl.ds(base, 2 * pad), :] = jnp.zeros((2 * pad, units), BF16)
    weights[pl.ds(base, classes), :] = w_self2[...]
    weights[pl.ds(base + pad, classes), :] = w_neigh2[...]
    dests, slots = send_rows.shape
    columns = send_rows[...].astype(F32).T
    row_id = lax.broadcasted_iota(jnp.int32, (slots, own), 1).astype(F32)
    slot_id = lax.broadcasted_iota(jnp.int32, (slots, own), 0)
    for d in range(dests):
        hit = (columns[:, d : d + 1] == row_id) & (slot_id < count[0, d])
        pick[pl.ds(d * slots, slots), :] = jnp.where(hit, 1.0, 0.0).astype(BF16)
    for k, piece in enumerate(pieces):
        turned[pl.ds(k * step, step), :] = piece[...]
    full[...] = turned[...].T
    packed[...] = mm(pick[...], full[...]).astype(BF16)


def first_kernel(pick, a_ref, full, source, state, packed):
    own, cols = full.shape
    total = spread(a_ref[:, : 2 * own], full[...]) + spread(a_ref[:, 2 * own :], source[...])
    agg = total.astype(BF16)
    packed[...] = mm(pick[...], agg).astype(BF16)
    state[:own, :cols] = full[...]
    state[:own, cols:] = agg
    state[own:, :cols] = source[...]
    state[own:, cols:] = jnp.zeros_like(source)


def forward_kernel(
    class_count, grad_scale, groups, ids, a_ref, state, landed, labels, *refs
):
    weights = refs[:groups]
    turned, mine, agg_mine, loss, slope, packed = refs[groups:]
    halo, cols = landed.shape
    own = state.shape[0] - halo
    units = weights[0].shape[1]
    step = cols // groups
    base = 2 * step * groups
    pad = turned.shape[0]
    slots = halo // packed.shape[0]
    near = state[:own, :]
    total = jnp.zeros((pad, own), F32)
    for k in range(groups):
        group = jnp.bitwise_xor(ids[0], k)
        begin = [pl.multiple_of(2 * step * group + part * step, step) for part in (0, 1)]
        w_one = jnp.concatenate([w[pl.ds(at, step), :] for at in begin for w in weights], axis=0)
        out, slope[k] = activate(mm(near, w_one), True)
        if halo == own:
            both = jnp.concatenate([state[own:, :cols], landed[...]], axis=1)
            far = activate(mm(both, w_one), False)
            held = spread(a_ref[...], jnp.concatenate([out, far], axis=0))
        else:

            def one(r, held, w_one=w_one):
                rows = pl.ds(pl.multiple_of(r * own, own), own)
                srcs = pl.ds(pl.multiple_of(2 * (r + 1) * own, own), 2 * own)
                lower = pl.ds(pl.multiple_of((r + 1) * own, own), own)
                both = jnp.concatenate([state[lower, :cols], landed[rows, :]], axis=1)
                return held + spread(a_ref[:, srcs], activate(mm(both, w_one), False))

            held = lax.fori_loop(0, halo // own, one, spread(a_ref[:, : 2 * own], out))
        rounded = held.astype(BF16)
        if k == 0:
            mine[...] = out
            agg_mine[...] = rounded
        total = total + mm_nt(weights[k][pl.ds(base, pad), :], out) + mm_nt(weights[k][pl.ds(base + pad, pad), :], rounded)
    class_id = lax.broadcasted_iota(jnp.int32, total.shape, 0)
    real = class_id < class_count
    top = jnp.max(jnp.where(real, total, -jnp.inf), axis=0, keepdims=True)
    shifted = total - top
    powers = jnp.where(real, jnp.exp(shifted), 0.0)
    sums = jnp.sum(powers, axis=0, keepdims=True)
    target = (class_id == labels[...]).astype(F32)
    turned[...] = ((powers / sums - target) * grad_scale).astype(BF16)
    row_loss = jnp.log(sums) - jnp.sum(shifted * target, axis=0, keepdims=True)
    loss[...] = jnp.broadcast_to(jnp.sum(row_loss, axis=1, keepdims=True), loss.shape)
    per_chunk = own // slots
    for c in range(halo // own):
        back = mm(turned[...], a_ref[:, pl.ds(2 * (c + 1) * own, own)]).T.astype(BF16)
        for d in range(per_chunk):
            put_message(packed, c * per_chunk + d, back[d * slots : (d + 1) * slots])


def message_shape(slots, pad):
    compact = BLOCK < pad <= BLOCK + BLOCK // 2 and slots % 32 == 0
    return (slots + slots // 2, BLOCK) if compact else (slots, pad)


def put_message(packed, d, rows):
    slots, pad = rows.shape
    if packed.shape[1:] == (slots, pad):
        packed[d] = rows
        return
    half, tail = slots // 2, pad - BLOCK
    packed[d, :slots, :] = rows[:, :BLOCK]
    filler = jnp.zeros((half, BLOCK // 2 - tail), BF16)
    packed[d, slots:, :] = jnp.concatenate([rows[:half, BLOCK:], filler, rows[half:, BLOCK:], filler], axis=1)


def take_message(packed, d, landed):
    slots, pad = landed.shape[0] // packed.shape[0], landed.shape[1]
    if packed.shape[1:] == (slots, pad):
        landed[pl.ds(d * slots, slots), :] = packed[d]
        return
    half, tail = slots // 2, pad - BLOCK
    landed[pl.ds(d * slots, slots), :BLOCK] = packed[d, :slots, :]
    landed[pl.ds(d * slots, half), BLOCK:] = packed[d, slots:, :tail]
    landed[pl.ds(d * slots + half, half), BLOCK:] = packed[d, slots:, BLOCK // 2 : BLOCK // 2 + tail]


def cut(rows, lanes, parts):
    across = lanes // BLOCK
    down = parts // across
    height = rows // down
    return [(slice(p % down * height, (p % down + 1) * height), slice(p // down * BLOCK, (p // down + 1) * BLOCK)) for p in range(parts)]


def backward_kernel(
    class_count, parts, groups, ids, turned, pick, a_ref, slope, features, state, mine, agg_mine, loss, landed, *refs
):
    weights = refs[:groups]
    if parts:
        out, rows, both = refs[groups:]
    else:
        out, both, rows = refs[groups:]
    own, units = mine.shape
    pad = turned.shape[0]
    step = features.shape[0]
    base = 2 * step * groups
    own_grads = mm(turned[...], mine[...])
    row = lax.broadcasted_iota(jnp.int32, own_grads.shape, 0)
    both[:, :units] = jnp.where(row == class_count, loss[0:1, 0:1], own_grads)
    both[:, units:] = mm(turned[...], agg_mine[...])
    for d in range(landed.shape[0]):
        take_message(landed, d, rows)
    high, low = halves(mm(turned[...], a_ref[:, :own]) + mm_tn(rows[...], pick[...]))
    wide = jnp.concatenate([turned[...], high, low], axis=0).T
    cols = state.shape[1] // 2
    left = jnp.concatenate([features[...], state[:own, cols:].T[:step]], axis=0)
    for k in range(groups):
        group = jnp.bitwise_xor(ids[0], k)
        w_neigh = weights[k][pl.ds(base + pad, pad), :]
        total = mm(wide, jnp.concatenate([weights[k][pl.ds(base, pad), :], w_neigh, w_neigh], axis=0))
        result = mm(left, (total * slope[k]).astype(BF16))
        if parts:
            for i in range(units // BLOCK):
                out[group * (units // BLOCK) + i, pl.ds(0, 2 * step), :] = result[:, i * BLOCK : (i + 1) * BLOCK]
        else:
            out[:, pl.ds(pl.multiple_of(group * units, units), units)] = result
    if parts:
        for p, (height, lanes) in enumerate(cut(*both.shape, parts)):
            out[p, pl.ds(2 * step, out.shape[1] - 2 * step), :] = both[height, lanes]


def sum_kernel(pieces, out):
    held = pieces[0]
    for k in range(1, pieces.shape[0]):
        held = held + pieces[k]
    for k in range(pieces.shape[0]):
        out[k] = held


def place_kernel(class_count, node_total, pieces, self1, neigh1, self2, neigh2, loss, both):
    step = self1.shape[0]
    for p, (rows, lanes) in enumerate(cut(*both.shape, pieces.shape[0])):
        both[rows, lanes] = pieces[p, pl.ds(2 * step, pieces.shape[1] - 2 * step), :]
    for p in range(pieces.shape[0]):
        at = pl.ds(p * BLOCK, BLOCK)
        self1[:, at] = pieces[p, pl.ds(0, step), :]
        neigh1[:, at] = pieces[p, pl.ds(step, step), :]
    units = self2.shape[1]
    self2[...] = both[:class_count, :units]
    neigh2[...] = both[:class_count, units:]
    loss[...] = both[class_count : class_count + 1, 0:1] / node_total


def swap(value, count):
    blocks = value.reshape(count, -1, value.shape[-1])
    return lax.all_to_all(blocks, "node", 0, 0, tiled=True)


def crossed(value, count, k):
    return lax.ppermute(value, "feat", [(i, i ^ k) for i in range(count)])


def shards(features, send_rows, send_count, tile_src, tile_val, labels, w_self1, w_neigh1, w_self2, w_neigh2):
    nodes, groups = lax.axis_size("node"), lax.axis_size("feat")
    own, step = features.shape
    slots = send_rows.shape[2]
    halo = nodes * slots
    total_src = own + halo
    cols = step * groups
    width = w_self1.shape[1]
    units, classes = w_self2.shape
    pad = -(-(classes + 1) // 16) * 16
    across = 2 * units // BLOCK
    parts = nodes if nodes % across == 0 and pad % (8 * (nodes // across)) == 0 and width == nodes * BLOCK else 0
    node_total = own * nodes
    grad_scale = 1.0 / math.sqrt(node_total)
    ids = lax.axis_index("feat").astype(jnp.int32).reshape(1)
    blocks = own // BLOCK
    packed_rows = 2 * step * groups + 2 * pad

    turned = features.T
    turned_all = [turned] + [crossed(turned, groups, k) for k in range(1, groups)]
    (a_mat,) = call(
        prepare_kernel,
        [((own, 2 * total_src), BF16)],
        (tile_src, tile_val),
        [(tile_val.shape, BF16), ((own, total_src), F32)],
        copies=blocks,
        moved=tile_val.size * 4,
        grant=54 * 2**20 - 4 * own * total_src - 3 * 10**5,
    )
    a_mat, ids, *turned_all = lax.optimization_barrier((a_mat, ids, *turned_all))
    pick, full, packed, packed_weights = call(
        functools.partial(pack_kernel, groups),
        [((halo, own), BF16), ((own, cols), BF16), ((halo, cols), BF16), ((packed_rows, units), BF16)],
        (send_count, send_rows[0], w_self1, w_neigh1, w_self2.T, w_neigh2.T, *turned_all),
        [((cols, own), BF16)],
        flops=2 * halo * own * cols,
        moved=halo * own * 2,
    )
    weights = [packed_weights] + [crossed(packed_weights, groups, 1 << i) for i in range(groups.bit_length() - 1)]
    source = swap(packed, nodes).reshape(halo, cols)
    state, packed = call(
        first_kernel,
        [((total_src, 2 * cols), BF16), ((halo, cols), BF16)],
        (pick, a_mat, full, source),
        flops=4 * own * total_src * cols,
        moved=4 * own * total_src,
    )
    packed, ids, *weights = lax.optimization_barrier((packed, ids, *weights))
    pieces = weights[:2]
    for i, half in enumerate(weights[2:], 1):
        pieces += [half] + [crossed(half, groups, k) for k in range(1, 1 << i)]
    packed, *weights = lax.optimization_barrier((packed, *pieces))
    landed = swap(packed, nodes).reshape(halo, cols)
    message = (nodes, *message_shape(slots, pad))
    turned_grads, mine, agg_mine, loss, slope, packed = call(
        functools.partial(forward_kernel, classes, grad_scale, groups),
        [
            ((pad, own), BF16),
            ((own, units), BF16),
            ((own, units), BF16),
            ((8, 128), F32),
            ((groups, own, units), F32),
            (message, BF16),
        ],
        (ids, a_mat, state, landed, labels.reshape(1, own), *weights),
        flops=8 * own * total_src * width,
        moved=16 * own * width,
    )
    landed = swap(packed, nodes)
    second_shape = (pad, 2 * units)
    grads_shape = (parts, 2 * step + pad * 2 * units // (BLOCK * parts), BLOCK) if parts else (2 * step, width)
    grads, *second = call(
        functools.partial(backward_kernel, classes, parts, groups),
        [(grads_shape, F32)] + ([] if parts else [(second_shape, F32)]),
        (ids, turned_grads, pick, a_mat, slope, turned, state, mine, agg_mine, loss, landed, *weights),
        [((halo, pad), BF16)] + ([(second_shape, F32)] if parts else []),
        flops=8 * own * pad * width,
        moved=12 * own * width,
    )
    if not parts:
        grads, second = lax.psum((grads, second[0]), "node")
        loss = second[classes, 0] / node_total
        return (loss, grads[:step], grads[step:], second[:classes, :units].T, second[:classes, units:].T)
    grads = swap(grads, nodes)
    (grads,) = call(sum_kernel, [(grads_shape, F32)], (grads,), moved=2**20)
    grads = swap(grads, nodes)
    grad_self1, grad_neigh1, grad_self2, grad_neigh2, loss = call(
        functools.partial(place_kernel, classes, node_total),
        [((step, width), F32)] * 2 + [((classes, units), F32)] * 2 + [((1, 1), F32)],
        (grads,),
        [(second_shape, F32)],
    )
    return (loss.reshape(()), grad_self1, grad_neigh1, grad_self2.T, grad_neigh2.T)


def solution(mesh):
    in_specs = (
        P("node", "feat"),
        P("node", None, None),
        P("node", None),
        P("node", None),
        P("node", None, None, None),
        P("node"),
        P("feat", None),
        P("feat", None),
        P("feat", None),
        P("feat", None),
    )
    out_specs = (P(), P("feat", None), P("feat", None), P("feat", None), P("feat", None))
    return jax.shard_map(shards, mesh=mesh, in_specs=in_specs, out_specs=out_specs, check_vma=False)
```

```python
import functools
import math

import jax
import jax.numpy as jnp
from jax import lax
from jax.experimental import pallas as pl
from jax.experimental.pallas import tpu as pltpu
from jax.sharding import PartitionSpec as P

BLOCK = 128
F32 = jnp.float32
BF16 = jnp.bfloat16
VMEM = pl.BlockSpec(memory_space=pltpu.VMEM)
HBM = pl.BlockSpec(memory_space=pltpu.HBM)
SMEM = pl.BlockSpec(memory_space=pltpu.SMEM)


def mm(a, b):
    return lax.dot_general(a, b, (((1,), (0,)), ((), ())), preferred_element_type=F32)


def mm_nt(a, b):
    return lax.dot_general(a, b, (((1,), (1,)), ((), ())), preferred_element_type=F32)


def mm_tn(a, b):
    return lax.dot_general(a, b, (((0,), (0,)), ((), ())), preferred_element_type=F32)


def halves(value):
    high = value.astype(BF16)
    return high, (value - high.astype(F32)).astype(BF16)


def spread(a, rows):
    own = a.shape[0]
    parts = []
    for c in range(rows.shape[0] // own):
        part = rows[c * own : (c + 1) * own]
        parts += [part, part]
    return mm(a, jnp.concatenate(parts, axis=0))


def activate(v, with_slope):
    scale = math.sqrt(2.0 / math.pi)
    square = v * v
    t = jnp.tanh(v * (scale + (scale * 0.044715) * square))
    half = 0.5 * v
    out = (half + half * t).astype(BF16)
    if not with_slope:
        return out
    return out, (0.5 + 0.5 * t) + half * (1.0 - t * t) * (scale + (scale * 3 * 0.044715) * square)


def size_of(shape, dtype):
    rows = -(-shape[-2] // 16) * 16 if len(shape) > 1 else 1
    return math.prod(shape[:-2]) * rows * (-(-shape[-1] // 128) * 128) * jnp.dtype(dtype).itemsize


def call(body, outs, args, scratch=(), copies=0, flops=0, moved=0, grant=0):
    specs = [SMEM if arg.dtype == jnp.int32 and arg.size < 512 else VMEM for arg in args]
    if copies:
        specs = [HBM] * len(args)
    room = sum(size_of(shape, dtype) for shape, dtype in [*outs, *scratch])
    room += sum(size_of(arg.shape, arg.dtype) for arg, spec in zip(args, specs) if spec is VMEM)
    return pl.pallas_call(
        body,
        out_shape=[jax.ShapeDtypeStruct(shape, dtype) for shape, dtype in outs],
        in_specs=specs,
        out_specs=[VMEM] * len(outs),
        scratch_shapes=[pltpu.VMEM(shape, dtype) for shape, dtype in scratch]
        + ([pltpu.SemaphoreType.DMA((copies,)), pltpu.SMEM(args[0].shape, jnp.int32)] if copies else []),
        compiler_params=pltpu.CompilerParams(vmem_limit_bytes=grant or min(room + 8 * 2**20, 56 * 2**20)),
        cost_estimate=pl.CostEstimate(flops=flops, bytes_accessed=moved, transcendentals=0),
    )(*args)


def prepare_kernel(src_in, tile_val, a_ref, tiles, dense, sems, tile_src):
    blocks, per_block = tile_val.shape[0], tile_val.shape[1]
    own = blocks * BLOCK
    src_copy = pltpu.make_async_copy(src_in, tile_src, sems.at[blocks])
    src_copy.start()
    copies = [pltpu.make_async_copy(tile_val.at[b], tiles.at[b], sems.at[b]) for b in range(blocks)]
    for copy in copies:
        copy.start()
    dense[...] = jnp.zeros_like(dense)
    src_copy.wait()
    for b in range(blocks):
        rows = pl.ds(b * BLOCK, BLOCK)
        copies[b].wait()

        def add(k, _, b=b, rows=rows):
            at = pl.ds(pl.multiple_of(tile_src[b, k] * BLOCK, BLOCK), BLOCK)
            dense[rows, at] = dense[rows, at] + tiles[b, k].astype(F32)
            return 0

        lax.fori_loop(0, per_block, add, 0)
        for c in range(dense.shape[1] // own):
            high, low = halves(dense[rows, pl.ds(c * own, own)])
            a_ref[rows, pl.ds(2 * c * own, own)] = high
            a_ref[rows, pl.ds((2 * c + 1) * own, own)] = low


def pack_kernel(groups, count, send_rows, w_self1, w_neigh1, w_self2, w_neigh2, *refs):
    pieces, (pick, full, packed, weights), (turned,) = refs[:groups], refs[groups : groups + 4], refs[groups + 4 :]
    step, own = pieces[0].shape
    classes, units = w_self2.shape
    base = 2 * step * groups
    pad = (weights.shape[0] - base) // 2
    for j in range(groups):
        at = pl.ds(j * units, units)
        weights[pl.ds(2 * step * j, step), :] = w_self1[:, at]
        weights[pl.ds(2 * step * j + step, step), :] = w_neigh1[:, at]
    weights[pl.ds(base, 2 * pad), :] = jnp.zeros((2 * pad, units), BF16)
    weights[pl.ds(base, classes), :] = w_self2[...]
    weights[pl.ds(base + pad, classes), :] = w_neigh2[...]
    dests, slots = send_rows.shape
    columns = send_rows[...].astype(F32).T
    row_id = lax.broadcasted_iota(jnp.int32, (slots, own), 1).astype(F32)
    slot_id = lax.broadcasted_iota(jnp.int32, (slots, own), 0)
    for d in range(dests):
        hit = (columns[:, d : d + 1] == row_id) & (slot_id < count[0, d])
        pick[pl.ds(d * slots, slots), :] = jnp.where(hit, 1.0, 0.0).astype(BF16)
    for k, piece in enumerate(pieces):
        turned[pl.ds(k * step, step), :] = piece[...]
    full[...] = turned[...].T
    packed[...] = mm(pick[...], full[...]).astype(BF16)


def first_kernel(pick, a_ref, full, source, state, packed):
    own, cols = full.shape
    total = spread(a_ref[:, : 2 * own], full[...]) + spread(a_ref[:, 2 * own :], source[...])
    agg = total.astype(BF16)
    packed[...] = mm(pick[...], agg).astype(BF16)
    state[:own, :cols] = full[...]
    state[:own, cols:] = agg
    state[own:, :cols] = source[...]
    state[own:, cols:] = jnp.zeros_like(source)


def forward_kernel(
    class_count, grad_scale, groups, ids, side, a_ref, state, landed, labels, *refs
):
    weights = refs[:groups]
    turned, slope, packed, *seconds = refs[groups:]
    halo, cols = landed.shape
    own = state.shape[0] - halo
    units = weights[0].shape[1]
    step = cols // groups
    base = 2 * step * groups
    pad = turned.shape[0]
    slots = halo // packed.shape[0]
    near = state[:own, :]
    total = jnp.zeros((pad, own), F32)
    for k in range(groups):
        group = lax.rem(ids[0] + groups - k, groups)
        begin = [pl.multiple_of(2 * step * group + part * step, step) for part in (0, 1)]
        w_one = jnp.concatenate([w[pl.ds(at, step), :] for at in begin for w in weights], axis=0)
        out, slope[k] = activate(mm(near, w_one), True)
        if halo == own:
            both = jnp.concatenate([state[own:, :cols], landed[...]], axis=1)
            far = activate(mm(both, w_one), False)
            held = spread(a_ref[...], jnp.concatenate([out, far], axis=0))
        else:

            def one(r, held, w_one=w_one):
                rows = pl.ds(pl.multiple_of(r * own, own), own)
                srcs = pl.ds(pl.multiple_of(2 * (r + 1) * own, own), 2 * own)
                lower = pl.ds(pl.multiple_of((r + 1) * own, own), own)
                both = jnp.concatenate([state[lower, :cols], landed[rows, :]], axis=1)
                return held + spread(a_ref[:, srcs], activate(mm(both, w_one), False))

            held = lax.fori_loop(0, halo // own, one, spread(a_ref[:, : 2 * own], out))
        rounded = held.astype(BF16)
        if k == 0:
            mine, agg_mine = out, rounded
        total = total + mm_nt(weights[k][pl.ds(base, pad), :], out) + mm_nt(weights[k][pl.ds(base + pad, pad), :], rounded)
    class_id = lax.broadcasted_iota(jnp.int32, total.shape, 0)
    real = class_id < class_count
    top = jnp.max(jnp.where(real, total, -jnp.inf), axis=0, keepdims=True)
    shifted = total - top
    powers = jnp.where(real, jnp.exp(shifted), 0.0)
    sums = jnp.sum(powers, axis=0, keepdims=True)
    target = (class_id == labels[...]).astype(F32)
    turned[...] = ((powers / sums - target) * grad_scale).astype(BF16)
    row_loss = jnp.log(sums) - jnp.sum(shifted * target, axis=0, keepdims=True)
    own_grads = mm(turned[...], mine)
    row = lax.broadcasted_iota(jnp.int32, own_grads.shape, 0)
    own_grads = jnp.where(row == class_count, jnp.sum(row_loss, axis=1, keepdims=True), own_grads)
    if len(seconds) == 1:
        seconds[0][:, :units] = own_grads
        seconds[0][:, units:] = mm(turned[...], agg_mine)
    else:
        keep, give, both = seconds
        both[0] = own_grads
        both[1] = mm(turned[...], agg_mine)
        keep[...] = both[side[0]]
        give[...] = both[1 - side[0]]
    per_chunk = own // slots
    for c in range(halo // own):
        back = mm(turned[...], a_ref[:, pl.ds(2 * (c + 1) * own, own)]).T.astype(BF16)
        for d in range(per_chunk):
            put_message(packed, c * per_chunk + d, back[d * slots : (d + 1) * slots])


def message_shape(slots, pad):
    compact = BLOCK < pad <= BLOCK + BLOCK // 2 and slots % 32 == 0
    return (slots + slots // 2, BLOCK) if compact else (slots, pad)


def put_message(packed, d, rows):
    slots, pad = rows.shape
    if packed.shape[1:] == (slots, pad):
        packed[d] = rows
        return
    half, tail = slots // 2, pad - BLOCK
    packed[d, :slots, :] = rows[:, :BLOCK]
    filler = jnp.zeros((half, BLOCK // 2 - tail), BF16)
    packed[d, slots:, :] = jnp.concatenate([rows[:half, BLOCK:], filler, rows[half:, BLOCK:], filler], axis=1)


def take_message(packed, d, landed):
    slots, pad = landed.shape[0] // packed.shape[0], landed.shape[1]
    if packed.shape[1:] == (slots, pad):
        landed[pl.ds(d * slots, slots), :] = packed[d]
        return
    half, tail = slots // 2, pad - BLOCK
    landed[pl.ds(d * slots, slots), :BLOCK] = packed[d, :slots, :]
    landed[pl.ds(d * slots, half), BLOCK:] = packed[d, slots:, :tail]
    landed[pl.ds(d * slots + half, half), BLOCK:] = packed[d, slots:, BLOCK // 2 : BLOCK // 2 + tail]


def backward_kernel(parts, groups, ids, turned, pick, a_ref, slope, features, state, landed, *refs):
    weights = refs[:groups]
    out, rows = refs[groups:]
    own = turned.shape[1]
    units = slope.shape[2]
    pad = turned.shape[0]
    step = features.shape[0]
    base = 2 * step * groups
    for d in range(landed.shape[0]):
        take_message(landed, d, rows)
    high, low = halves(mm(turned[...], a_ref[:, :own]) + mm_tn(rows[...], pick[...]))
    wide = jnp.concatenate([turned[...], high, low], axis=0).T
    cols = state.shape[1] // 2
    left = jnp.concatenate([features[...], state[:own, cols:].T[:step]], axis=0)
    for k in range(groups):
        group = lax.rem(ids[0] + groups - k, groups)
        w_neigh = weights[k][pl.ds(base + pad, pad), :]
        total = mm(wide, jnp.concatenate([weights[k][pl.ds(base, pad), :], w_neigh, w_neigh], axis=0))
        result = mm(left, (total * slope[k]).astype(BF16))
        if parts:
            for i in range(units // BLOCK):
                out[group * (units // BLOCK) + i] = result[:, i * BLOCK : (i + 1) * BLOCK]
        else:
            out[:, pl.ds(pl.multiple_of(group * units, units), units)] = result


def quarter(p, rows):
    height = rows // 4
    return slice(p // 2 * height, (p // 2 + 1) * height), slice(p % 2 * BLOCK, (p % 2 + 1) * BLOCK)


def join_kernel(grads, keep, other, out):
    step = grads.shape[1]
    height = keep.shape[0] // 4
    for p in range(grads.shape[0]):
        at = quarter(p, keep.shape[0])
        out[p, :step, :] = grads[p]
        out[p, step : step + height, :] = keep[at] + other[at]
        out[p, step + height :, :] = jnp.zeros((out.shape[1] - step - height, BLOCK), F32)


def sum_kernel(step, height, pieces, out):
    first = pieces[0, :step, :]
    second = [pieces[0, step : step + height, :], pieces[1, step : step + height, :]]
    for p in range(1, pieces.shape[0]):
        first = first + pieces[p, :step, :]
        if p > 1:
            second[p % 2] = second[p % 2] + pieces[p, step : step + height, :]
    for p in range(pieces.shape[0]):
        out[p, :step, :] = first
        out[p, step : step + height, :] = second[0]
        out[p, step + height :, :] = second[1]


def place_kernel(class_count, node_total, pieces, self1, neigh1, self2, neigh2, loss, both):
    step = self1.shape[0]
    units = self2.shape[1]
    height = both.shape[1] // 4
    for p in range(pieces.shape[0]):
        at = pl.ds(p * BLOCK, BLOCK)
        self1[:, at] = pieces[p, :step, :]
        neigh1[:, at] = pieces[p, step : 2 * step, :]
        rows, lanes = quarter(p, both.shape[1])
        both[0, rows, lanes] = pieces[p, 2 * step : 2 * step + height, :]
        both[1, rows, lanes] = pieces[p, 2 * step + height :, :]
    self2[...] = both[0, :class_count, :]
    neigh2[...] = both[1, :class_count, :]
    loss[...] = both[0, class_count : class_count + 1, 0:1] / node_total


def swap(value, count):
    blocks = value.reshape(count, -1, value.shape[-1])
    return lax.all_to_all(blocks, "node", 0, 0, tiled=True)


def gather_shifted(value, count):
    return [value] + [lax.ppermute(value, "feat", [(i, (i + k) % count) for i in range(count)]) for k in range(1, count)]


def shards(features, send_rows, send_count, tile_src, tile_val, labels, w_self1, w_neigh1, w_self2, w_neigh2):
    nodes, groups = lax.axis_size("node"), lax.axis_size("feat")
    own, step = features.shape
    slots = send_rows.shape[2]
    halo = nodes * slots
    total_src = own + halo
    cols = step * groups
    width = w_self1.shape[1]
    units, classes = w_self2.shape
    pad = -(-(classes + 1) // 16) * 16
    parts = nodes if nodes == 8 and units == 2 * BLOCK and width == nodes * BLOCK else 0
    node_total = own * nodes
    grad_scale = 1.0 / math.sqrt(node_total)
    ids = lax.axis_index("feat").astype(jnp.int32).reshape(1)
    side = (lax.axis_index("node") & 1).astype(jnp.int32).reshape(1)
    blocks = own // BLOCK
    packed_rows = 2 * step * groups + 2 * pad

    turned = features.T
    turned_all = gather_shifted(turned, groups)
    (a_mat,) = call(
        prepare_kernel,
        [((own, 2 * total_src), BF16)],
        (tile_src, tile_val),
        [(tile_val.shape, BF16), ((own, total_src), F32)],
        copies=blocks + 1,
        moved=tile_val.size * 4,
        grant=54 * 2**20 - 4 * own * total_src - 3 * 10**5,
    )
    a_mat, ids, side, *turned_all = lax.optimization_barrier((a_mat, ids, side, *turned_all))
    pick, full, packed, packed_weights = call(
        functools.partial(pack_kernel, groups),
        [((halo, own), BF16), ((own, cols), BF16), ((halo, cols), BF16), ((packed_rows, units), BF16)],
        (send_count, send_rows[0], w_self1, w_neigh1, w_self2.T, w_neigh2.T, *turned_all),
        [((cols, own), BF16)],
        flops=2 * halo * own * cols,
        moved=halo * own * 2,
    )
    weights = gather_shifted(packed_weights, groups)
    source = swap(packed, nodes).reshape(halo, cols)
    state, packed = call(
        first_kernel,
        [((total_src, 2 * cols), BF16), ((halo, cols), BF16)],
        (pick, a_mat, full, source),
        flops=4 * own * total_src * cols,
        moved=4 * own * total_src,
    )
    packed, ids, side, *weights = lax.optimization_barrier((packed, ids, side, *weights))
    landed = swap(packed, nodes).reshape(halo, cols)
    message = (nodes, *message_shape(slots, pad))
    second_shape = (pad, 2 * units)
    turned_grads, slope, packed, *seconds = call(
        functools.partial(forward_kernel, classes, grad_scale, groups),
        [((pad, own), BF16), ((groups, own, units), F32), (message, BF16)]
        + ([((pad, units), F32)] * 2 if parts else [(second_shape, F32)]),
        (ids, side, a_mat, state, landed, labels.reshape(1, own), *weights),
        [((2, pad, units), F32)] if parts else [],
        flops=8 * own * total_src * width,
        moved=16 * own * width,
    )
    if parts:
        keep, give = seconds
        other = lax.ppermute(give, "node", [(i, i ^ 1) for i in range(nodes)])
    landed = swap(packed, nodes)
    (grads,) = call(
        functools.partial(backward_kernel, parts, groups),
        [((parts, 2 * step, BLOCK) if parts else (2 * step, width), F32)],
        (ids, turned_grads, pick, a_mat, slope, turned, state, landed, *weights),
        [((halo, pad), BF16)],
        flops=8 * own * pad * width,
        moved=12 * own * width,
    )
    if not parts:
        grads, second = lax.psum((grads, seconds[0]), "node")
        loss = second[classes, 0] / node_total
        return (loss, grads[:step], grads[step:], second[:classes, :units].T, second[:classes, units:].T)
    height = pad // 4
    grads, other = lax.optimization_barrier((grads, other))
    (grads,) = call(join_kernel, [((nodes, -(-(2 * step + height) // 8) * 8, BLOCK), F32)], (grads, keep, other))
    grads = swap(grads, nodes)
    (grads,) = call(functools.partial(sum_kernel, 2 * step, height), [((nodes, 2 * step + 2 * height, BLOCK), F32)], (grads,))
    grads = swap(grads, nodes)
    grad_self1, grad_neigh1, grad_self2, grad_neigh2, loss = call(
        functools.partial(place_kernel, classes, node_total),
        [((step, width), F32)] * 2 + [((classes, units), F32)] * 2 + [((1, 1), F32)],
        (grads,),
        [((2, pad, units), F32)],
    )
    return (loss.reshape(()), grad_self1, grad_neigh1, grad_self2.T, grad_neigh2.T)


def solution(mesh):
    in_specs = (
        P("node", "feat"),
        P("node", None, None),
        P("node", None),
        P("node", None),
        P("node", None, None, None),
        P("node"),
        P("feat", None),
        P("feat", None),
        P("feat", None),
        P("feat", None),
    )
    out_specs = (P(), P("feat", None), P("feat", None), P("feat", None), P("feat", None))
    return jax.shard_map(shards, mesh=mesh, in_specs=in_specs, out_specs=out_specs, check_vma=False)
```

```python
import functools
import math

import jax
import jax.numpy as jnp
from jax import lax
from jax.experimental import pallas as pl
from jax.experimental.pallas import tpu as pltpu
from jax.sharding import PartitionSpec as P

BLOCK = 128
F32 = jnp.float32
BF16 = jnp.bfloat16
VMEM = pl.BlockSpec(memory_space=pltpu.VMEM)
HBM = pl.BlockSpec(memory_space=pltpu.HBM)
SMEM = pl.BlockSpec(memory_space=pltpu.SMEM)


def mm(a, b):
    return lax.dot_general(a, b, (((1,), (0,)), ((), ())), preferred_element_type=F32)


def mm_nt(a, b):
    return lax.dot_general(a, b, (((1,), (1,)), ((), ())), preferred_element_type=F32)


def mm_tn(a, b):
    return lax.dot_general(a, b, (((0,), (0,)), ((), ())), preferred_element_type=F32)


def halves(value):
    high = value.astype(BF16)
    return high, (value - high.astype(F32)).astype(BF16)


def spread(a, rows):
    own = a.shape[0]
    parts = []
    for c in range(rows.shape[0] // own):
        part = rows[c * own : (c + 1) * own]
        parts += [part, part]
    return mm(a, jnp.concatenate(parts, axis=0))


def activate(v, with_slope):
    scale = math.sqrt(2.0 / math.pi)
    square = v * v
    t = jnp.tanh(v * (scale + (scale * 0.044715) * square))
    half = 0.5 * v
    out = (half + half * t).astype(BF16)
    if not with_slope:
        return out
    return out, (0.5 + 0.5 * t) + half * (1.0 - t * t) * (scale + (scale * 3 * 0.044715) * square)


def size_of(shape, dtype):
    rows = -(-shape[-2] // 16) * 16 if len(shape) > 1 else 1
    return math.prod(shape[:-2]) * rows * (-(-shape[-1] // 128) * 128) * jnp.dtype(dtype).itemsize


def call(body, outs, args, scratch=(), copies=0, flops=0, moved=0, grant=0):
    specs = [SMEM if arg.dtype == jnp.int32 and arg.size < 512 else VMEM for arg in args]
    if copies:
        specs = [HBM] * len(args)
    room = sum(size_of(shape, dtype) for shape, dtype in [*outs, *scratch])
    room += sum(size_of(arg.shape, arg.dtype) for arg, spec in zip(args, specs) if spec is VMEM)
    return pl.pallas_call(
        body,
        out_shape=[jax.ShapeDtypeStruct(shape, dtype) for shape, dtype in outs],
        in_specs=specs,
        out_specs=[VMEM] * len(outs),
        scratch_shapes=[pltpu.VMEM(shape, dtype) for shape, dtype in scratch]
        + ([pltpu.SemaphoreType.DMA((copies,)), pltpu.SMEM(args[0].shape, jnp.int32)] if copies else []),
        compiler_params=pltpu.CompilerParams(vmem_limit_bytes=grant or min(room + 8 * 2**20, 56 * 2**20)),
        cost_estimate=pl.CostEstimate(flops=flops, bytes_accessed=moved, transcendentals=0),
    )(*args)


def prepare_kernel(src_in, tile_val, a_ref, tiles, dense, sems, tile_src):
    blocks, per_block = tile_val.shape[0], tile_val.shape[1]
    own = blocks * BLOCK
    src_copy = pltpu.make_async_copy(src_in, tile_src, sems.at[blocks])
    src_copy.start()
    copies = [pltpu.make_async_copy(tile_val.at[b], tiles.at[b], sems.at[b]) for b in range(blocks)]
    for copy in copies:
        copy.start()
    dense[...] = jnp.zeros_like(dense)
    src_copy.wait()
    for b in range(blocks):
        rows = pl.ds(b * BLOCK, BLOCK)
        copies[b].wait()

        def add(k, _, b=b, rows=rows):
            at = pl.ds(pl.multiple_of(tile_src[b, k] * BLOCK, BLOCK), BLOCK)
            dense[rows, at] = dense[rows, at] + tiles[b, k].astype(F32)
            return 0

        lax.fori_loop(0, per_block, add, 0)
        for c in range(dense.shape[1] // own):
            high, low = halves(dense[rows, pl.ds(c * own, own)])
            a_ref[rows, pl.ds(2 * c * own, own)] = high
            a_ref[rows, pl.ds((2 * c + 1) * own, own)] = low


def pack_kernel(groups, count, send_rows, w_self1, w_neigh1, w_self2, w_neigh2, *refs):
    pieces, (pick, full, packed, weights), (turned,) = refs[:groups], refs[groups : groups + 4], refs[groups + 4 :]
    step, own = pieces[0].shape
    classes, units = w_self2.shape
    base = 2 * step * groups
    pad = (weights.shape[0] - base) // 2
    for j in range(groups):
        at = pl.ds(j * units, units)
        weights[pl.ds(2 * step * j, step), :] = w_self1[:, at]
        weights[pl.ds(2 * step * j + step, step), :] = w_neigh1[:, at]
    weights[pl.ds(base, 2 * pad), :] = jnp.zeros((2 * pad, units), BF16)
    weights[pl.ds(base, classes), :] = w_self2[...]
    weights[pl.ds(base + pad, classes), :] = w_neigh2[...]
    dests, slots = send_rows.shape
    columns = send_rows[...].astype(F32).T
    row_id = lax.broadcasted_iota(jnp.int32, (slots, own), 1).astype(F32)
    slot_id = lax.broadcasted_iota(jnp.int32, (slots, own), 0)
    for d in range(dests):
        hit = (columns[:, d : d + 1] == row_id) & (slot_id < count[0, d])
        pick[pl.ds(d * slots, slots), :] = jnp.where(hit, 1.0, 0.0).astype(BF16)
    for k, piece in enumerate(pieces):
        turned[pl.ds(k * step, step), :] = piece[...]
    full[...] = turned[...].T
    packed[...] = mm(pick[...], full[...]).astype(BF16)


def first_kernel(pick, a_ref, full, source, state, packed):
    own, cols = full.shape
    total = spread(a_ref[:, : 2 * own], full[...]) + spread(a_ref[:, 2 * own :], source[...])
    agg = total.astype(BF16)
    packed[...] = mm(pick[...], agg).astype(BF16)
    state[:own, :cols] = full[...]
    state[:own, cols:] = agg
    state[own:, :cols] = source[...]
    state[own:, cols:] = jnp.zeros_like(source)


def forward_kernel(
    class_count, grad_scale, groups, ids, side, a_ref, state, landed, labels, *refs
):
    weights = refs[:groups]
    turned, slope, packed, *seconds = refs[groups:]
    halo, cols = landed.shape
    own = state.shape[0] - halo
    units = weights[0].shape[1]
    step = cols // groups
    base = 2 * step * groups
    pad = turned.shape[0]
    slots = halo // packed.shape[0]
    near = state[:own, :]
    total = jnp.zeros((pad, own), F32)
    for k in range(groups):
        group = lax.rem(ids[0] + groups - k, groups)
        begin = [pl.multiple_of(2 * step * group + part * step, step) for part in (0, 1)]
        w_one = jnp.concatenate([w[pl.ds(at, step), :] for at in begin for w in weights], axis=0)
        out, slope[k] = activate(mm(near, w_one), True)
        if halo == own:
            both = jnp.concatenate([state[own:, :cols], landed[...]], axis=1)
            far = activate(mm(both, w_one), False)
            held = spread(a_ref[...], jnp.concatenate([out, far], axis=0))
        else:

            def one(r, held, w_one=w_one):
                rows = pl.ds(pl.multiple_of(r * own, own), own)
                srcs = pl.ds(pl.multiple_of(2 * (r + 1) * own, own), 2 * own)
                lower = pl.ds(pl.multiple_of((r + 1) * own, own), own)
                both = jnp.concatenate([state[lower, :cols], landed[rows, :]], axis=1)
                return held + spread(a_ref[:, srcs], activate(mm(both, w_one), False))

            held = lax.fori_loop(0, halo // own, one, spread(a_ref[:, : 2 * own], out))
        rounded = held.astype(BF16)
        if k == 0:
            mine, agg_mine = out, rounded
        total = total + mm_nt(weights[k][pl.ds(base, pad), :], out) + mm_nt(weights[k][pl.ds(base + pad, pad), :], rounded)
    class_id = lax.broadcasted_iota(jnp.int32, total.shape, 0)
    real = class_id < class_count
    top = jnp.max(jnp.where(real, total, -jnp.inf), axis=0, keepdims=True)
    shifted = total - top
    powers = jnp.where(real, jnp.exp(shifted), 0.0)
    sums = jnp.sum(powers, axis=0, keepdims=True)
    target = (class_id == labels[...]).astype(F32)
    turned[...] = ((powers / sums - target) * grad_scale).astype(BF16)
    row_loss = jnp.log(sums) - jnp.sum(shifted * target, axis=0, keepdims=True)
    own_grads = mm(turned[...], mine)
    row = lax.broadcasted_iota(jnp.int32, own_grads.shape, 0)
    own_grads = jnp.where(row == class_count, jnp.sum(row_loss, axis=1, keepdims=True), own_grads)
    if len(seconds) == 1:
        seconds[0][:, :units] = own_grads
        seconds[0][:, units:] = mm(turned[...], agg_mine)
    else:
        keep, give, both = seconds
        both[0] = own_grads
        both[1] = mm(turned[...], agg_mine)
        keep[...] = both[side[0]]
        give[...] = both[1 - side[0]]
    per_chunk = own // slots
    for c in range(halo // own):
        back = mm(turned[...], a_ref[:, pl.ds(2 * (c + 1) * own, own)]).T.astype(BF16)
        for d in range(per_chunk):
            put_message(packed, c * per_chunk + d, back[d * slots : (d + 1) * slots])


def message_shape(slots, pad):
    compact = BLOCK < pad <= BLOCK + BLOCK // 2 and slots % 32 == 0
    return (slots + slots // 2, BLOCK) if compact else (slots, pad)


def put_message(packed, d, rows):
    slots, pad = rows.shape
    if packed.shape[1:] == (slots, pad):
        packed[d] = rows
        return
    half, tail = slots // 2, pad - BLOCK
    packed[d, :slots, :] = rows[:, :BLOCK]
    filler = jnp.zeros((half, BLOCK // 2 - tail), BF16)
    packed[d, slots:, :] = jnp.concatenate([rows[:half, BLOCK:], filler, rows[half:, BLOCK:], filler], axis=1)


def take_message(packed, d, landed):
    slots, pad = landed.shape[0] // packed.shape[0], landed.shape[1]
    if packed.shape[1:] == (slots, pad):
        landed[pl.ds(d * slots, slots), :] = packed[d]
        return
    half, tail = slots // 2, pad - BLOCK
    landed[pl.ds(d * slots, slots), :BLOCK] = packed[d, :slots, :]
    landed[pl.ds(d * slots, half), BLOCK:] = packed[d, slots:, :tail]
    landed[pl.ds(d * slots + half, half), BLOCK:] = packed[d, slots:, BLOCK // 2 : BLOCK // 2 + tail]


def backward_kernel(parts, groups, ids, turned, pick, a_ref, slope, features, state, landed, *refs):
    weights = refs[:groups]
    out, rows = refs[groups:]
    own = turned.shape[1]
    units = slope.shape[2]
    pad = turned.shape[0]
    step = features.shape[0]
    base = 2 * step * groups
    for d in range(landed.shape[0]):
        take_message(landed, d, rows)
    high, low = halves(mm(turned[...], a_ref[:, :own]) + mm_tn(rows[...], pick[...]))
    wide = jnp.concatenate([turned[...], high, low], axis=0).T
    cols = state.shape[1] // 2
    left = jnp.concatenate([features[...], state[:own, cols:].T[:step]], axis=0)
    for k in range(groups):
        group = lax.rem(ids[0] + groups - k, groups)
        w_neigh = weights[k][pl.ds(base + pad, pad), :]
        total = mm(wide, jnp.concatenate([weights[k][pl.ds(base, pad), :], w_neigh, w_neigh], axis=0))
        result = mm(left, (total * slope[k]).astype(BF16))
        if parts:
            for i in range(units // BLOCK):
                out[group * (units // BLOCK) + i] = result[:, i * BLOCK : (i + 1) * BLOCK]
        else:
            out[:, pl.ds(pl.multiple_of(group * units, units), units)] = result


def quarter(p, rows):
    height = rows // 4
    return slice(p // 2 * height, (p // 2 + 1) * height), slice(p % 2 * BLOCK, (p % 2 + 1) * BLOCK)


def join_kernel(grads, keep, other, out):
    step = grads.shape[1]
    height = keep.shape[0] // 4
    for p in range(grads.shape[0]):
        at = quarter(p, keep.shape[0])
        out[p, :step, :] = grads[p]
        out[p, step : step + height, :] = keep[at] + other[at]
        out[p, step + height :, :] = jnp.zeros((out.shape[1] - step - height, BLOCK), F32)


def sum_kernel(step, height, pieces, out):
    first = pieces[0, :step, :]
    second = [pieces[0, step : step + height, :], pieces[1, step : step + height, :]]
    for p in range(1, pieces.shape[0]):
        first = first + pieces[p, :step, :]
        if p > 1:
            second[p % 2] = second[p % 2] + pieces[p, step : step + height, :]
    for p in range(pieces.shape[0]):
        out[p, :step, :] = first
        out[p, step : step + height, :] = second[0]
        out[p, step + height :, :] = second[1]


def place_kernel(class_count, node_total, pieces, self1, neigh1, self2, neigh2, loss, both):
    step = self1.shape[0]
    units = self2.shape[1]
    height = both.shape[1] // 4
    for p in range(pieces.shape[0]):
        at = pl.ds(p * BLOCK, BLOCK)
        self1[:, at] = pieces[p, :step, :]
        neigh1[:, at] = pieces[p, step : 2 * step, :]
        rows, lanes = quarter(p, both.shape[1])
        both[0, rows, lanes] = pieces[p, 2 * step : 2 * step + height, :]
        both[1, rows, lanes] = pieces[p, 2 * step + height :, :]
    self2[...] = both[0, :class_count, :]
    neigh2[...] = both[1, :class_count, :]
    loss[...] = both[0, class_count : class_count + 1, 0:1] / node_total


def swap(value, count):
    blocks = value.reshape(count, -1, value.shape[-1])
    return lax.all_to_all(blocks, "node", 0, 0, tiled=True)


def gather_shifted(value, count):
    return [value] + [lax.ppermute(value, "feat", [(i, (i + k) % count) for i in range(count)]) for k in range(1, count)]


def shards(features, send_rows, send_count, tile_src, tile_val, labels, w_self1, w_neigh1, w_self2, w_neigh2):
    nodes, groups = lax.axis_size("node"), lax.axis_size("feat")
    own, step = features.shape
    slots = send_rows.shape[2]
    halo = nodes * slots
    total_src = own + halo
    cols = step * groups
    width = w_self1.shape[1]
    units, classes = w_self2.shape
    pad = -(-(classes + 1) // 16) * 16
    parts = nodes if nodes == 8 and units == 2 * BLOCK and width == nodes * BLOCK else 0
    node_total = own * nodes
    grad_scale = 1.0 / math.sqrt(node_total)
    ids = lax.axis_index("feat").astype(jnp.int32).reshape(1)
    side = (lax.axis_index("node") & 1).astype(jnp.int32).reshape(1)
    blocks = own // BLOCK
    packed_rows = 2 * step * groups + 2 * pad

    turned = features.T
    turned_all = gather_shifted(turned, groups)
    (a_mat,) = call(
        prepare_kernel,
        [((own, 2 * total_src), BF16)],
        (tile_src, tile_val),
        [(tile_val.shape, BF16), ((own, total_src), F32)],
        copies=blocks + 1,
        moved=tile_val.size * 4,
        grant=54 * 2**20 - 4 * own * total_src - 3 * 10**5,
    )
    a_mat, ids, side, *turned_all = lax.optimization_barrier((a_mat, ids, side, *turned_all))
    pick, full, packed, packed_weights = call(
        functools.partial(pack_kernel, groups),
        [((halo, own), BF16), ((own, cols), BF16), ((halo, cols), BF16), ((packed_rows, units), BF16)],
        (send_count, send_rows[0], w_self1, w_neigh1, w_self2.T, w_neigh2.T, *turned_all),
        [((cols, own), BF16)],
        flops=2 * halo * own * cols,
        moved=halo * own * 2,
    )
    weights = gather_shifted(packed_weights, groups)
    source = swap(packed, nodes).reshape(halo, cols)
    state, packed = call(
        first_kernel,
        [((total_src, 2 * cols), BF16), ((halo, cols), BF16)],
        (pick, a_mat, full, source),
        flops=4 * own * total_src * cols,
        moved=4 * own * total_src,
    )
    packed, ids, side, *weights = lax.optimization_barrier((packed, ids, side, *weights))
    landed = swap(packed, nodes).reshape(halo, cols)
    message = (nodes, *message_shape(slots, pad))
    second_shape = (pad, 2 * units)
    turned_grads, slope, packed, *seconds = call(
        functools.partial(forward_kernel, classes, grad_scale, groups),
        [((pad, own), BF16), ((groups, own, units), F32), (message, BF16)]
        + ([((pad, units), F32)] * 2 if parts else [(second_shape, F32)]),
        (ids, side, a_mat, state, landed, labels.reshape(1, own), *weights),
        [((2, pad, units), F32)] if parts else [],
        flops=8 * own * total_src * width,
        moved=16 * own * width,
    )
    if parts:
        keep, give = seconds
        other = lax.ppermute(give, "node", [(i, i ^ 1) for i in range(nodes)])
    landed = swap(packed, nodes)
    (grads,) = call(
        functools.partial(backward_kernel, parts, groups),
        [((parts, 2 * step, BLOCK) if parts else (2 * step, width), F32)],
        (ids, turned_grads, pick, a_mat, slope, turned, state, landed, *weights),
        [((halo, pad), BF16)],
    )
    if not parts:
        grads, second = lax.psum((grads, seconds[0]), "node")
        loss = second[classes, 0] / node_total
        return (loss, grads[:step], grads[step:], second[:classes, :units].T, second[:classes, units:].T)
    height = pad // 4
    grads, other = lax.optimization_barrier((grads, other))
    (grads,) = call(join_kernel, [((nodes, -(-(2 * step + height) // 8) * 8, BLOCK), F32)], (grads, keep, other))
    grads = swap(grads, nodes)
    (grads,) = call(functools.partial(sum_kernel, 2 * step, height), [((nodes, 2 * step + 2 * height, BLOCK), F32)], (grads,))
    grads = swap(grads, nodes)
    grad_self1, grad_neigh1, grad_self2, grad_neigh2, loss = call(
        functools.partial(place_kernel, classes, node_total),
        [((step, width), F32)] * 2 + [((classes, units), F32)] * 2 + [((1, 1), F32)],
        (grads,),
        [((2, pad, units), F32)],
    )
    return (loss.reshape(()), grad_self1, grad_neigh1, grad_self2.T, grad_neigh2.T)


def solution(mesh):
    in_specs = (
        P("node", "feat"),
        P("node", None, None),
        P("node", None),
        P("node", None),
        P("node", None, None, None),
        P("node"),
        P("feat", None),
        P("feat", None),
        P("feat", None),
        P("feat", None),
    )
    out_specs = (P(), P("feat", None), P("feat", None), P("feat", None), P("feat", None))
    return jax.shard_map(shards, mesh=mesh, in_specs=in_specs, out_specs=out_specs, check_vma=False)
```

```python
import functools
import math

import jax
import jax.numpy as jnp
from jax import lax
from jax.experimental import pallas as pl
from jax.experimental.pallas import tpu as pltpu
from jax.sharding import PartitionSpec as P

BLOCK = 128
F32 = jnp.float32
BF16 = jnp.bfloat16
VMEM = pl.BlockSpec(memory_space=pltpu.VMEM)
HBM = pl.BlockSpec(memory_space=pltpu.HBM)
SMEM = pl.BlockSpec(memory_space=pltpu.SMEM)


def mm(a, b):
    return lax.dot_general(a, b, (((1,), (0,)), ((), ())), preferred_element_type=F32)


def mm_nt(a, b):
    return lax.dot_general(a, b, (((1,), (1,)), ((), ())), preferred_element_type=F32)


def mm_tn(a, b):
    return lax.dot_general(a, b, (((0,), (0,)), ((), ())), preferred_element_type=F32)


def halves(value):
    high = value.astype(BF16)
    return high, (value - high.astype(F32)).astype(BF16)


def spread(a, rows):
    own = a.shape[0]
    parts = []
    for c in range(rows.shape[0] // own):
        part = rows[c * own : (c + 1) * own]
        parts += [part, part]
    return mm(a, jnp.concatenate(parts, axis=0))


def activate(v, with_slope):
    scale = math.sqrt(2.0 / math.pi)
    square = v * v
    t = jnp.tanh(v * (scale + (scale * 0.044715) * square))
    half = 0.5 * v
    out = (half + half * t).astype(BF16)
    if not with_slope:
        return out
    return out, (0.5 + 0.5 * t) + half * (1.0 - t * t) * (scale + (scale * 3 * 0.044715) * square)


def size_of(shape, dtype):
    rows = -(-shape[-2] // 16) * 16 if len(shape) > 1 else 1
    return math.prod(shape[:-2]) * rows * (-(-shape[-1] // 128) * 128) * jnp.dtype(dtype).itemsize


def call(body, outs, args, scratch=(), copies=0, flops=0, moved=0, grant=0):
    specs = [SMEM if arg.dtype == jnp.int32 and arg.size < 512 else VMEM for arg in args]
    if copies:
        specs = [HBM] * len(args)
    room = sum(size_of(shape, dtype) for shape, dtype in [*outs, *scratch])
    room += sum(size_of(arg.shape, arg.dtype) for arg, spec in zip(args, specs) if spec is VMEM)
    return pl.pallas_call(
        body,
        out_shape=[jax.ShapeDtypeStruct(shape, dtype) for shape, dtype in outs],
        in_specs=specs,
        out_specs=[VMEM] * len(outs),
        scratch_shapes=[pltpu.VMEM(shape, dtype) for shape, dtype in scratch]
        + ([pltpu.SemaphoreType.DMA((copies,)), pltpu.SMEM(args[0].shape, jnp.int32)] if copies else []),
        compiler_params=pltpu.CompilerParams(vmem_limit_bytes=grant or min(room + 8 * 2**20, 56 * 2**20)),
        cost_estimate=pl.CostEstimate(flops=flops, bytes_accessed=moved, transcendentals=0),
    )(*args)


def prepare_kernel(src_in, tile_val, a_ref, tiles, dense, sems, tile_src):
    blocks, per_block = tile_val.shape[0], tile_val.shape[1]
    own = blocks * BLOCK
    src_copy = pltpu.make_async_copy(src_in, tile_src, sems.at[blocks])
    src_copy.start()
    copies = [pltpu.make_async_copy(tile_val.at[b], tiles.at[b], sems.at[b]) for b in range(blocks)]
    for copy in copies:
        copy.start()
    dense[...] = jnp.zeros_like(dense)
    src_copy.wait()
    for b in range(blocks):
        rows = pl.ds(b * BLOCK, BLOCK)
        copies[b].wait()

        def add(k, _, b=b, rows=rows):
            at = pl.ds(pl.multiple_of(tile_src[b, k] * BLOCK, BLOCK), BLOCK)
            dense[rows, at] = dense[rows, at] + tiles[b, k].astype(F32)
            return 0

        lax.fori_loop(0, per_block, add, 0)
        for c in range(dense.shape[1] // own):
            high, low = halves(dense[rows, pl.ds(c * own, own)])
            a_ref[rows, pl.ds(2 * c * own, own)] = high
            a_ref[rows, pl.ds((2 * c + 1) * own, own)] = low


def pack_kernel(groups, count, send_rows, w_self1, w_neigh1, w_self2, w_neigh2, *refs):
    pieces, (pick, full, packed, weights), (turned,) = refs[:groups], refs[groups : groups + 4], refs[groups + 4 :]
    step, own = pieces[0].shape
    classes, units = w_self2.shape
    base = 2 * step * groups
    pad = (weights.shape[0] - base) // 2
    for j in range(groups):
        at = pl.ds(j * units, units)
        weights[pl.ds(2 * step * j, step), :] = w_self1[:, at]
        weights[pl.ds(2 * step * j + step, step), :] = w_neigh1[:, at]
    weights[pl.ds(base, 2 * pad), :] = jnp.zeros((2 * pad, units), BF16)
    weights[pl.ds(base, classes), :] = w_self2[...]
    weights[pl.ds(base + pad, classes), :] = w_neigh2[...]
    dests, slots = send_rows.shape
    columns = send_rows[...].astype(F32).T
    row_id = lax.broadcasted_iota(jnp.int32, (slots, own), 1).astype(F32)
    slot_id = lax.broadcasted_iota(jnp.int32, (slots, own), 0)
    for d in range(dests):
        hit = (columns[:, d : d + 1] == row_id) & (slot_id < count[0, d])
        pick[pl.ds(d * slots, slots), :] = jnp.where(hit, 1.0, 0.0).astype(BF16)
    for k, piece in enumerate(pieces):
        turned[pl.ds(k * step, step), :] = piece[...]
    full[...] = turned[...].T
    packed[...] = mm(pick[...], full[...]).astype(BF16)


def first_kernel(pick, a_ref, full, source, state, packed):
    own, cols = full.shape
    total = spread(a_ref[:, : 2 * own], full[...]) + spread(a_ref[:, 2 * own :], source[...])
    agg = total.astype(BF16)
    packed[...] = mm(pick[...], agg).astype(BF16)
    state[:own, :cols] = full[...]
    state[:own, cols:] = agg
    state[own:, :cols] = source[...]
    state[own:, cols:] = jnp.zeros_like(source)


def forward_kernel(
    class_count, grad_scale, groups, ids, a_ref, state, landed, labels, *refs
):
    weights = refs[:groups]
    turned, slope, packed, second = refs[groups:]
    halo, cols = landed.shape
    own = state.shape[0] - halo
    units = weights[0].shape[1]
    step = cols // groups
    base = 2 * step * groups
    pad = turned.shape[0]
    slots = halo // packed.shape[0]
    near = state[:own, :]
    total = jnp.zeros((pad, own), F32)
    for k in range(groups):
        group = lax.rem(ids[0] + groups - k, groups)
        begin = [pl.multiple_of(2 * step * group + part * step, step) for part in (0, 1)]
        w_one = jnp.concatenate([w[pl.ds(at, step), :] for at in begin for w in weights], axis=0)
        out, slope[k] = activate(mm(near, w_one), True)
        if halo == own:
            both = jnp.concatenate([state[own:, :cols], landed[...]], axis=1)
            far = activate(mm(both, w_one), False)
            held = spread(a_ref[...], jnp.concatenate([out, far], axis=0))
        else:

            def one(r, held, w_one=w_one):
                rows = pl.ds(pl.multiple_of(r * own, own), own)
                srcs = pl.ds(pl.multiple_of(2 * (r + 1) * own, own), 2 * own)
                lower = pl.ds(pl.multiple_of((r + 1) * own, own), own)
                both = jnp.concatenate([state[lower, :cols], landed[rows, :]], axis=1)
                return held + spread(a_ref[:, srcs], activate(mm(both, w_one), False))

            held = lax.fori_loop(0, halo // own, one, spread(a_ref[:, : 2 * own], out))
        rounded = held.astype(BF16)
        if k == 0:
            mine, agg_mine = out, rounded
        total = total + mm_nt(weights[k][pl.ds(base, pad), :], out) + mm_nt(weights[k][pl.ds(base + pad, pad), :], rounded)
    class_id = lax.broadcasted_iota(jnp.int32, total.shape, 0)
    real = class_id < class_count
    top = jnp.max(jnp.where(real, total, -jnp.inf), axis=0, keepdims=True)
    shifted = total - top
    powers = jnp.where(real, jnp.exp(shifted), 0.0)
    sums = jnp.sum(powers, axis=0, keepdims=True)
    target = (class_id == labels[...]).astype(F32)
    turned[...] = ((powers / sums - target) * grad_scale).astype(BF16)
    row_loss = jnp.log(sums) - jnp.sum(shifted * target, axis=0, keepdims=True)
    own_grads = mm(turned[...], mine)
    row = lax.broadcasted_iota(jnp.int32, own_grads.shape, 0)
    own_grads = jnp.where(row == class_count, jnp.sum(row_loss, axis=1, keepdims=True), own_grads)
    second[0] = own_grads
    second[1] = mm(turned[...], agg_mine)
    per_chunk = own // slots
    for c in range(halo // own):
        back = mm(turned[...], a_ref[:, pl.ds(2 * (c + 1) * own, own)]).T.astype(BF16)
        for d in range(per_chunk):
            put_message(packed, c * per_chunk + d, back[d * slots : (d + 1) * slots])


def message_shape(slots, pad):
    compact = BLOCK < pad <= BLOCK + BLOCK // 2 and slots % 32 == 0
    return (slots + slots // 2, BLOCK) if compact else (slots, pad)


def put_message(packed, d, rows):
    slots, pad = rows.shape
    if packed.shape[1:] == (slots, pad):
        packed[d] = rows
        return
    half, tail = slots // 2, pad - BLOCK
    packed[d, :slots, :] = rows[:, :BLOCK]
    filler = jnp.zeros((half, BLOCK // 2 - tail), BF16)
    packed[d, slots:, :] = jnp.concatenate([rows[:half, BLOCK:], filler, rows[half:, BLOCK:], filler], axis=1)


def take_message(packed, d, landed):
    slots, pad = landed.shape[0] // packed.shape[0], landed.shape[1]
    if packed.shape[1:] == (slots, pad):
        landed[pl.ds(d * slots, slots), :] = packed[d]
        return
    half, tail = slots // 2, pad - BLOCK
    landed[pl.ds(d * slots, slots), :BLOCK] = packed[d, :slots, :]
    landed[pl.ds(d * slots, half), BLOCK:] = packed[d, slots:, :tail]
    landed[pl.ds(d * slots + half, half), BLOCK:] = packed[d, slots:, BLOCK // 2 : BLOCK // 2 + tail]


def backward_kernel(parts, groups, ids, turned, pick, a_ref, slope, features, state, landed, *refs):
    weights = refs[:groups]
    out, rows = refs[groups:]
    own = turned.shape[1]
    units = slope.shape[2]
    pad = turned.shape[0]
    step = features.shape[0]
    base = 2 * step * groups
    for d in range(landed.shape[0]):
        take_message(landed, d, rows)
    high, low = halves(mm(turned[...], a_ref[:, :own]) + mm_tn(rows[...], pick[...]))
    wide = jnp.concatenate([turned[...], high, low], axis=0).T
    cols = state.shape[1] // 2
    left = jnp.concatenate([features[...], state[:own, cols:].T[:step]], axis=0)
    for k in range(groups):
        group = lax.rem(ids[0] + groups - k, groups)
        w_neigh = weights[k][pl.ds(base + pad, pad), :]
        total = mm(wide, jnp.concatenate([weights[k][pl.ds(base, pad), :], w_neigh, w_neigh], axis=0))
        result = mm(left, (total * slope[k]).astype(BF16))
        if parts:
            for i in range(units // BLOCK):
                out[group * (units // BLOCK) + i] = result[:, i * BLOCK : (i + 1) * BLOCK]
        else:
            out[:, pl.ds(pl.multiple_of(group * units, units), units)] = result


def quarter(p, rows):
    height = rows // 4
    return slice(p // 2 * height, (p // 2 + 1) * height), slice(p % 2 * BLOCK, (p % 2 + 1) * BLOCK)


def join_kernel(side, grads, second, other, out, total):
    step = grads.shape[1]
    height = total.shape[0] // 4
    total[...] = second[side[0]] + other[side[0]]
    for p in range(grads.shape[0]):
        out[p, :step, :] = grads[p]
        out[p, step : step + height, :] = total[quarter(p, total.shape[0])]
        out[p, step + height :, :] = jnp.zeros((out.shape[1] - step - height, BLOCK), F32)


def sum_kernel(step, height, pieces, out):
    first = pieces[0, :step, :]
    second = [pieces[0, step : step + height, :], pieces[1, step : step + height, :]]
    for p in range(1, pieces.shape[0]):
        first = first + pieces[p, :step, :]
        if p > 1:
            second[p % 2] = second[p % 2] + pieces[p, step : step + height, :]
    for p in range(pieces.shape[0]):
        out[p, :step, :] = first
        out[p, step : step + height, :] = second[0]
        out[p, step + height :, :] = second[1]


def place_kernel(class_count, node_total, pieces, self1, neigh1, self2, neigh2, loss, both):
    step = self1.shape[0]
    units = self2.shape[1]
    height = both.shape[1] // 4
    for p in range(pieces.shape[0]):
        at = pl.ds(p * BLOCK, BLOCK)
        self1[:, at] = pieces[p, :step, :]
        neigh1[:, at] = pieces[p, step : 2 * step, :]
        rows, lanes = quarter(p, both.shape[1])
        both[0, rows, lanes] = pieces[p, 2 * step : 2 * step + height, :]
        both[1, rows, lanes] = pieces[p, 2 * step + height :, :]
    self2[...] = both[0, :class_count, :]
    neigh2[...] = both[1, :class_count, :]
    loss[...] = both[0, class_count : class_count + 1, 0:1] / node_total


def swap(value, count):
    blocks = value.reshape(count, -1, value.shape[-1])
    return lax.all_to_all(blocks, "node", 0, 0, tiled=True)


def gather_shifted(value, count):
    return [value] + [lax.ppermute(value, "feat", [(i, (i + k) % count) for i in range(count)]) for k in range(1, count)]


def shards(features, send_rows, send_count, tile_src, tile_val, labels, w_self1, w_neigh1, w_self2, w_neigh2):
    nodes, groups = lax.axis_size("node"), lax.axis_size("feat")
    own, step = features.shape
    slots = send_rows.shape[2]
    halo = nodes * slots
    total_src = own + halo
    cols = step * groups
    width = w_self1.shape[1]
    units, classes = w_self2.shape
    pad = -(-(classes + 1) // 16) * 16
    parts = nodes if nodes == 8 and units == 2 * BLOCK and width == nodes * BLOCK else 0
    node_total = own * nodes
    grad_scale = 1.0 / math.sqrt(node_total)
    ids = lax.axis_index("feat").astype(jnp.int32).reshape(1)
    side = (lax.axis_index("node") & 1).astype(jnp.int32).reshape(1)
    blocks = own // BLOCK
    packed_rows = 2 * step * groups + 2 * pad

    turned = features.T
    turned_all = gather_shifted(turned, groups)
    (a_mat,) = call(
        prepare_kernel,
        [((own, 2 * total_src), BF16)],
        (tile_src, tile_val),
        [(tile_val.shape, BF16), ((own, total_src), F32)],
        copies=blocks + 1,
        moved=tile_val.size * 4,
        grant=54 * 2**20 - 4 * own * total_src - 3 * 10**5,
    )
    a_mat, ids, side, *turned_all = lax.optimization_barrier((a_mat, ids, side, *turned_all))
    pick, full, packed, packed_weights = call(
        functools.partial(pack_kernel, groups),
        [((halo, own), BF16), ((own, cols), BF16), ((halo, cols), BF16), ((packed_rows, units), BF16)],
        (send_count, send_rows[0], w_self1, w_neigh1, w_self2.T, w_neigh2.T, *turned_all),
        [((cols, own), BF16)],
        flops=2 * halo * own * cols,
        moved=halo * own * 2,
    )
    weights = gather_shifted(packed_weights, groups)
    source = swap(packed, nodes).reshape(halo, cols)
    state, packed = call(
        first_kernel,
        [((total_src, 2 * cols), BF16), ((halo, cols), BF16)],
        (pick, a_mat, full, source),
        flops=4 * own * total_src * cols,
        moved=4 * own * total_src,
    )
    packed, ids, side, *weights = lax.optimization_barrier((packed, ids, side, *weights))
    landed = swap(packed, nodes).reshape(halo, cols)
    message = (nodes, *message_shape(slots, pad))
    turned_grads, slope, packed, second = call(
        functools.partial(forward_kernel, classes, grad_scale, groups),
        [((pad, own), BF16), ((groups, own, units), F32), (message, BF16), ((2, pad, units), F32)],
        (ids, a_mat, state, landed, labels.reshape(1, own), *weights),
        flops=8 * own * total_src * width,
        moved=16 * own * width,
    )
    if parts:
        other = lax.ppermute(second, "node", [(i, i ^ 1) for i in range(nodes)])
    landed = swap(packed, nodes)
    (grads,) = call(
        functools.partial(backward_kernel, parts, groups),
        [((parts, 2 * step, BLOCK) if parts else (2 * step, width), F32)],
        (ids, turned_grads, pick, a_mat, slope, turned, state, landed, *weights),
        [((halo, pad), BF16)],
    )
    if not parts:
        grads, second = lax.psum((grads, second), "node")
        loss = second[0, classes, 0] / node_total
        return (loss, grads[:step], grads[step:], second[0, :classes].T, second[1, :classes].T)
    height = pad // 4
    grads, other = lax.optimization_barrier((grads, other))
    (grads,) = call(
        join_kernel,
        [((nodes, -(-(2 * step + height) // 8) * 8, BLOCK), F32)],
        (side, grads, second, other),
        [((pad, units), F32)],
    )
    grads = swap(grads, nodes)
    (grads,) = call(functools.partial(sum_kernel, 2 * step, height), [((nodes, 2 * step + 2 * height, BLOCK), F32)], (grads,))
    grads = swap(grads, nodes)
    grad_self1, grad_neigh1, grad_self2, grad_neigh2, loss = call(
        functools.partial(place_kernel, classes, node_total),
        [((step, width), F32)] * 2 + [((classes, units), F32)] * 2 + [((1, 1), F32)],
        (grads,),
        [((2, pad, units), F32)],
    )
    return (loss.reshape(()), grad_self1, grad_neigh1, grad_self2.T, grad_neigh2.T)


def solution(mesh):
    in_specs = (
        P("node", "feat"),
        P("node", None, None),
        P("node", None),
        P("node", None),
        P("node", None, None, None),
        P("node"),
        P("feat", None),
        P("feat", None),
        P("feat", None),
        P("feat", None),
    )
    out_specs = (P(), P("feat", None), P("feat", None), P("feat", None), P("feat", None))
    return jax.shard_map(shards, mesh=mesh, in_specs=in_specs, out_specs=out_specs, check_vma=False)
```

```python
import functools
import math

import jax
import jax.numpy as jnp
from jax import lax
from jax.experimental import pallas as pl
from jax.experimental.pallas import tpu as pltpu
from jax.sharding import PartitionSpec as P

BLOCK = 128
F32 = jnp.float32
BF16 = jnp.bfloat16
VMEM = pl.BlockSpec(memory_space=pltpu.VMEM)
HBM = pl.BlockSpec(memory_space=pltpu.HBM)
SMEM = pl.BlockSpec(memory_space=pltpu.SMEM)


def mm(a, b):
    return lax.dot_general(a, b, (((1,), (0,)), ((), ())), preferred_element_type=F32)


def mm_tn(a, b):
    return lax.dot_general(a, b, (((0,), (0,)), ((), ())), preferred_element_type=F32)


def halves(value):
    high = value.astype(BF16)
    return high, (value - high.astype(F32)).astype(BF16)


def spread(a, rows):
    own = a.shape[0]
    parts = []
    for c in range(rows.shape[0] // own):
        part = rows[c * own : (c + 1) * own]
        parts += [part, part]
    return mm(a, jnp.concatenate(parts, axis=0))


def activate(v, with_slope):
    scale = math.sqrt(2.0 / math.pi)
    square = v * v
    t = jnp.tanh(v * (scale + (scale * 0.044715) * square))
    half = 0.5 * v
    out = (half + half * t).astype(BF16)
    if not with_slope:
        return out
    return out, (0.5 + 0.5 * t) + half * (1.0 - t * t) * (scale + (scale * 3 * 0.044715) * square)


def size_of(shape, dtype):
    rows = -(-shape[-2] // 16) * 16 if len(shape) > 1 else 1
    return math.prod(shape[:-2]) * rows * (-(-shape[-1] // 128) * 128) * jnp.dtype(dtype).itemsize


def call(body, outs, args, scratch=(), copies=0, flops=0, moved=0, grant=0):
    specs = [SMEM if arg.dtype == jnp.int32 and arg.size < 512 else VMEM for arg in args]
    if copies:
        specs = [HBM] * len(args)
    room = sum(size_of(shape, dtype) for shape, dtype in [*outs, *scratch])
    room += sum(size_of(arg.shape, arg.dtype) for arg, spec in zip(args, specs) if spec is VMEM)
    return pl.pallas_call(
        body,
        out_shape=[jax.ShapeDtypeStruct(shape, dtype) for shape, dtype in outs],
        in_specs=specs,
        out_specs=[VMEM] * len(outs),
        scratch_shapes=[pltpu.VMEM(shape, dtype) for shape, dtype in scratch]
        + ([pltpu.SemaphoreType.DMA((copies,)), pltpu.SMEM(args[0].shape, jnp.int32)] if copies else []),
        compiler_params=pltpu.CompilerParams(vmem_limit_bytes=grant or min(room + 8 * 2**20, 56 * 2**20)),
        cost_estimate=pl.CostEstimate(flops=flops, bytes_accessed=moved, transcendentals=0),
    )(*args)


def prepare_kernel(src_in, tile_val, a_ref, tiles, dense, sems, tile_src):
    blocks, per_block = tile_val.shape[0], tile_val.shape[1]
    own = blocks * BLOCK
    src_copy = pltpu.make_async_copy(src_in, tile_src, sems.at[blocks])
    src_copy.start()
    copies = [pltpu.make_async_copy(tile_val.at[b], tiles.at[b], sems.at[b]) for b in range(blocks)]
    for copy in copies:
        copy.start()
    dense[...] = jnp.zeros_like(dense)
    src_copy.wait()
    for b in range(blocks):
        rows = pl.ds(b * BLOCK, BLOCK)
        copies[b].wait()

        def add(k, _, b=b, rows=rows):
            at = pl.ds(pl.multiple_of(tile_src[b, k] * BLOCK, BLOCK), BLOCK)
            dense[rows, at] = dense[rows, at] + tiles[b, k].astype(F32)
            return 0

        lax.fori_loop(0, per_block, add, 0)
        for c in range(dense.shape[1] // own):
            high, low = halves(dense[rows, pl.ds(c * own, own)])
            a_ref[rows, pl.ds(2 * c * own, own)] = high
            a_ref[rows, pl.ds((2 * c + 1) * own, own)] = low


def pack_kernel(groups, count, send_rows, w_self1, w_neigh1, w_self2, w_neigh2, *refs):
    pieces, (pick, full, packed, weights), (turned,) = refs[:groups], refs[groups : groups + 4], refs[groups + 4 :]
    step, own = pieces[0].shape
    classes, units = w_self2.shape
    base = 2 * step * groups
    pad = (weights.shape[0] - base) // 2
    for j in range(groups):
        at = pl.ds(j * units, units)
        weights[pl.ds(2 * step * j, step), :] = w_self1[:, at]
        weights[pl.ds(2 * step * j + step, step), :] = w_neigh1[:, at]
    weights[pl.ds(base, 2 * pad), :] = jnp.zeros((2 * pad, units), BF16)
    weights[pl.ds(base, classes), :] = w_self2[...]
    weights[pl.ds(base + pad, classes), :] = w_neigh2[...]
    dests, slots = send_rows.shape
    columns = send_rows[...].astype(F32).T
    row_id = lax.broadcasted_iota(jnp.int32, (slots, own), 1).astype(F32)
    slot_id = lax.broadcasted_iota(jnp.int32, (slots, own), 0)
    for d in range(dests):
        hit = (columns[:, d : d + 1] == row_id) & (slot_id < count[0, d])
        pick[pl.ds(d * slots, slots), :] = jnp.where(hit, 1.0, 0.0).astype(BF16)
    for k, piece in enumerate(pieces):
        turned[pl.ds(k * step, step), :] = piece[...]
    full[...] = turned[...].T
    packed[...] = mm(pick[...], full[...]).astype(BF16)


def first_kernel(pick, a_ref, full, source, state, packed):
    own, cols = full.shape
    total = spread(a_ref[:, : 2 * own], full[...]) + spread(a_ref[:, 2 * own :], source[...])
    agg = total.astype(BF16)
    packed[...] = mm(pick[...], agg).astype(BF16)
    state[:own, :cols] = full[...]
    state[:own, cols:] = agg
    state[own:, :cols] = source[...]
    state[own:, cols:] = jnp.zeros_like(source)


def forward_kernel(
    class_count, grad_scale, groups, ids, a_ref, state, landed, labels, *refs
):
    weights = refs[:groups]
    turned, slope, packed, second = refs[groups:]
    halo, cols = landed.shape
    own = state.shape[0] - halo
    units = weights[0].shape[1]
    step = cols // groups
    base = 2 * step * groups
    pad = turned.shape[0]
    slots = halo // packed.shape[0]
    near = state[:own, :]
    total = jnp.zeros((own, pad), F32)
    for k in range(groups):
        group = lax.rem(ids[0] + groups - k, groups)
        begin = [pl.multiple_of(2 * step * group + part * step, step) for part in (0, 1)]
        w_one = jnp.concatenate([w[pl.ds(at, step), :] for at in begin for w in weights], axis=0)
        out, slope[k] = activate(mm(near, w_one), True)
        if halo == own:
            both = jnp.concatenate([state[own:, :cols], landed[...]], axis=1)
            far = activate(mm(both, w_one), False)
            held = spread(a_ref[...], jnp.concatenate([out, far], axis=0))
        else:

            def one(r, held, w_one=w_one):
                rows = pl.ds(pl.multiple_of(r * own, own), own)
                srcs = pl.ds(pl.multiple_of(2 * (r + 1) * own, own), 2 * own)
                lower = pl.ds(pl.multiple_of((r + 1) * own, own), own)
                both = jnp.concatenate([state[lower, :cols], landed[rows, :]], axis=1)
                return held + spread(a_ref[:, srcs], activate(mm(both, w_one), False))

            held = lax.fori_loop(0, halo // own, one, spread(a_ref[:, : 2 * own], out))
        rounded = held.astype(BF16)
        if k == 0:
            mine, agg_mine = out, rounded
        w_self, w_neigh = weights[k][pl.ds(base, pad), :].T, weights[k][pl.ds(base + pad, pad), :].T
        total = total + mm(jnp.concatenate([out, rounded], axis=1), jnp.concatenate([w_self, w_neigh], axis=0))
    total = total.T
    class_id = lax.broadcasted_iota(jnp.int32, total.shape, 0)
    real = class_id < class_count
    top = jnp.max(jnp.where(real, total, -jnp.inf), axis=0, keepdims=True)
    shifted = total - top
    powers = jnp.where(real, jnp.exp(shifted), 0.0)
    sums = jnp.sum(powers, axis=0, keepdims=True)
    target = (class_id == labels[...]).astype(F32)
    turned[...] = ((powers / sums - target) * grad_scale).astype(BF16)
    row_loss = jnp.log(sums) - jnp.sum(shifted * target, axis=0, keepdims=True)
    own_grads = mm(turned[...], mine)
    row = lax.broadcasted_iota(jnp.int32, own_grads.shape, 0)
    own_grads = jnp.where(row == class_count, jnp.sum(row_loss, axis=1, keepdims=True), own_grads)
    second[0] = own_grads
    second[1] = mm(turned[...], agg_mine)
    per_chunk = own // slots
    for c in range(halo // own):
        back = mm(turned[...], a_ref[:, pl.ds(2 * (c + 1) * own, own)]).T.astype(BF16)
        for d in range(per_chunk):
            put_message(packed, c * per_chunk + d, back[d * slots : (d + 1) * slots])


def message_shape(slots, pad):
    compact = BLOCK < pad <= BLOCK + BLOCK // 2 and slots % 32 == 0
    return (slots + slots // 2, BLOCK) if compact else (slots, pad)


def put_message(packed, d, rows):
    slots, pad = rows.shape
    if packed.shape[1:] == (slots, pad):
        packed[d] = rows
        return
    half, tail = slots // 2, pad - BLOCK
    packed[d, :slots, :] = rows[:, :BLOCK]
    filler = jnp.zeros((half, BLOCK // 2 - tail), BF16)
    packed[d, slots:, :] = jnp.concatenate([rows[:half, BLOCK:], filler, rows[half:, BLOCK:], filler], axis=1)


def take_message(packed, d, landed):
    slots, pad = landed.shape[0] // packed.shape[0], landed.shape[1]
    if packed.shape[1:] == (slots, pad):
        landed[pl.ds(d * slots, slots), :] = packed[d]
        return
    half, tail = slots // 2, pad - BLOCK
    landed[pl.ds(d * slots, slots), :BLOCK] = packed[d, :slots, :]
    landed[pl.ds(d * slots, half), BLOCK:] = packed[d, slots:, :tail]
    landed[pl.ds(d * slots + half, half), BLOCK:] = packed[d, slots:, BLOCK // 2 : BLOCK // 2 + tail]


def backward_kernel(parts, groups, ids, turned, pick, a_ref, slope, features, state, landed, *refs):
    weights = refs[:groups]
    out, rows = refs[groups:]
    own = turned.shape[1]
    units = slope.shape[2]
    pad = turned.shape[0]
    step = features.shape[0]
    base = 2 * step * groups
    for d in range(landed.shape[0]):
        take_message(landed, d, rows)
    high, low = halves(mm(turned[...], a_ref[:, :own]) + mm_tn(rows[...], pick[...]))
    wide = jnp.concatenate([turned[...], high, low], axis=0).T
    cols = state.shape[1] // 2
    left = jnp.concatenate([features[...], state[:own, cols:].T[:step]], axis=0)
    for k in range(groups):
        group = lax.rem(ids[0] + groups - k, groups)
        w_neigh = weights[k][pl.ds(base + pad, pad), :]
        total = mm(wide, jnp.concatenate([weights[k][pl.ds(base, pad), :], w_neigh, w_neigh], axis=0))
        result = mm(left, (total * slope[k]).astype(BF16))
        if parts:
            for i in range(units // BLOCK):
                out[group * (units // BLOCK) + i] = result[:, i * BLOCK : (i + 1) * BLOCK]
        else:
            out[:, pl.ds(pl.multiple_of(group * units, units), units)] = result


def quarter(p, rows):
    height = rows // 4
    return slice(p // 2 * height, (p // 2 + 1) * height), slice(p % 2 * BLOCK, (p % 2 + 1) * BLOCK)


def join_kernel(side, grads, second, other, out, total):
    step = grads.shape[1]
    height = total.shape[0] // 4
    total[...] = second[side[0]] + other[side[0]]
    for p in range(grads.shape[0]):
        out[p, :step, :] = grads[p]
        out[p, step : step + height, :] = total[quarter(p, total.shape[0])]
        out[p, step + height :, :] = jnp.zeros((out.shape[1] - step - height, BLOCK), F32)


def sum_kernel(step, height, pieces, out):
    first = pieces[0, :step, :]
    second = [pieces[0, step : step + height, :], pieces[1, step : step + height, :]]
    for p in range(1, pieces.shape[0]):
        first = first + pieces[p, :step, :]
        if p > 1:
            second[p % 2] = second[p % 2] + pieces[p, step : step + height, :]
    for p in range(pieces.shape[0]):
        out[p, :step, :] = first
        out[p, step : step + height, :] = second[0]
        out[p, step + height :, :] = second[1]


def place_kernel(class_count, node_total, pieces, self1, neigh1, self2, neigh2, loss, both):
    step = self1.shape[0]
    units = self2.shape[1]
    height = both.shape[1] // 4
    for p in range(pieces.shape[0]):
        at = pl.ds(p * BLOCK, BLOCK)
        self1[:, at] = pieces[p, :step, :]
        neigh1[:, at] = pieces[p, step : 2 * step, :]
        rows, lanes = quarter(p, both.shape[1])
        both[0, rows, lanes] = pieces[p, 2 * step : 2 * step + height, :]
        both[1, rows, lanes] = pieces[p, 2 * step + height :, :]
    self2[...] = both[0, :class_count, :]
    neigh2[...] = both[1, :class_count, :]
    loss[...] = both[0, class_count : class_count + 1, 0:1] / node_total


def swap(value, count):
    blocks = value.reshape(count, -1, value.shape[-1])
    return lax.all_to_all(blocks, "node", 0, 0, tiled=True)


def gather_shifted(value, count):
    return [value] + [lax.ppermute(value, "feat", [(i, (i + k) % count) for i in range(count)]) for k in range(1, count)]


def shards(features, send_rows, send_count, tile_src, tile_val, labels, w_self1, w_neigh1, w_self2, w_neigh2):
    nodes, groups = lax.axis_size("node"), lax.axis_size("feat")
    own, step = features.shape
    slots = send_rows.shape[2]
    halo = nodes * slots
    total_src = own + halo
    cols = step * groups
    width = w_self1.shape[1]
    units, classes = w_self2.shape
    pad = -(-(classes + 1) // 16) * 16
    parts = nodes if nodes == 8 and units == 2 * BLOCK and width == nodes * BLOCK else 0
    node_total = own * nodes
    grad_scale = 1.0 / math.sqrt(node_total)
    ids = lax.axis_index("feat").astype(jnp.int32).reshape(1)
    side = (lax.axis_index("node") & 1).astype(jnp.int32).reshape(1)
    blocks = own // BLOCK
    packed_rows = 2 * step * groups + 2 * pad

    turned = features.T
    turned_all = gather_shifted(turned, groups)
    (a_mat,) = call(
        prepare_kernel,
        [((own, 2 * total_src), BF16)],
        (tile_src, tile_val),
        [(tile_val.shape, BF16), ((own, total_src), F32)],
        copies=blocks + 1,
        moved=tile_val.size * 4,
        grant=54 * 2**20 - 4 * own * total_src - 3 * 10**5,
    )
    a_mat, ids, side, *turned_all = lax.optimization_barrier((a_mat, ids, side, *turned_all))
    pick, full, packed, packed_weights = call(
        functools.partial(pack_kernel, groups),
        [((halo, own), BF16), ((own, cols), BF16), ((halo, cols), BF16), ((packed_rows, units), BF16)],
        (send_count, send_rows[0], w_self1, w_neigh1, w_self2.T, w_neigh2.T, *turned_all),
        [((cols, own), BF16)],
        flops=2 * halo * own * cols,
        moved=halo * own * 2,
    )
    weights = gather_shifted(packed_weights, groups)
    source = swap(packed, nodes).reshape(halo, cols)
    state, packed = call(
        first_kernel,
        [((total_src, 2 * cols), BF16), ((halo, cols), BF16)],
        (pick, a_mat, full, source),
        flops=4 * own * total_src * cols,
        moved=4 * own * total_src,
    )
    packed, ids, side, *weights = lax.optimization_barrier((packed, ids, side, *weights))
    landed = swap(packed, nodes).reshape(halo, cols)
    message = (nodes, *message_shape(slots, pad))
    turned_grads, slope, packed, second = call(
        functools.partial(forward_kernel, classes, grad_scale, groups),
        [((pad, own), BF16), ((groups, own, units), F32), (message, BF16), ((2, pad, units), F32)],
        (ids, a_mat, state, landed, labels.reshape(1, own), *weights),
        flops=8 * own * total_src * width,
        moved=16 * own * width,
    )
    if parts:
        other = lax.ppermute(second, "node", [(i, i ^ 1) for i in range(nodes)])
    landed = swap(packed, nodes)
    (grads,) = call(
        functools.partial(backward_kernel, parts, groups),
        [((parts, 2 * step, BLOCK) if parts else (2 * step, width), F32)],
        (ids, turned_grads, pick, a_mat, slope, turned, state, landed, *weights),
        [((halo, pad), BF16)],
    )
    if not parts:
        grads, second = lax.psum((grads, second), "node")
        loss = second[0, classes, 0] / node_total
        return (loss, grads[:step], grads[step:], second[0, :classes].T, second[1, :classes].T)
    height = pad // 4
    grads, other = lax.optimization_barrier((grads, other))
    (grads,) = call(
        join_kernel,
        [((nodes, -(-(2 * step + height) // 8) * 8, BLOCK), F32)],
        (side, grads, second, other),
        [((pad, units), F32)],
    )
    grads = swap(grads, nodes)
    (grads,) = call(functools.partial(sum_kernel, 2 * step, height), [((nodes, 2 * step + 2 * height, BLOCK), F32)], (grads,))
    grads = swap(grads, nodes)
    grad_self1, grad_neigh1, grad_self2, grad_neigh2, loss = call(
        functools.partial(place_kernel, classes, node_total),
        [((step, width), F32)] * 2 + [((classes, units), F32)] * 2 + [((1, 1), F32)],
        (grads,),
        [((2, pad, units), F32)],
    )
    return (loss.reshape(()), grad_self1, grad_neigh1, grad_self2.T, grad_neigh2.T)


def solution(mesh):
    in_specs = (
        P("node", "feat"),
        P("node", None, None),
        P("node", None),
        P("node", None),
        P("node", None, None, None),
        P("node"),
        P("feat", None),
        P("feat", None),
        P("feat", None),
        P("feat", None),
    )
    out_specs = (P(), P("feat", None), P("feat", None), P("feat", None), P("feat", None))
    return jax.shard_map(shards, mesh=mesh, in_specs=in_specs, out_specs=out_specs, check_vma=False)
```

```python
import functools
import math

import jax
import jax.numpy as jnp
from jax import lax
from jax.experimental import pallas as pl
from jax.experimental.pallas import tpu as pltpu
from jax.sharding import PartitionSpec as P

BLOCK = 128
F32 = jnp.float32
BF16 = jnp.bfloat16
VMEM = pl.BlockSpec(memory_space=pltpu.VMEM)
HBM = pl.BlockSpec(memory_space=pltpu.HBM)
SMEM = pl.BlockSpec(memory_space=pltpu.SMEM)


def mm(a, b):
    return lax.dot_general(a, b, (((1,), (0,)), ((), ())), preferred_element_type=F32)


def mm_tn(a, b):
    return lax.dot_general(a, b, (((0,), (0,)), ((), ())), preferred_element_type=F32)


def halves(value):
    high = value.astype(BF16)
    return high, (value - high.astype(F32)).astype(BF16)


def spread(a, rows):
    both = mm(a, rows)
    half = both.shape[0] // 2
    return both[:half] + both[half:]


def activate(v, with_slope):
    scale = math.sqrt(2.0 / math.pi)
    square = v * v
    t = jnp.tanh(v * (scale + (scale * 0.044715) * square))
    half = 0.5 * v
    out = (half + half * t).astype(BF16)
    if not with_slope:
        return out
    return out, (0.5 + 0.5 * t) + half * (1.0 - t * t) * (scale + (scale * 3 * 0.044715) * square)


def size_of(shape, dtype):
    rows = -(-shape[-2] // 16) * 16 if len(shape) > 1 else 1
    return math.prod(shape[:-2]) * rows * (-(-shape[-1] // 128) * 128) * jnp.dtype(dtype).itemsize


def call(body, outs, args, scratch=(), copies=0, flops=0, moved=0, grant=0):
    specs = [SMEM if arg.dtype == jnp.int32 and arg.size < 512 else VMEM for arg in args]
    if copies:
        specs = [HBM] * len(args)
    room = sum(size_of(shape, dtype) for shape, dtype in [*outs, *scratch])
    room += sum(size_of(arg.shape, arg.dtype) for arg, spec in zip(args, specs) if spec is VMEM)
    return pl.pallas_call(
        body,
        out_shape=[jax.ShapeDtypeStruct(shape, dtype) for shape, dtype in outs],
        in_specs=specs,
        out_specs=[VMEM] * len(outs),
        scratch_shapes=[pltpu.VMEM(shape, dtype) for shape, dtype in scratch]
        + ([pltpu.SemaphoreType.DMA((copies,)), pltpu.SMEM(args[0].shape, jnp.int32)] if copies else []),
        compiler_params=pltpu.CompilerParams(vmem_limit_bytes=grant or min(room + 8 * 2**20, 56 * 2**20)),
        cost_estimate=pl.CostEstimate(flops=flops, bytes_accessed=moved, transcendentals=0),
    )(*args)


def prepare_kernel(src_in, tile_val, a_ref, tiles, dense, sems, tile_src):
    blocks, per_block = tile_val.shape[0], tile_val.shape[1]
    own = blocks * BLOCK
    src_copy = pltpu.make_async_copy(src_in, tile_src, sems.at[blocks])
    src_copy.start()
    copies = [pltpu.make_async_copy(tile_val.at[b], tiles.at[b], sems.at[b]) for b in range(blocks)]
    for copy in copies:
        copy.start()
    dense[...] = jnp.zeros_like(dense)
    src_copy.wait()
    for b in range(blocks):
        rows = pl.ds(b * BLOCK, BLOCK)
        copies[b].wait()

        def add(k, _, b=b, rows=rows):
            at = pl.ds(pl.multiple_of(tile_src[b, k] * BLOCK, BLOCK), BLOCK)
            dense[rows, at] = dense[rows, at] + tiles[b, k].astype(F32)
            return 0

        lax.fori_loop(0, per_block, add, 0)
        high, low = halves(dense[rows, :])
        a_ref[rows, :] = high
        a_ref[pl.ds(own + b * BLOCK, BLOCK), :] = low


def pack_kernel(groups, count, send_rows, w_self1, w_neigh1, w_self2, w_neigh2, *refs):
    pieces, (pick, full, packed, weights), (turned,) = refs[:groups], refs[groups : groups + 4], refs[groups + 4 :]
    step, own = pieces[0].shape
    classes, units = w_self2.shape
    base = 2 * step * groups
    pad = (weights.shape[0] - base) // 2
    for j in range(groups):
        at = pl.ds(j * units, units)
        weights[pl.ds(2 * step * j, step), :] = w_self1[:, at]
        weights[pl.ds(2 * step * j + step, step), :] = w_neigh1[:, at]
    weights[pl.ds(base, 2 * pad), :] = jnp.zeros((2 * pad, units), BF16)
    weights[pl.ds(base, classes), :] = w_self2[...]
    weights[pl.ds(base + pad, classes), :] = w_neigh2[...]
    dests, slots = send_rows.shape
    columns = send_rows[...].astype(F32).T
    row_id = lax.broadcasted_iota(jnp.int32, (slots, own), 1).astype(F32)
    slot_id = lax.broadcasted_iota(jnp.int32, (slots, own), 0)
    for d in range(dests):
        hit = (columns[:, d : d + 1] == row_id) & (slot_id < count[0, d])
        pick[pl.ds(d * slots, slots), :] = jnp.where(hit, 1.0, 0.0).astype(BF16)
    for k, piece in enumerate(pieces):
        turned[pl.ds(k * step, step), :] = piece[...]
    full[...] = turned[...].T
    packed[...] = mm(pick[...], full[...]).astype(BF16)


def first_kernel(pick, a_ref, full, source, state, packed):
    own, cols = full.shape
    total = spread(a_ref[:, :own], full[...]) + spread(a_ref[:, own:], source[...])
    agg = total.astype(BF16)
    packed[...] = mm(pick[...], agg).astype(BF16)
    state[:own, :cols] = full[...]
    state[:own, cols:] = agg
    state[own:, :cols] = source[...]
    state[own:, cols:] = jnp.zeros_like(source)


def forward_kernel(
    class_count, grad_scale, groups, ids, a_ref, state, landed, labels, *refs
):
    weights = refs[:groups]
    turned, slope, packed, second = refs[groups:]
    halo, cols = landed.shape
    own = state.shape[0] - halo
    units = weights[0].shape[1]
    step = cols // groups
    base = 2 * step * groups
    pad = turned.shape[0]
    slots = halo // packed.shape[0]
    near = state[:own, :]
    total = jnp.zeros((own, pad), F32)
    for k in range(groups):
        group = lax.rem(ids[0] + groups - k, groups)
        begin = [pl.multiple_of(2 * step * group + part * step, step) for part in (0, 1)]
        w_one = jnp.concatenate([w[pl.ds(at, step), :] for at in begin for w in weights], axis=0)
        out, slope[k] = activate(mm(near, w_one), True)
        if halo == own:
            both = jnp.concatenate([state[own:, :cols], landed[...]], axis=1)
            far = activate(mm(both, w_one), False)
            held = spread(a_ref[...], jnp.concatenate([out, far], axis=0))
        else:

            def one(r, held, w_one=w_one):
                rows = pl.ds(pl.multiple_of(r * own, own), own)
                srcs = pl.ds(pl.multiple_of((r + 1) * own, own), own)
                lower = pl.ds(pl.multiple_of((r + 1) * own, own), own)
                both = jnp.concatenate([state[lower, :cols], landed[rows, :]], axis=1)
                return held + spread(a_ref[:, srcs], activate(mm(both, w_one), False))

            held = lax.fori_loop(0, halo // own, one, spread(a_ref[:, :own], out))
        rounded = held.astype(BF16)
        if k == 0:
            mine, agg_mine = out, rounded
        w_self, w_neigh = weights[k][pl.ds(base, pad), :].T, weights[k][pl.ds(base + pad, pad), :].T
        total = total + mm(jnp.concatenate([out, rounded], axis=1), jnp.concatenate([w_self, w_neigh], axis=0))
    total = total.T
    class_id = lax.broadcasted_iota(jnp.int32, total.shape, 0)
    real = class_id < class_count
    top = jnp.max(jnp.where(real, total, -jnp.inf), axis=0, keepdims=True)
    shifted = total - top
    powers = jnp.where(real, jnp.exp(shifted), 0.0)
    sums = jnp.sum(powers, axis=0, keepdims=True)
    target = (class_id == labels[...]).astype(F32)
    turned[...] = ((powers / sums - target) * grad_scale).astype(BF16)
    row_loss = jnp.log(sums) - jnp.sum(shifted * target, axis=0, keepdims=True)
    own_grads = mm(turned[...], mine)
    row = lax.broadcasted_iota(jnp.int32, own_grads.shape, 0)
    own_grads = jnp.where(row == class_count, jnp.sum(row_loss, axis=1, keepdims=True), own_grads)
    second[0] = own_grads
    second[1] = mm(turned[...], agg_mine)
    per_chunk = own // slots
    for c in range(halo // own):
        back = mm(turned[...], a_ref[:own, pl.ds((c + 1) * own, own)]).T.astype(BF16)
        for d in range(per_chunk):
            put_message(packed, c * per_chunk + d, back[d * slots : (d + 1) * slots])


def message_shape(slots, pad):
    compact = BLOCK < pad <= BLOCK + BLOCK // 2 and slots % 32 == 0
    return (slots + slots // 2, BLOCK) if compact else (slots, pad)


def put_message(packed, d, rows):
    slots, pad = rows.shape
    if packed.shape[1:] == (slots, pad):
        packed[d] = rows
        return
    half, tail = slots // 2, pad - BLOCK
    packed[d, :slots, :] = rows[:, :BLOCK]
    filler = jnp.zeros((half, BLOCK // 2 - tail), BF16)
    packed[d, slots:, :] = jnp.concatenate([rows[:half, BLOCK:], filler, rows[half:, BLOCK:], filler], axis=1)


def take_message(packed, d, landed):
    slots, pad = landed.shape[0] // packed.shape[0], landed.shape[1]
    if packed.shape[1:] == (slots, pad):
        landed[pl.ds(d * slots, slots), :] = packed[d]
        return
    half, tail = slots // 2, pad - BLOCK
    landed[pl.ds(d * slots, slots), :BLOCK] = packed[d, :slots, :]
    landed[pl.ds(d * slots, half), BLOCK:] = packed[d, slots:, :tail]
    landed[pl.ds(d * slots + half, half), BLOCK:] = packed[d, slots:, BLOCK // 2 : BLOCK // 2 + tail]


def backward_kernel(parts, groups, ids, turned, pick, a_ref, slope, features, state, landed, *refs):
    weights = refs[:groups]
    out, rows = refs[groups:]
    own = turned.shape[1]
    units = slope.shape[2]
    pad = turned.shape[0]
    step = features.shape[0]
    base = 2 * step * groups
    for d in range(landed.shape[0]):
        take_message(landed, d, rows)
    high, low = halves(mm(turned[...], a_ref[:own, :own]) + mm_tn(rows[...], pick[...]))
    wide = jnp.concatenate([turned[...], high, low], axis=0).T
    cols = state.shape[1] // 2
    left = jnp.concatenate([features[...], state[:own, cols:].T[:step]], axis=0)
    for k in range(groups):
        group = lax.rem(ids[0] + groups - k, groups)
        w_neigh = weights[k][pl.ds(base + pad, pad), :]
        total = mm(wide, jnp.concatenate([weights[k][pl.ds(base, pad), :], w_neigh, w_neigh], axis=0))
        result = mm(left, (total * slope[k]).astype(BF16))
        if parts:
            for i in range(units // BLOCK):
                out[group * (units // BLOCK) + i] = result[:, i * BLOCK : (i + 1) * BLOCK]
        else:
            out[:, pl.ds(pl.multiple_of(group * units, units), units)] = result


def quarter(p, rows):
    height = rows // 4
    return slice(p // 2 * height, (p // 2 + 1) * height), slice(p % 2 * BLOCK, (p % 2 + 1) * BLOCK)


def join_kernel(side, grads, second, other, out, total):
    step = grads.shape[1]
    height = total.shape[0] // 4
    total[...] = second[side[0]] + other[side[0]]
    for p in range(grads.shape[0]):
        out[p, :step, :] = grads[p]
        out[p, step : step + height, :] = total[quarter(p, total.shape[0])]
        out[p, step + height :, :] = jnp.zeros((out.shape[1] - step - height, BLOCK), F32)


def sum_kernel(step, height, pieces, out):
    first = pieces[0, :step, :]
    second = [pieces[0, step : step + height, :], pieces[1, step : step + height, :]]
    for p in range(1, pieces.shape[0]):
        first = first + pieces[p, :step, :]
        if p > 1:
            second[p % 2] = second[p % 2] + pieces[p, step : step + height, :]
    for p in range(pieces.shape[0]):
        out[p, :step, :] = first
        out[p, step : step + height, :] = second[0]
        out[p, step + height :, :] = second[1]


def place_kernel(class_count, node_total, pieces, self1, neigh1, self2, neigh2, loss, both):
    step = self1.shape[0]
    units = self2.shape[1]
    height = both.shape[1] // 4
    for p in range(pieces.shape[0]):
        at = pl.ds(p * BLOCK, BLOCK)
        self1[:, at] = pieces[p, :step, :]
        neigh1[:, at] = pieces[p, step : 2 * step, :]
        rows, lanes = quarter(p, both.shape[1])
        both[0, rows, lanes] = pieces[p, 2 * step : 2 * step + height, :]
        both[1, rows, lanes] = pieces[p, 2 * step + height :, :]
    self2[...] = both[0, :class_count, :]
    neigh2[...] = both[1, :class_count, :]
    loss[...] = both[0, class_count : class_count + 1, 0:1] / node_total


def swap(value, count):
    blocks = value.reshape(count, -1, value.shape[-1])
    return lax.all_to_all(blocks, "node", 0, 0, tiled=True)


def gather_shifted(value, count):
    return [value] + [lax.ppermute(value, "feat", [(i, (i + k) % count) for i in range(count)]) for k in range(1, count)]


def shards(features, send_rows, send_count, tile_src, tile_val, labels, w_self1, w_neigh1, w_self2, w_neigh2):
    nodes, groups = lax.axis_size("node"), lax.axis_size("feat")
    own, step = features.shape
    slots = send_rows.shape[2]
    halo = nodes * slots
    total_src = own + halo
    cols = step * groups
    width = w_self1.shape[1]
    units, classes = w_self2.shape
    pad = -(-(classes + 1) // 16) * 16
    parts = nodes if nodes == 8 and units == 2 * BLOCK and width == nodes * BLOCK else 0
    node_total = own * nodes
    grad_scale = 1.0 / math.sqrt(node_total)
    ids = lax.axis_index("feat").astype(jnp.int32).reshape(1)
    side = (lax.axis_index("node") & 1).astype(jnp.int32).reshape(1)
    blocks = own // BLOCK
    packed_rows = 2 * step * groups + 2 * pad

    turned = features.T
    turned_all = gather_shifted(turned, groups)
    (a_mat,) = call(
        prepare_kernel,
        [((2 * own, total_src), BF16)],
        (tile_src, tile_val),
        [(tile_val.shape, BF16), ((own, total_src), F32)],
        copies=blocks + 1,
        moved=tile_val.size * 4,
        grant=54 * 2**20 - 4 * own * total_src - 3 * 10**5,
    )
    a_mat, ids, side, *turned_all = lax.optimization_barrier((a_mat, ids, side, *turned_all))
    pick, full, packed, packed_weights = call(
        functools.partial(pack_kernel, groups),
        [((halo, own), BF16), ((own, cols), BF16), ((halo, cols), BF16), ((packed_rows, units), BF16)],
        (send_count, send_rows[0], w_self1, w_neigh1, w_self2.T, w_neigh2.T, *turned_all),
        [((cols, own), BF16)],
        flops=2 * halo * own * cols,
        moved=halo * own * 2,
    )
    weights = gather_shifted(packed_weights, groups)
    source = swap(packed, nodes).reshape(halo, cols)
    state, packed = call(
        first_kernel,
        [((total_src, 2 * cols), BF16), ((halo, cols), BF16)],
        (pick, a_mat, full, source),
        flops=4 * own * total_src * cols,
        moved=4 * own * total_src,
    )
    packed, ids, side, *weights = lax.optimization_barrier((packed, ids, side, *weights))
    landed = swap(packed, nodes).reshape(halo, cols)
    message = (nodes, *message_shape(slots, pad))
    turned_grads, slope, packed, second = call(
        functools.partial(forward_kernel, classes, grad_scale, groups),
        [((pad, own), BF16), ((groups, own, units), F32), (message, BF16), ((2, pad, units), F32)],
        (ids, a_mat, state, landed, labels.reshape(1, own), *weights),
        flops=8 * own * total_src * width,
        moved=16 * own * width,
    )
    if parts:
        other = lax.ppermute(second, "node", [(i, i ^ 1) for i in range(nodes)])
    landed = swap(packed, nodes)
    (grads,) = call(
        functools.partial(backward_kernel, parts, groups),
        [((parts, 2 * step, BLOCK) if parts else (2 * step, width), F32)],
        (ids, turned_grads, pick, a_mat, slope, turned, state, landed, *weights),
        [((halo, pad), BF16)],
    )
    if not parts:
        grads, second = lax.psum((grads, second), "node")
        loss = second[0, classes, 0] / node_total
        return (loss, grads[:step], grads[step:], second[0, :classes].T, second[1, :classes].T)
    height = pad // 4
    grads, other = lax.optimization_barrier((grads, other))
    (grads,) = call(
        join_kernel,
        [((nodes, -(-(2 * step + height) // 8) * 8, BLOCK), F32)],
        (side, grads, second, other),
        [((pad, units), F32)],
    )
    grads = swap(grads, nodes)
    (grads,) = call(functools.partial(sum_kernel, 2 * step, height), [((nodes, 2 * step + 2 * height, BLOCK), F32)], (grads,))
    grads = swap(grads, nodes)
    grad_self1, grad_neigh1, grad_self2, grad_neigh2, loss = call(
        functools.partial(place_kernel, classes, node_total),
        [((step, width), F32)] * 2 + [((classes, units), F32)] * 2 + [((1, 1), F32)],
        (grads,),
        [((2, pad, units), F32)],
    )
    return (loss.reshape(()), grad_self1, grad_neigh1, grad_self2.T, grad_neigh2.T)


def solution(mesh):
    in_specs = (
        P("node", "feat"),
        P("node", None, None),
        P("node", None),
        P("node", None),
        P("node", None, None, None),
        P("node"),
        P("feat", None),
        P("feat", None),
        P("feat", None),
        P("feat", None),
    )
    out_specs = (P(), P("feat", None), P("feat", None), P("feat", None), P("feat", None))
    return jax.shard_map(shards, mesh=mesh, in_specs=in_specs, out_specs=out_specs, check_vma=False)
```

```python
import functools
import math

import jax
import jax.numpy as jnp
from jax import lax
from jax.experimental import pallas as pl
from jax.experimental.pallas import tpu as pltpu
from jax.sharding import PartitionSpec as P

BLOCK = 128
F32 = jnp.float32
BF16 = jnp.bfloat16
VMEM = pl.BlockSpec(memory_space=pltpu.VMEM)
HBM = pl.BlockSpec(memory_space=pltpu.HBM)
SMEM = pl.BlockSpec(memory_space=pltpu.SMEM)


def mm(a, b):
    return lax.dot_general(a, b, (((1,), (0,)), ((), ())), preferred_element_type=F32)


def mm_nt(a, b):
    return lax.dot_general(a, b, (((1,), (1,)), ((), ())), preferred_element_type=F32)


def mm_tn(a, b):
    return lax.dot_general(a, b, (((0,), (0,)), ((), ())), preferred_element_type=F32)


def halves(value):
    high = value.astype(BF16)
    return high, (value - high.astype(F32)).astype(BF16)


def spread(a, rows):
    own = a.shape[0]
    parts = []
    for c in range(rows.shape[0] // own):
        part = rows[c * own : (c + 1) * own]
        parts += [part, part]
    return mm(a, jnp.concatenate(parts, axis=0))


def activate(v, with_slope):
    scale = math.sqrt(2.0 / math.pi)
    square = v * v
    t = jnp.tanh(v * (scale + (scale * 0.044715) * square))
    half = 0.5 * v
    out = (half + half * t).astype(BF16)
    if not with_slope:
        return out
    return out, (0.5 + 0.5 * t) + half * (1.0 - t * t) * (scale + (scale * 3 * 0.044715) * square)


def size_of(shape, dtype):
    rows = -(-shape[-2] // 16) * 16 if len(shape) > 1 else 1
    return math.prod(shape[:-2]) * rows * (-(-shape[-1] // 128) * 128) * jnp.dtype(dtype).itemsize


def call(body, outs, args, scratch=(), copies=0, flops=0, moved=0, grant=0):
    specs = [SMEM if arg.dtype == jnp.int32 and arg.size < 512 else VMEM for arg in args]
    if copies:
        specs = [HBM] * len(args)
    room = sum(size_of(shape, dtype) for shape, dtype in [*outs, *scratch])
    room += sum(size_of(arg.shape, arg.dtype) for arg, spec in zip(args, specs) if spec is VMEM)
    return pl.pallas_call(
        body,
        out_shape=[jax.ShapeDtypeStruct(shape, dtype) for shape, dtype in outs],
        in_specs=specs,
        out_specs=[VMEM] * len(outs),
        scratch_shapes=[pltpu.VMEM(shape, dtype) for shape, dtype in scratch]
        + ([pltpu.SemaphoreType.DMA((copies,)), pltpu.SMEM(args[0].shape, jnp.int32)] if copies else []),
        compiler_params=pltpu.CompilerParams(vmem_limit_bytes=grant or min(room + 8 * 2**20, 56 * 2**20)),
        cost_estimate=pl.CostEstimate(flops=flops, bytes_accessed=moved, transcendentals=0),
    )(*args)


def prepare_kernel(src_in, tile_val, a_ref, tiles, dense, sems, tile_src):
    blocks, per_block = tile_val.shape[0], tile_val.shape[1]
    own = blocks * BLOCK
    src_copy = pltpu.make_async_copy(src_in, tile_src, sems.at[blocks])
    src_copy.start()
    copies = [pltpu.make_async_copy(tile_val.at[b], tiles.at[b], sems.at[b]) for b in range(blocks)]
    for copy in copies:
        copy.start()
    dense[...] = jnp.zeros_like(dense)
    src_copy.wait()
    for b in range(blocks):
        rows = pl.ds(b * BLOCK, BLOCK)
        copies[b].wait()

        def add(k, _, b=b, rows=rows):
            at = pl.ds(pl.multiple_of(tile_src[b, k] * BLOCK, BLOCK), BLOCK)
            dense[rows, at] = dense[rows, at] + tiles[b, k].astype(F32)
            return 0

        lax.fori_loop(0, per_block, add, 0)
        for c in range(dense.shape[1] // own):
            high, low = halves(dense[rows, pl.ds(c * own, own)])
            a_ref[rows, pl.ds(2 * c * own, own)] = high
            a_ref[rows, pl.ds((2 * c + 1) * own, own)] = low


def pack_kernel(groups, count, send_rows, w_self1, w_neigh1, w_self2, w_neigh2, *refs):
    pieces, (pick, full, packed, weights), (turned,) = refs[:groups], refs[groups : groups + 4], refs[groups + 4 :]
    step, own = pieces[0].shape
    classes, units = w_self2.shape
    base = 2 * step * groups
    pad = (weights.shape[0] - base) // 2
    for j in range(groups):
        at = pl.ds(j * units, units)
        weights[pl.ds(2 * step * j, step), :] = w_self1[:, at]
        weights[pl.ds(2 * step * j + step, step), :] = w_neigh1[:, at]
    weights[pl.ds(base, 2 * pad), :] = jnp.zeros((2 * pad, units), BF16)
    weights[pl.ds(base, classes), :] = w_self2[...]
    weights[pl.ds(base + pad, classes), :] = w_neigh2[...]
    dests, slots = send_rows.shape
    columns = send_rows[...].astype(F32).T
    row_id = lax.broadcasted_iota(jnp.int32, (slots, own), 1).astype(F32)
    slot_id = lax.broadcasted_iota(jnp.int32, (slots, own), 0)
    for d in range(dests):
        hit = (columns[:, d : d + 1] == row_id) & (slot_id < count[0, d])
        pick[pl.ds(d * slots, slots), :] = jnp.where(hit, 1.0, 0.0).astype(BF16)
    for k, piece in enumerate(pieces):
        turned[pl.ds(k * step, step), :] = piece[...]
    full[...] = turned[...].T
    packed[...] = mm(pick[...], full[...]).astype(BF16)


def first_kernel(pick, a_ref, full, source, state, packed):
    own, cols = full.shape
    total = spread(a_ref[:, : 2 * own], full[...]) + spread(a_ref[:, 2 * own :], source[...])
    agg = total.astype(BF16)
    packed[...] = mm(pick[...], agg).astype(BF16)
    state[:own, :cols] = full[...]
    state[:own, cols:] = agg
    state[own:, :cols] = source[...]
    state[own:, cols:] = jnp.zeros_like(source)


def forward_kernel(
    class_count, grad_scale, groups, ids, a_ref, state, landed, labels, *refs
):
    weights = refs[:groups]
    turned, slope, packed, second = refs[groups:]
    halo, cols = landed.shape
    own = state.shape[0] - halo
    units = weights[0].shape[1]
    step = cols // groups
    base = 2 * step * groups
    pad = turned.shape[0]
    slots = halo // packed.shape[0]
    near = state[:own, :]
    total = jnp.zeros((own, pad), F32)
    for k in range(groups):
        group = lax.rem(ids[0] + groups - k, groups)
        begin = [pl.multiple_of(2 * step * group + part * step, step) for part in (0, 1)]
        w_one = jnp.concatenate([w[pl.ds(at, step), :] for at in begin for w in weights], axis=0)
        out, slope[k] = activate(mm(near, w_one), True)
        if halo == own:
            both = jnp.concatenate([state[own:, :cols], landed[...]], axis=1)
            far = activate(mm(both, w_one), False)
            held = spread(a_ref[...], jnp.concatenate([out, far], axis=0))
        else:

            def one(r, held, w_one=w_one):
                rows = pl.ds(pl.multiple_of(r * own, own), own)
                srcs = pl.ds(pl.multiple_of(2 * (r + 1) * own, own), 2 * own)
                lower = pl.ds(pl.multiple_of((r + 1) * own, own), own)
                both = jnp.concatenate([state[lower, :cols], landed[rows, :]], axis=1)
                return held + spread(a_ref[:, srcs], activate(mm(both, w_one), False))

            held = lax.fori_loop(0, halo // own, one, spread(a_ref[:, : 2 * own], out))
        rounded = held.astype(BF16)
        if k == 0:
            mine, agg_mine = out, rounded
        w_pair = jnp.concatenate([weights[k][pl.ds(base, pad), :], weights[k][pl.ds(base + pad, pad), :]], axis=1)
        total = total + mm_nt(jnp.concatenate([out, rounded], axis=1), w_pair)
    total = total.T
    class_id = lax.broadcasted_iota(jnp.int32, total.shape, 0)
    real = class_id < class_count
    top = jnp.max(jnp.where(real, total, -jnp.inf), axis=0, keepdims=True)
    shifted = total - top
    powers = jnp.where(real, jnp.exp(shifted), 0.0)
    sums = jnp.sum(powers, axis=0, keepdims=True)
    target = (class_id == labels[...]).astype(F32)
    turned[...] = ((powers / sums - target) * grad_scale).astype(BF16)
    row_loss = jnp.log(sums) - jnp.sum(shifted * target, axis=0, keepdims=True)
    own_grads = mm(turned[...], mine)
    row = lax.broadcasted_iota(jnp.int32, own_grads.shape, 0)
    own_grads = jnp.where(row == class_count, jnp.sum(row_loss, axis=1, keepdims=True), own_grads)
    second[0] = own_grads
    second[1] = mm(turned[...], agg_mine)
    per_chunk = own // slots
    for c in range(halo // own):
        back = mm(turned[...], a_ref[:, pl.ds(2 * (c + 1) * own, own)]).astype(BF16).T
        for d in range(per_chunk):
            put_message(packed, c * per_chunk + d, back[d * slots : (d + 1) * slots])


def message_shape(slots, pad):
    compact = BLOCK < pad <= BLOCK + BLOCK // 2 and slots % 32 == 0
    return (slots + slots // 2, BLOCK) if compact else (slots, pad)


def put_message(packed, d, rows):
    slots, pad = rows.shape
    if packed.shape[1:] == (slots, pad):
        packed[d] = rows
        return
    half, tail = slots // 2, pad - BLOCK
    packed[d, :slots, :] = rows[:, :BLOCK]
    filler = jnp.zeros((half, BLOCK // 2 - tail), BF16)
    packed[d, slots:, :] = jnp.concatenate([rows[:half, BLOCK:], filler, rows[half:, BLOCK:], filler], axis=1)


def take_message(packed, d, landed):
    slots, pad = landed.shape[0] // packed.shape[0], landed.shape[1]
    if packed.shape[1:] == (slots, pad):
        landed[pl.ds(d * slots, slots), :] = packed[d]
        return
    half, tail = slots // 2, pad - BLOCK
    landed[pl.ds(d * slots, slots), :BLOCK] = packed[d, :slots, :]
    landed[pl.ds(d * slots, half), BLOCK:] = packed[d, slots:, :tail]
    landed[pl.ds(d * slots + half, half), BLOCK:] = packed[d, slots:, BLOCK // 2 : BLOCK // 2 + tail]


def backward_kernel(parts, groups, ids, turned, pick, a_ref, slope, features, state, landed, *refs):
    weights = refs[:groups]
    out, rows = refs[groups:]
    own = turned.shape[1]
    units = slope.shape[2]
    pad = turned.shape[0]
    step = features.shape[0]
    base = 2 * step * groups
    for d in range(landed.shape[0]):
        take_message(landed, d, rows)
    high, low = halves(mm(turned[...], a_ref[:, :own]) + mm_tn(rows[...], pick[...]))
    wide = jnp.concatenate([turned[...], high, low], axis=0).T
    cols = state.shape[1] // 2
    left = jnp.concatenate([features[...], state[:own, cols:].T[:step]], axis=0)
    for k in range(groups):
        group = lax.rem(ids[0] + groups - k, groups)
        w_neigh = weights[k][pl.ds(base + pad, pad), :]
        total = mm(wide, jnp.concatenate([weights[k][pl.ds(base, pad), :], w_neigh, w_neigh], axis=0))
        result = mm(left, (total * slope[k]).astype(BF16))
        if parts:
            for i in range(units // BLOCK):
                out[group * (units // BLOCK) + i] = result[:, i * BLOCK : (i + 1) * BLOCK]
        else:
            out[:, pl.ds(pl.multiple_of(group * units, units), units)] = result


def quarter(p, rows):
    height = rows // 4
    return slice(p // 2 * height, (p // 2 + 1) * height), slice(p % 2 * BLOCK, (p % 2 + 1) * BLOCK)


def join_kernel(side, grads, second, other, out, total):
    step = grads.shape[1]
    height = total.shape[0] // 4
    total[...] = second[side[0]] + other[side[0]]
    for p in range(grads.shape[0]):
        out[p, :step, :] = grads[p]
        out[p, step : step + height, :] = total[quarter(p, total.shape[0])]
        out[p, step + height :, :] = jnp.zeros((out.shape[1] - step - height, BLOCK), F32)


def sum_kernel(step, height, pieces, out):
    first = pieces[0, :step, :]
    second = [pieces[0, step : step + height, :], pieces[1, step : step + height, :]]
    for p in range(1, pieces.shape[0]):
        first = first + pieces[p, :step, :]
        if p > 1:
            second[p % 2] = second[p % 2] + pieces[p, step : step + height, :]
    for p in range(pieces.shape[0]):
        out[p, :step, :] = first
        out[p, step : step + height, :] = second[0]
        out[p, step + height :, :] = second[1]


def place_kernel(class_count, node_total, pieces, self1, neigh1, self2, neigh2, loss, both):
    step = self1.shape[0]
    units = self2.shape[1]
    height = both.shape[1] // 4
    for p in range(pieces.shape[0]):
        at = pl.ds(p * BLOCK, BLOCK)
        self1[:, at] = pieces[p, :step, :]
        neigh1[:, at] = pieces[p, step : 2 * step, :]
        rows, lanes = quarter(p, both.shape[1])
        both[0, rows, lanes] = pieces[p, 2 * step : 2 * step + height, :]
        both[1, rows, lanes] = pieces[p, 2 * step + height :, :]
    self2[...] = both[0, :class_count, :]
    neigh2[...] = both[1, :class_count, :]
    loss[...] = both[0, class_count : class_count + 1, 0:1] / node_total


def swap(value, count):
    blocks = value.reshape(count, -1, value.shape[-1])
    return lax.all_to_all(blocks, "node", 0, 0, tiled=True)


def gather_shifted(value, count):
    return [value] + [lax.ppermute(value, "feat", [(i, (i + k) % count) for i in range(count)]) for k in range(1, count)]


def shards(features, send_rows, send_count, tile_src, tile_val, labels, w_self1, w_neigh1, w_self2, w_neigh2):
    nodes, groups = lax.axis_size("node"), lax.axis_size("feat")
    own, step = features.shape
    slots = send_rows.shape[2]
    halo = nodes * slots
    total_src = own + halo
    cols = step * groups
    width = w_self1.shape[1]
    units, classes = w_self2.shape
    pad = -(-(classes + 1) // 16) * 16
    parts = nodes if nodes == 8 and units == 2 * BLOCK and width == nodes * BLOCK else 0
    node_total = own * nodes
    grad_scale = 1.0 / math.sqrt(node_total)
    ids = lax.axis_index("feat").astype(jnp.int32).reshape(1)
    side = (lax.axis_index("node") & 1).astype(jnp.int32).reshape(1)
    blocks = own // BLOCK
    packed_rows = 2 * step * groups + 2 * pad

    turned = features.T
    turned_all = gather_shifted(turned, groups)
    (a_mat,) = call(
        prepare_kernel,
        [((own, 2 * total_src), BF16)],
        (tile_src, tile_val),
        [(tile_val.shape, BF16), ((own, total_src), F32)],
        copies=blocks + 1,
        moved=tile_val.size * 4,
        grant=54 * 2**20 - 4 * own * total_src - 3 * 10**5,
    )
    a_mat, ids, side, *turned_all = lax.optimization_barrier((a_mat, ids, side, *turned_all))
    pick, full, packed, packed_weights = call(
        functools.partial(pack_kernel, groups),
        [((halo, own), BF16), ((own, cols), BF16), ((halo, cols), BF16), ((packed_rows, units), BF16)],
        (send_count, send_rows[0], w_self1, w_neigh1, w_self2.T, w_neigh2.T, *turned_all),
        [((cols, own), BF16)],
        flops=2 * halo * own * cols,
        moved=halo * own * 2,
    )
    weights = gather_shifted(packed_weights, groups)
    source = swap(packed, nodes).reshape(halo, cols)
    state, packed = call(
        first_kernel,
        [((total_src, 2 * cols), BF16), ((halo, cols), BF16)],
        (pick, a_mat, full, source),
        flops=4 * own * total_src * cols,
        moved=4 * own * total_src,
    )
    packed, ids, side, *weights = lax.optimization_barrier((packed, ids, side, *weights))
    landed = swap(packed, nodes).reshape(halo, cols)
    message = (nodes, *message_shape(slots, pad))
    turned_grads, slope, packed, second = call(
        functools.partial(forward_kernel, classes, grad_scale, groups),
        [((pad, own), BF16), ((groups, own, units), F32), (message, BF16), ((2, pad, units), F32)],
        (ids, a_mat, state, landed, labels.reshape(1, own), *weights),
        flops=8 * own * total_src * width,
        moved=16 * own * width,
    )
    if parts:
        other = lax.ppermute(second, "node", [(i, i ^ 1) for i in range(nodes)])
    landed = swap(packed, nodes)
    (grads,) = call(
        functools.partial(backward_kernel, parts, groups),
        [((parts, 2 * step, BLOCK) if parts else (2 * step, width), F32)],
        (ids, turned_grads, pick, a_mat, slope, turned, state, landed, *weights),
        [((halo, pad), BF16)],
    )
    if not parts:
        grads, second = lax.psum((grads, second), "node")
        loss = second[0, classes, 0] / node_total
        return (loss, grads[:step], grads[step:], second[0, :classes].T, second[1, :classes].T)
    height = pad // 4
    grads, other = lax.optimization_barrier((grads, other))
    (grads,) = call(
        join_kernel,
        [((nodes, -(-(2 * step + height) // 8) * 8, BLOCK), F32)],
        (side, grads, second, other),
        [((pad, units), F32)],
    )
    grads = swap(grads, nodes)
    (grads,) = call(functools.partial(sum_kernel, 2 * step, height), [((nodes, 2 * step + 2 * height, BLOCK), F32)], (grads,))
    grads = swap(grads, nodes)
    grad_self1, grad_neigh1, grad_self2, grad_neigh2, loss = call(
        functools.partial(place_kernel, classes, node_total),
        [((step, width), F32)] * 2 + [((classes, units), F32)] * 2 + [((1, 1), F32)],
        (grads,),
        [((2, pad, units), F32)],
    )
    return (loss.reshape(()), grad_self1, grad_neigh1, grad_self2.T, grad_neigh2.T)


def solution(mesh):
    in_specs = (
        P("node", "feat"),
        P("node", None, None),
        P("node", None),
        P("node", None),
        P("node", None, None, None),
        P("node"),
        P("feat", None),
        P("feat", None),
        P("feat", None),
        P("feat", None),
    )
    out_specs = (P(), P("feat", None), P("feat", None), P("feat", None), P("feat", None))
    return jax.shard_map(shards, mesh=mesh, in_specs=in_specs, out_specs=out_specs, check_vma=False)
```

```python
import functools
import math

import jax
import jax.numpy as jnp
from jax import lax
from jax.experimental import pallas as pl
from jax.experimental.pallas import tpu as pltpu
from jax.sharding import PartitionSpec as P

BLOCK = 128
F32 = jnp.float32
BF16 = jnp.bfloat16
VMEM = pl.BlockSpec(memory_space=pltpu.VMEM)
HBM = pl.BlockSpec(memory_space=pltpu.HBM)
SMEM = pl.BlockSpec(memory_space=pltpu.SMEM)


def mm(a, b):
    return lax.dot_general(a, b, (((1,), (0,)), ((), ())), preferred_element_type=F32)


def mm_tn(a, b):
    return lax.dot_general(a, b, (((0,), (0,)), ((), ())), preferred_element_type=F32)


def halves(value):
    high = value.astype(BF16)
    return high, (value - high.astype(F32)).astype(BF16)


def spread(a, rows):
    own = a.shape[0]
    parts = []
    for c in range(rows.shape[0] // own):
        part = rows[c * own : (c + 1) * own]
        parts += [part, part]
    return mm(a, jnp.concatenate(parts, axis=0))


def activate(v, with_slope):
    scale = math.sqrt(2.0 / math.pi)
    square = v * v
    t = jnp.tanh(v * (scale + (scale * 0.044715) * square))
    half = 0.5 * v
    out = (half + half * t).astype(BF16)
    if not with_slope:
        return out
    return out, (0.5 + 0.5 * t) + half * (1.0 - t * t) * (scale + (scale * 3 * 0.044715) * square)


def size_of(shape, dtype):
    rows = -(-shape[-2] // 16) * 16 if len(shape) > 1 else 1
    return math.prod(shape[:-2]) * rows * (-(-shape[-1] // 128) * 128) * jnp.dtype(dtype).itemsize


def call(body, outs, args, scratch=(), copies=0, flops=0, moved=0, grant=0):
    specs = [SMEM if arg.dtype == jnp.int32 and arg.size < 512 else VMEM for arg in args]
    if copies:
        specs = [HBM] * len(args)
    room = sum(size_of(shape, dtype) for shape, dtype in [*outs, *scratch])
    room += sum(size_of(arg.shape, arg.dtype) for arg, spec in zip(args, specs) if spec is VMEM)
    return pl.pallas_call(
        body,
        out_shape=[jax.ShapeDtypeStruct(shape, dtype) for shape, dtype in outs],
        in_specs=specs,
        out_specs=[VMEM] * len(outs),
        scratch_shapes=[pltpu.VMEM(shape, dtype) for shape, dtype in scratch]
        + ([pltpu.SemaphoreType.DMA((copies,)), pltpu.SMEM(args[0].shape, jnp.int32)] if copies else []),
        compiler_params=pltpu.CompilerParams(vmem_limit_bytes=grant or min(room + 8 * 2**20, 56 * 2**20)),
        cost_estimate=pl.CostEstimate(flops=flops, bytes_accessed=moved, transcendentals=0),
    )(*args)


def prepare_kernel(src_in, tile_val, a_ref, tiles, dense, sems, tile_src):
    blocks, per_block = tile_val.shape[0], tile_val.shape[1]
    own = blocks * BLOCK
    src_copy = pltpu.make_async_copy(src_in, tile_src, sems.at[blocks])
    src_copy.start()
    copies = [pltpu.make_async_copy(tile_val.at[b], tiles.at[b], sems.at[b]) for b in range(blocks)]
    for copy in copies:
        copy.start()
    dense[...] = jnp.zeros_like(dense)
    src_copy.wait()
    for b in range(blocks):
        rows = pl.ds(b * BLOCK, BLOCK)
        copies[b].wait()

        def add(k, _, b=b, rows=rows):
            at = pl.ds(pl.multiple_of(tile_src[b, k] * BLOCK, BLOCK), BLOCK)
            dense[rows, at] = dense[rows, at] + tiles[b, k].astype(F32)
            return 0

        lax.fori_loop(0, per_block, add, 0)
        for c in range(dense.shape[1] // own):
            high, low = halves(dense[rows, pl.ds(c * own, own)])
            a_ref[rows, pl.ds(2 * c * own, own)] = high
            a_ref[rows, pl.ds((2 * c + 1) * own, own)] = low


def pack_kernel(groups, ids, count, send_rows, w_self1, w_neigh1, w_self2, w_neigh2, *refs):
    pieces, (pick, full, packed, weights), (turned,) = refs[:groups], refs[groups : groups + 4], refs[groups + 4 :]
    step, own = pieces[0].shape
    classes, units = w_self2.shape
    base = 2 * step * groups
    pad = (weights.shape[0] - base) // 2
    for j in range(groups):
        at = pl.ds(j * units, units)
        weights[pl.ds(2 * step * j, step), :] = w_self1[:, at]
        weights[pl.ds(2 * step * j + step, step), :] = w_neigh1[:, at]
    weights[pl.ds(base, 2 * pad), :] = jnp.zeros((2 * pad, units), BF16)
    weights[pl.ds(base, classes), :] = w_self2[...]
    weights[pl.ds(base + pad, classes), :] = w_neigh2[...]
    dests, slots = send_rows.shape
    columns = send_rows[...].astype(F32).T
    row_id = lax.broadcasted_iota(jnp.int32, (slots, own), 1).astype(F32)
    slot_id = lax.broadcasted_iota(jnp.int32, (slots, own), 0)
    for d in range(dests):
        hit = (columns[:, d : d + 1] == row_id) & (slot_id < count[0, d])
        pick[pl.ds(d * slots, slots), :] = jnp.where(hit, 1.0, 0.0).astype(BF16)
    turned[:step] = pieces[0][...]
    for k in range(1, groups):
        place = lax.rem(ids[0] + groups - jnp.bitwise_xor(ids[0], k), groups)
        turned[pl.ds(pl.multiple_of(place * step, step), step), :] = pieces[k][...]
    full[...] = turned[...].T
    packed[...] = mm(pick[...], full[...]).astype(BF16)


def first_kernel(pick, a_ref, full, source, state, packed):
    own, cols = full.shape
    total = spread(a_ref[:, : 2 * own], full[...]) + spread(a_ref[:, 2 * own :], source[...])
    agg = total.astype(BF16)
    packed[...] = mm(pick[...], agg).astype(BF16)
    state[:own, :cols] = full[...]
    state[:own, cols:] = agg
    state[own:, :cols] = source[...]
    state[own:, cols:] = jnp.zeros_like(source)


def forward_kernel(
    class_count, grad_scale, groups, ids, a_ref, state, landed, labels, *refs
):
    weights = refs[:groups]
    turned, slope, packed, second = refs[groups:]
    halo, cols = landed.shape
    own = state.shape[0] - halo
    units = weights[0].shape[1]
    step = cols // groups
    base = 2 * step * groups
    pad = turned.shape[0]
    slots = halo // packed.shape[0]
    near = state[:own, :]
    total = jnp.zeros((own, pad), F32)
    for k in range(groups):
        group = lax.rem(ids[0] + groups - k, groups)
        begin = [pl.multiple_of(2 * step * group + part * step, step) for part in (0, 1)]
        w_one = jnp.concatenate([w[pl.ds(at, step), :] for at in begin for w in weights], axis=0)
        out, slope[k] = activate(mm(near, w_one), True)
        if halo == own:
            both = jnp.concatenate([state[own:, :cols], landed[...]], axis=1)
            far = activate(mm(both, w_one), False)
            held = spread(a_ref[...], jnp.concatenate([out, far], axis=0))
        else:

            def one(r, held, w_one=w_one):
                rows = pl.ds(pl.multiple_of(r * own, own), own)
                srcs = pl.ds(pl.multiple_of(2 * (r + 1) * own, own), 2 * own)
                lower = pl.ds(pl.multiple_of((r + 1) * own, own), own)
                both = jnp.concatenate([state[lower, :cols], landed[rows, :]], axis=1)
                return held + spread(a_ref[:, srcs], activate(mm(both, w_one), False))

            held = lax.fori_loop(0, halo // own, one, spread(a_ref[:, : 2 * own], out))
        rounded = held.astype(BF16)
        if k == 0:
            mine, agg_mine = out, rounded
        w_self, w_neigh = weights[k][pl.ds(base, pad), :].T, weights[k][pl.ds(base + pad, pad), :].T
        total = total + mm(jnp.concatenate([out, rounded], axis=1), jnp.concatenate([w_self, w_neigh], axis=0))
    total = total.T
    class_id = lax.broadcasted_iota(jnp.int32, total.shape, 0)
    real = class_id < class_count
    top = jnp.max(jnp.where(real, total, -jnp.inf), axis=0, keepdims=True)
    shifted = total - top
    powers = jnp.where(real, jnp.exp(shifted), 0.0)
    sums = jnp.sum(powers, axis=0, keepdims=True)
    target = (class_id == labels[...]).astype(F32)
    turned[...] = ((powers / sums - target) * grad_scale).astype(BF16)
    row_loss = jnp.log(sums) - jnp.sum(shifted * target, axis=0, keepdims=True)
    own_grads = mm(turned[...], mine)
    row = lax.broadcasted_iota(jnp.int32, own_grads.shape, 0)
    own_grads = jnp.where(row == class_count, jnp.sum(row_loss, axis=1, keepdims=True), own_grads)
    second[0] = own_grads
    second[1] = mm(turned[...], agg_mine)
    per_chunk = own // slots
    for c in range(halo // own):
        back = mm(turned[...], a_ref[:, pl.ds(2 * (c + 1) * own, own)]).T.astype(BF16)
        for d in range(per_chunk):
            put_message(packed, c * per_chunk + d, back[d * slots : (d + 1) * slots])


def message_shape(slots, pad):
    compact = BLOCK < pad <= BLOCK + BLOCK // 2 and slots % 32 == 0
    return (slots + slots // 2, BLOCK) if compact else (slots, pad)


def put_message(packed, d, rows):
    slots, pad = rows.shape
    if packed.shape[1:] == (slots, pad):
        packed[d] = rows
        return
    half, tail = slots // 2, pad - BLOCK
    packed[d, :slots, :] = rows[:, :BLOCK]
    filler = jnp.zeros((half, BLOCK // 2 - tail), BF16)
    packed[d, slots:, :] = jnp.concatenate([rows[:half, BLOCK:], filler, rows[half:, BLOCK:], filler], axis=1)


def take_message(packed, d, landed):
    slots, pad = landed.shape[0] // packed.shape[0], landed.shape[1]
    if packed.shape[1:] == (slots, pad):
        landed[pl.ds(d * slots, slots), :] = packed[d]
        return
    half, tail = slots // 2, pad - BLOCK
    landed[pl.ds(d * slots, slots), :BLOCK] = packed[d, :slots, :]
    landed[pl.ds(d * slots, half), BLOCK:] = packed[d, slots:, :tail]
    landed[pl.ds(d * slots + half, half), BLOCK:] = packed[d, slots:, BLOCK // 2 : BLOCK // 2 + tail]


def backward_kernel(parts, groups, ids, turned, pick, a_ref, slope, features, state, landed, *refs):
    weights = refs[:groups]
    out, rows = refs[groups:]
    own = turned.shape[1]
    units = slope.shape[2]
    pad = turned.shape[0]
    step = features.shape[0]
    base = 2 * step * groups
    for d in range(landed.shape[0]):
        take_message(landed, d, rows)
    high, low = halves(mm(turned[...], a_ref[:, :own]) + mm_tn(rows[...], pick[...]))
    wide = jnp.concatenate([turned[...], high, low], axis=0).T
    cols = state.shape[1] // 2
    left = jnp.concatenate([features[...], state[:own, cols:].T[:step]], axis=0)
    for k in range(groups):
        group = lax.rem(ids[0] + groups - k, groups)
        w_neigh = weights[k][pl.ds(base + pad, pad), :]
        total = mm(wide, jnp.concatenate([weights[k][pl.ds(base, pad), :], w_neigh, w_neigh], axis=0))
        result = mm(left, (total * slope[k]).astype(BF16))
        if parts:
            for i in range(units // BLOCK):
                out[group * (units // BLOCK) + i] = result[:, i * BLOCK : (i + 1) * BLOCK]
        else:
            out[:, pl.ds(pl.multiple_of(group * units, units), units)] = result


def quarter(p, rows):
    height = rows // 4
    return slice(p // 2 * height, (p // 2 + 1) * height), slice(p % 2 * BLOCK, (p % 2 + 1) * BLOCK)


def join_kernel(side, grads, second, other, out, total):
    step = grads.shape[1]
    height = total.shape[0] // 4
    total[...] = second[side[0]] + other[side[0]]
    for p in range(grads.shape[0]):
        out[p, :step, :] = grads[p]
        out[p, step : step + height, :] = total[quarter(p, total.shape[0])]
        out[p, step + height :, :] = jnp.zeros((out.shape[1] - step - height, BLOCK), F32)


def sum_kernel(step, height, pieces, out):
    first = pieces[0, :step, :]
    second = [pieces[0, step : step + height, :], pieces[1, step : step + height, :]]
    for p in range(1, pieces.shape[0]):
        first = first + pieces[p, :step, :]
        if p > 1:
            second[p % 2] = second[p % 2] + pieces[p, step : step + height, :]
    for p in range(pieces.shape[0]):
        out[p, :step, :] = first
        out[p, step : step + height, :] = second[0]
        out[p, step + height :, :] = second[1]


def place_kernel(class_count, node_total, pieces, self1, neigh1, self2, neigh2, loss, both):
    step = self1.shape[0]
    units = self2.shape[1]
    height = both.shape[1] // 4
    for p in range(pieces.shape[0]):
        at = pl.ds(p * BLOCK, BLOCK)
        self1[:, at] = pieces[p, :step, :]
        neigh1[:, at] = pieces[p, step : 2 * step, :]
        rows, lanes = quarter(p, both.shape[1])
        both[0, rows, lanes] = pieces[p, 2 * step : 2 * step + height, :]
        both[1, rows, lanes] = pieces[p, 2 * step + height :, :]
    self2[...] = both[0, :class_count, :]
    neigh2[...] = both[1, :class_count, :]
    loss[...] = both[0, class_count : class_count + 1, 0:1] / node_total


def swap(value, count):
    blocks = value.reshape(count, -1, value.shape[-1])
    return lax.all_to_all(blocks, "node", 0, 0, tiled=True)


def gather_shifted(value, count):
    return [value] + [lax.ppermute(value, "feat", [(i, (i + k) % count) for i in range(count)]) for k in range(1, count)]


def shards(features, send_rows, send_count, tile_src, tile_val, labels, w_self1, w_neigh1, w_self2, w_neigh2):
    nodes, groups = lax.axis_size("node"), lax.axis_size("feat")
    own, step = features.shape
    slots = send_rows.shape[2]
    halo = nodes * slots
    total_src = own + halo
    cols = step * groups
    width = w_self1.shape[1]
    units, classes = w_self2.shape
    pad = -(-(classes + 1) // 16) * 16
    parts = nodes if nodes == 8 and units == 2 * BLOCK and width == nodes * BLOCK else 0
    node_total = own * nodes
    grad_scale = 1.0 / math.sqrt(node_total)
    ids = lax.axis_index("feat").astype(jnp.int32).reshape(1)
    side = (lax.axis_index("node") & 1).astype(jnp.int32).reshape(1)
    blocks = own // BLOCK
    packed_rows = 2 * step * groups + 2 * pad

    turned = features.T
    turned_all = [turned] + [lax.ppermute(turned, "feat", [(i, i ^ k) for i in range(groups)]) for k in range(1, groups)]
    (a_mat,) = call(
        prepare_kernel,
        [((own, 2 * total_src), BF16)],
        (tile_src, tile_val),
        [(tile_val.shape, BF16), ((own, total_src), F32)],
        copies=blocks + 1,
        moved=tile_val.size * 4,
        grant=54 * 2**20 - 4 * own * total_src - 3 * 10**5,
    )
    a_mat, ids, side, *turned_all = lax.optimization_barrier((a_mat, ids, side, *turned_all))
    pick, full, packed, packed_weights = call(
        functools.partial(pack_kernel, groups),
        [((halo, own), BF16), ((own, cols), BF16), ((halo, cols), BF16), ((packed_rows, units), BF16)],
        (ids, send_count, send_rows[0], w_self1, w_neigh1, w_self2.T, w_neigh2.T, *turned_all),
        [((cols, own), BF16)],
        flops=2 * halo * own * cols,
        moved=halo * own * 2,
    )
    weights = gather_shifted(packed_weights, groups)
    source = swap(packed, nodes).reshape(halo, cols)
    state, packed = call(
        first_kernel,
        [((total_src, 2 * cols), BF16), ((halo, cols), BF16)],
        (pick, a_mat, full, source),
        flops=4 * own * total_src * cols,
        moved=4 * own * total_src,
    )
    packed, ids, side, *weights = lax.optimization_barrier((packed, ids, side, *weights))
    landed = swap(packed, nodes).reshape(halo, cols)
    message = (nodes, *message_shape(slots, pad))
    turned_grads, slope, packed, second = call(
        functools.partial(forward_kernel, classes, grad_scale, groups),
        [((pad, own), BF16), ((groups, own, units), F32), (message, BF16), ((2, pad, units), F32)],
        (ids, a_mat, state, landed, labels.reshape(1, own), *weights),
        flops=8 * own * total_src * width,
        moved=16 * own * width,
    )
    if parts:
        other = lax.ppermute(second, "node", [(i, i ^ 1) for i in range(nodes)])
    landed = swap(packed, nodes)
    (grads,) = call(
        functools.partial(backward_kernel, parts, groups),
        [((parts, 2 * step, BLOCK) if parts else (2 * step, width), F32)],
        (ids, turned_grads, pick, a_mat, slope, turned, state, landed, *weights),
        [((halo, pad), BF16)],
    )
    if not parts:
        grads, second = lax.psum((grads, second), "node")
        loss = second[0, classes, 0] / node_total
        return (loss, grads[:step], grads[step:], second[0, :classes].T, second[1, :classes].T)
    height = pad // 4
    grads, other = lax.optimization_barrier((grads, other))
    (grads,) = call(
        join_kernel,
        [((nodes, -(-(2 * step + height) // 8) * 8, BLOCK), F32)],
        (side, grads, second, other),
        [((pad, units), F32)],
    )
    grads = swap(grads, nodes)
    (grads,) = call(functools.partial(sum_kernel, 2 * step, height), [((nodes, 2 * step + 2 * height, BLOCK), F32)], (grads,))
    grads = swap(grads, nodes)
    grad_self1, grad_neigh1, grad_self2, grad_neigh2, loss = call(
        functools.partial(place_kernel, classes, node_total),
        [((step, width), F32)] * 2 + [((classes, units), F32)] * 2 + [((1, 1), F32)],
        (grads,),
        [((2, pad, units), F32)],
    )
    return (loss.reshape(()), grad_self1, grad_neigh1, grad_self2.T, grad_neigh2.T)


def solution(mesh):
    in_specs = (
        P("node", "feat"),
        P("node", None, None),
        P("node", None),
        P("node", None),
        P("node", None, None, None),
        P("node"),
        P("feat", None),
        P("feat", None),
        P("feat", None),
        P("feat", None),
    )
    out_specs = (P(), P("feat", None), P("feat", None), P("feat", None), P("feat", None))
    return jax.shard_map(shards, mesh=mesh, in_specs=in_specs, out_specs=out_specs, check_vma=False)
```

```python
import functools
import math

import jax
import jax.numpy as jnp
from jax import lax
from jax.experimental import pallas as pl
from jax.experimental.pallas import tpu as pltpu
from jax.sharding import PartitionSpec as P

BLOCK = 128
F32 = jnp.float32
BF16 = jnp.bfloat16
VMEM = pl.BlockSpec(memory_space=pltpu.VMEM)
HBM = pl.BlockSpec(memory_space=pltpu.HBM)
SMEM = pl.BlockSpec(memory_space=pltpu.SMEM)


def mm(a, b):
    return lax.dot_general(a, b, (((1,), (0,)), ((), ())), preferred_element_type=F32)


def mm_tn(a, b):
    return lax.dot_general(a, b, (((0,), (0,)), ((), ())), preferred_element_type=F32)


def halves(value):
    high = value.astype(BF16)
    return high, (value - high.astype(F32)).astype(BF16)


def spread(a, rows):
    own = a.shape[0]
    parts = []
    for c in range(rows.shape[0] // own):
        part = rows[c * own : (c + 1) * own]
        parts += [part, part]
    return mm(a, jnp.concatenate(parts, axis=0))


def activate(v, with_slope):
    scale = math.sqrt(2.0 / math.pi)
    square = v * v
    t = jnp.tanh(v * (scale + (scale * 0.044715) * square))
    half = 0.5 * v
    out = (half + half * t).astype(BF16)
    if not with_slope:
        return out
    return out, (0.5 + 0.5 * t) + half * (1.0 - t * t) * (scale + (scale * 3 * 0.044715) * square)


def size_of(shape, dtype):
    rows = -(-shape[-2] // 16) * 16 if len(shape) > 1 else 1
    return math.prod(shape[:-2]) * rows * (-(-shape[-1] // 128) * 128) * jnp.dtype(dtype).itemsize


def call(body, outs, args, scratch=(), copies=0, flops=0, moved=0, grant=0):
    specs = [SMEM if arg.dtype == jnp.int32 and arg.size < 512 else VMEM for arg in args]
    if copies:
        specs = [HBM] * len(args)
    room = sum(size_of(shape, dtype) for shape, dtype in [*outs, *scratch])
    room += sum(size_of(arg.shape, arg.dtype) for arg, spec in zip(args, specs) if spec is VMEM)
    return pl.pallas_call(
        body,
        out_shape=[jax.ShapeDtypeStruct(shape, dtype) for shape, dtype in outs],
        in_specs=specs,
        out_specs=[VMEM] * len(outs),
        scratch_shapes=[pltpu.VMEM(shape, dtype) for shape, dtype in scratch]
        + ([pltpu.SemaphoreType.DMA((copies,)), pltpu.SMEM(args[0].shape, jnp.int32)] if copies else []),
        compiler_params=pltpu.CompilerParams(vmem_limit_bytes=grant or min(room + 8 * 2**20, 56 * 2**20)),
        cost_estimate=pl.CostEstimate(flops=flops, bytes_accessed=moved, transcendentals=0),
    )(*args)


def prepare_kernel(src_in, tile_val, a_ref, tiles, dense, sems, tile_src):
    blocks, per_block = tile_val.shape[0], tile_val.shape[1]
    own = blocks * BLOCK
    src_copy = pltpu.make_async_copy(src_in, tile_src, sems.at[blocks])
    src_copy.start()
    copies = [pltpu.make_async_copy(tile_val.at[b], tiles.at[b], sems.at[b]) for b in range(blocks)]
    for copy in copies:
        copy.start()
    dense[...] = jnp.zeros_like(dense)
    src_copy.wait()
    for b in range(blocks):
        rows = pl.ds(b * BLOCK, BLOCK)
        copies[b].wait()

        def add(k, _, b=b, rows=rows):
            at = pl.ds(pl.multiple_of(tile_src[b, k] * BLOCK, BLOCK), BLOCK)
            dense[rows, at] = dense[rows, at] + tiles[b, k].astype(F32)
            return 0

        lax.fori_loop(0, per_block, add, 0)
        for c in range(dense.shape[1] // own):
            high, low = halves(dense[rows, pl.ds(c * own, own)])
            a_ref[rows, pl.ds(2 * c * own, own)] = high
            a_ref[rows, pl.ds((2 * c + 1) * own, own)] = low


def weights_kernel(w_self1, w_neigh1, w_self2, w_neigh2, weights):
    step, units = w_self1.shape[0], weights.shape[1]
    groups = w_self1.shape[1] // units
    classes = w_self2.shape[0]
    base = 2 * step * groups
    pad = (weights.shape[0] - base) // 2
    for j in range(groups):
        at = pl.ds(j * units, units)
        weights[pl.ds(2 * step * j, step), :] = w_self1[:, at]
        weights[pl.ds(2 * step * j + step, step), :] = w_neigh1[:, at]
    weights[pl.ds(base, 2 * pad), :] = jnp.zeros((2 * pad, units), BF16)
    weights[pl.ds(base, classes), :] = w_self2[...]
    weights[pl.ds(base + pad, classes), :] = w_neigh2[...]


def pack_kernel(groups, ids, count, send_rows, *refs):
    pieces, (pick, full, packed), (turned,) = refs[:groups], refs[groups : groups + 3], refs[groups + 3 :]
    step, own = pieces[0].shape
    dests, slots = send_rows.shape
    columns = send_rows[...].astype(F32).T
    row_id = lax.broadcasted_iota(jnp.int32, (slots, own), 1).astype(F32)
    slot_id = lax.broadcasted_iota(jnp.int32, (slots, own), 0)
    for d in range(dests):
        hit = (columns[:, d : d + 1] == row_id) & (slot_id < count[0, d])
        pick[pl.ds(d * slots, slots), :] = jnp.where(hit, 1.0, 0.0).astype(BF16)
    turned[:step] = pieces[0][...]
    for k in range(1, groups):
        place = lax.rem(ids[0] + groups - jnp.bitwise_xor(ids[0], k), groups)
        turned[pl.ds(pl.multiple_of(place * step, step), step), :] = pieces[k][...]
    full[...] = turned[...].T
    packed[...] = mm(pick[...], full[...]).astype(BF16)


def first_kernel(pick, a_ref, full, source, state, packed):
    own, cols = full.shape
    total = spread(a_ref[:, : 2 * own], full[...]) + spread(a_ref[:, 2 * own :], source[...])
    agg = total.astype(BF16)
    packed[...] = mm(pick[...], agg).astype(BF16)
    state[:own, :cols] = full[...]
    state[:own, cols:] = agg
    state[own:, :cols] = source[...]
    state[own:, cols:] = jnp.zeros_like(source)


def forward_kernel(
    class_count, grad_scale, groups, ids, a_ref, state, landed, labels, *refs
):
    weights = refs[:groups]
    turned, slope, packed, second = refs[groups:]
    halo, cols = landed.shape
    own = state.shape[0] - halo
    units = weights[0].shape[1]
    step = cols // groups
    base = 2 * step * groups
    pad = turned.shape[0]
    slots = halo // packed.shape[0]
    near = state[:own, :]
    total = jnp.zeros((own, pad), F32)
    for k in range(groups):
        group = lax.rem(ids[0] + groups - k, groups)
        begin = [pl.multiple_of(2 * step * group + part * step, step) for part in (0, 1)]
        w_one = jnp.concatenate([w[pl.ds(at, step), :] for at in begin for w in weights], axis=0)
        out, slope[k] = activate(mm(near, w_one), True)
        if halo == own:
            both = jnp.concatenate([state[own:, :cols], landed[...]], axis=1)
            far = activate(mm(both, w_one), False)
            held = spread(a_ref[...], jnp.concatenate([out, far], axis=0))
        else:

            def one(r, held, w_one=w_one):
                rows = pl.ds(pl.multiple_of(r * own, own), own)
                srcs = pl.ds(pl.multiple_of(2 * (r + 1) * own, own), 2 * own)
                lower = pl.ds(pl.multiple_of((r + 1) * own, own), own)
                both = jnp.concatenate([state[lower, :cols], landed[rows, :]], axis=1)
                return held + spread(a_ref[:, srcs], activate(mm(both, w_one), False))

            held = lax.fori_loop(0, halo // own, one, spread(a_ref[:, : 2 * own], out))
        rounded = held.astype(BF16)
        if k == 0:
            mine, agg_mine = out, rounded
        w_self, w_neigh = weights[k][pl.ds(base, pad), :].T, weights[k][pl.ds(base + pad, pad), :].T
        total = total + mm(jnp.concatenate([out, rounded], axis=1), jnp.concatenate([w_self, w_neigh], axis=0))
    total = total.T
    class_id = lax.broadcasted_iota(jnp.int32, total.shape, 0)
    real = class_id < class_count
    top = jnp.max(jnp.where(real, total, -jnp.inf), axis=0, keepdims=True)
    shifted = total - top
    powers = jnp.where(real, jnp.exp(shifted), 0.0)
    sums = jnp.sum(powers, axis=0, keepdims=True)
    target = (class_id == labels[...]).astype(F32)
    turned[...] = ((powers / sums - target) * grad_scale).astype(BF16)
    row_loss = jnp.log(sums) - jnp.sum(shifted * target, axis=0, keepdims=True)
    own_grads = mm(turned[...], mine)
    row = lax.broadcasted_iota(jnp.int32, own_grads.shape, 0)
    own_grads = jnp.where(row == class_count, jnp.sum(row_loss, axis=1, keepdims=True), own_grads)
    second[0] = own_grads
    second[1] = mm(turned[...], agg_mine)
    per_chunk = own // slots
    for c in range(halo // own):
        back = mm(turned[...], a_ref[:, pl.ds(2 * (c + 1) * own, own)]).T.astype(BF16)
        for d in range(per_chunk):
            put_message(packed, c * per_chunk + d, back[d * slots : (d + 1) * slots])


def message_shape(slots, pad):
    compact = BLOCK < pad <= BLOCK + BLOCK // 2 and slots % 32 == 0
    return (slots + slots // 2, BLOCK) if compact else (slots, pad)


def put_message(packed, d, rows):
    slots, pad = rows.shape
    if packed.shape[1:] == (slots, pad):
        packed[d] = rows
        return
    half, tail = slots // 2, pad - BLOCK
    packed[d, :slots, :] = rows[:, :BLOCK]
    filler = jnp.zeros((half, BLOCK // 2 - tail), BF16)
    packed[d, slots:, :] = jnp.concatenate([rows[:half, BLOCK:], filler, rows[half:, BLOCK:], filler], axis=1)


def take_message(packed, d, landed):
    slots, pad = landed.shape[0] // packed.shape[0], landed.shape[1]
    if packed.shape[1:] == (slots, pad):
        landed[pl.ds(d * slots, slots), :] = packed[d]
        return
    half, tail = slots // 2, pad - BLOCK
    landed[pl.ds(d * slots, slots), :BLOCK] = packed[d, :slots, :]
    landed[pl.ds(d * slots, half), BLOCK:] = packed[d, slots:, :tail]
    landed[pl.ds(d * slots + half, half), BLOCK:] = packed[d, slots:, BLOCK // 2 : BLOCK // 2 + tail]


def backward_kernel(parts, groups, ids, turned, pick, a_ref, slope, features, state, landed, *refs):
    weights = refs[:groups]
    out, rows = refs[groups:]
    own = turned.shape[1]
    units = slope.shape[2]
    pad = turned.shape[0]
    step = features.shape[0]
    base = 2 * step * groups
    for d in range(landed.shape[0]):
        take_message(landed, d, rows)
    high, low = halves(mm(turned[...], a_ref[:, :own]) + mm_tn(rows[...], pick[...]))
    wide = jnp.concatenate([turned[...], high, low], axis=0).T
    cols = state.shape[1] // 2
    left = jnp.concatenate([features[...], state[:own, cols:].T[:step]], axis=0)
    for k in range(groups):
        group = lax.rem(ids[0] + groups - k, groups)
        w_neigh = weights[k][pl.ds(base + pad, pad), :]
        total = mm(wide, jnp.concatenate([weights[k][pl.ds(base, pad), :], w_neigh, w_neigh], axis=0))
        result = mm(left, (total * slope[k]).astype(BF16))
        if parts:
            for i in range(units // BLOCK):
                out[group * (units // BLOCK) + i] = result[:, i * BLOCK : (i + 1) * BLOCK]
        else:
            out[:, pl.ds(pl.multiple_of(group * units, units), units)] = result


def quarter(p, rows):
    height = rows // 4
    return slice(p // 2 * height, (p // 2 + 1) * height), slice(p % 2 * BLOCK, (p % 2 + 1) * BLOCK)


def join_kernel(side, grads, second, other, out, total):
    step = grads.shape[1]
    height = total.shape[0] // 4
    total[...] = second[side[0]] + other[side[0]]
    for p in range(grads.shape[0]):
        out[p, :step, :] = grads[p]
        out[p, step : step + height, :] = total[quarter(p, total.shape[0])]
        out[p, step + height :, :] = jnp.zeros((out.shape[1] - step - height, BLOCK), F32)


def sum_kernel(step, height, pieces, out):
    first = pieces[0, :step, :]
    second = [pieces[0, step : step + height, :], pieces[1, step : step + height, :]]
    for p in range(1, pieces.shape[0]):
        first = first + pieces[p, :step, :]
        if p > 1:
            second[p % 2] = second[p % 2] + pieces[p, step : step + height, :]
    for p in range(pieces.shape[0]):
        out[p, :step, :] = first
        out[p, step : step + height, :] = second[0]
        out[p, step + height :, :] = second[1]


def place_kernel(class_count, node_total, pieces, self1, neigh1, self2, neigh2, loss, both):
    step = self1.shape[0]
    units = self2.shape[1]
    height = both.shape[1] // 4
    for p in range(pieces.shape[0]):
        at = pl.ds(p * BLOCK, BLOCK)
        self1[:, at] = pieces[p, :step, :]
        neigh1[:, at] = pieces[p, step : 2 * step, :]
        rows, lanes = quarter(p, both.shape[1])
        both[0, rows, lanes] = pieces[p, 2 * step : 2 * step + height, :]
        both[1, rows, lanes] = pieces[p, 2 * step + height :, :]
    self2[...] = both[0, :class_count, :]
    neigh2[...] = both[1, :class_count, :]
    loss[...] = both[0, class_count : class_count + 1, 0:1] / node_total


def swap(value, count):
    blocks = value.reshape(count, -1, value.shape[-1])
    return lax.all_to_all(blocks, "node", 0, 0, tiled=True)


def gather_shifted(value, count):
    return [value] + [lax.ppermute(value, "feat", [(i, (i + k) % count) for i in range(count)]) for k in range(1, count)]


def shards(features, send_rows, send_count, tile_src, tile_val, labels, w_self1, w_neigh1, w_self2, w_neigh2):
    nodes, groups = lax.axis_size("node"), lax.axis_size("feat")
    own, step = features.shape
    slots = send_rows.shape[2]
    halo = nodes * slots
    total_src = own + halo
    cols = step * groups
    width = w_self1.shape[1]
    units, classes = w_self2.shape
    pad = -(-(classes + 1) // 16) * 16
    parts = nodes if nodes == 8 and units == 2 * BLOCK and width == nodes * BLOCK else 0
    node_total = own * nodes
    grad_scale = 1.0 / math.sqrt(node_total)
    ids = lax.axis_index("feat").astype(jnp.int32).reshape(1)
    side = (lax.axis_index("node") & 1).astype(jnp.int32).reshape(1)
    blocks = own // BLOCK
    packed_rows = 2 * step * groups + 2 * pad

    turned = features.T
    turned_all = [turned] + [lax.ppermute(turned, "feat", [(i, i ^ k) for i in range(groups)]) for k in range(1, groups)]
    (a_mat,) = call(
        prepare_kernel,
        [((own, 2 * total_src), BF16)],
        (tile_src, tile_val),
        [(tile_val.shape, BF16), ((own, total_src), F32)],
        copies=blocks + 1,
        moved=tile_val.size * 4,
        grant=54 * 2**20 - 4 * own * total_src - 3 * 10**5,
    )
    a_mat, *pairs = lax.optimization_barrier((a_mat, w_self1, w_neigh1, w_self2.T, w_neigh2.T))
    (packed_weights,) = call(weights_kernel, [((packed_rows, units), BF16)], pairs)
    packed_weights, ids, *turned_all = lax.optimization_barrier((packed_weights, ids, *turned_all))
    weights = gather_shifted(packed_weights, groups)
    pick, full, packed = call(
        functools.partial(pack_kernel, groups),
        [((halo, own), BF16), ((own, cols), BF16), ((halo, cols), BF16)],
        (ids, send_count, send_rows[0], *turned_all),
        [((cols, own), BF16)],
        flops=2 * halo * own * cols,
        moved=halo * own * 2,
    )
    source = swap(packed, nodes).reshape(halo, cols)
    state, packed = call(
        first_kernel,
        [((total_src, 2 * cols), BF16), ((halo, cols), BF16)],
        (pick, a_mat, full, source),
        flops=4 * own * total_src * cols,
        moved=4 * own * total_src,
    )
    packed, ids, side, *weights = lax.optimization_barrier((packed, ids, side, *weights))
    landed = swap(packed, nodes).reshape(halo, cols)
    message = (nodes, *message_shape(slots, pad))
    turned_grads, slope, packed, second = call(
        functools.partial(forward_kernel, classes, grad_scale, groups),
        [((pad, own), BF16), ((groups, own, units), F32), (message, BF16), ((2, pad, units), F32)],
        (ids, a_mat, state, landed, labels.reshape(1, own), *weights),
        flops=8 * own * total_src * width,
        moved=16 * own * width,
    )
    if parts:
        other = lax.ppermute(second, "node", [(i, i ^ 1) for i in range(nodes)])
    landed = swap(packed, nodes)
    (grads,) = call(
        functools.partial(backward_kernel, parts, groups),
        [((parts, 2 * step, BLOCK) if parts else (2 * step, width), F32)],
        (ids, turned_grads, pick, a_mat, slope, turned, state, landed, *weights),
        [((halo, pad), BF16)],
    )
    if not parts:
        grads, second = lax.psum((grads, second), "node")
        loss = second[0, classes, 0] / node_total
        return (loss, grads[:step], grads[step:], second[0, :classes].T, second[1, :classes].T)
    height = pad // 4
    grads, other = lax.optimization_barrier((grads, other))
    (grads,) = call(
        join_kernel,
        [((nodes, -(-(2 * step + height) // 8) * 8, BLOCK), F32)],
        (side, grads, second, other),
        [((pad, units), F32)],
    )
    grads = swap(grads, nodes)
    (grads,) = call(functools.partial(sum_kernel, 2 * step, height), [((nodes, 2 * step + 2 * height, BLOCK), F32)], (grads,))
    grads = swap(grads, nodes)
    grad_self1, grad_neigh1, grad_self2, grad_neigh2, loss = call(
        functools.partial(place_kernel, classes, node_total),
        [((step, width), F32)] * 2 + [((classes, units), F32)] * 2 + [((1, 1), F32)],
        (grads,),
        [((2, pad, units), F32)],
    )
    return (loss.reshape(()), grad_self1, grad_neigh1, grad_self2.T, grad_neigh2.T)


def solution(mesh):
    in_specs = (
        P("node", "feat"),
        P("node", None, None),
        P("node", None),
        P("node", None),
        P("node", None, None, None),
        P("node"),
        P("feat", None),
        P("feat", None),
        P("feat", None),
        P("feat", None),
    )
    out_specs = (P(), P("feat", None), P("feat", None), P("feat", None), P("feat", None))
    return jax.shard_map(shards, mesh=mesh, in_specs=in_specs, out_specs=out_specs, check_vma=False)
```

```python
import functools
import math

import jax
import jax.numpy as jnp
from jax import lax
from jax.experimental import pallas as pl
from jax.experimental.pallas import tpu as pltpu
from jax.sharding import PartitionSpec as P

BLOCK = 128
F32 = jnp.float32
BF16 = jnp.bfloat16
VMEM = pl.BlockSpec(memory_space=pltpu.VMEM)
HBM = pl.BlockSpec(memory_space=pltpu.HBM)
SMEM = pl.BlockSpec(memory_space=pltpu.SMEM)


def mm(a, b):
    return lax.dot_general(a, b, (((1,), (0,)), ((), ())), preferred_element_type=F32)


def mm_tn(a, b):
    return lax.dot_general(a, b, (((0,), (0,)), ((), ())), preferred_element_type=F32)


def halves(value):
    high = value.astype(BF16)
    return high, (value - high.astype(F32)).astype(BF16)


def spread(a, rows):
    own = a.shape[0]
    parts = []
    for c in range(rows.shape[0] // own):
        part = rows[c * own : (c + 1) * own]
        parts += [part, part]
    return mm(a, jnp.concatenate(parts, axis=0))


def activate(v, with_slope):
    scale = math.sqrt(2.0 / math.pi)
    square = v * v
    t = jnp.tanh(v * (scale + (scale * 0.044715) * square))
    half = 0.5 * v
    out = (half + half * t).astype(BF16)
    if not with_slope:
        return out
    return out, (0.5 + 0.5 * t) + half * (1.0 - t * t) * (scale + (scale * 3 * 0.044715) * square)


def size_of(shape, dtype):
    rows = -(-shape[-2] // 16) * 16 if len(shape) > 1 else 1
    return math.prod(shape[:-2]) * rows * (-(-shape[-1] // 128) * 128) * jnp.dtype(dtype).itemsize


def call(body, outs, args, scratch=(), copies=0, flops=0, moved=0, grant=0):
    specs = [SMEM if arg.dtype == jnp.int32 and arg.size < 512 else VMEM for arg in args]
    if copies:
        specs = [HBM] * len(args)
    room = sum(size_of(shape, dtype) for shape, dtype in [*outs, *scratch])
    room += sum(size_of(arg.shape, arg.dtype) for arg, spec in zip(args, specs) if spec is VMEM)
    return pl.pallas_call(
        body,
        out_shape=[jax.ShapeDtypeStruct(shape, dtype) for shape, dtype in outs],
        in_specs=specs,
        out_specs=[VMEM] * len(outs),
        scratch_shapes=[pltpu.VMEM(shape, dtype) for shape, dtype in scratch]
        + ([pltpu.SemaphoreType.DMA((copies,)), pltpu.SMEM(args[0].shape, jnp.int32)] if copies else []),
        compiler_params=pltpu.CompilerParams(vmem_limit_bytes=grant or min(room + 8 * 2**20, 56 * 2**20)),
        cost_estimate=pl.CostEstimate(flops=flops, bytes_accessed=moved, transcendentals=0),
    )(*args)


def prepare_kernel(src_in, tile_val, a_ref, tiles, dense, sems, tile_src):
    blocks, per_block = tile_val.shape[0], tile_val.shape[1]
    own = blocks * BLOCK
    src_copy = pltpu.make_async_copy(src_in, tile_src, sems.at[blocks])
    src_copy.start()
    copies = [pltpu.make_async_copy(tile_val.at[b], tiles.at[b], sems.at[b]) for b in range(blocks)]
    for copy in copies:
        copy.start()
    dense[...] = jnp.zeros_like(dense)
    src_copy.wait()
    for b in range(blocks):
        rows = pl.ds(b * BLOCK, BLOCK)
        copies[b].wait()

        def add(k, _, b=b, rows=rows):
            at = pl.ds(pl.multiple_of(tile_src[b, k] * BLOCK, BLOCK), BLOCK)
            dense[rows, at] = dense[rows, at] + tiles[b, k].astype(F32)
            return 0

        lax.fori_loop(0, per_block, add, 0)
        for c in range(dense.shape[1] // own):
            high, low = halves(dense[rows, pl.ds(c * own, own)])
            a_ref[rows, pl.ds(2 * c * own, own)] = high
            a_ref[rows, pl.ds((2 * c + 1) * own, own)] = low


def weights_kernel(w_self1, w_neigh1, w_self2, w_neigh2, weights):
    step, units = w_self1.shape[0], weights.shape[1]
    groups = w_self1.shape[1] // units
    classes = w_self2.shape[0]
    base = 2 * step * groups
    pad = (weights.shape[0] - base) // 2
    for j in range(groups):
        at = pl.ds(j * units, units)
        weights[pl.ds(2 * step * j, step), :] = w_self1[:, at]
        weights[pl.ds(2 * step * j + step, step), :] = w_neigh1[:, at]
    weights[pl.ds(base, 2 * pad), :] = jnp.zeros((2 * pad, units), BF16)
    weights[pl.ds(base, classes), :] = w_self2[...]
    weights[pl.ds(base + pad, classes), :] = w_neigh2[...]


def pack_kernel(groups, ids, count, send_rows, *refs):
    pieces, (pick, full, packed), (turned,) = refs[:groups], refs[groups : groups + 3], refs[groups + 3 :]
    step, own = pieces[0].shape
    dests, slots = send_rows.shape
    columns = send_rows[...].astype(F32).T
    row_id = lax.broadcasted_iota(jnp.int32, (slots, own), 1).astype(F32)
    slot_id = lax.broadcasted_iota(jnp.int32, (slots, own), 0)
    for d in range(dests):
        hit = (columns[:, d : d + 1] == row_id) & (slot_id < count[0, d])
        pick[pl.ds(d * slots, slots), :] = jnp.where(hit, 1.0, 0.0).astype(BF16)
    turned[:step] = pieces[0][...]
    for k in range(1, groups):
        place = lax.rem(ids[0] + groups - jnp.bitwise_xor(ids[0], k), groups)
        turned[pl.ds(pl.multiple_of(place * step, step), step), :] = pieces[k][...]
    full[...] = turned[...].T
    packed[...] = mm(pick[...], full[...]).astype(BF16)


def first_kernel(pick, a_ref, full, source, state, packed):
    own, cols = full.shape
    total = spread(a_ref[:, : 2 * own], full[...]) + spread(a_ref[:, 2 * own :], source[...])
    agg = total.astype(BF16)
    packed[...] = mm(pick[...], agg).astype(BF16)
    state[:own, :cols] = full[...]
    state[:own, cols:] = agg
    state[own:, :cols] = source[...]
    state[own:, cols:] = jnp.zeros_like(source)


def forward_kernel(
    class_count, grad_scale, groups, ids, a_ref, state, landed, labels, *refs
):
    weights = refs[:groups]
    turned, slope, packed, second = refs[groups:]
    halo, cols = landed.shape
    own = state.shape[0] - halo
    units = weights[0].shape[1]
    step = cols // groups
    base = 2 * step * groups
    pad = turned.shape[0]
    slots = halo // packed.shape[0]
    near = state[:own, :]
    total = jnp.zeros((own, pad), F32)
    for k in range(groups):
        group = lax.rem(ids[0] + groups - k, groups)
        begin = [pl.multiple_of(2 * step * group + part * step, step) for part in (0, 1)]
        w_one = jnp.concatenate([w[pl.ds(at, step), :] for at in begin for w in weights], axis=0)
        out, slope[k] = activate(mm(near, w_one), True)
        if halo == own:
            both = jnp.concatenate([state[own:, :cols], landed[...]], axis=1)
            far = activate(mm(both, w_one), False)
            held = spread(a_ref[...], jnp.concatenate([out, far], axis=0))
        else:

            def one(r, held, w_one=w_one):
                rows = pl.ds(pl.multiple_of(r * own, own), own)
                srcs = pl.ds(pl.multiple_of(2 * (r + 1) * own, own), 2 * own)
                lower = pl.ds(pl.multiple_of((r + 1) * own, own), own)
                both = jnp.concatenate([state[lower, :cols], landed[rows, :]], axis=1)
                return held + spread(a_ref[:, srcs], activate(mm(both, w_one), False))

            held = lax.fori_loop(0, halo // own, one, spread(a_ref[:, : 2 * own], out))
        rounded = held.astype(BF16)
        if k == 0:
            mine, agg_mine = out, rounded
        w_self, w_neigh = weights[k][pl.ds(base, pad), :].T, weights[k][pl.ds(base + pad, pad), :].T
        total = total + mm(jnp.concatenate([out, rounded], axis=1), jnp.concatenate([w_self, w_neigh], axis=0))
    total = total.T
    class_id = lax.broadcasted_iota(jnp.int32, total.shape, 0)
    real = class_id < class_count
    top = jnp.max(jnp.where(real, total, -jnp.inf), axis=0, keepdims=True)
    shifted = total - top
    powers = jnp.where(real, jnp.exp(shifted), 0.0)
    sums = jnp.sum(powers, axis=0, keepdims=True)
    target = (class_id == labels[...]).astype(F32)
    turned[...] = ((powers / sums - target) * grad_scale).astype(BF16)
    row_loss = jnp.log(sums) - jnp.sum(shifted * target, axis=0, keepdims=True)
    own_grads = mm(turned[...], mine)
    row = lax.broadcasted_iota(jnp.int32, own_grads.shape, 0)
    own_grads = jnp.where(row == class_count, jnp.sum(row_loss, axis=1, keepdims=True), own_grads)
    second[0] = own_grads
    second[1] = mm(turned[...], agg_mine)
    per_chunk = own // slots
    for c in range(halo // own):
        back = mm(turned[...], a_ref[:, pl.ds(2 * (c + 1) * own, own)]).T.astype(BF16)
        for d in range(per_chunk):
            put_message(packed, c * per_chunk + d, back[d * slots : (d + 1) * slots])


def message_shape(slots, pad):
    compact = BLOCK < pad <= BLOCK + BLOCK // 2 and slots % 32 == 0
    return (slots + slots // 2, BLOCK) if compact else (slots, pad)


def put_message(packed, d, rows):
    slots, pad = rows.shape
    if packed.shape[1:] == (slots, pad):
        packed[d] = rows
        return
    half, tail = slots // 2, pad - BLOCK
    packed[d, :slots, :] = rows[:, :BLOCK]
    filler = jnp.zeros((half, BLOCK // 2 - tail), BF16)
    packed[d, slots:, :] = jnp.concatenate([rows[:half, BLOCK:], filler, rows[half:, BLOCK:], filler], axis=1)


def take_message(packed, d, landed):
    slots, pad = landed.shape[0] // packed.shape[0], landed.shape[1]
    if packed.shape[1:] == (slots, pad):
        landed[pl.ds(d * slots, slots), :] = packed[d]
        return
    half, tail = slots // 2, pad - BLOCK
    landed[pl.ds(d * slots, slots), :BLOCK] = packed[d, :slots, :]
    landed[pl.ds(d * slots, half), BLOCK:] = packed[d, slots:, :tail]
    landed[pl.ds(d * slots + half, half), BLOCK:] = packed[d, slots:, BLOCK // 2 : BLOCK // 2 + tail]


def backward_kernel(parts, groups, ids, turned, pick, a_ref, slope, features, state, landed, *refs):
    weights = refs[:groups]
    out, rows = refs[groups:]
    own = turned.shape[1]
    units = slope.shape[2]
    pad = turned.shape[0]
    step = features.shape[0]
    base = 2 * step * groups
    for d in range(landed.shape[0]):
        take_message(landed, d, rows)
    high, low = halves(mm(turned[...], a_ref[:, :own]) + mm_tn(rows[...], pick[...]))
    wide = jnp.concatenate([turned[...], high, low], axis=0).T
    cols = state.shape[1] // 2
    left = jnp.concatenate([features[...], state[:own, cols:].T[:step]], axis=0)
    for k in range(groups):
        group = lax.rem(ids[0] + groups - k, groups)
        w_neigh = weights[k][pl.ds(base + pad, pad), :]
        total = mm(wide, jnp.concatenate([weights[k][pl.ds(base, pad), :], w_neigh, w_neigh], axis=0))
        result = mm(left, (total * slope[k]).astype(BF16))
        if parts:
            for i in range(units // BLOCK):
                out[group * (units // BLOCK) + i] = result[:, i * BLOCK : (i + 1) * BLOCK]
        else:
            out[:, pl.ds(pl.multiple_of(group * units, units), units)] = result


def quarter(p, rows):
    height = rows // 4
    return slice(p // 2 * height, (p // 2 + 1) * height), slice(p % 2 * BLOCK, (p % 2 + 1) * BLOCK)


def join_kernel(side, grads, second, other, out, total):
    step = grads.shape[1]
    height = total.shape[0] // 4
    total[...] = second[side[0]] + other[side[0]]
    for p in range(grads.shape[0]):
        out[p, :step, :] = grads[p]
        out[p, step : step + height, :] = total[quarter(p, total.shape[0])]
        out[p, step + height :, :] = jnp.zeros((out.shape[1] - step - height, BLOCK), F32)


def sum_kernel(step, height, pieces, out):
    first = pieces[0, :step, :]
    second = [pieces[0, step : step + height, :], pieces[1, step : step + height, :]]
    for p in range(1, pieces.shape[0]):
        first = first + pieces[p, :step, :]
        if p > 1:
            second[p % 2] = second[p % 2] + pieces[p, step : step + height, :]
    for p in range(pieces.shape[0]):
        out[p, :step, :] = first
        out[p, step : step + height, :] = second[0]
        out[p, step + height :, :] = second[1]


def place_kernel(class_count, node_total, pieces, self1, neigh1, self2, neigh2, loss, both):
    step = self1.shape[0]
    units = self2.shape[1]
    height = both.shape[1] // 4
    for p in range(pieces.shape[0]):
        at = pl.ds(p * BLOCK, BLOCK)
        self1[:, at] = pieces[p, :step, :]
        neigh1[:, at] = pieces[p, step : 2 * step, :]
        rows, lanes = quarter(p, both.shape[1])
        both[0, rows, lanes] = pieces[p, 2 * step : 2 * step + height, :]
        both[1, rows, lanes] = pieces[p, 2 * step + height :, :]
    self2[...] = both[0, :class_count, :]
    neigh2[...] = both[1, :class_count, :]
    loss[...] = both[0, class_count : class_count + 1, 0:1] / node_total


def swap(value, count):
    blocks = value.reshape(count, -1, value.shape[-1])
    return lax.all_to_all(blocks, "node", 0, 0, tiled=True)


def gather_shifted(value, count):
    return [value] + [lax.ppermute(value, "feat", [(i, (i + k) % count) for i in range(count)]) for k in range(1, count)]


def shards(features, send_rows, send_count, tile_src, tile_val, labels, w_self1, w_neigh1, w_self2, w_neigh2):
    nodes, groups = lax.axis_size("node"), lax.axis_size("feat")
    own, step = features.shape
    slots = send_rows.shape[2]
    halo = nodes * slots
    total_src = own + halo
    cols = step * groups
    width = w_self1.shape[1]
    units, classes = w_self2.shape
    pad = -(-(classes + 1) // 16) * 16
    parts = nodes if nodes == 8 and units == 2 * BLOCK and width == nodes * BLOCK else 0
    node_total = own * nodes
    grad_scale = 1.0 / math.sqrt(node_total)
    ids = lax.axis_index("feat").astype(jnp.int32).reshape(1)
    side = (lax.axis_index("node") & 1).astype(jnp.int32).reshape(1)
    blocks = own // BLOCK
    packed_rows = 2 * step * groups + 2 * pad

    turned = features.T
    turned_all = [turned] + [lax.ppermute(turned, "feat", [(i, i ^ k) for i in range(groups)]) for k in range(1, groups)]
    (a_mat,) = call(
        prepare_kernel,
        [((own, 2 * total_src), BF16)],
        (tile_src, tile_val),
        [(tile_val.shape, BF16), ((own, total_src), F32)],
        copies=blocks + 1,
        moved=tile_val.size * 4,
        grant=54 * 2**20 - 4 * own * total_src - 3 * 10**5,
    )
    a_mat, *pairs = lax.optimization_barrier((a_mat, w_self1, w_neigh1, w_self2.T, w_neigh2.T))
    (packed_weights,) = call(weights_kernel, [((packed_rows, units), BF16)], pairs)
    packed_weights, ids, side, *turned_all = lax.optimization_barrier((packed_weights, ids, side, *turned_all))
    weights = gather_shifted(packed_weights, groups)
    pick, full, packed = call(
        functools.partial(pack_kernel, groups),
        [((halo, own), BF16), ((own, cols), BF16), ((halo, cols), BF16)],
        (ids, send_count, send_rows[0], *turned_all),
        [((cols, own), BF16)],
        flops=2 * halo * own * cols,
        moved=halo * own * 2,
    )
    source = swap(packed, nodes).reshape(halo, cols)
    state, packed = call(
        first_kernel,
        [((total_src, 2 * cols), BF16), ((halo, cols), BF16)],
        (pick, a_mat, full, source),
        flops=4 * own * total_src * cols,
        moved=4 * own * total_src,
    )
    packed, ids, side, *weights = lax.optimization_barrier((packed, ids, side, *weights))
    landed = swap(packed, nodes).reshape(halo, cols)
    message = (nodes, *message_shape(slots, pad))
    turned_grads, slope, packed, second = call(
        functools.partial(forward_kernel, classes, grad_scale, groups),
        [((pad, own), BF16), ((groups, own, units), F32), (message, BF16), ((2, pad, units), F32)],
        (ids, a_mat, state, landed, labels.reshape(1, own), *weights),
        flops=8 * own * total_src * width,
        moved=16 * own * width,
    )
    if parts:
        other = lax.ppermute(second, "node", [(i, i ^ 1) for i in range(nodes)])
    landed = swap(packed, nodes)
    (grads,) = call(
        functools.partial(backward_kernel, parts, groups),
        [((parts, 2 * step, BLOCK) if parts else (2 * step, width), F32)],
        (ids, turned_grads, pick, a_mat, slope, turned, state, landed, *weights),
        [((halo, pad), BF16)],
    )
    if not parts:
        grads, second = lax.psum((grads, second), "node")
        loss = second[0, classes, 0] / node_total
        return (loss, grads[:step], grads[step:], second[0, :classes].T, second[1, :classes].T)
    height = pad // 4
    grads, other = lax.optimization_barrier((grads, other))
    (grads,) = call(
        join_kernel,
        [((nodes, -(-(2 * step + height) // 8) * 8, BLOCK), F32)],
        (side, grads, second, other),
        [((pad, units), F32)],
    )
    grads = swap(grads, nodes)
    (grads,) = call(functools.partial(sum_kernel, 2 * step, height), [((nodes, 2 * step + 2 * height, BLOCK), F32)], (grads,))
    grads = swap(grads, nodes)
    grad_self1, grad_neigh1, grad_self2, grad_neigh2, loss = call(
        functools.partial(place_kernel, classes, node_total),
        [((step, width), F32)] * 2 + [((classes, units), F32)] * 2 + [((1, 1), F32)],
        (grads,),
        [((2, pad, units), F32)],
    )
    return (loss.reshape(()), grad_self1, grad_neigh1, grad_self2.T, grad_neigh2.T)


def solution(mesh):
    in_specs = (
        P("node", "feat"),
        P("node", None, None),
        P("node", None),
        P("node", None),
        P("node", None, None, None),
        P("node"),
        P("feat", None),
        P("feat", None),
        P("feat", None),
        P("feat", None),
    )
    out_specs = (P(), P("feat", None), P("feat", None), P("feat", None), P("feat", None))
    return jax.shard_map(shards, mesh=mesh, in_specs=in_specs, out_specs=out_specs, check_vma=False)
```

```python
import functools
import math

import jax
import jax.numpy as jnp
from jax import lax
from jax.experimental import pallas as pl
from jax.experimental.pallas import tpu as pltpu
from jax.sharding import PartitionSpec as P

BLOCK = 128
F32 = jnp.float32
BF16 = jnp.bfloat16
VMEM = pl.BlockSpec(memory_space=pltpu.VMEM)
HBM = pl.BlockSpec(memory_space=pltpu.HBM)
SMEM = pl.BlockSpec(memory_space=pltpu.SMEM)


def mm(a, b):
    return lax.dot_general(a, b, (((1,), (0,)), ((), ())), preferred_element_type=F32)


def mm_tn(a, b):
    return lax.dot_general(a, b, (((0,), (0,)), ((), ())), preferred_element_type=F32)


def halves(value):
    high = value.astype(BF16)
    return high, (value - high.astype(F32)).astype(BF16)


def spread(a, rows):
    own = a.shape[0]
    parts = []
    for c in range(rows.shape[0] // own):
        part = rows[c * own : (c + 1) * own]
        parts += [part, part]
    return mm(a, jnp.concatenate(parts, axis=0))


def activate(v, with_slope):
    scale = math.sqrt(2.0 / math.pi)
    square = v * v
    t = jnp.tanh(v * (scale + (scale * 0.044715) * square))
    half = 0.5 * v
    out = (half + half * t).astype(BF16)
    if not with_slope:
        return out
    return out, (0.5 + 0.5 * t) + half * (1.0 - t * t) * (scale + (scale * 3 * 0.044715) * square)


def size_of(shape, dtype):
    rows = -(-shape[-2] // 16) * 16 if len(shape) > 1 else 1
    return math.prod(shape[:-2]) * rows * (-(-shape[-1] // 128) * 128) * jnp.dtype(dtype).itemsize


def call(body, outs, args, scratch=(), copies=0, flops=0, moved=0, grant=0):
    specs = [SMEM if arg.dtype == jnp.int32 and arg.size < 512 else VMEM for arg in args]
    if copies:
        specs = [HBM] * len(args)
    room = sum(size_of(shape, dtype) for shape, dtype in [*outs, *scratch])
    room += sum(size_of(arg.shape, arg.dtype) for arg, spec in zip(args, specs) if spec is VMEM)
    return pl.pallas_call(
        body,
        out_shape=[jax.ShapeDtypeStruct(shape, dtype) for shape, dtype in outs],
        in_specs=specs,
        out_specs=[VMEM] * len(outs),
        scratch_shapes=[pltpu.VMEM(shape, dtype) for shape, dtype in scratch]
        + ([pltpu.SemaphoreType.DMA((copies,)), pltpu.SMEM(args[0].shape, jnp.int32)] if copies else []),
        compiler_params=pltpu.CompilerParams(vmem_limit_bytes=grant or min(room + 8 * 2**20, 56 * 2**20)),
        cost_estimate=pl.CostEstimate(flops=flops, bytes_accessed=moved, transcendentals=0),
    )(*args)


def prepare_kernel(src_in, tile_val, a_ref, tiles, dense, sems, tile_src):
    blocks, per_block = tile_val.shape[0], tile_val.shape[1]
    own = blocks * BLOCK
    src_copy = pltpu.make_async_copy(src_in, tile_src, sems.at[blocks])
    src_copy.start()
    copies = [pltpu.make_async_copy(tile_val.at[b], tiles.at[b], sems.at[b]) for b in range(blocks)]
    for copy in copies:
        copy.start()
    dense[...] = jnp.zeros_like(dense)
    src_copy.wait()
    for b in range(blocks):
        rows = pl.ds(b * BLOCK, BLOCK)
        copies[b].wait()

        def add(k, _, b=b, rows=rows):
            at = pl.ds(pl.multiple_of(tile_src[b, k] * BLOCK, BLOCK), BLOCK)
            dense[rows, at] = dense[rows, at] + tiles[b, k].astype(F32)
            return 0

        lax.fori_loop(0, per_block, add, 0)
        for c in range(dense.shape[1] // own):
            high, low = halves(dense[rows, pl.ds(c * own, own)])
            a_ref[rows, pl.ds(2 * c * own, own)] = high
            a_ref[rows, pl.ds((2 * c + 1) * own, own)] = low


def weights_kernel(w_self1, w_neigh1, w_self2, w_neigh2, weights):
    step, units = w_self1.shape[0], weights.shape[1]
    groups = w_self1.shape[1] // units
    classes = w_self2.shape[0]
    base = 2 * step * groups
    pad = (weights.shape[0] - base) // 2
    for j in range(groups):
        at = pl.ds(j * units, units)
        weights[pl.ds(2 * step * j, step), :] = w_self1[:, at]
        weights[pl.ds(2 * step * j + step, step), :] = w_neigh1[:, at]
    weights[pl.ds(base, 2 * pad), :] = jnp.zeros((2 * pad, units), BF16)
    weights[pl.ds(base, classes), :] = w_self2[...]
    weights[pl.ds(base + pad, classes), :] = w_neigh2[...]


def pack_kernel(groups, ids, count, send_rows, *refs):
    pieces, (pick, full, packed), (turned,) = refs[:groups], refs[groups : groups + 3], refs[groups + 3 :]
    step, own = pieces[0].shape
    dests, slots = send_rows.shape
    columns = send_rows[...].astype(F32).T
    row_id = lax.broadcasted_iota(jnp.int32, (slots, own), 1).astype(F32)
    slot_id = lax.broadcasted_iota(jnp.int32, (slots, own), 0)
    for d in range(dests):
        hit = (columns[:, d : d + 1] == row_id) & (slot_id < count[0, d])
        pick[pl.ds(d * slots, slots), :] = jnp.where(hit, 1.0, 0.0).astype(BF16)
    turned[:step] = pieces[0][...]
    for k in range(1, groups):
        place = lax.rem(ids[0] + groups - jnp.bitwise_xor(ids[0], k), groups)
        turned[pl.ds(pl.multiple_of(place * step, step), step), :] = pieces[k][...]
    full[...] = turned[...].T
    packed[...] = mm(pick[...], full[...]).astype(BF16)


def first_kernel(pick, a_ref, full, source, features, state, packed, left):
    own, cols = full.shape
    total = spread(a_ref[:, : 2 * own], full[...]) + spread(a_ref[:, 2 * own :], source[...])
    agg = total.astype(BF16)
    packed[...] = mm(pick[...], agg).astype(BF16)
    state[:own, :cols] = full[...]
    state[:own, cols:] = agg
    state[own:, :cols] = source[...]
    state[own:, cols:] = jnp.zeros_like(source)
    step = features.shape[0]
    left[:step] = features[...]
    left[step:] = agg.T[:step]


def forward_kernel(
    class_count, grad_scale, groups, ids, a_ref, state, landed, labels, *refs
):
    weights = refs[:groups]
    turned, slope, packed, second = refs[groups:]
    halo, cols = landed.shape
    own = state.shape[0] - halo
    units = weights[0].shape[1]
    step = cols // groups
    base = 2 * step * groups
    pad = turned.shape[0]
    slots = halo // packed.shape[0]
    near = state[:own, :]
    total = jnp.zeros((own, pad), F32)
    for k in range(groups):
        group = lax.rem(ids[0] + groups - k, groups)
        begin = [pl.multiple_of(2 * step * group + part * step, step) for part in (0, 1)]
        w_one = jnp.concatenate([w[pl.ds(at, step), :] for at in begin for w in weights], axis=0)
        out, slope[k] = activate(mm(near, w_one), True)
        if halo == own:
            both = jnp.concatenate([state[own:, :cols], landed[...]], axis=1)
            far = activate(mm(both, w_one), False)
            held = spread(a_ref[...], jnp.concatenate([out, far], axis=0))
        else:

            def one(r, held, w_one=w_one):
                rows = pl.ds(pl.multiple_of(r * own, own), own)
                srcs = pl.ds(pl.multiple_of(2 * (r + 1) * own, own), 2 * own)
                lower = pl.ds(pl.multiple_of((r + 1) * own, own), own)
                both = jnp.concatenate([state[lower, :cols], landed[rows, :]], axis=1)
                return held + spread(a_ref[:, srcs], activate(mm(both, w_one), False))

            held = lax.fori_loop(0, halo // own, one, spread(a_ref[:, : 2 * own], out))
        rounded = held.astype(BF16)
        if k == 0:
            mine, agg_mine = out, rounded
        w_self, w_neigh = weights[k][pl.ds(base, pad), :].T, weights[k][pl.ds(base + pad, pad), :].T
        total = total + mm(jnp.concatenate([out, rounded], axis=1), jnp.concatenate([w_self, w_neigh], axis=0))
    total = total.T
    class_id = lax.broadcasted_iota(jnp.int32, total.shape, 0)
    real = class_id < class_count
    top = jnp.max(jnp.where(real, total, -jnp.inf), axis=0, keepdims=True)
    shifted = total - top
    powers = jnp.where(real, jnp.exp(shifted), 0.0)
    sums = jnp.sum(powers, axis=0, keepdims=True)
    target = (class_id == labels[...]).astype(F32)
    turned[...] = ((powers / sums - target) * grad_scale).astype(BF16)
    row_loss = jnp.log(sums) - jnp.sum(shifted * target, axis=0, keepdims=True)
    own_grads = mm(turned[...], mine)
    row = lax.broadcasted_iota(jnp.int32, own_grads.shape, 0)
    own_grads = jnp.where(row == class_count, jnp.sum(row_loss, axis=1, keepdims=True), own_grads)
    second[0] = own_grads
    second[1] = mm(turned[...], agg_mine)
    per_chunk = own // slots
    for c in range(halo // own):
        back = mm(turned[...], a_ref[:, pl.ds(2 * (c + 1) * own, own)]).T.astype(BF16)
        for d in range(per_chunk):
            put_message(packed, c * per_chunk + d, back[d * slots : (d + 1) * slots])


def message_shape(slots, pad):
    compact = BLOCK < pad <= BLOCK + BLOCK // 2 and slots % 32 == 0
    return (slots + slots // 2, BLOCK) if compact else (slots, pad)


def put_message(packed, d, rows):
    slots, pad = rows.shape
    if packed.shape[1:] == (slots, pad):
        packed[d] = rows
        return
    half, tail = slots // 2, pad - BLOCK
    packed[d, :slots, :] = rows[:, :BLOCK]
    filler = jnp.zeros((half, BLOCK // 2 - tail), BF16)
    packed[d, slots:, :] = jnp.concatenate([rows[:half, BLOCK:], filler, rows[half:, BLOCK:], filler], axis=1)


def take_message(packed, d, landed):
    slots, pad = landed.shape[0] // packed.shape[0], landed.shape[1]
    if packed.shape[1:] == (slots, pad):
        landed[pl.ds(d * slots, slots), :] = packed[d]
        return
    half, tail = slots // 2, pad - BLOCK
    landed[pl.ds(d * slots, slots), :BLOCK] = packed[d, :slots, :]
    landed[pl.ds(d * slots, half), BLOCK:] = packed[d, slots:, :tail]
    landed[pl.ds(d * slots + half, half), BLOCK:] = packed[d, slots:, BLOCK // 2 : BLOCK // 2 + tail]


def backward_kernel(parts, groups, ids, turned, pick, a_ref, slope, left, landed, *refs):
    weights = refs[:groups]
    out, rows = refs[groups:]
    own = turned.shape[1]
    units = slope.shape[2]
    pad = turned.shape[0]
    step = left.shape[0] // 2
    base = 2 * step * groups
    for d in range(landed.shape[0]):
        take_message(landed, d, rows)
    high, low = halves(mm(turned[...], a_ref[:, :own]) + mm_tn(rows[...], pick[...]))
    wide = jnp.concatenate([turned[...], high, low], axis=0).T
    for k in range(groups):
        group = lax.rem(ids[0] + groups - k, groups)
        w_neigh = weights[k][pl.ds(base + pad, pad), :]
        total = mm(wide, jnp.concatenate([weights[k][pl.ds(base, pad), :], w_neigh, w_neigh], axis=0))
        result = mm(left[...], (total * slope[k]).astype(BF16))
        if parts:
            for i in range(units // BLOCK):
                out[group * (units // BLOCK) + i] = result[:, i * BLOCK : (i + 1) * BLOCK]
        else:
            out[:, pl.ds(pl.multiple_of(group * units, units), units)] = result


def quarter(p, rows):
    height = rows // 4
    return slice(p // 2 * height, (p // 2 + 1) * height), slice(p % 2 * BLOCK, (p % 2 + 1) * BLOCK)


def join_kernel(side, grads, second, other, out, total):
    step = grads.shape[1]
    height = total.shape[0] // 4
    total[...] = second[side[0]] + other[side[0]]
    for p in range(grads.shape[0]):
        out[p, :step, :] = grads[p]
        out[p, step : step + height, :] = total[quarter(p, total.shape[0])]
        out[p, step + height :, :] = jnp.zeros((out.shape[1] - step - height, BLOCK), F32)


def sum_kernel(step, height, pieces, out):
    first = pieces[0, :step, :]
    second = [pieces[0, step : step + height, :], pieces[1, step : step + height, :]]
    for p in range(1, pieces.shape[0]):
        first = first + pieces[p, :step, :]
        if p > 1:
            second[p % 2] = second[p % 2] + pieces[p, step : step + height, :]
    for p in range(pieces.shape[0]):
        out[p, :step, :] = first
        out[p, step : step + height, :] = second[0]
        out[p, step + height :, :] = second[1]


def place_kernel(class_count, node_total, pieces, self1, neigh1, self2, neigh2, loss, both):
    step = self1.shape[0]
    units = self2.shape[1]
    height = both.shape[1] // 4
    for p in range(pieces.shape[0]):
        at = pl.ds(p * BLOCK, BLOCK)
        self1[:, at] = pieces[p, :step, :]
        neigh1[:, at] = pieces[p, step : 2 * step, :]
        rows, lanes = quarter(p, both.shape[1])
        both[0, rows, lanes] = pieces[p, 2 * step : 2 * step + height, :]
        both[1, rows, lanes] = pieces[p, 2 * step + height :, :]
    self2[...] = both[0, :class_count, :]
    neigh2[...] = both[1, :class_count, :]
    loss[...] = both[0, class_count : class_count + 1, 0:1] / node_total


def swap(value, count):
    blocks = value.reshape(count, -1, value.shape[-1])
    return lax.all_to_all(blocks, "node", 0, 0, tiled=True)


def gather_shifted(value, count):
    return [value] + [lax.ppermute(value, "feat", [(i, (i + k) % count) for i in range(count)]) for k in range(1, count)]


def shards(features, send_rows, send_count, tile_src, tile_val, labels, w_self1, w_neigh1, w_self2, w_neigh2):
    nodes, groups = lax.axis_size("node"), lax.axis_size("feat")
    own, step = features.shape
    slots = send_rows.shape[2]
    halo = nodes * slots
    total_src = own + halo
    cols = step * groups
    width = w_self1.shape[1]
    units, classes = w_self2.shape
    pad = -(-(classes + 1) // 16) * 16
    parts = nodes if nodes == 8 and units == 2 * BLOCK and width == nodes * BLOCK else 0
    node_total = own * nodes
    grad_scale = 1.0 / math.sqrt(node_total)
    ids = lax.axis_index("feat").astype(jnp.int32).reshape(1)
    side = (lax.axis_index("node") & 1).astype(jnp.int32).reshape(1)
    blocks = own // BLOCK
    packed_rows = 2 * step * groups + 2 * pad

    turned = features.T
    turned_all = [turned] + [lax.ppermute(turned, "feat", [(i, i ^ k) for i in range(groups)]) for k in range(1, groups)]
    (a_mat,) = call(
        prepare_kernel,
        [((own, 2 * total_src), BF16)],
        (tile_src, tile_val),
        [(tile_val.shape, BF16), ((own, total_src), F32)],
        copies=blocks + 1,
        moved=tile_val.size * 4,
        grant=54 * 2**20 - 4 * own * total_src - 3 * 10**5,
    )
    a_mat, *pairs = lax.optimization_barrier((a_mat, w_self1, w_neigh1, w_self2.T, w_neigh2.T))
    (packed_weights,) = call(weights_kernel, [((packed_rows, units), BF16)], pairs)
    packed_weights, ids, side, *turned_all = lax.optimization_barrier((packed_weights, ids, side, *turned_all))
    weights = gather_shifted(packed_weights, groups)
    pick, full, packed = call(
        functools.partial(pack_kernel, groups),
        [((halo, own), BF16), ((own, cols), BF16), ((halo, cols), BF16)],
        (ids, send_count, send_rows[0], *turned_all),
        [((cols, own), BF16)],
        flops=2 * halo * own * cols,
        moved=halo * own * 2,
    )
    source = swap(packed, nodes).reshape(halo, cols)
    state, packed, left = call(
        first_kernel,
        [((total_src, 2 * cols), BF16), ((halo, cols), BF16), ((2 * step, own), BF16)],
        (pick, a_mat, full, source, turned),
        flops=4 * own * total_src * cols,
        moved=4 * own * total_src,
    )
    packed, ids, side, *weights = lax.optimization_barrier((packed, ids, side, *weights))
    landed = swap(packed, nodes).reshape(halo, cols)
    message = (nodes, *message_shape(slots, pad))
    turned_grads, slope, packed, second = call(
        functools.partial(forward_kernel, classes, grad_scale, groups),
        [((pad, own), BF16), ((groups, own, units), F32), (message, BF16), ((2, pad, units), F32)],
        (ids, a_mat, state, landed, labels.reshape(1, own), *weights),
        flops=8 * own * total_src * width,
        moved=16 * own * width,
    )
    if parts:
        other = lax.ppermute(second, "node", [(i, i ^ 1) for i in range(nodes)])
    landed = swap(packed, nodes)
    (grads,) = call(
        functools.partial(backward_kernel, parts, groups),
        [((parts, 2 * step, BLOCK) if parts else (2 * step, width), F32)],
        (ids, turned_grads, pick, a_mat, slope, left, landed, *weights),
        [((halo, pad), BF16)],
    )
    if not parts:
        grads, second = lax.psum((grads, second), "node")
        loss = second[0, classes, 0] / node_total
        return (loss, grads[:step], grads[step:], second[0, :classes].T, second[1, :classes].T)
    height = pad // 4
    grads, other = lax.optimization_barrier((grads, other))
    (grads,) = call(
        join_kernel,
        [((nodes, -(-(2 * step + height) // 8) * 8, BLOCK), F32)],
        (side, grads, second, other),
        [((pad, units), F32)],
    )
    grads = swap(grads, nodes)
    (grads,) = call(functools.partial(sum_kernel, 2 * step, height), [((nodes, 2 * step + 2 * height, BLOCK), F32)], (grads,))
    grads = swap(grads, nodes)
    grad_self1, grad_neigh1, grad_self2, grad_neigh2, loss = call(
        functools.partial(place_kernel, classes, node_total),
        [((step, width), F32)] * 2 + [((classes, units), F32)] * 2 + [((1, 1), F32)],
        (grads,),
        [((2, pad, units), F32)],
    )
    return (loss.reshape(()), grad_self1, grad_neigh1, grad_self2.T, grad_neigh2.T)


def solution(mesh):
    in_specs = (
        P("node", "feat"),
        P("node", None, None),
        P("node", None),
        P("node", None),
        P("node", None, None, None),
        P("node"),
        P("feat", None),
        P("feat", None),
        P("feat", None),
        P("feat", None),
    )
    out_specs = (P(), P("feat", None), P("feat", None), P("feat", None), P("feat", None))
    return jax.shard_map(shards, mesh=mesh, in_specs=in_specs, out_specs=out_specs, check_vma=False)
```

```python
import functools
import math

import jax
import jax.numpy as jnp
from jax import lax
from jax.experimental import pallas as pl
from jax.experimental.pallas import tpu as pltpu
from jax.sharding import PartitionSpec as P

BLOCK = 128
F32 = jnp.float32
BF16 = jnp.bfloat16
VMEM = pl.BlockSpec(memory_space=pltpu.VMEM)
HBM = pl.BlockSpec(memory_space=pltpu.HBM)
SMEM = pl.BlockSpec(memory_space=pltpu.SMEM)


def mm(a, b):
    return lax.dot_general(a, b, (((1,), (0,)), ((), ())), preferred_element_type=F32)


def mm_tn(a, b):
    return lax.dot_general(a, b, (((0,), (0,)), ((), ())), preferred_element_type=F32)


def halves(value):
    high = value.astype(BF16)
    return high, (value - high.astype(F32)).astype(BF16)


def spread(a, rows):
    own = a.shape[0]
    parts = []
    for c in range(rows.shape[0] // own):
        part = rows[c * own : (c + 1) * own]
        parts += [part, part]
    return mm(a, jnp.concatenate(parts, axis=0))


def activate(v, with_slope):
    scale = math.sqrt(2.0 / math.pi)
    square = v * v
    t = jnp.tanh(v * (scale + (scale * 0.044715) * square))
    half = 0.5 * v
    out = (half + half * t).astype(BF16)
    if not with_slope:
        return out
    return out, (0.5 + 0.5 * t) + half * (1.0 - t * t) * (scale + (scale * 3 * 0.044715) * square)


def size_of(shape, dtype):
    rows = -(-shape[-2] // 16) * 16 if len(shape) > 1 else 1
    return math.prod(shape[:-2]) * rows * (-(-shape[-1] // 128) * 128) * jnp.dtype(dtype).itemsize


def call(body, outs, args, scratch=(), copies=0, flops=0, moved=0, grant=0):
    specs = [SMEM if arg.dtype == jnp.int32 and arg.size < 512 else VMEM for arg in args]
    if copies:
        specs = [HBM] * len(args)
    room = sum(size_of(shape, dtype) for shape, dtype in [*outs, *scratch])
    room += sum(size_of(arg.shape, arg.dtype) for arg, spec in zip(args, specs) if spec is VMEM)
    return pl.pallas_call(
        body,
        out_shape=[jax.ShapeDtypeStruct(shape, dtype) for shape, dtype in outs],
        in_specs=specs,
        out_specs=[VMEM] * len(outs),
        scratch_shapes=[pltpu.VMEM(shape, dtype) for shape, dtype in scratch]
        + ([pltpu.SemaphoreType.DMA((copies,)), pltpu.SMEM(args[0].shape, jnp.int32)] if copies else []),
        compiler_params=pltpu.CompilerParams(vmem_limit_bytes=grant or min(room + 8 * 2**20, 56 * 2**20)),
        cost_estimate=pl.CostEstimate(flops=flops, bytes_accessed=moved, transcendentals=0),
    )(*args)


def prepare_kernel(src_in, tile_val, a_ref, tiles, dense, sems, tile_src):
    blocks, per_block = tile_val.shape[0], tile_val.shape[1]
    own = blocks * BLOCK
    src_copy = pltpu.make_async_copy(src_in, tile_src, sems.at[blocks])
    src_copy.start()
    copies = [pltpu.make_async_copy(tile_val.at[b], tiles.at[b], sems.at[b]) for b in range(blocks)]
    for copy in copies:
        copy.start()
    dense[...] = jnp.zeros_like(dense)
    src_copy.wait()
    for b in range(blocks):
        rows = pl.ds(b * BLOCK, BLOCK)
        copies[b].wait()

        def add(k, _, b=b, rows=rows):
            at = pl.ds(pl.multiple_of(tile_src[b, k] * BLOCK, BLOCK), BLOCK)
            dense[rows, at] = dense[rows, at] + tiles[b, k].astype(F32)
            return 0

        lax.fori_loop(0, per_block, add, 0)
        for c in range(dense.shape[1] // own):
            high, low = halves(dense[rows, pl.ds(c * own, own)])
            a_ref[rows, pl.ds(2 * c * own, own)] = high
            a_ref[rows, pl.ds((2 * c + 1) * own, own)] = low


def weights_kernel(w_self1, w_neigh1, w_self2, w_neigh2, weights):
    step, units = w_self1.shape[0], weights.shape[1]
    groups = w_self1.shape[1] // units
    classes = w_self2.shape[0]
    base = 2 * step * groups
    pad = (weights.shape[0] - base) // 2
    for j in range(groups):
        at = pl.ds(j * units, units)
        weights[pl.ds(2 * step * j, step), :] = w_self1[:, at]
        weights[pl.ds(2 * step * j + step, step), :] = w_neigh1[:, at]
    weights[pl.ds(base, 2 * pad), :] = jnp.zeros((2 * pad, units), BF16)
    weights[pl.ds(base, classes), :] = w_self2[...]
    weights[pl.ds(base + pad, classes), :] = w_neigh2[...]


def pack_kernel(groups, ids, count, send_rows, *refs):
    pieces, (pick, full, packed), (turned,) = refs[:groups], refs[groups : groups + 3], refs[groups + 3 :]
    step, own = pieces[0].shape
    dests, slots = send_rows.shape
    columns = send_rows[...].astype(F32).T
    row_id = lax.broadcasted_iota(jnp.int32, (slots, own), 1).astype(F32)
    slot_id = lax.broadcasted_iota(jnp.int32, (slots, own), 0)
    for d in range(dests):
        hit = (columns[:, d : d + 1] == row_id) & (slot_id < count[0, d])
        pick[pl.ds(d * slots, slots), :] = jnp.where(hit, 1.0, 0.0).astype(BF16)
    turned[:step] = pieces[0][...]
    for k in range(1, groups):
        place = lax.rem(ids[0] + groups - jnp.bitwise_xor(ids[0], k), groups)
        turned[pl.ds(pl.multiple_of(place * step, step), step), :] = pieces[k][...]
    full[...] = turned[...].T
    packed[...] = mm(pick[...], full[...]).astype(BF16)


def first_kernel(pick, a_ref, full, source, state, packed):
    own, cols = full.shape
    total = spread(a_ref[:, : 2 * own], full[...]) + spread(a_ref[:, 2 * own :], source[...])
    agg = total.astype(BF16)
    packed[...] = mm(pick[...], agg).astype(BF16)
    state[:own, :cols] = full[...]
    state[:own, cols:] = agg
    state[own:, :cols] = source[...]


def forward_kernel(
    class_count, grad_scale, groups, ids, a_ref, state, landed, labels, *refs
):
    weights = refs[:groups]
    turned, slope, packed, second = refs[groups:]
    halo, cols = landed.shape
    own = state.shape[0] - halo
    units = weights[0].shape[1]
    step = cols // groups
    base = 2 * step * groups
    pad = turned.shape[0]
    slots = halo // packed.shape[0]
    near = state[:own, :]
    total = jnp.zeros((own, pad), F32)
    for k in range(groups):
        group = lax.rem(ids[0] + groups - k, groups)
        begin = [pl.multiple_of(2 * step * group + part * step, step) for part in (0, 1)]
        w_one = jnp.concatenate([w[pl.ds(at, step), :] for at in begin for w in weights], axis=0)
        out, slope[k] = activate(mm(near, w_one), True)
        if halo == own:
            both = jnp.concatenate([state[own:, :cols], landed[...]], axis=1)
            far = activate(mm(both, w_one), False)
            held = spread(a_ref[...], jnp.concatenate([out, far], axis=0))
        else:

            def one(r, held, w_one=w_one):
                rows = pl.ds(pl.multiple_of(r * own, own), own)
                srcs = pl.ds(pl.multiple_of(2 * (r + 1) * own, own), 2 * own)
                lower = pl.ds(pl.multiple_of((r + 1) * own, own), own)
                both = jnp.concatenate([state[lower, :cols], landed[rows, :]], axis=1)
                return held + spread(a_ref[:, srcs], activate(mm(both, w_one), False))

            held = lax.fori_loop(0, halo // own, one, spread(a_ref[:, : 2 * own], out))
        rounded = held.astype(BF16)
        if k == 0:
            mine, agg_mine = out, rounded
        w_self, w_neigh = weights[k][pl.ds(base, pad), :].T, weights[k][pl.ds(base + pad, pad), :].T
        total = total + mm(jnp.concatenate([out, rounded], axis=1), jnp.concatenate([w_self, w_neigh], axis=0))
    total = total.T
    class_id = lax.broadcasted_iota(jnp.int32, total.shape, 0)
    real = class_id < class_count
    top = jnp.max(jnp.where(real, total, -jnp.inf), axis=0, keepdims=True)
    shifted = total - top
    powers = jnp.where(real, jnp.exp(shifted), 0.0)
    sums = jnp.sum(powers, axis=0, keepdims=True)
    target = (class_id == labels[...]).astype(F32)
    turned[...] = ((powers / sums - target) * grad_scale).astype(BF16)
    row_loss = jnp.log(sums) - jnp.sum(shifted * target, axis=0, keepdims=True)
    own_grads = mm(turned[...], mine)
    row = lax.broadcasted_iota(jnp.int32, own_grads.shape, 0)
    own_grads = jnp.where(row == class_count, jnp.sum(row_loss, axis=1, keepdims=True), own_grads)
    second[0] = own_grads
    second[1] = mm(turned[...], agg_mine)
    per_chunk = own // slots
    for c in range(halo // own):
        back = mm(turned[...], a_ref[:, pl.ds(2 * (c + 1) * own, own)]).T.astype(BF16)
        for d in range(per_chunk):
            put_message(packed, c * per_chunk + d, back[d * slots : (d + 1) * slots])


def message_shape(slots, pad):
    compact = BLOCK < pad <= BLOCK + BLOCK // 2 and slots % 32 == 0
    return (slots + slots // 2, BLOCK) if compact else (slots, pad)


def put_message(packed, d, rows):
    slots, pad = rows.shape
    if packed.shape[1:] == (slots, pad):
        packed[d] = rows
        return
    half, tail = slots // 2, pad - BLOCK
    packed[d, :slots, :] = rows[:, :BLOCK]
    filler = jnp.zeros((half, BLOCK // 2 - tail), BF16)
    packed[d, slots:, :] = jnp.concatenate([rows[:half, BLOCK:], filler, rows[half:, BLOCK:], filler], axis=1)


def take_message(packed, d, landed):
    slots, pad = landed.shape[0] // packed.shape[0], landed.shape[1]
    if packed.shape[1:] == (slots, pad):
        landed[pl.ds(d * slots, slots), :] = packed[d]
        return
    half, tail = slots // 2, pad - BLOCK
    landed[pl.ds(d * slots, slots), :BLOCK] = packed[d, :slots, :]
    landed[pl.ds(d * slots, half), BLOCK:] = packed[d, slots:, :tail]
    landed[pl.ds(d * slots + half, half), BLOCK:] = packed[d, slots:, BLOCK // 2 : BLOCK // 2 + tail]


def backward_kernel(parts, groups, ids, turned, pick, a_ref, slope, features, state, landed, *refs):
    weights = refs[:groups]
    out, rows = refs[groups:]
    own = turned.shape[1]
    units = slope.shape[2]
    pad = turned.shape[0]
    step = features.shape[0]
    base = 2 * step * groups
    for d in range(landed.shape[0]):
        take_message(landed, d, rows)
    high, low = halves(mm(turned[...], a_ref[:, :own]) + mm_tn(rows[...], pick[...]))
    wide = jnp.concatenate([turned[...], high, low], axis=0).T
    cols = state.shape[1] // 2
    left = jnp.concatenate([features[...], state[:own, cols:].T[:step]], axis=0)
    for k in range(groups):
        group = lax.rem(ids[0] + groups - k, groups)
        w_neigh = weights[k][pl.ds(base + pad, pad), :]
        total = mm(wide, jnp.concatenate([weights[k][pl.ds(base, pad), :], w_neigh, w_neigh], axis=0))
        result = mm(left, (total * slope[k]).astype(BF16))
        if parts:
            for i in range(units // BLOCK):
                out[group * (units // BLOCK) + i] = result[:, i * BLOCK : (i + 1) * BLOCK]
        else:
            out[:, pl.ds(pl.multiple_of(group * units, units), units)] = result


def quarter(p, rows):
    height = rows // 4
    return slice(p // 2 * height, (p // 2 + 1) * height), slice(p % 2 * BLOCK, (p % 2 + 1) * BLOCK)


def join_kernel(side, grads, second, other, out, total):
    step = grads.shape[1]
    height = total.shape[0] // 4
    total[...] = second[side[0]] + other[side[0]]
    for p in range(grads.shape[0]):
        out[p, :step, :] = grads[p]
        out[p, step : step + height, :] = total[quarter(p, total.shape[0])]
        out[p, step + height :, :] = jnp.zeros((out.shape[1] - step - height, BLOCK), F32)


def sum_kernel(step, height, pieces, out):
    first = pieces[0, :step, :]
    second = [pieces[0, step : step + height, :], pieces[1, step : step + height, :]]
    for p in range(1, pieces.shape[0]):
        first = first + pieces[p, :step, :]
        if p > 1:
            second[p % 2] = second[p % 2] + pieces[p, step : step + height, :]
    for p in range(pieces.shape[0]):
        out[p, :step, :] = first
        out[p, step : step + height, :] = second[0]
        out[p, step + height :, :] = second[1]


def place_kernel(class_count, node_total, pieces, self1, neigh1, self2, neigh2, loss, both):
    step = self1.shape[0]
    units = self2.shape[1]
    height = both.shape[1] // 4
    for p in range(pieces.shape[0]):
        at = pl.ds(p * BLOCK, BLOCK)
        self1[:, at] = pieces[p, :step, :]
        neigh1[:, at] = pieces[p, step : 2 * step, :]
        rows, lanes = quarter(p, both.shape[1])
        both[0, rows, lanes] = pieces[p, 2 * step : 2 * step + height, :]
        both[1, rows, lanes] = pieces[p, 2 * step + height :, :]
    self2[...] = both[0, :class_count, :]
    neigh2[...] = both[1, :class_count, :]
    loss[...] = both[0, class_count : class_count + 1, 0:1] / node_total


def swap(value, count):
    blocks = value.reshape(count, -1, value.shape[-1])
    return lax.all_to_all(blocks, "node", 0, 0, tiled=True)


def gather_shifted(value, count):
    return [value] + [lax.ppermute(value, "feat", [(i, (i + k) % count) for i in range(count)]) for k in range(1, count)]


def shards(features, send_rows, send_count, tile_src, tile_val, labels, w_self1, w_neigh1, w_self2, w_neigh2):
    nodes, groups = lax.axis_size("node"), lax.axis_size("feat")
    own, step = features.shape
    slots = send_rows.shape[2]
    halo = nodes * slots
    total_src = own + halo
    cols = step * groups
    width = w_self1.shape[1]
    units, classes = w_self2.shape
    pad = -(-(classes + 1) // 16) * 16
    parts = nodes if nodes == 8 and units == 2 * BLOCK and width == nodes * BLOCK else 0
    node_total = own * nodes
    grad_scale = 1.0 / math.sqrt(node_total)
    ids = lax.axis_index("feat").astype(jnp.int32).reshape(1)
    side = (lax.axis_index("node") & 1).astype(jnp.int32).reshape(1)
    blocks = own // BLOCK
    packed_rows = 2 * step * groups + 2 * pad

    turned = features.T
    turned_all = [turned] + [lax.ppermute(turned, "feat", [(i, i ^ k) for i in range(groups)]) for k in range(1, groups)]
    (a_mat,) = call(
        prepare_kernel,
        [((own, 2 * total_src), BF16)],
        (tile_src, tile_val),
        [(tile_val.shape, BF16), ((own, total_src), F32)],
        copies=blocks + 1,
        moved=tile_val.size * 4,
        grant=54 * 2**20 - 4 * own * total_src - 3 * 10**5,
    )
    a_mat, *pairs = lax.optimization_barrier((a_mat, w_self1, w_neigh1, w_self2.T, w_neigh2.T))
    (packed_weights,) = call(weights_kernel, [((packed_rows, units), BF16)], pairs)
    packed_weights, ids, side, *turned_all = lax.optimization_barrier((packed_weights, ids, side, *turned_all))
    weights = gather_shifted(packed_weights, groups)
    pick, full, packed = call(
        functools.partial(pack_kernel, groups),
        [((halo, own), BF16), ((own, cols), BF16), ((halo, cols), BF16)],
        (ids, send_count, send_rows[0], *turned_all),
        [((cols, own), BF16)],
        flops=2 * halo * own * cols,
        moved=halo * own * 2,
    )
    source = swap(packed, nodes).reshape(halo, cols)
    state, packed = call(
        first_kernel,
        [((total_src, 2 * cols), BF16), ((halo, cols), BF16)],
        (pick, a_mat, full, source),
        flops=4 * own * total_src * cols,
        moved=4 * own * total_src,
    )
    packed, ids, side, *weights = lax.optimization_barrier((packed, ids, side, *weights))
    landed = swap(packed, nodes).reshape(halo, cols)
    message = (nodes, *message_shape(slots, pad))
    turned_grads, slope, packed, second = call(
        functools.partial(forward_kernel, classes, grad_scale, groups),
        [((pad, own), BF16), ((groups, own, units), F32), (message, BF16), ((2, pad, units), F32)],
        (ids, a_mat, state, landed, labels.reshape(1, own), *weights),
        flops=8 * own * total_src * width,
        moved=16 * own * width,
    )
    if parts:
        other = lax.ppermute(second, "node", [(i, i ^ 1) for i in range(nodes)])
    landed = swap(packed, nodes)
    (grads,) = call(
        functools.partial(backward_kernel, parts, groups),
        [((parts, 2 * step, BLOCK) if parts else (2 * step, width), F32)],
        (ids, turned_grads, pick, a_mat, slope, turned, state, landed, *weights),
        [((halo, pad), BF16)],
    )
    if not parts:
        grads, second = lax.psum((grads, second), "node")
        loss = second[0, classes, 0] / node_total
        return (loss, grads[:step], grads[step:], second[0, :classes].T, second[1, :classes].T)
    height = pad // 4
    grads, other = lax.optimization_barrier((grads, other))
    (grads,) = call(
        join_kernel,
        [((nodes, -(-(2 * step + height) // 8) * 8, BLOCK), F32)],
        (side, grads, second, other),
        [((pad, units), F32)],
    )
    grads = swap(grads, nodes)
    (grads,) = call(functools.partial(sum_kernel, 2 * step, height), [((nodes, 2 * step + 2 * height, BLOCK), F32)], (grads,))
    grads = swap(grads, nodes)
    grad_self1, grad_neigh1, grad_self2, grad_neigh2, loss = call(
        functools.partial(place_kernel, classes, node_total),
        [((step, width), F32)] * 2 + [((classes, units), F32)] * 2 + [((1, 1), F32)],
        (grads,),
        [((2, pad, units), F32)],
    )
    return (loss.reshape(()), grad_self1, grad_neigh1, grad_self2.T, grad_neigh2.T)


def solution(mesh):
    in_specs = (
        P("node", "feat"),
        P("node", None, None),
        P("node", None),
        P("node", None),
        P("node", None, None, None),
        P("node"),
        P("feat", None),
        P("feat", None),
        P("feat", None),
        P("feat", None),
    )
    out_specs = (P(), P("feat", None), P("feat", None), P("feat", None), P("feat", None))
    return jax.shard_map(shards, mesh=mesh, in_specs=in_specs, out_specs=out_specs, check_vma=False)
```
